32 devices in a mesh: lat: 4 (over y, x), lon: 8 (over z, core).
Axes of the slice: x: 2, y: 2, z: 4, core: 2. Of those that a mesh axis runs over, the one named last changes fastest.
Arguments:
- model_state: float32 [5, 4, 3584, 1024], P(None, None, 'lon', 'lat'), may hold values from -6 to 6
- diffusion: float32 [2, 1024], P(None, 'lat'), may hold values from 0.02 to 0.24
- coupling: float32 [4, 5, 5], replicated, may hold values from -2.5 to 2.5
- cutoff: int32 [256], replicated, may hold values from 1 to 896, as said below
- strip_list: int32 [256, 4], P(('lat', 'lon')), may hold values from 0 to 447, as said below
- nest_place: int32 [32, 8, 2], P(('lat', 'lon')), may hold values from 0 to 1872
Outputs:
- advanced_state: float32 [5, 4, 3584, 1024], P(None, None, 'lon', 'lat')
- nest_boundary: float32 [32, 5, 4, 2048], P(('lat', 'lon'))
The draws below stay inside these ranges and needn't reach their ends.
Inputs may be any that keep to these rules, and one draw needn't show every extreme that they name: cutoff[b] is the number of kept wavenumbers of band row b; the values 1 and 896 both occur. `strip_list`: in the 8 rows of one device: column 0 names an owner (an index of lon) and no owner is named by more than 2 of these rows; at every index of lat some owner is named by exactly 2 rows of every device of that index. Column 1 is a longitude column within the device's block (below 448), column 2 a row offset within the block (at most 240), column 3 a length of 1 to 16; every device has a strip of length 16.
All inputs are finite; a program needn't handle non-finite values.
Results may differ from the reference program's by a relative error of at most 0.0001.
Values sent between devices are 32-bit elements; how exact they have to be, the bound alone decides.
No kernel may reach another device: no remote copies, remote signals or barrier semaphores. Data moves between devices by JAX's collectives and lax.ppermute only.
A program may use at most 384 MiB of HBM per device.

```python
import math
import jax
import jax.numpy as jnp
from jax import lax

NLON = 3584
FIELDS = 5
LEVELS = 4
LAT_DEV = 256
POLAR = 128
CAP = 2
STRIP = 16
RATIO = 11
NB = 2048
LON_DEV = 448
NLAT = 1024
KC = 896
SLOTS = 8
N_LAT = 4
N_LON = 8


def draw_cutoff(key, part):
    value_key, place_key = jax.random.split(key)
    strip_values = jax.random.randint(value_key, (2 * POLAR,), 1, KC + 1)
    places = jax.random.permutation(place_key, 2 * POLAR)
    index_line = jnp.arange(2 * POLAR)
    strip_values = jnp.where(index_line == places[0], KC, strip_values)
    strip_values = jnp.where(index_line == places[1], 1, strip_values)
    return strip_values.astype(jnp.int32)


def draw_strip_list(key, part):
    sources = N_LAT * N_LON
    lon_block = NLON // N_LON
    hot_key, source_key, column_key, offset_key, length_key, longest_key = jax.random.split(key, 6)
    hottest = jax.random.randint(hot_key, (N_LAT,), 0, N_LON)
    hot_each = jnp.repeat(hottest, N_LON)

    def one_source(source_seed, hot_owner):
        pick_key, order_key = jax.random.split(source_seed)
        others = (hot_owner + 1 + jnp.arange((N_LON - 1) * CAP) // CAP) % N_LON
        chosen = jax.random.permutation(pick_key, others)[:SLOTS - CAP]
        owners = jnp.concatenate([jnp.zeros((CAP,), jnp.int32) + hot_owner, chosen.astype(jnp.int32)])
        return jax.random.permutation(order_key, owners)
    owners = jax.vmap(one_source)(jax.random.split(source_key, sources), hot_each)
    columns = jax.random.randint(column_key, (sources, SLOTS), 0, lon_block)
    offsets = jax.random.randint(offset_key, (sources, SLOTS), 0, LAT_DEV - STRIP + 1)
    lengths = jax.random.randint(length_key, (sources, SLOTS), 1, STRIP + 1)
    longest = jax.random.randint(longest_key, (sources, 1), 0, SLOTS)
    lengths = jnp.where(jnp.arange(SLOTS)[None, :] == longest, STRIP, lengths)
    stacked = jnp.stack([owners.astype(jnp.int32), columns.astype(jnp.int32), offsets.astype(jnp.int32), lengths.astype(jnp.int32)], axis=-1)
    return stacked.reshape(sources * SLOTS, 4).astype(jnp.int32)


def set_ends(result, own_key, low, high):
    index_at = [jax.random.randint(jax.random.fold_in(own_key, axis), (), 0, length) for axis, length in enumerate(result.shape)]
    main_axis = result.shape.index(max(result.shape))
    next_to = index_at[:main_axis] + [(index_at[main_axis] + 1) % result.shape[main_axis]] + index_at[main_axis + 1:]
    return result.at[tuple(index_at)].set(low).at[tuple(next_to)].set(high)


def shard_levels(own_key, shape, cuts, least, high):
    def one(dim, blocks):
        heights = jax.random.uniform(jax.random.fold_in(jax.random.fold_in(own_key, 6), dim), (blocks,), jnp.float32, least / len(cuts), high / len(cuts))
        return jnp.repeat(jnp.exp(heights), shape[dim] // blocks).reshape((-1,) + (1,) * (len(shape) - dim - 1))

    level = one(*cuts[0])
    for cut in cuts[1:]:
        level = level * one(*cut)
    return level


def centred(rng, shape, width, bound, pieces=(), kind=jnp.bfloat16):
    gain = shard_levels(rng, shape, pieces, -0.22, 0.18) if pieces else 1.0
    array = jax.random.normal(rng, shape, jnp.float32) * width * gain
    return jnp.minimum(jnp.maximum(array, -bound), bound).astype(kind)


def setup_inputs(seed: int = 0) -> dict:
    splits = jax.random.split(jax.random.key(seed), 7)
    return {
        "model_state": centred(splits[0], (FIELDS, LEVELS, NLON, NLAT), 1.0, 6.0, ((2, 8), (3, 4)), jnp.float32),
        "diffusion": jnp.clip(jnp.exp(math.log(0.24) - 2.4849066 * jax.random.uniform(splits[1], (2, NLAT), jnp.float32) ** shard_levels(splits[1], (2, NLAT), ((1, 4),), -0.2, 0.2)), 0.02, 0.24),
        "coupling": centred(splits[2], (LEVELS, FIELDS, FIELDS), FIELDS ** -0.5, 2.5, (), jnp.float32),
        "cutoff": draw_cutoff(jax.random.fold_in(splits[6], 71), 0),
        "strip_list": draw_strip_list(jax.random.fold_in(splits[6], 71), 0),
        "nest_place": set_ends(jax.random.randint(splits[5], (N_LAT * N_LON, N_LON, CAP), 0, NB - STRIP * RATIO + 1), jax.random.fold_in(splits[5], 1), 0, NB - STRIP * RATIO).astype(jnp.int32),
    }


def nest_forcing(updated, strip_list, nest_place):
    top_wavenumber_kept = lax.Precision.HIGHEST
    lists = strip_list.reshape(N_LAT, N_LON, SLOTS, 4)
    lat_ids = jnp.arange(N_LAT, dtype=jnp.int32)[:, None, None]
    lon_ids = jnp.arange(N_LON, dtype=jnp.int32)[None, :, None]
    owners = lists[..., 0]
    columns = (lon_ids * LON_DEV + lists[..., 1]).astype(jnp.int32)
    offsets = (lat_ids * LAT_DEV + lists[..., 2]).astype(jnp.int32)
    lengths = lists[..., 3]
    zero = jnp.zeros((), jnp.int32)

    def cut_strip(column, offset):
        return lax.dynamic_slice(updated, (zero, zero, column, offset), (FIELDS, LEVELS, 1, STRIP))[:, :, 0, :]

    boundary_strips = jax.vmap(cut_strip)(columns.reshape(-1), offsets.reshape(-1))
    positions = jnp.arange(STRIP, dtype=jnp.int32)
    boundary_strips = jnp.where(positions[None, None, None, :] < lengths.reshape(-1)[:, None, None, None], boundary_strips, 0.0)
    slot_ids = jnp.arange(SLOTS, dtype=jnp.int32)
    earlier = slot_ids[None, :] < slot_ids[:, None]
    same = owners[..., :, None] == owners[..., None, :]
    rank = jnp.sum((same & earlier).astype(jnp.int32), axis=-1)
    owner_rows = (lat_ids * N_LON + owners).astype(jnp.int32)
    begins = nest_place[owner_rows, jnp.broadcast_to(lon_ids, owners.shape), rank]
    nest_points = jnp.arange(STRIP * RATIO, dtype=jnp.int32)
    filter_table = jnp.maximum(RATIO - jnp.abs(nest_points[None, :] - positions[:, None] * RATIO), 0).astype(jnp.float32) / RATIO
    sources = N_LAT * N_LON
    boundary_strips = boundary_strips.reshape(sources, SLOTS, FIELDS, LEVELS, STRIP)
    owner_rows = owner_rows.reshape(sources, SLOTS)
    begins = begins.reshape(sources, SLOTS)

    def add_source(strip_index, total):
        strip_values = jnp.einsum("icvj,jk->ikcv", boundary_strips[strip_index], filter_table, precision=top_wavenumber_kept)
        return total.at[owner_rows[strip_index][:, None], begins[strip_index][:, None] + nest_points[None, :]].add(strip_values)

    total = lax.fori_loop(0, sources, add_source, jnp.zeros((sources, NB, FIELDS, LEVELS), jnp.float32))
    return jnp.transpose(total, (0, 2, 3, 1))


def reference(model_state, diffusion, coupling, cutoff, strip_list, nest_place):
    top_wavenumber_kept = lax.Precision.HIGHEST
    east = jnp.roll(model_state, -1, axis=2)
    west = jnp.roll(model_state, 1, axis=2)
    padded = jnp.pad(model_state, ((0, 0), (0, 0), (0, 0), (1, 1)))
    blended = jnp.einsum("lfg,glij->flij", coupling, model_state, precision=top_wavenumber_kept)
    updated = model_state + diffusion[0] * (east + west - 2.0 * model_state) + diffusion[1] * (padded[..., :-2] + padded[..., 2:] - 2.0 * model_state) + blended
    rows = jnp.concatenate([updated[..., :POLAR], updated[..., NLAT - POLAR:]], axis=3)
    spectrum = jnp.fft.rfft(rows, axis=2)
    wavenumber = jnp.arange(NLON // 2 + 1, dtype=jnp.int32)[:, None]
    spectrum = jnp.where(wavenumber < cutoff[None, :], spectrum, 0.0)
    filtered = jnp.fft.irfft(spectrum, n=NLON, axis=2).astype(updated.dtype)
    advanced_state = updated.at[..., :POLAR].set(filtered[..., :POLAR])
    advanced_state = advanced_state.at[..., NLAT - POLAR:].set(filtered[..., POLAR:])
    boundary = nest_forcing(updated, strip_list, nest_place)
    return advanced_state, boundary
```

```python
import functools
import math

import jax
import jax.numpy as jnp
import numpy as np
from jax import lax
from jax.experimental import pallas as pl
from jax.experimental.pallas import tpu as pltpu
from jax.sharding import PartitionSpec as P

POLAR = 128
CAP = 2
STRIP = 16
RATIO = 11
NB = 2048
KC = 896
NEAR_RANK = 15
FAR_RANK = 5
LANES = 2 * POLAR
VMEM_LIMIT = 48 * 1024 * 1024
F32 = jnp.float32
BF16 = jnp.bfloat16


def ceil8(value):
    return -(-value // 8) * 8


def split_table(table):
    high = table.astype(jnp.bfloat16)
    low = (table - high.astype(np.float64)).astype(jnp.bfloat16)
    return high, low


@functools.lru_cache(maxsize=None)
def filter_tables(count, width):
    total = count * width
    place = np.arange(width)
    difference = place[:, None] - place[None, :]
    sine = np.sin(np.pi * difference / total) * total
    near = np.where(difference == 0, 0.0, 1.0 / np.where(difference == 0, 1.0, sine))
    ranks, senders, receivers = [], [], []
    for shift in range(1, count):
        signed = shift if shift <= count // 2 else shift - count
        block = 1.0 / (np.sin(np.pi * (signed * width + difference) / total) * total)
        left, values, right = np.linalg.svd(block)
        rank = NEAR_RANK if abs(signed) == 1 else FAR_RANK
        root = np.sqrt(values[:rank])
        padded = ceil8(rank)
        sender = np.zeros((padded, width))
        sender[:rank] = right[:rank] * root[:, None]
        receiver = np.zeros((width, padded))
        receiver[:, :rank] = left[:, :rank] * root[None, :]
        ranks.append(rank)
        senders.append(sender)
        receivers.append(receiver)
    return (
        tuple(ranks),
        split_table(near),
        split_table(np.concatenate(senders, axis=0)),
        split_table(np.concatenate(receivers, axis=1)),
    )


def split_value(value):
    high = value.astype(BF16)
    return high, (value - high.astype(F32)).astype(BF16)


def table_dot(high, low, value):
    value_high, value_low = split_value(value)
    return (
        jnp.dot(high, value_high, preferred_element_type=F32)
        + jnp.dot(high, value_low, preferred_element_type=F32)
        + jnp.dot(low, value_high, preferred_element_type=F32)
    )


def edge_kernel(state, first, last, north, south):
    fields, _, columns, rows = state.shape
    lane = lax.broadcasted_iota(jnp.int32, (columns, 128), 1)
    first[...] = jnp.zeros(first.shape, F32)
    last[...] = jnp.zeros(last.shape, F32)
    edges = jnp.zeros((columns, 128), F32)
    for f in range(fields):
        first[0, f : f + 1, :] = state[f, 0, 0:1, :]
        last[0, f : f + 1, :] = state[f, 0, columns - 1 : columns, :]
        edges = jnp.where(lane == f, state[f, 0, :, 0:1], edges)
        edges = jnp.where(lane == 8 + f, state[f, 0, :, rows - 1 : rows], edges)
    turned = edges.T
    north[0] = turned[0:8]
    south[0] = turned[8:16]


def stencil_kernel(
    ranks,
    meta,
    coupling,
    strips,
    state,
    west_halo,
    east_halo,
    north_halo,
    south_halo,
    diffusion,
    cosine,
    sine,
    send_high,
    send_low,
    updated,
    *rest,
):
    payloads = rest[: len(ranks)]
    own, placed, rows_cut = rest[len(ranks) :]
    level = pl.program_id(0)
    fields, _, columns, rows = state.shape
    step = 16
    lane = lax.broadcasted_iota(jnp.int32, (step, rows), 1)
    along = jnp.broadcast_to(diffusion[0:1, :], (step, rows))
    across = jnp.broadcast_to(diffusion[1:2, :], (step, rows))
    centre = 1.0 - 2.0 * along - 2.0 * across
    halo = jnp.concatenate(
        [north_halo[0], south_halo[0], jnp.zeros((112, columns), F32)], axis=0
    ).T
    weights = [[coupling[level, f * fields + g] for g in range(fields)] for f in range(fields)]
    for begin in range(0, columns, step):
        end = begin + step
        here = [state[f, 0, begin:end, :] for f in range(fields)]
        for f in range(fields):
            if begin == 0:
                west = jnp.concatenate(
                    [west_halo[0, f : f + 1, :], state[f, 0, 0 : step - 1, :]], axis=0
                )
            else:
                west = state[f, 0, begin - 1 : end - 1, :]
            if end == columns:
                east = jnp.concatenate(
                    [state[f, 0, begin + 1 : end, :], east_halo[0, f : f + 1, :]], axis=0
                )
            else:
                east = state[f, 0, begin + 1 : end + 1, :]
            north = jnp.where(
                lane == 0, halo[begin:end, f : f + 1], pltpu.roll(here[f], 1, 1)
            )
            south = jnp.where(
                lane == rows - 1,
                halo[begin:end, 8 + f : 9 + f],
                pltpu.roll(here[f], rows - 1, 1),
            )
            result = centre * here[f] + along * (east + west) + across * (north + south)
            for g in range(fields):
                result = result + weights[f][g] * here[g]
            updated[f, 0, begin:end, :] = result

    lon_index = meta[2]
    slots = strips.shape[0]
    shifts = len(ranks) + 1
    placed[...] = jnp.zeros(placed.shape, F32)
    rows_cut[...] = jnp.zeros(rows_cut.shape, F32)
    strip_lane = lax.broadcasted_iota(jnp.int32, (8, LANES), 1)
    owners = [strips[s, 0] for s in range(slots)]
    for s in range(slots):
        column, offset, length = strips[s, 1], strips[s, 2], strips[s, 3]
        rank = jnp.int32(0)
        for earlier in range(s):
            rank = rank + (owners[earlier] == owners[s]).astype(jnp.int32)
        for f in range(fields):
            rows_cut[f : f + 1, :] = updated[f, 0, pl.ds(column, 1), :]
        base = (lon_index * CAP + rank) * STRIP
        moved = pltpu.roll(rows_cut[...], lax.rem(base - offset + 2 * rows, rows), 1)
        inside = (strip_lane >= base) & (strip_lane < base + length)
        shift = lax.rem(owners[s] - lon_index + shifts, shifts)
        placed[shift] = placed[shift] + jnp.where(inside, moved, 0.0)
    own[0] = placed[0]

    start = pl.multiple_of(meta[0] * POLAR, POLAR)
    for f in range(fields):
        row = updated[f, 0, :, pl.ds(start, POLAR)]
        value = jnp.concatenate([row * cosine[...], row * sine[...]], axis=1)
        sent = table_dot(send_high[...], send_low[...], value)
        place = 0
        for payload, rank in zip(payloads, ranks):
            payload[0, f * rank : (f + 1) * rank, :] = sent[place : place + rank, :]
            place += ceil8(rank)
    for index, (payload, rank) in enumerate(zip(payloads, ranks)):
        payload[0, fields * rank : fields * (rank + 1), :] = placed[index + 1][0:fields, :]


def near_kernel(meta, rows, cosine, sine, middle, near_high, near_low, out):
    @pl.when(meta[1] == 1)
    def _():
        for f in range(rows.shape[0]):
            row = rows[f, 0]
            value = jnp.concatenate([row * cosine[...], row * sine[...]], axis=1)
            total = table_dot(near_high[...], near_low[...], value)
            out[f, 0] = (
                sine[...] * total[:, :POLAR]
                - cosine[...] * total[:, POLAR:]
                + middle[0:1, :] * row
            )

    @pl.when(meta[1] == 0)
    def _():
        out[...] = rows[...]


def far_kernel(ranks, meta, rows, cosine, sine, turn, far_high, far_low, own, begins, *rest):
    payloads = rest[: len(ranks)]
    out, boundary, arrived, hats = rest[len(ranks) :]
    level = pl.program_id(0)
    fields = rows.shape[0]

    @pl.when(level == 0)
    def _():
        point = lax.broadcasted_iota(jnp.int32, hats.shape, 1)
        place = lax.broadcasted_iota(jnp.int32, hats.shape, 0) % STRIP
        offset = point - begins[:, 0:1]
        hat = jnp.maximum(RATIO - jnp.abs(offset - place * RATIO), 0)
        hat = jnp.where((offset >= 0) & (offset < STRIP * RATIO), hat, 0)
        hats[...] = hat.astype(F32).astype(BF16)
        arrived[...] = jnp.zeros(arrived.shape, F32)

    pieces = own[0][0:fields, :]
    for payload, rank in zip(payloads, ranks):
        pieces = pieces + payload[0, fields * rank : fields * (rank + 1), :]
    high, rest_of = split_value(pieces)
    middle, low = split_value(pieces - high.astype(F32))
    del rest_of
    total = (
        jnp.dot(high, hats[...], preferred_element_type=F32)
        + jnp.dot(middle, hats[...], preferred_element_type=F32)
        + jnp.dot(low, hats[...], preferred_element_type=F32)
    ) * (1.0 / RATIO)
    for f in range(fields):
        boundary[0, f, pl.ds(level, 1), :] = total[f : f + 1, :]

    @pl.when(meta[1] == 1)
    def _():
        for f in range(fields):
            place = 0
            for index, (payload, rank) in enumerate(zip(payloads, ranks)):
                cosines = payload[0, f * rank : (f + 1) * rank, :POLAR]
                sines = payload[0, f * rank : (f + 1) * rank, POLAR:]
                turn_cos = turn[index : index + 1, :POLAR]
                turn_sin = turn[index : index + 1, POLAR:]
                arrived[place : place + rank, :POLAR] = turn_cos * cosines + turn_sin * sines
                arrived[place : place + rank, POLAR:] = turn_cos * sines - turn_sin * cosines
                place += ceil8(rank)
            value = table_dot(far_high[...], far_low[...], arrived[...])
            out[f, 0] = (
                rows[f, 0] + sine[...] * value[:, :POLAR] - cosine[...] * value[:, POLAR:]
            )

    @pl.when(meta[1] == 0)
    def _():
        out[...] = rows[...]


def ring(count, shift):
    return [(i, (i + shift) % count) for i in range(count)]


def phase_table(kept, steps, period):
    phase = (2 * kept - 1)[None, :] * steps[:, None] % (2 * period)
    angle = phase.astype(F32) * (math.pi / period)
    return jnp.cos(angle), jnp.sin(angle)


def compressed(model_state, diffusion, coupling, cutoff, strip_list, nest_place):
    lat_index = lax.axis_index("lat")
    lon_index = lax.axis_index("lon")
    lat_count = lax.axis_size("lat")
    lon_count = lax.axis_size("lon")
    fields, levels, columns, rows = model_state.shape
    total_columns = columns * lon_count
    ranks, near, send, receive = filter_tables(lon_count, columns)
    params = pltpu.CompilerParams(vmem_limit_bytes=VMEM_LIMIT)

    is_south = lat_index == lat_count - 1
    is_polar = (lat_index == 0) | is_south
    part = jnp.where(is_south, rows // POLAR - 1, 0)
    meta = jnp.stack([part, is_polar.astype(jnp.int32), lon_index]).astype(jnp.int32)
    kept = jnp.where(lat_index < lat_count // 2, cutoff[:POLAR], cutoff[POLAR:])
    cosine, sine = phase_table(kept, jnp.arange(columns, dtype=jnp.int32), total_columns)
    turn = jnp.concatenate(
        phase_table(kept, jnp.arange(1, lon_count, dtype=jnp.int32), lon_count), axis=1
    )
    turn = jnp.pad(turn, ((0, ceil8(lon_count - 1) - (lon_count - 1)), (0, 0)))
    sign = np.ones((ceil8(lon_count - 1), 1), np.float32)
    sign[lon_count // 2 : lon_count - 1] = -1.0
    turn = turn * sign
    middle = ((2 * kept - 1).astype(F32) / total_columns)[None, :]

    whole = lambda *shape: pl.BlockSpec(shape, lambda l, *_: (0,) * len(shape))
    by_level = lambda *shape: pl.BlockSpec((1,) + shape, lambda l, *_: (l,) + (0,) * len(shape))
    state_spec = pl.BlockSpec((fields, 1, columns, rows), lambda l, *_: (0, l, 0, 0))
    polar_spec = pl.BlockSpec((fields, 1, columns, POLAR), lambda l, m: (0, l, 0, m[0]))
    smem = pl.BlockSpec(memory_space=pltpu.SMEM)

    with jax.named_scope("edges"):
        first, last, north, south = pl.pallas_call(
            edge_kernel,
            grid=(levels,),
            in_specs=[state_spec],
            out_specs=[by_level(8, rows)] * 2 + [by_level(8, columns)] * 2,
            out_shape=[jax.ShapeDtypeStruct((levels, 8, rows), F32)] * 2
            + [jax.ShapeDtypeStruct((levels, 8, columns), F32)] * 2,
            compiler_params=params,
        )(model_state)

    with jax.named_scope("halo"):
        west_halo = lax.ppermute(last, "lon", ring(lon_count, 1))
        east_halo = lax.ppermute(first, "lon", ring(lon_count, -1))
        north_halo = lax.ppermute(south, "lat", [(i, i + 1) for i in range(lat_count - 1)])
        south_halo = lax.ppermute(north, "lat", [(i + 1, i) for i in range(lat_count - 1)])

    payload_rows = [ceil8(fields * (rank + 1)) for rank in ranks]
    send_rows = send[0].shape[0]
    with jax.named_scope("stencil"):
        updated, *outgoing = pl.pallas_call(
            functools.partial(stencil_kernel, ranks),
            grid_spec=pltpu.PrefetchScalarGridSpec(
                num_scalar_prefetch=1,
                grid=(levels,),
                in_specs=[
                    smem,
                    smem,
                    state_spec,
                    by_level(8, rows),
                    by_level(8, rows),
                    by_level(8, columns),
                    by_level(8, columns),
                    whole(2, rows),
                    whole(columns, POLAR),
                    whole(columns, POLAR),
                    whole(send_rows, columns),
                    whole(send_rows, columns),
                ],
                out_specs=[state_spec]
                + [by_level(size, LANES) for size in payload_rows]
                + [by_level(8, LANES)],
                scratch_shapes=[
                    pltpu.VMEM((lon_count, 8, LANES), F32),
                    pltpu.VMEM((8, rows), F32),
                ],
            ),
            out_shape=[jax.ShapeDtypeStruct(model_state.shape, F32)]
            + [jax.ShapeDtypeStruct((levels, size, LANES), F32) for size in payload_rows]
            + [jax.ShapeDtypeStruct((levels, 8, LANES), F32)],
            compiler_params=params,
        )(
            meta,
            coupling.reshape(levels, fields * fields),
            strip_list,
            model_state,
            west_halo,
            east_halo,
            north_halo,
            south_halo,
            diffusion,
            cosine,
            sine,
            *[jnp.asarray(table) for table in send],
        )
    own = outgoing.pop()

    with jax.named_scope("exchange"):
        incoming = [
            lax.ppermute(payload, "lon", ring(lon_count, shift + 1))
            for shift, payload in enumerate(outgoing)
        ]

    with jax.named_scope("near"):
        passes = 3 * 2 * 2 * fields * levels * columns * columns * POLAR
        advanced = pl.pallas_call(
            near_kernel,
            grid_spec=pltpu.PrefetchScalarGridSpec(
                num_scalar_prefetch=1,
                grid=(levels,),
                in_specs=[
                    polar_spec,
                    whole(columns, POLAR),
                    whole(columns, POLAR),
                    whole(1, POLAR),
                    whole(columns, columns),
                    whole(columns, columns),
                ],
                out_specs=polar_spec,
            ),
            out_shape=jax.ShapeDtypeStruct(model_state.shape, F32),
            input_output_aliases={1: 0},
            compiler_params=params,
            cost_estimate=pl.CostEstimate(
                flops=passes,
                bytes_accessed=8 * fields * levels * columns * POLAR,
                transcendentals=0,
            ),
        )(meta, updated, cosine, sine, middle, *[jnp.asarray(table) for table in near])

    with jax.named_scope("far"):
        sources = lon_count * CAP * STRIP
        begins = jnp.broadcast_to(
            jnp.repeat(nest_place.reshape(-1), STRIP)[:, None], (sources, 128)
        )
        advanced, boundary = pl.pallas_call(
            functools.partial(far_kernel, ranks),
            grid_spec=pltpu.PrefetchScalarGridSpec(
                num_scalar_prefetch=1,
                grid=(levels,),
                in_specs=[
                    polar_spec,
                    whole(columns, POLAR),
                    whole(columns, POLAR),
                    whole(*turn.shape),
                    whole(columns, send_rows),
                    whole(columns, send_rows),
                    by_level(8, LANES),
                    whole(sources, 128),
                ]
                + [by_level(size, LANES) for size in payload_rows],
                out_specs=[polar_spec, whole(1, fields, levels, NB)],
                scratch_shapes=[
                    pltpu.VMEM((send_rows, LANES), F32),
                    pltpu.VMEM((sources, NB), BF16),
                ],
            ),
            out_shape=[
                jax.ShapeDtypeStruct(model_state.shape, F32),
                jax.ShapeDtypeStruct((1, fields, levels, NB), F32),
            ],
            input_output_aliases={1: 0},
            compiler_params=params,
        )(
            meta,
            advanced,
            cosine,
            sine,
            turn,
            *[jnp.asarray(table) for table in receive],
            own,
            begins,
            *incoming,
        )
    return advanced, boundary


def padded_2(block, sides, width):
    for axis, dim in sides:
        count = lax.axis_size(axis)
        forward = [(i, i + 1) for i in range(count - 1)]
        forward.append((count - 1, 0))
        backward = [(target, source) for source, target in forward]
        low = lax.ppermute(
            lax.slice_in_dim(block, block.shape[dim] - width, None, axis=dim), axis, forward
        )
        high = lax.ppermute(lax.slice_in_dim(block, 0, width, axis=dim), axis, backward)
        block = jnp.concatenate([low, block, high], axis=dim)
    return block


def spectral_filter(rows, kept):
    top_wavenumber_kept = lax.Precision.HIGHEST
    length = rows.shape[3]
    width = math.gcd(KC, 128)
    column_grid = lax.broadcasted_iota(jnp.int32, (length, width), 0)
    step_output = jnp.zeros_like(rows)
    for block_index in range(KC // width):
        wavenumber = block_index * width + lax.broadcasted_iota(jnp.int32, (length, width), 1)
        phase = column_grid * wavenumber % length
        angle = phase.astype(jnp.float32) * (2.0 * math.pi / length)
        cosine = jnp.cos(angle)
        sine = jnp.sin(angle)
        along = block_index * width + jnp.arange(width, dtype=jnp.int32)
        scale = jnp.where(along == 0, 1.0 / length, 2.0 / length)
        weight = jnp.where(along[None, :] < kept[:, None], scale[None, :], 0.0)
        real_part = (
            jnp.einsum("flrn,nk->flrk", rows, cosine, precision=top_wavenumber_kept) * weight
        )
        imaginary_component = (
            jnp.einsum("flrn,nk->flrk", rows, sine, precision=top_wavenumber_kept) * weight
        )
        step_output = (
            step_output
            + jnp.einsum("flrk,nk->flrn", real_part, cosine, precision=top_wavenumber_kept)
            + jnp.einsum("flrk,nk->flrn", imaginary_component, sine, precision=top_wavenumber_kept)
        )
    return step_output


def polar_pass(work_rows, kept_start, kept_table):
    count = work_rows.shape[2] // lax.axis_size("lon")
    kept = lax.dynamic_slice_in_dim(kept_table, kept_start + lax.axis_index("lon") * count, count)
    return lax.all_to_all(
        spectral_filter(
            lax.all_to_all(work_rows, "lon", split_axis=2, concat_axis=3, tiled=True), kept
        ),
        "lon",
        split_axis=3,
        concat_axis=2,
        tiled=True,
    )


def transposed(model_state, diffusion, coupling, cutoff, strip_list, nest_place):
    top_wavenumber_kept = lax.Precision.HIGHEST
    lat_index = lax.axis_index("lat")
    lat_count = lax.axis_size("lat")
    lon_count = lax.axis_size("lon")
    fields, levels, lon_local, lat_local = model_state.shape
    padded = padded_2(model_state, (("lat", 3), ("lon", 2)), 1)
    east_west = padded[:, :, 2:, 1:-1] + padded[:, :, :-2, 1:-1]
    row_place = lax.broadcasted_iota(jnp.int32, (1, 1, 1, lat_local), 3)
    northern = jnp.where((lat_index == 0) & (row_place == 0), 0.0, padded[:, :, 1:-1, :-2])
    southern = jnp.where(
        (lat_index == lat_count - 1) & (row_place == lat_local - 1), 0.0, padded[:, :, 1:-1, 2:]
    )
    blended = jnp.einsum("lfg,glij->flij", coupling, model_state, precision=top_wavenumber_kept)
    updated = (
        model_state
        + diffusion[0] * (east_west - 2.0 * model_state)
        + diffusion[1] * (northern + southern - 2.0 * model_state)
        + blended
    )
    is_south = lat_index == lat_count - 1
    is_polar = (lat_index == 0) | is_south
    start = jnp.where(is_south, lat_local - POLAR, 0).astype(jnp.int32)
    band_base = jnp.where(lat_index < lat_count // 2, 0, POLAR).astype(jnp.int32)
    block_rows = lax.dynamic_slice_in_dim(updated, start, POLAR, 3)
    polar_rows = jnp.transpose(block_rows, (0, 1, 3, 2))
    filtered = polar_pass(polar_rows, band_base, cutoff)
    new_rows = jnp.where(is_polar, jnp.transpose(filtered, (0, 1, 3, 2)), block_rows)
    advanced_state = lax.dynamic_update_slice_in_dim(updated, new_rows, start, 3)
    slots = strip_list.shape[0]
    owners = strip_list[:, 0]
    columns = strip_list[:, 1]
    offsets = strip_list[:, 2]
    lengths = strip_list[:, 3]
    zero = jnp.zeros((), jnp.int32)

    def cut_strip(column, offset):
        return lax.dynamic_slice(
            updated, (zero, zero, column, offset), (fields, levels, 1, STRIP)
        ).reshape(fields * levels, STRIP)

    boundary_strips = jax.vmap(cut_strip)(columns, offsets)
    inside = lax.broadcasted_iota(jnp.int32, (1, 1, STRIP), 2) < lengths[:, None, None]
    boundary_strips = jnp.where(inside, boundary_strips, 0.0).reshape(
        slots, fields * levels * STRIP
    )
    slot_ids = jnp.arange(slots, dtype=jnp.int32)
    earlier = slot_ids[None, :] < slot_ids[:, None]
    same = owners[:, None] == owners[None, :]
    rank = jnp.sum((same & earlier).astype(jnp.int32), axis=1)
    target = owners * CAP + rank
    routing = (jnp.arange(lon_count * CAP, dtype=jnp.int32)[:, None] == target[None, :]).astype(
        jnp.float32
    )
    outgoing = jnp.dot(
        routing, boundary_strips, precision=top_wavenumber_kept, preferred_element_type=jnp.float32
    ).reshape(lon_count, CAP, fields * levels * STRIP)
    arrived = lax.all_to_all(outgoing, "lon", split_axis=0, concat_axis=0, tiled=True)
    total = lon_count * CAP
    group = math.gcd(total, 16)
    pieces = arrived.reshape(total // group, group, fields * levels, STRIP)
    starts = nest_place.reshape(total // group, group)
    point = lax.broadcasted_iota(jnp.int32, (1, 1, NB), 2)
    row_step = lax.broadcasted_iota(jnp.int32, (1, STRIP, 1), 1) * RATIO

    def accumulate(carry, item):
        piece, begin = item
        offset = point - begin[:, None, None]
        hat = jnp.maximum(RATIO - jnp.abs(offset - row_step), 0)
        hat = (
            jnp.where((offset >= 0) & (offset < STRIP * RATIO), hat, 0).astype(jnp.float32) / RATIO
        )
        return (carry + jnp.einsum("gat,gtp->ap", piece, hat, precision=top_wavenumber_kept), None)

    boundary = lax.scan(
        accumulate, jnp.zeros((fields * levels, NB), jnp.float32), (pieces, starts)
    )[0]
    return (advanced_state, boundary.reshape(1, fields, levels, NB))


def local(model_state, *others):
    columns = model_state.shape[2]
    fits = lax.axis_size("lon") * CAP * STRIP == LANES and model_state.shape[3] == LANES
    if fits and columns % 16 == 0 and columns >= 8 * NEAR_RANK:
        return compressed(model_state, *others)
    return transposed(model_state, *others)


def solution(mesh):
    return jax.shard_map(
        local,
        mesh=mesh,
        in_specs=(
            P(None, None, "lon", "lat"),
            P(None, "lat"),
            P(),
            P(),
            P(("lat", "lon"), None),
            P(("lat", "lon"), None, None),
        ),
        out_specs=(P(None, None, "lon", "lat"), P(("lat", "lon"), None, None, None)),
        check_vma=False,
    )
```

```python
import functools
import math

import jax
import jax.numpy as jnp
import numpy as np
from jax import lax
from jax.experimental import pallas as pl
from jax.experimental.pallas import tpu as pltpu
from jax.sharding import PartitionSpec as P

POLAR = 128
CAP = 2
STRIP = 16
RATIO = 11
NB = 2048
KC = 896
RANK = 24
STEP = 32
VMEM_LIMIT = 48 * 1024 * 1024
F32 = jnp.float32
BF16 = jnp.bfloat16


def ceil8(value):
    return -(-value // 8) * 8


def split_table(table):
    high = table.astype(jnp.bfloat16)
    low = (table - high.astype(np.float64)).astype(jnp.bfloat16)
    return high, low


@functools.lru_cache(maxsize=None)
def filter_tables(count, width):
    total = count * width
    place = np.arange(width)
    difference = place[:, None] - place[None, :]
    sine = np.sin(np.pi * difference / total) * total
    near = np.where(difference == 0, 0.0, 1.0 / np.where(difference == 0, 1.0, sine))
    blocks = []
    for shift in range(1, count):
        signed = shift if shift <= count // 2 else shift - count
        blocks.append(1.0 / (np.sin(np.pi * (signed * width + difference) / total) * total))
    basis = np.linalg.svd(np.concatenate(blocks, axis=0), full_matrices=False)[2][:RANK]
    receivers = np.concatenate([block @ basis.T for block in blocks], axis=1)
    near_high, near_low = split_table(near)
    send_high, send_low = split_table(basis)
    far_high, far_low = split_table(receivers)
    return (
        np.concatenate([near_high, near_high, near_low], axis=1),
        np.concatenate([send_high, send_low], axis=0),
        np.concatenate([far_high, far_high, far_low], axis=1),
    )


def split_value(value):
    high = value.astype(BF16)
    return high, (value - high.astype(F32)).astype(BF16)


def modulated(row, cosine, sine):
    return jnp.concatenate([row * cosine[...], row * sine[...]], axis=1)


def stacked(value):
    high, low = split_value(value)
    return jnp.concatenate([high, low, high], axis=0)


def lon_edge_kernel(low, high, first, last):
    first[...] = jnp.zeros(first.shape, F32)
    last[...] = jnp.zeros(last.shape, F32)
    for f in range(low.shape[0]):
        first[0, f : f + 1, :] = low[f, 0, 0:1, :]
        last[0, f : f + 1, :] = high[f, 0, 7:8, :]


def lat_edge_kernel(state, north, south):
    fields, _, columns, rows = state.shape
    lane = lax.broadcasted_iota(jnp.int32, (columns, 128), 1)
    edges = jnp.zeros((columns, 128), F32)
    for f in range(fields):
        edges = jnp.where(lane == f, state[f, 0, :, 0:1], edges)
        edges = jnp.where(lane == 8 + f, state[f, 0, :, rows - 1 : rows], edges)
    turned = edges.T
    north[0] = turned[0:8]
    south[0] = turned[8:16]


def half_stencil(part, weights, state, west_halo, east_halo, diffusion, halo, store):
    fields, _, columns, _ = state.shape
    mine = pl.ds(pl.multiple_of(part * POLAR, POLAR), POLAR)
    other = pl.ds(pl.multiple_of((1 - part) * POLAR, POLAR), POLAR)
    lane = lax.broadcasted_iota(jnp.int32, (STEP, POLAR), 1)
    along = jnp.broadcast_to(diffusion[0:1, mine], (STEP, POLAR))
    across = jnp.broadcast_to(diffusion[1:2, mine], (STEP, POLAR))
    centre = 1.0 - 2.0 * along - 2.0 * across
    inner = lane == (1 - part) * (POLAR - 1)
    turn = jnp.where(part == 0, POLAR - 1, 1)
    lowest, highest = lane == 0, lane == POLAR - 1
    for begin in range(0, columns, STEP):
        end = begin + STEP
        here = [state[f, 0, begin:end, mine] for f in range(fields)]
        for f in range(fields):
            if begin == 0:
                west = jnp.concatenate(
                    [west_halo[0, f : f + 1, mine], state[f, 0, 0 : end - 1, mine]], axis=0
                )
            else:
                west = state[f, 0, begin - 1 : end - 1, mine]
            if end == columns:
                east = jnp.concatenate(
                    [state[f, 0, begin + 1 : end, mine], east_halo[0, f : f + 1, mine]], axis=0
                )
            else:
                east = state[f, 0, begin + 1 : end + 1, mine]
            edge = pltpu.roll(state[f, 0, begin:end, other], turn, 1)
            outer = 0.0 if halo is None else halo[begin:end, f : f + 1]
            edge = jnp.where(inner, edge, outer)
            north = jnp.where(lowest, edge, pltpu.roll(here[f], 1, 1))
            south = jnp.where(highest, edge, pltpu.roll(here[f], POLAR - 1, 1))
            result = centre * here[f] + along * (east + west) + across * (north + south)
            for g in range(fields):
                result = result + weights[f][g] * here[g]
            store(f, begin, end, result)


def coupling_at(coupling, level, fields):
    return [[coupling[level, f * fields + g] for g in range(fields)] for f in range(fields)]


def polar_kernel(
    meta, coupling, state, west_halo, east_halo, diffusion, cosine, sine, send, updated, sent
):
    fields = state.shape[0]
    weights = coupling_at(coupling, pl.program_id(0), fields)

    def store(f, begin, end, result):
        updated[f, 0, begin:end, :] = result

    half_stencil(meta[0], weights, state, west_halo, east_halo, diffusion, None, store)
    for f in range(fields):
        high, low = split_value(modulated(updated[f, 0], cosine, sine))
        both = jnp.dot(send[...], high, preferred_element_type=F32)
        cross = jnp.dot(send[0:RANK, :], low, preferred_element_type=F32)
        sent[0, f * RANK : (f + 1) * RANK, :] = both[:RANK] + both[RANK:] + cross


def rest_kernel(
    meta,
    coupling,
    strips,
    state,
    polar,
    west_halo,
    east_halo,
    north_halo,
    south_halo,
    diffusion,
    advanced,
    cut,
    halo,
    rows_cut,
):
    fields, _, columns, rows = state.shape
    part = meta[0]
    weights = coupling_at(coupling, pl.program_id(0), fields)
    halo[...] = jnp.concatenate(
        [north_halo[0], south_halo[0], jnp.zeros((112, columns), F32)], axis=0
    ).T
    outer = pltpu.roll(halo[...], jnp.where(part == 0, 120, 0), 1)

    def store(f, begin, end, result):
        advanced[f, 0, begin:end, :] = result

    half_stencil(1 - part, weights, state, west_halo, east_halo, diffusion, outer, store)

    slots = strips.shape[0]
    cut[...] = jnp.zeros(cut.shape, F32)
    rows_cut[...] = jnp.zeros(rows_cut.shape, F32)
    lane = lax.broadcasted_iota(jnp.int32, (8, POLAR), 1)
    corner = (lane[0:1] == 0) & (part == 0)
    owners = [strips[s, 0] for s in range(slots)]
    for s in range(slots):
        column, offset, length = strips[s, 1], strips[s, 2], strips[s, 3]
        rank = jnp.int32(0)
        for earlier in range(s):
            rank = rank + (owners[earlier] == owners[s]).astype(jnp.int32)
        beyond = halo[pl.ds(column, 1), :] * diffusion[1:2, 0:1]
        for f in range(fields):
            missing = jnp.where(corner, pltpu.roll(beyond, (POLAR - f) % POLAR, 1), 0.0)
            inside = polar[f, 0, pl.ds(column, 1), :] + missing
            outside = advanced[f, 0, pl.ds(column, 1), :]
            rows_cut[f : f + 1, 0:POLAR] = jnp.where(part == 0, inside, outside)
            rows_cut[f : f + 1, POLAR:] = jnp.where(part == 0, outside, inside)
        base = owners[s] * STRIP
        moved = pltpu.roll(rows_cut[...], lax.rem(base - offset + rows, rows), 1)[:, 0:POLAR]
        within = (lane >= base) & (lane < base + length)
        place = pl.ds(pl.multiple_of(rank * 8, 8), 8)
        cut[0, place, :] = cut[0, place, :] + jnp.where(within, moved, 0.0)


def near_kernel(meta, rows, north_halo, diffusion, cosine, sine, middle, near, out):
    fields, _, columns, _ = rows.shape

    @pl.when(meta[1] == 1)
    def _():
        for f in range(fields):
            row = rows[f, 0]
            value = stacked(modulated(row, cosine, sine))
            total = jnp.dot(near[...], value, preferred_element_type=F32)
            out[f, 0] = (
                sine[...] * total[:, :POLAR]
                - cosine[...] * total[:, POLAR:]
                + middle[0:1, :] * row
            )

    @pl.when(meta[1] == 0)
    def _():
        halo = jnp.concatenate([north_halo[0], jnp.zeros((120, columns), F32)], axis=0).T
        lowest = lax.broadcasted_iota(jnp.int32, (columns, POLAR), 1) == 0
        for f in range(fields):
            beyond = halo[:, f : f + 1] * diffusion[1:2, 0:POLAR]
            out[f, 0] = rows[f, 0] + jnp.where(lowest, beyond, 0.0)


def far_kernel(shifts, meta, held, rows, cosine, sine, turn, far, *rest):
    del held
    incoming = rest[:shifts]
    out, arrived = rest[shifts:]
    fields = rows.shape[0]

    @pl.when(meta[1] == 1)
    def _():
        for f in range(fields):
            for index in range(shifts):
                cosines = incoming[index][0, 0, f * RANK : (f + 1) * RANK, :POLAR]
                sines = incoming[index][0, 0, f * RANK : (f + 1) * RANK, POLAR:]
                turn_cos = turn[index : index + 1, :POLAR]
                turn_sin = turn[index : index + 1, POLAR:]
                place = slice(index * RANK, (index + 1) * RANK)
                arrived[place, :POLAR] = turn_cos * cosines + turn_sin * sines
                arrived[place, POLAR:] = turn_cos * sines - turn_sin * cosines
            total = jnp.dot(far[...], stacked(arrived[...]), preferred_element_type=F32)
            out[f, 0] = rows[f, 0] + sine[...] * total[:, :POLAR] - cosine[...] * total[:, POLAR:]

    @pl.when(meta[1] == 0)
    def _():
        out[...] = rows[...]


def boundary_kernel(meta, cut, begins, boundary):
    sources, levels = cut.shape[0:2]
    fields = boundary.shape[1]
    lane = lax.broadcasted_iota(jnp.int32, (8, POLAR), 1)
    home = meta[2] * STRIP
    pieces = []
    for l in range(levels):
        groups = []
        for group in range(sources * CAP * STRIP // POLAR):
            piece = jnp.zeros((8, POLAR), F32)
            for index in range(POLAR // STRIP):
                source, rank = divmod(group * (POLAR // STRIP) + index, CAP)
                place = index * STRIP
                moved = pltpu.roll(
                    cut[source, l, rank * 8 : rank * 8 + 8, :],
                    lax.rem(place - home + POLAR, POLAR),
                    1,
                )
                piece = jnp.where((lane >= place) & (lane < place + STRIP), moved, piece)
            groups.append(piece)
        pieces.append(jnp.concatenate(groups, axis=1))
    pieces = jnp.concatenate(pieces, axis=0)
    shape = (sources * CAP * STRIP, NB)
    offset = lax.broadcasted_iota(jnp.int32, shape, 1) - begins[:, 0:1]
    place = lax.broadcasted_iota(jnp.int32, shape, 0) % STRIP
    hat = jnp.maximum(RATIO - jnp.abs(offset - place * RATIO), 0)
    hat = jnp.where((offset >= 0) & (offset < STRIP * RATIO), hat, 0)
    hat = hat.astype(F32).astype(BF16)
    high = pieces.astype(BF16)
    middle, low = split_value(pieces - high.astype(F32))
    total = jnp.dot(
        jnp.concatenate([high, middle, low], axis=0), hat, preferred_element_type=F32
    )
    size = levels * 8
    total = (total[:size] + total[size : 2 * size] + total[2 * size :]) * (1.0 / RATIO)
    for l in range(levels):
        for f in range(fields):
            boundary[0, f, l : l + 1, :] = total[l * 8 + f : l * 8 + f + 1, :]


def ring(count, shift):
    return [(i, (i + shift) % count) for i in range(count)]


def phase_table(kept, steps, period):
    phase = (2 * kept - 1)[None, :] * steps[:, None] % (2 * period)
    angle = phase.astype(F32) * (math.pi / period)
    return jnp.cos(angle), jnp.sin(angle)


def cost(flops, bytes_accessed):
    return pl.CostEstimate(flops=flops, bytes_accessed=bytes_accessed, transcendentals=0)


def compressed(model_state, diffusion, coupling, cutoff, strip_list, nest_place):
    lat_index = lax.axis_index("lat")
    lon_index = lax.axis_index("lon")
    lat_count = lax.axis_size("lat")
    lon_count = lax.axis_size("lon")
    fields, levels, columns, rows = model_state.shape
    total_columns = columns * lon_count
    shifts = lon_count - 1
    near, send, far = [jnp.asarray(table) for table in filter_tables(lon_count, columns)]
    params = pltpu.CompilerParams(vmem_limit_bytes=VMEM_LIMIT)
    shape = lambda *sizes: jax.ShapeDtypeStruct(sizes, F32)
    half_bytes = 4 * fields * levels * columns * POLAR

    is_south = lat_index == lat_count - 1
    is_polar = (lat_index == 0) | is_south
    part = jnp.where(is_south, rows // POLAR - 1, 0)
    meta = jnp.stack([part, is_polar.astype(jnp.int32), lon_index]).astype(jnp.int32)
    kept = jnp.where(lat_index < lat_count // 2, cutoff[:POLAR], cutoff[POLAR:])
    cosine, sine = phase_table(kept, jnp.arange(columns, dtype=jnp.int32), total_columns)
    turn = jnp.concatenate(
        phase_table(kept, jnp.arange(1, lon_count, dtype=jnp.int32), lon_count), axis=1
    )
    turn = jnp.pad(turn, ((0, ceil8(shifts) - shifts), (0, 0)))
    sign = np.ones((ceil8(shifts), 1), np.float32)
    sign[lon_count // 2 : shifts] = -1.0
    turn = turn * sign
    middle = ((2 * kept - 1).astype(F32) / total_columns)[None, :]
    coupling = coupling.reshape(levels, fields * fields)

    whole = lambda *sizes: pl.BlockSpec(sizes, lambda l, *_: (0,) * len(sizes))
    by_level = lambda *sizes: pl.BlockSpec((1,) + sizes, lambda l, *_: (l,) + (0,) * len(sizes))
    state_spec = pl.BlockSpec((fields, 1, columns, rows), lambda l, *_: (0, l, 0, 0))
    half_spec = pl.BlockSpec((fields, 1, columns, POLAR), lambda l, *_: (0, l, 0, 0))
    polar_spec = pl.BlockSpec((fields, 1, columns, POLAR), lambda l, m: (0, l, 0, m[0]))
    rest_spec = pl.BlockSpec((fields, 1, columns, POLAR), lambda l, m: (0, l, 0, 1 - m[0]))
    smem = pl.BlockSpec(memory_space=pltpu.SMEM)
    lon_halo = by_level(8, rows)
    lat_halo = by_level(8, columns)
    table = whole(columns, POLAR)

    def grid(in_specs, out_specs, scratch=()):
        return pltpu.PrefetchScalarGridSpec(
            num_scalar_prefetch=1,
            grid=(levels,),
            in_specs=in_specs,
            out_specs=out_specs,
            scratch_shapes=list(scratch),
        )

    with jax.named_scope("lon_edges"):
        first, last = pl.pallas_call(
            lon_edge_kernel,
            grid=(levels,),
            in_specs=[
                pl.BlockSpec((fields, 1, 8, rows), lambda l: (0, l, 0, 0)),
                pl.BlockSpec((fields, 1, 8, rows), lambda l: (0, l, columns // 8 - 1, 0)),
            ],
            out_specs=[lon_halo] * 2,
            out_shape=[shape(levels, 8, rows)] * 2,
            compiler_params=params,
            cost_estimate=cost(0, 16 * fields * levels * 8 * rows),
        )(model_state, model_state)
    with jax.named_scope("lon_halo"):
        west_halo = lax.ppermute(last, "lon", ring(lon_count, 1))
        east_halo = lax.ppermute(first, "lon", ring(lon_count, -1))

    with jax.named_scope("lat_edges"):
        north, south = pl.pallas_call(
            lat_edge_kernel,
            grid=(levels,),
            in_specs=[state_spec],
            out_specs=[lat_halo] * 2,
            out_shape=[shape(levels, 8, columns)] * 2,
            compiler_params=params,
            cost_estimate=cost(0, 2 * half_bytes),
        )(model_state)
    with jax.named_scope("lat_halo"):
        north_halo = lax.ppermute(south, "lat", [(i, i + 1) for i in range(lat_count - 1)])
        south_halo = lax.ppermute(north, "lat", [(i + 1, i) for i in range(lat_count - 1)])

    with jax.named_scope("polar_half"):
        polar, sent = pl.pallas_call(
            polar_kernel,
            grid_spec=grid(
                [
                    smem,
                    state_spec,
                    lon_halo,
                    lon_halo,
                    whole(2, rows),
                    table,
                    table,
                    whole(2 * RANK, columns),
                ],
                [half_spec, by_level(fields * RANK, 2 * POLAR)],
            ),
            out_shape=[
                shape(fields, levels, columns, POLAR),
                shape(levels, fields * RANK, 2 * POLAR),
            ],
            compiler_params=params,
            cost_estimate=cost(0, 3 * half_bytes),
        )(meta, coupling, model_state, west_halo, east_halo, diffusion, cosine, sine, send)
    with jax.named_scope("factors_gather"):
        gathered = lax.all_gather(sent, "lon", axis=0, tiled=False)

    with jax.named_scope("other_half"):
        advanced, cut = pl.pallas_call(
            rest_kernel,
            grid_spec=grid(
                [
                    smem,
                    smem,
                    state_spec,
                    half_spec,
                    lon_halo,
                    lon_halo,
                    lat_halo,
                    lat_halo,
                    whole(2, rows),
                ],
                [rest_spec, by_level(CAP * 8, POLAR)],
                [pltpu.VMEM((columns, 128), F32), pltpu.VMEM((8, rows), F32)],
            ),
            out_shape=[shape(*model_state.shape), shape(levels, CAP * 8, POLAR)],
            compiler_params=params,
            cost_estimate=cost(0, 4 * half_bytes),
        )(
            meta,
            coupling,
            strip_list,
            model_state,
            polar,
            west_halo,
            east_halo,
            north_halo,
            south_halo,
            diffusion,
        )
    with jax.named_scope("strips_gather"):
        cuts = lax.all_gather(cut, "lon", axis=0, tiled=False)

    with jax.named_scope("near"):
        filtered = pl.pallas_call(
            near_kernel,
            grid_spec=grid(
                [
                    half_spec,
                    lat_halo,
                    whole(2, rows),
                    table,
                    table,
                    whole(1, POLAR),
                    whole(columns, 3 * columns),
                ],
                half_spec,
            ),
            out_shape=shape(*polar.shape),
            input_output_aliases={1: 0},
            compiler_params=params,
            cost_estimate=cost(12 * fields * levels * columns * columns * POLAR, 2 * half_bytes),
        )(meta, polar, north_halo, diffusion, cosine, sine, middle, near)

    with jax.named_scope("far"):
        source = lambda shift: pl.BlockSpec(
            (1, 1, fields * RANK, 2 * POLAR),
            lambda l, m: (lax.rem(m[2] + lon_count - shift, lon_count), l, 0, 0),
        )
        advanced = pl.pallas_call(
            functools.partial(far_kernel, shifts),
            grid_spec=grid(
                [
                    pl.BlockSpec(memory_space=pl.ANY),
                    half_spec,
                    table,
                    table,
                    whole(*turn.shape),
                    whole(columns, 3 * shifts * RANK),
                ]
                + [source(shift) for shift in range(1, lon_count)],
                polar_spec,
                [pltpu.VMEM((shifts * RANK, 2 * POLAR), F32)],
            ),
            out_shape=shape(*model_state.shape),
            input_output_aliases={1: 0},
            compiler_params=params,
        )(meta, advanced, filtered, cosine, sine, turn, far, *[gathered] * shifts)

    with jax.named_scope("boundary"):
        sources = lon_count * CAP * STRIP
        begins = jnp.broadcast_to(
            jnp.repeat(nest_place.reshape(-1), STRIP)[:, None], (sources, 128)
        )
        boundary = pl.pallas_call(
            boundary_kernel,
            in_specs=[smem] + [pl.BlockSpec(memory_space=pltpu.VMEM)] * 2,
            out_specs=pl.BlockSpec(memory_space=pltpu.VMEM),
            out_shape=shape(1, fields, levels, NB),
            compiler_params=params,
        )(meta, cuts, begins)
    return advanced, boundary


def padded_2(block, sides, width):
    for axis, dim in sides:
        count = lax.axis_size(axis)
        forward = [(i, i + 1) for i in range(count - 1)]
        forward.append((count - 1, 0))
        backward = [(target, source) for source, target in forward]
        low = lax.ppermute(
            lax.slice_in_dim(block, block.shape[dim] - width, None, axis=dim), axis, forward
        )
        high = lax.ppermute(lax.slice_in_dim(block, 0, width, axis=dim), axis, backward)
        block = jnp.concatenate([low, block, high], axis=dim)
    return block


def spectral_filter(rows, kept):
    top_wavenumber_kept = lax.Precision.HIGHEST
    length = rows.shape[3]
    width = math.gcd(KC, 128)
    column_grid = lax.broadcasted_iota(jnp.int32, (length, width), 0)
    step_output = jnp.zeros_like(rows)
    for block_index in range(KC // width):
        wavenumber = block_index * width + lax.broadcasted_iota(jnp.int32, (length, width), 1)
        phase = column_grid * wavenumber % length
        angle = phase.astype(jnp.float32) * (2.0 * math.pi / length)
        cosine = jnp.cos(angle)
        sine = jnp.sin(angle)
        along = block_index * width + jnp.arange(width, dtype=jnp.int32)
        scale = jnp.where(along == 0, 1.0 / length, 2.0 / length)
        weight = jnp.where(along[None, :] < kept[:, None], scale[None, :], 0.0)
        real_part = (
            jnp.einsum("flrn,nk->flrk", rows, cosine, precision=top_wavenumber_kept) * weight
        )
        imaginary_component = (
            jnp.einsum("flrn,nk->flrk", rows, sine, precision=top_wavenumber_kept) * weight
        )
        step_output = (
            step_output
            + jnp.einsum("flrk,nk->flrn", real_part, cosine, precision=top_wavenumber_kept)
            + jnp.einsum("flrk,nk->flrn", imaginary_component, sine, precision=top_wavenumber_kept)
        )
    return step_output


def polar_pass(work_rows, kept_start, kept_table):
    count = work_rows.shape[2] // lax.axis_size("lon")
    kept = lax.dynamic_slice_in_dim(kept_table, kept_start + lax.axis_index("lon") * count, count)
    return lax.all_to_all(
        spectral_filter(
            lax.all_to_all(work_rows, "lon", split_axis=2, concat_axis=3, tiled=True), kept
        ),
        "lon",
        split_axis=3,
        concat_axis=2,
        tiled=True,
    )


def transposed(model_state, diffusion, coupling, cutoff, strip_list, nest_place):
    top_wavenumber_kept = lax.Precision.HIGHEST
    lat_index = lax.axis_index("lat")
    lat_count = lax.axis_size("lat")
    lon_count = lax.axis_size("lon")
    fields, levels, lon_local, lat_local = model_state.shape
    padded = padded_2(model_state, (("lat", 3), ("lon", 2)), 1)
    east_west = padded[:, :, 2:, 1:-1] + padded[:, :, :-2, 1:-1]
    row_place = lax.broadcasted_iota(jnp.int32, (1, 1, 1, lat_local), 3)
    northern = jnp.where((lat_index == 0) & (row_place == 0), 0.0, padded[:, :, 1:-1, :-2])
    southern = jnp.where(
        (lat_index == lat_count - 1) & (row_place == lat_local - 1), 0.0, padded[:, :, 1:-1, 2:]
    )
    blended = jnp.einsum("lfg,glij->flij", coupling, model_state, precision=top_wavenumber_kept)
    updated = (
        model_state
        + diffusion[0] * (east_west - 2.0 * model_state)
        + diffusion[1] * (northern + southern - 2.0 * model_state)
        + blended
    )
    is_south = lat_index == lat_count - 1
    is_polar = (lat_index == 0) | is_south
    start = jnp.where(is_south, lat_local - POLAR, 0).astype(jnp.int32)
    band_base = jnp.where(lat_index < lat_count // 2, 0, POLAR).astype(jnp.int32)
    block_rows = lax.dynamic_slice_in_dim(updated, start, POLAR, 3)
    polar_rows = jnp.transpose(block_rows, (0, 1, 3, 2))
    filtered = polar_pass(polar_rows, band_base, cutoff)
    new_rows = jnp.where(is_polar, jnp.transpose(filtered, (0, 1, 3, 2)), block_rows)
    advanced_state = lax.dynamic_update_slice_in_dim(updated, new_rows, start, 3)
    slots = strip_list.shape[0]
    owners = strip_list[:, 0]
    columns = strip_list[:, 1]
    offsets = strip_list[:, 2]
    lengths = strip_list[:, 3]
    zero = jnp.zeros((), jnp.int32)

    def cut_strip(column, offset):
        return lax.dynamic_slice(
            updated, (zero, zero, column, offset), (fields, levels, 1, STRIP)
        ).reshape(fields * levels, STRIP)

    boundary_strips = jax.vmap(cut_strip)(columns, offsets)
    inside = lax.broadcasted_iota(jnp.int32, (1, 1, STRIP), 2) < lengths[:, None, None]
    boundary_strips = jnp.where(inside, boundary_strips, 0.0).reshape(
        slots, fields * levels * STRIP
    )
    slot_ids = jnp.arange(slots, dtype=jnp.int32)
    earlier = slot_ids[None, :] < slot_ids[:, None]
    same = owners[:, None] == owners[None, :]
    rank = jnp.sum((same & earlier).astype(jnp.int32), axis=1)
    target = owners * CAP + rank
    routing = (jnp.arange(lon_count * CAP, dtype=jnp.int32)[:, None] == target[None, :]).astype(
        jnp.float32
    )
    outgoing = jnp.dot(
        routing, boundary_strips, precision=top_wavenumber_kept, preferred_element_type=jnp.float32
    ).reshape(lon_count, CAP, fields * levels * STRIP)
    arrived = lax.all_to_all(outgoing, "lon", split_axis=0, concat_axis=0, tiled=True)
    total = lon_count * CAP
    group = math.gcd(total, 16)
    pieces = arrived.reshape(total // group, group, fields * levels, STRIP)
    starts = nest_place.reshape(total // group, group)
    point = lax.broadcasted_iota(jnp.int32, (1, 1, NB), 2)
    row_step = lax.broadcasted_iota(jnp.int32, (1, STRIP, 1), 1) * RATIO

    def accumulate(carry, item):
        piece, begin = item
        offset = point - begin[:, None, None]
        hat = jnp.maximum(RATIO - jnp.abs(offset - row_step), 0)
        hat = (
            jnp.where((offset >= 0) & (offset < STRIP * RATIO), hat, 0).astype(jnp.float32) / RATIO
        )
        return (carry + jnp.einsum("gat,gtp->ap", piece, hat, precision=top_wavenumber_kept), None)

    boundary = lax.scan(
        accumulate, jnp.zeros((fields * levels, NB), jnp.float32), (pieces, starts)
    )[0]
    return (advanced_state, boundary.reshape(1, fields, levels, NB))


def local(model_state, *others):
    columns = model_state.shape[2]
    fits = lax.axis_size("lon") * STRIP == POLAR and model_state.shape[3] == 2 * POLAR
    if fits and columns % STEP == 0 and columns >= 8 * RANK:
        return compressed(model_state, *others)
    return transposed(model_state, *others)


def solution(mesh):
    return jax.shard_map(
        local,
        mesh=mesh,
        in_specs=(
            P(None, None, "lon", "lat"),
            P(None, "lat"),
            P(),
            P(),
            P(("lat", "lon"), None),
            P(("lat", "lon"), None, None),
        ),
        out_specs=(P(None, None, "lon", "lat"), P(("lat", "lon"), None, None, None)),
        check_vma=False,
    )
```

```python
import functools
import math

import jax
import jax.numpy as jnp
import numpy as np
from jax import lax
from jax.experimental import pallas as pl
from jax.experimental.pallas import tpu as pltpu
from jax.sharding import PartitionSpec as P

POLAR = 128
CAP = 2
STRIP = 16
RATIO = 11
NB = 2048
KC = 896
RANKS = (14, 5, 4)
STEP = 16
HELD = 80
VMEM_LIMIT = 48 * 1024 * 1024
F32 = jnp.float32
BF16 = jnp.bfloat16


def ceil8(value):
    return -(-value // 8) * 8


def split_table(table):
    high = table.astype(jnp.bfloat16)
    low = (table - high.astype(np.float64)).astype(jnp.bfloat16)
    return high, low


@functools.lru_cache(maxsize=None)
def filter_tables(count, width):
    total = count * width
    place = np.arange(width)
    difference = place[:, None] - place[None, :]
    sine = np.sin(np.pi * difference / total) * total
    near = np.where(difference == 0, 0.0, 1.0 / np.where(difference == 0, 1.0, sine))
    ranks, senders, receivers = [], [], []
    for shift in range(1, count):
        signed = shift if shift <= count // 2 else shift - count
        block = 1.0 / (np.sin(np.pi * (signed * width + difference) / total) * total)
        left, values, right = np.linalg.svd(block)
        rank = RANKS[min(abs(signed), len(RANKS)) - 1]
        root = np.sqrt(values[:rank])
        padded = ceil8(rank)
        sender = np.zeros((padded, width))
        sender[:rank] = right[:rank] * root[:, None]
        receiver = np.zeros((width, padded))
        receiver[:, :rank] = left[:, :rank] * root[None, :]
        ranks.append(rank)
        senders.append(sender)
        receivers.append(receiver)
    receivers = np.concatenate(receivers, axis=1)
    receivers = np.pad(receivers, ((0, 0), (0, HELD - receivers.shape[1])))
    near_high, near_low = split_table(near)
    send_high, send_low = split_table(np.concatenate(senders, axis=0))
    far_high, far_low = split_table(receivers)
    return (
        tuple(ranks),
        np.concatenate([near_high, near_high, near_low], axis=1),
        np.concatenate([send_high, send_low], axis=0),
        np.concatenate([far_high, far_high, far_low], axis=1),
    )


def split_value(value):
    high = value.astype(BF16)
    return high, (value - high.astype(F32)).astype(BF16)


def modulated(row, cosine, sine):
    return jnp.concatenate([row * cosine[...], row * sine[...]], axis=1)


def stacked(value):
    high, low = split_value(value)
    return jnp.concatenate([high, low, high], axis=0)


def strip_rows(slots):
    return slots // 2


def payload_rows(rank, slots):
    return ceil8(slots * rank + strip_rows(slots))


def edge_kernel(meta, state, lon_pair, lon_cross, lat_pair, lat_cross, held, sems):
    fields, levels, columns, rows = state.shape
    copies = [
        [
            pltpu.make_async_copy(state.at[f, l], held.at[l, f], sems.at[l, f])
            for f in range(fields)
        ]
        for l in range(levels)
    ]
    for l in range(levels):
        for f in range(fields):
            copies[l][f].start()
    lane = lax.broadcasted_iota(jnp.int32, (columns, 128), 1)
    lon_odd = lax.rem(meta[2], 2) == 1
    lat_odd = lax.rem(meta[3], 2) == 1
    lon_pair[...] = jnp.zeros(lon_pair.shape, F32)
    lon_cross[...] = jnp.zeros(lon_cross.shape, F32)
    for l in range(levels):
        edges = jnp.zeros((columns, 128), F32)
        for f in range(fields):
            copies[l][f].wait()
            first = held[l, f, 0:1, :]
            last = held[l, f, columns - 1 : columns, :]
            lon_pair[l, f : f + 1, :] = jnp.where(lon_odd, first, last)
            lon_cross[l, f : f + 1, :] = jnp.where(lon_odd, last, first)
            edges = jnp.where(lane == f, held[l, f, :, 0:1], edges)
            edges = jnp.where(lane == 8 + f, held[l, f, :, rows - 1 : rows], edges)
        turned = edges.T
        north, south = turned[0:8], turned[8:16]
        lat_pair[l] = jnp.where(lat_odd, north, south)
        lat_cross[l] = jnp.where(lat_odd, south, north)


def stencil_kernel(
    ranks,
    meta,
    coupling,
    strips,
    lon_pair,
    lon_cross,
    lat_pair,
    lat_cross,
    diffusion,
    cosine,
    sine,
    send,
    state,
    updated,
    own,
    *rest,
):
    payloads = rest[: len(ranks)]
    held, made, factors, placed, rows_cut, in_sems, out_sems = rest[len(ranks) :]
    fields, levels, columns, rows = state.shape

    def copy_in(l, f):
        return pltpu.make_async_copy(state.at[f, l], held.at[l, f], in_sems.at[l, f])

    def copy_out(l, f):
        return pltpu.make_async_copy(made.at[l, f], updated.at[f, l], out_sems.at[l, f])

    for l in range(levels):
        for f in range(fields):
            copy_in(l, f).start()

    lane = lax.broadcasted_iota(jnp.int32, (STEP, rows), 1)
    along = jnp.broadcast_to(diffusion[0:1, :], (STEP, rows))
    across = jnp.broadcast_to(diffusion[1:2, :], (STEP, rows))
    centre = 1.0 - 2.0 * along - 2.0 * across
    start = pl.multiple_of(meta[0] * POLAR, POLAR)
    lon_odd = lax.rem(meta[2], 2) == 1
    lat_odd = lax.rem(meta[3], 2) == 1
    half = send.shape[0] // 2

    def one_level(l, carry):
        for f in range(fields):
            copy_in(l, f).wait()
        weights = [
            [coupling[l, f * fields + g] for g in range(fields)] for f in range(fields)
        ]
        west_halo = jnp.where(lon_odd, lon_pair[l], lon_cross[l])
        east_halo = jnp.where(lon_odd, lon_cross[l], lon_pair[l])
        north_halo = jnp.where(lat_odd, lat_pair[l], lat_cross[l])
        south_halo = jnp.where(lat_odd, lat_cross[l], lat_pair[l])
        halo = jnp.concatenate(
            [north_halo, south_halo, jnp.zeros((112, columns), F32)], axis=0
        ).T
        for begin in range(0, columns, STEP):
            end = begin + STEP
            here = [held[l, f, begin:end, :] for f in range(fields)]
            for f in range(fields):
                if begin == 0:
                    west = jnp.concatenate(
                        [west_halo[f : f + 1, :], held[l, f, 0 : STEP - 1, :]], axis=0
                    )
                else:
                    west = held[l, f, begin - 1 : end - 1, :]
                if end == columns:
                    east = jnp.concatenate(
                        [held[l, f, begin + 1 : end, :], east_halo[f : f + 1, :]], axis=0
                    )
                else:
                    east = held[l, f, begin + 1 : end + 1, :]
                north = jnp.where(
                    lane == 0, halo[begin:end, f : f + 1], pltpu.roll(here[f], 1, 1)
                )
                south = jnp.where(
                    lane == rows - 1,
                    halo[begin:end, 8 + f : 9 + f],
                    pltpu.roll(here[f], rows - 1, 1),
                )
                result = centre * here[f] + along * (east + west) + across * (north + south)
                for g in range(fields):
                    result = result + weights[f][g] * here[g]
                made[l, f, begin:end, :] = result
        for f in range(fields):
            copy_out(l, f).start()
        for f in range(fields):
            row = made[l, f, :, pl.ds(start, POLAR)]
            high, low = split_value(modulated(row, cosine, sine))
            both = jnp.dot(send[...], high, preferred_element_type=F32)
            cross = jnp.dot(send[0:half, :], low, preferred_element_type=F32)
            factors[l * fields + f] = both[:half] + both[half:] + cross
        return carry

    lax.fori_loop(0, levels, one_level, 0)

    lon_index = meta[2]
    slots = strips.shape[0]
    lists = fields * levels
    each = strip_rows(lists)
    shifts = len(ranks) + 1
    placed[...] = jnp.zeros(placed.shape, F32)
    rows_cut[...] = jnp.zeros(rows_cut.shape, F32)
    strip_lane = lax.broadcasted_iota(jnp.int32, (16, rows), 1)
    owners = [strips[s, 0] for s in range(slots)]
    for s in range(slots):
        column, offset, length = strips[s, 1], strips[s, 2], strips[s, 3]
        rank = jnp.int32(0)
        for earlier in range(s):
            rank = rank + (owners[earlier] == owners[s]).astype(jnp.int32)
        for l in range(levels):
            for f in range(fields):
                side, place = divmod(l * fields + f, each)
                rows_cut[s, side, place : place + 1, :] = made[l, f, pl.ds(column, 1), :]
        base = lax.rem(lon_index * CAP + rank, POLAR // STRIP) * STRIP
        shift = lax.rem(owners[s] - lon_index + shifts, shifts)
        for side in range(2):
            where = side * POLAR + base
            moved = pltpu.roll(rows_cut[s, side], lax.rem(where - offset + rows, rows), 1)
            inside = (strip_lane >= where) & (strip_lane < where + length)
            placed[shift] = placed[shift] + jnp.where(inside, moved, 0.0)
    own[...] = placed[0]

    place = 0
    for index, (payload, rank) in enumerate(zip(payloads, ranks)):
        for item in range(lists):
            payload[item * rank : (item + 1) * rank, :] = factors[item, place : place + rank, :]
        payload[lists * rank : lists * rank + each, :] = placed[index + 1][0:each, :]
        unused = payload.shape[0] - lists * rank - each
        if unused:
            payload[lists * rank + each :, :] = jnp.zeros((unused, rows), F32)
        place += ceil8(rank)
    for l in range(levels):
        for f in range(fields):
            copy_out(l, f).wait()


def near_kernel(
    meta, begins, cosine, sine, middle, near, rows, late_a, late_b, out, out_a, out_b, hats,
    held, made, in_sems, out_sems,
):
    del late_a, late_b, out_a, out_b
    fields, levels, columns, _ = rows.shape
    mine = pl.ds(pl.multiple_of(meta[0] * POLAR, POLAR), POLAR)

    def copy_in(item):
        l, f = item // fields, item % fields
        return pltpu.make_async_copy(rows.at[f, l, :, mine], held.at[item], in_sems.at[item])

    def copy_out(item):
        l, f = item // fields, item % fields
        return pltpu.make_async_copy(made.at[item], out.at[f, l, :, mine], out_sems.at[item])

    @pl.when(meta[1] == 1)
    def _():
        for item in range(fields * levels):
            copy_in(item).start()

    point = lax.broadcasted_iota(jnp.int32, hats.shape, 1)
    place = lax.broadcasted_iota(jnp.int32, hats.shape, 0) % STRIP
    offset = point - begins[:, 0:1]
    hat = jnp.maximum(RATIO - jnp.abs(offset - place * RATIO), 0)
    hat = jnp.where((offset >= 0) & (offset < STRIP * RATIO), hat, 0)
    hats[...] = hat.astype(F32).astype(BF16)

    @pl.when(meta[1] == 1)
    def _():
        def one(item, carry):
            copy_in(item).wait()
            row = held[item]
            value = stacked(modulated(row, cosine, sine))
            total = jnp.dot(near[...], value, preferred_element_type=F32)
            made[item] = (
                sine[...] * total[:, :POLAR]
                - cosine[...] * total[:, POLAR:]
                + middle[0:1, :] * row
            )
            copy_out(item).start()
            return carry

        lax.fori_loop(0, fields * levels, one, 0)
        for item in range(fields * levels):
            copy_out(item).wait()


def far_kernel(ranks, meta, cosine, sine, turn, far, hats, own, *rest):
    payloads = rest[: len(ranks)]
    rows, out, boundary, held, made, arrived, in_sems, out_sems = rest[len(ranks) :]
    fields, levels, columns, _ = rows.shape
    lists = fields * levels
    each = strip_rows(lists)
    shifts = len(ranks) + 1
    mine = pl.ds(pl.multiple_of(meta[0] * POLAR, POLAR), POLAR)

    def copy_in(item):
        l, f = item // fields, item % fields
        return pltpu.make_async_copy(rows.at[f, l, :, mine], held.at[item], in_sems.at[item])

    def copy_out(item):
        l, f = item // fields, item % fields
        return pltpu.make_async_copy(made.at[item], out.at[f, l, :, mine], out_sems.at[item])

    @pl.when(meta[1] == 1)
    def _():
        for item in range(lists):
            copy_in(item).start()
        for item in range(lists):
            arrived[item, HELD - 16 :, :] = jnp.zeros((16, 2 * POLAR), F32)
        place = 0
        for index, (payload, rank) in enumerate(zip(payloads, ranks)):
            turn_cos = turn[index : index + 1, :POLAR]
            turn_sin = turn[index : index + 1, POLAR:]
            for item in range(lists):
                cosines = payload[item * rank : (item + 1) * rank, :POLAR]
                sines = payload[item * rank : (item + 1) * rank, POLAR:]
                arrived[item, place : place + rank, :POLAR] = (
                    turn_cos * cosines + turn_sin * sines
                )
                arrived[item, place : place + rank, POLAR:] = (
                    turn_cos * sines - turn_sin * cosines
                )
                if rank < ceil8(rank):
                    arrived[item, place + rank : place + ceil8(rank), :] = jnp.zeros(
                        (ceil8(rank) - rank, 2 * POLAR), F32
                    )
            place += ceil8(rank)

        def one(item, carry):
            total = jnp.dot(far[...], stacked(arrived[item]), preferred_element_type=F32)
            copy_in(item).wait()
            made[item] = (
                held[item] + sine[...] * total[:, :POLAR] - cosine[...] * total[:, POLAR:]
            )
            copy_out(item).start()
            return carry

        lax.fori_loop(0, lists, one, 0)

    groups = shifts * CAP * STRIP // POLAR
    sides = [[jnp.zeros((each, POLAR), F32)] * groups for _ in range(2)]
    for index in range(shifts):
        if index == 0:
            arrival = own[0:each, :]
        else:
            rank = ranks[index - 1]
            arrival = payloads[index - 1][lists * rank : lists * rank + each, :]
        source = lax.rem(meta[2] - index + shifts, shifts)
        group_at = lax.div(source, POLAR // (CAP * STRIP))
        for side in range(2):
            part = arrival[:, side * POLAR : (side + 1) * POLAR]
            for group in range(groups):
                sides[side][group] = sides[side][group] + jnp.where(group_at == group, part, 0.0)
    pieces = jnp.concatenate(
        [jnp.concatenate(side, axis=1) for side in sides], axis=0
    )
    high = pieces.astype(BF16)
    middle, low = split_value(pieces - high.astype(F32))
    total = jnp.dot(high, hats[...], preferred_element_type=F32)
    total = total + jnp.dot(middle, hats[...], preferred_element_type=F32)
    total = total + jnp.dot(low, hats[...], preferred_element_type=F32)
    total = total * (1.0 / RATIO)
    for l in range(levels):
        for f in range(fields):
            item = l * fields + f
            boundary[0, f, l : l + 1, :] = total[item : item + 1, :]

    @pl.when(meta[1] == 1)
    def _():
        for item in range(lists):
            copy_out(item).wait()


def ring(count, shift):
    return [(i, (i + shift) % count) for i in range(count)]


def swaps(pairs):
    return [pair for a, b in pairs for pair in ((a, b), (b, a))]


def phase_table(kept, steps, period):
    phase = (2 * kept - 1)[None, :] * steps[:, None] % (2 * period)
    angle = phase.astype(F32) * (math.pi / period)
    return jnp.cos(angle), jnp.sin(angle)


def compressed(model_state, diffusion, coupling, cutoff, strip_list, nest_place):
    lat_index = lax.axis_index("lat")
    lon_index = lax.axis_index("lon")
    lat_count = lax.axis_size("lat")
    lon_count = lax.axis_size("lon")
    fields, levels, columns, rows = model_state.shape
    lists = fields * levels
    total_columns = columns * lon_count
    ranks, *tables = filter_tables(lon_count, columns)
    near, send, far = [jnp.asarray(table) for table in tables]
    params = pltpu.CompilerParams(vmem_limit_bytes=VMEM_LIMIT)
    shape = lambda *sizes: jax.ShapeDtypeStruct(sizes, F32)
    whole_state = shape(*model_state.shape)

    is_south = lat_index == lat_count - 1
    is_polar = (lat_index == 0) | is_south
    part = jnp.where(is_south, rows // POLAR - 1, 0)
    meta = jnp.stack([part, is_polar.astype(jnp.int32), lon_index, lat_index]).astype(jnp.int32)
    kept = jnp.where(lat_index < lat_count // 2, cutoff[:POLAR], cutoff[POLAR:])
    cosine, sine = phase_table(kept, jnp.arange(columns, dtype=jnp.int32), total_columns)
    turn = jnp.concatenate(
        phase_table(kept, jnp.arange(1, lon_count, dtype=jnp.int32), lon_count), axis=1
    )
    turn = jnp.pad(turn, ((0, 1), (0, 0)))
    sign = np.ones((lon_count, 1), np.float32)
    sign[lon_count // 2 : lon_count - 1] = -1.0
    turn = turn * sign
    middle = ((2 * kept - 1).astype(F32) / total_columns)[None, :]
    begins = jnp.broadcast_to(
        jnp.repeat(nest_place.reshape(-1), STRIP)[:, None], (lon_count * CAP * STRIP, 128)
    )

    smem = pl.BlockSpec(memory_space=pltpu.SMEM)
    vmem = pl.BlockSpec(memory_space=pltpu.VMEM)
    hbm = pl.BlockSpec(memory_space=pl.ANY)
    level_sems = pltpu.SemaphoreType.DMA((levels, fields))
    list_sems = pltpu.SemaphoreType.DMA((lists,))
    state_scratch = pltpu.VMEM((levels, fields, columns, rows), F32)
    polar_scratch = pltpu.VMEM((lists, columns, POLAR), F32)

    with jax.named_scope("edges"):
        edges = pl.pallas_call(
            edge_kernel,
            in_specs=[smem, hbm],
            out_specs=[vmem] * 4,
            out_shape=[shape(levels, 8, rows)] * 2 + [shape(levels, 8, columns)] * 2,
            scratch_shapes=[state_scratch, level_sems],
            compiler_params=params,
        )(meta, model_state)

    with jax.named_scope("halo"):
        lon_pairs = [(i, i + 1) for i in range(0, lon_count, 2)]
        lon_crosses = [(i, (i + 1) % lon_count) for i in range(1, lon_count, 2)]
        lat_pairs = [(i, i + 1) for i in range(0, lat_count, 2)]
        lat_crosses = [(i, i + 1) for i in range(1, lat_count - 1, 2)]
        halos = [
            lax.ppermute(edges[0], "lon", swaps(lon_pairs)),
            lax.ppermute(edges[1], "lon", swaps(lon_crosses)),
            lax.ppermute(edges[2], "lat", swaps(lat_pairs)),
            lax.ppermute(edges[3], "lat", swaps(lat_crosses)),
        ]

    sizes = [payload_rows(rank, lists) for rank in ranks]
    with jax.named_scope("stencil"):
        updated, own, *outgoing = pl.pallas_call(
            functools.partial(stencil_kernel, ranks),
            in_specs=[smem] * 3 + [vmem] * 8 + [hbm],
            out_specs=[hbm] + [vmem] * (1 + len(ranks)),
            out_shape=[whole_state, shape(16, rows)] + [shape(size, rows) for size in sizes],
            scratch_shapes=[
                state_scratch,
                state_scratch,
                pltpu.VMEM((lists, send.shape[0] // 2, rows), F32),
                pltpu.VMEM((lon_count, 16, rows), F32),
                pltpu.VMEM((strip_list.shape[0], 2, 16, rows), F32),
                level_sems,
                level_sems,
            ],
            compiler_params=params,
        )(
            meta,
            coupling.reshape(levels, fields * fields),
            strip_list,
            *halos,
            diffusion,
            cosine,
            sine,
            send,
            model_state,
        )

    def exchange(shift, payload):
        return lax.ppermute(payload, "lon", ring(lon_count, shift))

    late = (2, lon_count - 2)
    with jax.named_scope("exchange"):
        incoming = {
            shift: exchange(shift, outgoing[shift - 1])
            for shift in range(1, lon_count)
            if shift not in late
        }

    with jax.named_scope("near"):
        late_payloads = [outgoing[shift - 1] for shift in late]
        advanced, *late_payloads, hats = pl.pallas_call(
            near_kernel,
            in_specs=[smem] + [vmem] * 5 + [hbm] * 3,
            out_specs=[hbm] * 3 + [vmem],
            out_shape=[whole_state]
            + [shape(*payload.shape) for payload in late_payloads]
            + [jax.ShapeDtypeStruct((begins.shape[0], NB), BF16)],
            input_output_aliases={6: 0, 7: 1, 8: 2},
            scratch_shapes=[polar_scratch, polar_scratch, list_sems, list_sems],
            compiler_params=params,
            cost_estimate=pl.CostEstimate(
                flops=12 * lists * columns * columns * POLAR,
                bytes_accessed=8 * lists * columns * POLAR,
                transcendentals=0,
            ),
        )(meta, begins, cosine, sine, middle, near, updated, *late_payloads)

    with jax.named_scope("late_exchange"):
        for shift, payload in zip(late, late_payloads):
            incoming[shift] = exchange(shift, payload)

    with jax.named_scope("far"):
        advanced, boundary = pl.pallas_call(
            functools.partial(far_kernel, ranks),
            in_specs=[smem] + [vmem] * (6 + len(ranks)) + [hbm],
            out_specs=[hbm, vmem],
            out_shape=[whole_state, shape(1, fields, levels, NB)],
            input_output_aliases={7 + len(ranks): 0},
            scratch_shapes=[
                polar_scratch,
                polar_scratch,
                pltpu.VMEM((lists, HELD, rows), F32),
                list_sems,
                list_sems,
            ],
            compiler_params=params,
        )(
            meta,
            cosine,
            sine,
            turn,
            far,
            hats,
            own,
            *[incoming[shift] for shift in range(1, lon_count)],
            advanced,
        )
    return advanced, boundary


def padded_2(block, sides, width):
    for axis, dim in sides:
        count = lax.axis_size(axis)
        forward = [(i, i + 1) for i in range(count - 1)]
        forward.append((count - 1, 0))
        backward = [(target, source) for source, target in forward]
        low = lax.ppermute(
            lax.slice_in_dim(block, block.shape[dim] - width, None, axis=dim), axis, forward
        )
        high = lax.ppermute(lax.slice_in_dim(block, 0, width, axis=dim), axis, backward)
        block = jnp.concatenate([low, block, high], axis=dim)
    return block


def spectral_filter(rows, kept):
    top_wavenumber_kept = lax.Precision.HIGHEST
    length = rows.shape[3]
    width = math.gcd(KC, 128)
    column_grid = lax.broadcasted_iota(jnp.int32, (length, width), 0)
    step_output = jnp.zeros_like(rows)
    for block_index in range(KC // width):
        wavenumber = block_index * width + lax.broadcasted_iota(jnp.int32, (length, width), 1)
        phase = column_grid * wavenumber % length
        angle = phase.astype(jnp.float32) * (2.0 * math.pi / length)
        cosine = jnp.cos(angle)
        sine = jnp.sin(angle)
        along = block_index * width + jnp.arange(width, dtype=jnp.int32)
        scale = jnp.where(along == 0, 1.0 / length, 2.0 / length)
        weight = jnp.where(along[None, :] < kept[:, None], scale[None, :], 0.0)
        real_part = (
            jnp.einsum("flrn,nk->flrk", rows, cosine, precision=top_wavenumber_kept) * weight
        )
        imaginary_component = (
            jnp.einsum("flrn,nk->flrk", rows, sine, precision=top_wavenumber_kept) * weight
        )
        step_output = (
            step_output
            + jnp.einsum("flrk,nk->flrn", real_part, cosine, precision=top_wavenumber_kept)
            + jnp.einsum("flrk,nk->flrn", imaginary_component, sine, precision=top_wavenumber_kept)
        )
    return step_output


def polar_pass(work_rows, kept_start, kept_table):
    count = work_rows.shape[2] // lax.axis_size("lon")
    kept = lax.dynamic_slice_in_dim(kept_table, kept_start + lax.axis_index("lon") * count, count)
    return lax.all_to_all(
        spectral_filter(
            lax.all_to_all(work_rows, "lon", split_axis=2, concat_axis=3, tiled=True), kept
        ),
        "lon",
        split_axis=3,
        concat_axis=2,
        tiled=True,
    )


def transposed(model_state, diffusion, coupling, cutoff, strip_list, nest_place):
    top_wavenumber_kept = lax.Precision.HIGHEST
    lat_index = lax.axis_index("lat")
    lat_count = lax.axis_size("lat")
    lon_count = lax.axis_size("lon")
    fields, levels, lon_local, lat_local = model_state.shape
    padded = padded_2(model_state, (("lat", 3), ("lon", 2)), 1)
    east_west = padded[:, :, 2:, 1:-1] + padded[:, :, :-2, 1:-1]
    row_place = lax.broadcasted_iota(jnp.int32, (1, 1, 1, lat_local), 3)
    northern = jnp.where((lat_index == 0) & (row_place == 0), 0.0, padded[:, :, 1:-1, :-2])
    southern = jnp.where(
        (lat_index == lat_count - 1) & (row_place == lat_local - 1), 0.0, padded[:, :, 1:-1, 2:]
    )
    blended = jnp.einsum("lfg,glij->flij", coupling, model_state, precision=top_wavenumber_kept)
    updated = (
        model_state
        + diffusion[0] * (east_west - 2.0 * model_state)
        + diffusion[1] * (northern + southern - 2.0 * model_state)
        + blended
    )
    is_south = lat_index == lat_count - 1
    is_polar = (lat_index == 0) | is_south
    start = jnp.where(is_south, lat_local - POLAR, 0).astype(jnp.int32)
    band_base = jnp.where(lat_index < lat_count // 2, 0, POLAR).astype(jnp.int32)
    block_rows = lax.dynamic_slice_in_dim(updated, start, POLAR, 3)
    polar_rows = jnp.transpose(block_rows, (0, 1, 3, 2))
    filtered = polar_pass(polar_rows, band_base, cutoff)
    new_rows = jnp.where(is_polar, jnp.transpose(filtered, (0, 1, 3, 2)), block_rows)
    advanced_state = lax.dynamic_update_slice_in_dim(updated, new_rows, start, 3)
    slots = strip_list.shape[0]
    owners = strip_list[:, 0]
    columns = strip_list[:, 1]
    offsets = strip_list[:, 2]
    lengths = strip_list[:, 3]
    zero = jnp.zeros((), jnp.int32)

    def cut_strip(column, offset):
        return lax.dynamic_slice(
            updated, (zero, zero, column, offset), (fields, levels, 1, STRIP)
        ).reshape(fields * levels, STRIP)

    boundary_strips = jax.vmap(cut_strip)(columns, offsets)
    inside = lax.broadcasted_iota(jnp.int32, (1, 1, STRIP), 2) < lengths[:, None, None]
    boundary_strips = jnp.where(inside, boundary_strips, 0.0).reshape(
        slots, fields * levels * STRIP
    )
    slot_ids = jnp.arange(slots, dtype=jnp.int32)
    earlier = slot_ids[None, :] < slot_ids[:, None]
    same = owners[:, None] == owners[None, :]
    rank = jnp.sum((same & earlier).astype(jnp.int32), axis=1)
    target = owners * CAP + rank
    routing = (jnp.arange(lon_count * CAP, dtype=jnp.int32)[:, None] == target[None, :]).astype(
        jnp.float32
    )
    outgoing = jnp.dot(
        routing, boundary_strips, precision=top_wavenumber_kept, preferred_element_type=jnp.float32
    ).reshape(lon_count, CAP, fields * levels * STRIP)
    arrived = lax.all_to_all(outgoing, "lon", split_axis=0, concat_axis=0, tiled=True)
    total = lon_count * CAP
    group = math.gcd(total, 16)
    pieces = arrived.reshape(total // group, group, fields * levels, STRIP)
    starts = nest_place.reshape(total // group, group)
    point = lax.broadcasted_iota(jnp.int32, (1, 1, NB), 2)
    row_step = lax.broadcasted_iota(jnp.int32, (1, STRIP, 1), 1) * RATIO

    def accumulate(carry, item):
        piece, begin = item
        offset = point - begin[:, None, None]
        hat = jnp.maximum(RATIO - jnp.abs(offset - row_step), 0)
        hat = (
            jnp.where((offset >= 0) & (offset < STRIP * RATIO), hat, 0).astype(jnp.float32) / RATIO
        )
        return (carry + jnp.einsum("gat,gtp->ap", piece, hat, precision=top_wavenumber_kept), None)

    boundary = lax.scan(
        accumulate, jnp.zeros((fields * levels, NB), jnp.float32), (pieces, starts)
    )[0]
    return (advanced_state, boundary.reshape(1, fields, levels, NB))


def local(model_state, *others):
    columns = model_state.shape[2]
    fits = lax.axis_size("lon") * STRIP == POLAR and model_state.shape[3] == 2 * POLAR
    if fits and columns % STEP == 0 and columns >= 2 * HELD:
        return compressed(model_state, *others)
    return transposed(model_state, *others)


def solution(mesh):
    return jax.shard_map(
        local,
        mesh=mesh,
        in_specs=(
            P(None, None, "lon", "lat"),
            P(None, "lat"),
            P(),
            P(),
            P(("lat", "lon"), None),
            P(("lat", "lon"), None, None),
        ),
        out_specs=(P(None, None, "lon", "lat"), P(("lat", "lon"), None, None, None)),
        check_vma=False,
    )
```

```python
import functools
import math

import jax
import jax.numpy as jnp
import numpy as np
from jax import lax
from jax.experimental import pallas as pl
from jax.experimental.pallas import tpu as pltpu
from jax.sharding import PartitionSpec as P

POLAR = 128
CAP = 2
STRIP = 16
RATIO = 11
NB = 2048
KC = 896
RANKS = (14, 5, 4)
STEP = 16
HELD = 80
EARLY_LISTS = 12
VMEM_LIMIT = 24 * 1024 * 1024
F32 = jnp.float32
BF16 = jnp.bfloat16


def ceil8(value):
    return -(-value // 8) * 8


def split_table(table):
    high = table.astype(jnp.bfloat16)
    low = (table - high.astype(np.float64)).astype(jnp.bfloat16)
    return high, low


@functools.lru_cache(maxsize=None)
def filter_tables(count, width):
    total = count * width
    place = np.arange(width)
    difference = place[:, None] - place[None, :]
    sine = np.sin(np.pi * difference / total) * total
    near = np.where(difference == 0, 0.0, 1.0 / np.where(difference == 0, 1.0, sine))
    ranks, senders, receivers = [], [], []
    for shift in range(1, count):
        signed = shift if shift <= count // 2 else shift - count
        block = 1.0 / (np.sin(np.pi * (signed * width + difference) / total) * total)
        left, values, right = np.linalg.svd(block)
        rank = RANKS[min(abs(signed), len(RANKS)) - 1]
        root = np.sqrt(values[:rank])
        padded = ceil8(rank)
        sender = np.zeros((padded, width))
        sender[:rank] = right[:rank] * root[:, None]
        receiver = np.zeros((width, padded))
        receiver[:, :rank] = left[:, :rank] * root[None, :]
        ranks.append(rank)
        senders.append(sender)
        receivers.append(receiver)
    receivers = np.concatenate(receivers, axis=1)
    receivers = np.pad(receivers, ((0, 0), (0, HELD - receivers.shape[1])))
    near_high, near_low = split_table(near)
    send_high, send_low = split_table(np.concatenate(senders, axis=0))
    far_high, far_low = split_table(receivers)
    return (
        tuple(ranks),
        np.concatenate([near_high, near_high, near_low], axis=1),
        np.concatenate([send_high, send_low], axis=0),
        np.concatenate(senders, axis=0)[:, (0, -1)].astype(np.float32),
        np.concatenate([far_high, far_high, far_low], axis=1),
    )


def split_value(value):
    high = value.astype(BF16)
    return high, (value - high.astype(F32)).astype(BF16)


def modulated(row, cosine, sine):
    return jnp.concatenate([row * cosine[...], row * sine[...]], axis=1)


def stacked(value):
    high, low = split_value(value)
    return jnp.concatenate([high, low, high], axis=0)


def strip_rows(slots):
    return slots // 2


def payload_rows(rank, slots):
    return ceil8(slots * rank + strip_rows(slots))


def interior_kernel(
    meta, coupling, diffusion, state, lon_pair, lon_cross, lat_pair, lat_cross, made, held, sems
):
    fields, levels, columns, rows = state.shape

    def copy_in(l, f):
        return pltpu.make_async_copy(state.at[f, l], held.at[l, f], sems.at[l, f])

    for l in range(levels):
        for f in range(fields):
            copy_in(l, f).start()
    lon_odd = lax.rem(meta[2], 2) == 1
    lat_odd = lax.rem(meta[3], 2) == 1
    lon_pair[...] = jnp.zeros(lon_pair.shape, F32)
    lon_cross[...] = jnp.zeros(lon_cross.shape, F32)
    lane = lax.broadcasted_iota(jnp.int32, (STEP, rows), 1)
    edge_lane = lax.broadcasted_iota(jnp.int32, (columns, 128), 1)
    along = jnp.broadcast_to(diffusion[0:1, :], (STEP, rows))
    across = jnp.broadcast_to(diffusion[1:2, :], (STEP, rows))
    centre = 1.0 - 2.0 * along - 2.0 * across
    across_north = jnp.where(lane == 0, 0.0, across)
    across_south = jnp.where(lane == rows - 1, 0.0, across)
    nothing = jnp.zeros((1, rows), F32)

    def one_level(l, carry):
        for f in range(fields):
            copy_in(l, f).wait()
        weights = [
            [coupling[l, f * fields + g] for g in range(fields)] for f in range(fields)
        ]
        for begin in range(0, columns, STEP):
            end = begin + STEP
            here = [held[l, f, begin:end, :] for f in range(fields)]
            for f in range(fields):
                if begin == 0:
                    west = jnp.concatenate([nothing, held[l, f, 0 : STEP - 1, :]], axis=0)
                else:
                    west = held[l, f, begin - 1 : end - 1, :]
                if end == columns:
                    east = jnp.concatenate([held[l, f, begin + 1 : end, :], nothing], axis=0)
                else:
                    east = held[l, f, begin + 1 : end + 1, :]
                result = centre * here[f] + along * (east + west)
                result = result + across_north * pltpu.roll(here[f], 1, 1)
                result = result + across_south * pltpu.roll(here[f], rows - 1, 1)
                for g in range(fields):
                    result = result + weights[f][g] * here[g]
                made[l, f, begin:end, :] = result
        edges = jnp.zeros((columns, 128), F32)
        for f in range(fields):
            first = held[l, f, 0:1, :]
            last = held[l, f, columns - 1 : columns, :]
            lon_pair[l, f : f + 1, :] = jnp.where(lon_odd, first, last)
            lon_cross[l, f : f + 1, :] = jnp.where(lon_odd, last, first)
            edges = jnp.where(edge_lane == f, held[l, f, :, 0:1], edges)
            edges = jnp.where(edge_lane == 8 + f, held[l, f, :, rows - 1 : rows], edges)
        turned = edges.T
        north, south = turned[0:8], turned[8:16]
        lat_pair[l] = jnp.where(lat_odd, north, south)
        lat_cross[l] = jnp.where(lat_odd, south, north)
        return carry

    lax.fori_loop(0, levels, one_level, 0)


def factor_kernel(meta, begins, cosine, sine, send, made, factors, hats):
    levels, fields = made.shape[0:2]
    half = send.shape[0] // 2
    mine = pl.ds(pl.multiple_of(meta[0] * POLAR, POLAR), POLAR)

    @pl.when(meta[1] == 1)
    def _():
        def one_level(l, carry):
            for f in range(fields):
                high, low = split_value(modulated(made[l, f, :, mine], cosine, sine))
                both = jnp.dot(send[...], high, preferred_element_type=F32)
                cross = jnp.dot(send[0:half, :], low, preferred_element_type=F32)
                factors[l * fields + f] = both[:half] + both[half:] + cross
            return carry

        lax.fori_loop(0, levels, one_level, 0)

    @pl.when(meta[1] == 0)
    def _():
        factors[...] = jnp.zeros(factors.shape, F32)

    point = lax.broadcasted_iota(jnp.int32, hats.shape, 1)
    place = lax.broadcasted_iota(jnp.int32, hats.shape, 0) % STRIP
    offset = point - begins[:, 0:1]
    hat = jnp.maximum(RATIO - jnp.abs(offset - place * RATIO), 0)
    hat = jnp.where((offset >= 0) & (offset < STRIP * RATIO), hat, 0)
    hats[...] = hat.astype(F32).astype(BF16)


def halo_kernel(
    ranks,
    meta,
    strips,
    lon_pair,
    lon_cross,
    lat_pair,
    lat_cross,
    diffusion,
    cosine,
    sine,
    ends,
    factors,
    interior,
    made,
    advanced,
    own,
    *rest,
):
    payloads = rest[: len(ranks)]
    placed, rows_cut, sems = rest[len(ranks) :]
    levels, fields, columns, rows = made.shape
    mine = pl.ds(pl.multiple_of(meta[0] * POLAR, POLAR), POLAR)
    other = pl.ds(pl.multiple_of((1 - meta[0]) * POLAR, POLAR), POLAR)

    def copy_out(l, f, lanes, side):
        return pltpu.make_async_copy(
            made.at[l, f, :, lanes], advanced.at[f, l, :, lanes], sems.at[side, l, f]
        )

    lon_odd = lax.rem(meta[2], 2) == 1
    lat_odd = lax.rem(meta[3], 2) == 1
    lane = lax.broadcasted_iota(jnp.int32, (1, POLAR), 1)
    along = diffusion[0:1, :]
    across_north = jnp.where(lane == 0, diffusion[1:2, :POLAR], 0.0)
    across_south = jnp.where(lane == POLAR - 1, diffusion[1:2, POLAR:], 0.0)
    for l in range(levels):
        west_halo = along * jnp.where(lon_odd, lon_pair[l], lon_cross[l])
        east_halo = along * jnp.where(lon_odd, lon_cross[l], lon_pair[l])
        north_halo = jnp.where(lat_odd, lat_pair[l], lat_cross[l])
        south_halo = jnp.where(lat_odd, lat_cross[l], lat_pair[l])
        halo = jnp.concatenate(
            [north_halo, south_halo, jnp.zeros((112, columns), F32)], axis=0
        ).T
        for f in range(fields):
            made[l, f, :, :POLAR] = interior[l, f, :, :POLAR] + halo[:, f : f + 1] * across_north
            made[l, f, :, POLAR:] = (
                interior[l, f, :, POLAR:] + halo[:, 8 + f : 9 + f] * across_south
            )
            made[l, f, 0:1, :] += west_halo[f : f + 1, :]
            made[l, f, columns - 1 : columns, :] += east_halo[f : f + 1, :]
            copy_out(l, f, other, 0).start()

        @pl.when(meta[1] == 0)
        def _():
            for f in range(fields):
                copy_out(l, f, mine, 1).start()

    lon_index = meta[2]
    slots = strips.shape[0]
    lists = fields * levels
    each = strip_rows(lists)
    shifts = len(ranks) + 1
    placed[...] = jnp.zeros(placed.shape, F32)
    rows_cut[...] = jnp.zeros(rows_cut.shape, F32)
    strip_lane = lax.broadcasted_iota(jnp.int32, (16, rows), 1)
    owners = [strips[s, 0] for s in range(slots)]
    for s in range(slots):
        column, offset, length = strips[s, 1], strips[s, 2], strips[s, 3]
        rank = jnp.int32(0)
        for earlier in range(s):
            rank = rank + (owners[earlier] == owners[s]).astype(jnp.int32)
        for l in range(levels):
            for f in range(fields):
                side, place = divmod(l * fields + f, each)
                rows_cut[s, side, place : place + 1, :] = made[l, f, pl.ds(column, 1), :]
        base = lax.rem(lon_index * CAP + rank, POLAR // STRIP) * STRIP
        shift = lax.rem(owners[s] - lon_index + shifts, shifts)
        for side in range(2):
            where = side * POLAR + base
            moved = pltpu.roll(rows_cut[s, side], lax.rem(where - offset + rows, rows), 1)
            inside = (strip_lane >= where) & (strip_lane < where + length)
            placed[shift] = placed[shift] + jnp.where(inside, moved, 0.0)
    own[...] = placed[0]

    missing = []
    for l in range(levels):
        for f in range(fields):
            pair = []
            for column, pair_first in ((0, True), (columns - 1, False)):
                odd_side = lon_pair if pair_first else lon_cross
                even_side = lon_cross if pair_first else lon_pair
                row = jnp.where(
                    lon_odd, odd_side[l, f : f + 1, mine], even_side[l, f : f + 1, mine]
                )
                row = row * diffusion[0:1, mine]
                turn_cos = cosine[column : column + 1, :]
                turn_sin = sine[column : column + 1, :]
                pair.append(jnp.concatenate([row * turn_cos, row * turn_sin], axis=1))
            missing.append(pair)
    place = 0
    for index, (payload, rank) in enumerate(zip(payloads, ranks)):
        first = ends[place : place + rank, 0:1]
        last = ends[place : place + rank, 1:2]
        for item in range(lists):
            west, east = missing[item]
            payload[item * rank : (item + 1) * rank, :] = (
                factors[item, place : place + rank, :] + first * west + last * east
            )
        payload[lists * rank : lists * rank + each, :] = placed[index + 1][0:each, :]
        unused = payload.shape[0] - lists * rank - each
        if unused:
            payload[lists * rank + each :, :] = jnp.zeros((unused, rows), F32)
        place += ceil8(rank)
    for l in range(levels):
        for f in range(fields):
            copy_out(l, f, other, 0).wait()

        @pl.when(meta[1] == 0)
        def _():
            for f in range(fields):
                copy_out(l, f, mine, 1).wait()


def near_kernel(begin, passed, meta, cosine, sine, middle, near, made, *rest):
    filtered = rest[passed]
    fields = made.shape[1]
    mine = pl.ds(pl.multiple_of(meta[0] * POLAR, POLAR), POLAR)

    @pl.when(meta[1] == 1)
    def _():
        def one(item, carry):
            row = made[(begin + item) // fields, (begin + item) % fields, :, mine]
            value = stacked(modulated(row, cosine, sine))
            total = jnp.dot(near[...], value, preferred_element_type=F32)
            filtered[item] = (
                sine[...] * total[:, :POLAR]
                - cosine[...] * total[:, POLAR:]
                + middle[0:1, :] * row
            )
            return carry

        lax.fori_loop(0, filtered.shape[0], one, 0)


def far_kernel(ranks, meta, cosine, sine, turn, far, hats, own, *rest):
    payloads = rest[: len(ranks)]
    near_first, near_last, _, out, boundary, filtered, arrived, sems = rest[len(ranks) :]
    fields, levels = out.shape[0:2]
    lists = fields * levels
    each = strip_rows(lists)
    shifts = len(ranks) + 1
    mine = pl.ds(pl.multiple_of(meta[0] * POLAR, POLAR), POLAR)

    def copy_out(item):
        l, f = item // fields, item % fields
        return pltpu.make_async_copy(filtered.at[item], out.at[f, l, :, mine], sems.at[item])

    @pl.when(meta[1] == 1)
    def _():
        for item in range(lists):
            arrived[item, HELD - 16 :, :] = jnp.zeros((16, 2 * POLAR), F32)
        place = 0
        for index, (payload, rank) in enumerate(zip(payloads, ranks)):
            turn_cos = turn[index : index + 1, :POLAR]
            turn_sin = turn[index : index + 1, POLAR:]
            for item in range(lists):
                cosines = payload[item * rank : (item + 1) * rank, :POLAR]
                sines = payload[item * rank : (item + 1) * rank, POLAR:]
                arrived[item, place : place + rank, :POLAR] = (
                    turn_cos * cosines + turn_sin * sines
                )
                arrived[item, place : place + rank, POLAR:] = (
                    turn_cos * sines - turn_sin * cosines
                )
                if rank < ceil8(rank):
                    arrived[item, place + rank : place + ceil8(rank), :] = jnp.zeros(
                        (ceil8(rank) - rank, 2 * POLAR), F32
                    )
            place += ceil8(rank)

        def add(item, near):
            total = jnp.dot(far[...], stacked(arrived[item]), preferred_element_type=F32)
            filtered[item] = near + sine[...] * total[:, :POLAR] - cosine[...] * total[:, POLAR:]
            copy_out(item).start()

        def one_first(item, carry):
            add(item, near_first[item])
            return carry

        def one_last(item, carry):
            add(near_first.shape[0] + item, near_last[item])
            return carry

        lax.fori_loop(0, near_first.shape[0], one_first, 0)
        lax.fori_loop(0, near_last.shape[0], one_last, 0)

    groups = shifts * CAP * STRIP // POLAR
    sides = [[jnp.zeros((each, POLAR), F32)] * groups for _ in range(2)]
    for index in range(shifts):
        if index == 0:
            arrival = own[0:each, :]
        else:
            rank = ranks[index - 1]
            arrival = payloads[index - 1][lists * rank : lists * rank + each, :]
        source = lax.rem(meta[2] - index + shifts, shifts)
        group_at = lax.div(source, POLAR // (CAP * STRIP))
        for side in range(2):
            part = arrival[:, side * POLAR : (side + 1) * POLAR]
            for group in range(groups):
                sides[side][group] = sides[side][group] + jnp.where(group_at == group, part, 0.0)
    pieces = jnp.concatenate([jnp.concatenate(side, axis=1) for side in sides], axis=0)
    high = pieces.astype(BF16)
    middle, low = split_value(pieces - high.astype(F32))
    total = jnp.dot(high, hats[...], preferred_element_type=F32)
    total = total + jnp.dot(middle, hats[...], preferred_element_type=F32)
    total = total + jnp.dot(low, hats[...], preferred_element_type=F32)
    total = total * (1.0 / RATIO)
    for l in range(levels):
        for f in range(fields):
            item = l * fields + f
            boundary[0, f, l : l + 1, :] = total[item : item + 1, :]

    @pl.when(meta[1] == 1)
    def _():
        for item in range(lists):
            copy_out(item).wait()


def ring(count, shift):
    return [(i, (i + shift) % count) for i in range(count)]


def swaps(pairs):
    return [pair for a, b in pairs for pair in ((a, b), (b, a))]


def phase_table(kept, steps, period):
    phase = (2 * kept - 1)[None, :] * steps[:, None] % (2 * period)
    angle = phase.astype(F32) * (math.pi / period)
    return jnp.cos(angle), jnp.sin(angle)


def compressed(model_state, diffusion, coupling, cutoff, strip_list, nest_place):
    lat_index = lax.axis_index("lat")
    lon_index = lax.axis_index("lon")
    lat_count = lax.axis_size("lat")
    lon_count = lax.axis_size("lon")
    fields, levels, columns, rows = model_state.shape
    lists = fields * levels
    total_columns = columns * lon_count
    ranks, *tables = filter_tables(lon_count, columns)
    near, send, ends, far = [jnp.asarray(table) for table in tables]
    params = pltpu.CompilerParams(vmem_limit_bytes=VMEM_LIMIT)
    shape = lambda *sizes: jax.ShapeDtypeStruct(sizes, F32)
    whole_state = shape(*model_state.shape)

    is_south = lat_index == lat_count - 1
    is_polar = (lat_index == 0) | is_south
    part = jnp.where(is_south, rows // POLAR - 1, 0)
    meta = jnp.stack([part, is_polar.astype(jnp.int32), lon_index, lat_index]).astype(jnp.int32)
    kept = jnp.where(lat_index < lat_count // 2, cutoff[:POLAR], cutoff[POLAR:])
    cosine, sine = phase_table(kept, jnp.arange(columns, dtype=jnp.int32), total_columns)
    turn = jnp.concatenate(
        phase_table(kept, jnp.arange(1, lon_count, dtype=jnp.int32), lon_count), axis=1
    )
    turn = jnp.pad(turn, ((0, 1), (0, 0)))
    sign = np.ones((lon_count, 1), np.float32)
    sign[lon_count // 2 : lon_count - 1] = -1.0
    turn = turn * sign
    middle = ((2 * kept - 1).astype(F32) / total_columns)[None, :]
    begins = jnp.broadcast_to(
        jnp.repeat(nest_place.reshape(-1), STRIP)[:, None], (lon_count * CAP * STRIP, 128)
    )

    smem = pl.BlockSpec(memory_space=pltpu.SMEM)
    vmem = pl.BlockSpec(memory_space=pltpu.VMEM)
    hbm = pl.BlockSpec(memory_space=pl.ANY)
    block = shape(levels, fields, columns, rows)

    with jax.named_scope("interior"):
        *edges, interior = pl.pallas_call(
            interior_kernel,
            in_specs=[smem, smem, vmem, hbm],
            out_specs=[vmem] * 5,
            out_shape=[shape(levels, 8, rows)] * 2 + [shape(levels, 8, columns)] * 2 + [block],
            scratch_shapes=[
                pltpu.VMEM(block.shape, F32),
                pltpu.SemaphoreType.DMA((levels, fields)),
            ],
            compiler_params=params,
        )(meta, coupling.reshape(levels, fields * fields), diffusion, model_state)

    with jax.named_scope("halo"):
        lon_pairs = [(i, i + 1) for i in range(0, lon_count, 2)]
        lon_crosses = [(i, (i + 1) % lon_count) for i in range(1, lon_count, 2)]
        lat_pairs = [(i, i + 1) for i in range(0, lat_count, 2)]
        lat_crosses = [(i, i + 1) for i in range(1, lat_count - 1, 2)]
        halos = [
            lax.ppermute(edges[0], "lon", swaps(lon_pairs)),
            lax.ppermute(edges[1], "lon", swaps(lon_crosses)),
            lax.ppermute(edges[2], "lat", swaps(lat_pairs)),
            lax.ppermute(edges[3], "lat", swaps(lat_crosses)),
        ]

    with jax.named_scope("factors"):
        factors, hats = pl.pallas_call(
            factor_kernel,
            in_specs=[smem] + [vmem] * 5,
            out_specs=[vmem] * 2,
            out_shape=[
                shape(lists, send.shape[0] // 2, rows),
                jax.ShapeDtypeStruct((begins.shape[0], NB), BF16),
            ],
            compiler_params=params,
            cost_estimate=pl.CostEstimate(
                flops=6 * lists * send.shape[0] * columns * rows,
                bytes_accessed=4 * lists * columns * POLAR,
                transcendentals=0,
            ),
        )(meta, begins, cosine, sine, send, interior)

    sizes = [payload_rows(rank, lists) for rank in ranks]
    with jax.named_scope("halo_share"):
        made, advanced, own, *outgoing = pl.pallas_call(
            functools.partial(halo_kernel, ranks),
            in_specs=[smem] * 2 + [vmem] * 10,
            out_specs=[vmem, hbm] + [vmem] * (1 + len(ranks)),
            out_shape=[block, whole_state, shape(16, rows)]
            + [shape(size, rows) for size in sizes],
            input_output_aliases={11: 0},
            scratch_shapes=[
                pltpu.VMEM((lon_count, 16, rows), F32),
                pltpu.VMEM((strip_list.shape[0], 2, 16, rows), F32),
                pltpu.SemaphoreType.DMA((2, levels, fields)),
            ],
            compiler_params=params,
        )(meta, strip_list, *halos, diffusion, cosine, sine, ends, factors, interior)

    def exchange(shift, payload):
        return lax.ppermute(payload, "lon", ring(lon_count, shift))

    late = (2, lon_count - 2)
    with jax.named_scope("exchange"):
        incoming = {
            shift: exchange(shift, outgoing[shift - 1])
            for shift in range(1, lon_count)
            if shift not in late
        }

    def near_part(begin, end, passed):
        return pl.pallas_call(
            functools.partial(near_kernel, begin, len(passed)),
            in_specs=[smem] + [vmem] * 5 + [hbm] * len(passed),
            out_specs=[vmem] + [hbm] * len(passed),
            out_shape=[shape(end - begin, columns, POLAR)]
            + [shape(*payload.shape) for payload in passed],
            input_output_aliases={6 + index: 1 + index for index in range(len(passed))},
            compiler_params=params,
            cost_estimate=pl.CostEstimate(
                flops=12 * (end - begin) * columns * columns * POLAR,
                bytes_accessed=8 * (end - begin) * columns * POLAR,
                transcendentals=0,
            ),
        )(meta, cosine, sine, middle, near, made, *passed)

    with jax.named_scope("near"):
        near_first, *passed = near_part(0, EARLY_LISTS, [outgoing[shift - 1] for shift in late])
    with jax.named_scope("late_exchange"):
        for shift, payload in zip(late, passed):
            incoming[shift] = exchange(shift, payload)
    with jax.named_scope("near_rest"):
        early = [shift for shift in range(1, lon_count) if shift not in late]
        near_last, *passed = near_part(EARLY_LISTS, lists, [incoming[shift] for shift in early])
        incoming.update(zip(early, passed))

    with jax.named_scope("far"):
        advanced, boundary = pl.pallas_call(
            functools.partial(far_kernel, ranks),
            in_specs=[smem] + [vmem] * (8 + len(ranks)) + [hbm],
            out_specs=[hbm, vmem],
            out_shape=[whole_state, shape(1, fields, levels, NB)],
            input_output_aliases={9 + len(ranks): 0},
            scratch_shapes=[
                pltpu.VMEM((lists, columns, POLAR), F32),
                pltpu.VMEM((lists, HELD, rows), F32),
                pltpu.SemaphoreType.DMA((lists,)),
            ],
            compiler_params=params,
        )(
            meta,
            cosine,
            sine,
            turn,
            far,
            hats,
            own,
            *[incoming[shift] for shift in range(1, lon_count)],
            near_first,
            near_last,
            advanced,
        )
    return advanced, boundary


def padded_2(block, sides, width):
    for axis, dim in sides:
        count = lax.axis_size(axis)
        forward = [(i, i + 1) for i in range(count - 1)]
        forward.append((count - 1, 0))
        backward = [(target, source) for source, target in forward]
        low = lax.ppermute(
            lax.slice_in_dim(block, block.shape[dim] - width, None, axis=dim), axis, forward
        )
        high = lax.ppermute(lax.slice_in_dim(block, 0, width, axis=dim), axis, backward)
        block = jnp.concatenate([low, block, high], axis=dim)
    return block


def spectral_filter(rows, kept):
    top_wavenumber_kept = lax.Precision.HIGHEST
    length = rows.shape[3]
    width = math.gcd(KC, 128)
    column_grid = lax.broadcasted_iota(jnp.int32, (length, width), 0)
    step_output = jnp.zeros_like(rows)
    for block_index in range(KC // width):
        wavenumber = block_index * width + lax.broadcasted_iota(jnp.int32, (length, width), 1)
        phase = column_grid * wavenumber % length
        angle = phase.astype(jnp.float32) * (2.0 * math.pi / length)
        cosine = jnp.cos(angle)
        sine = jnp.sin(angle)
        along = block_index * width + jnp.arange(width, dtype=jnp.int32)
        scale = jnp.where(along == 0, 1.0 / length, 2.0 / length)
        weight = jnp.where(along[None, :] < kept[:, None], scale[None, :], 0.0)
        real_part = (
            jnp.einsum("flrn,nk->flrk", rows, cosine, precision=top_wavenumber_kept) * weight
        )
        imaginary_component = (
            jnp.einsum("flrn,nk->flrk", rows, sine, precision=top_wavenumber_kept) * weight
        )
        step_output = (
            step_output
            + jnp.einsum("flrk,nk->flrn", real_part, cosine, precision=top_wavenumber_kept)
            + jnp.einsum("flrk,nk->flrn", imaginary_component, sine, precision=top_wavenumber_kept)
        )
    return step_output


def polar_pass(work_rows, kept_start, kept_table):
    count = work_rows.shape[2] // lax.axis_size("lon")
    kept = lax.dynamic_slice_in_dim(kept_table, kept_start + lax.axis_index("lon") * count, count)
    return lax.all_to_all(
        spectral_filter(
            lax.all_to_all(work_rows, "lon", split_axis=2, concat_axis=3, tiled=True), kept
        ),
        "lon",
        split_axis=3,
        concat_axis=2,
        tiled=True,
    )


def transposed(model_state, diffusion, coupling, cutoff, strip_list, nest_place):
    top_wavenumber_kept = lax.Precision.HIGHEST
    lat_index = lax.axis_index("lat")
    lat_count = lax.axis_size("lat")
    lon_count = lax.axis_size("lon")
    fields, levels, lon_local, lat_local = model_state.shape
    padded = padded_2(model_state, (("lat", 3), ("lon", 2)), 1)
    east_west = padded[:, :, 2:, 1:-1] + padded[:, :, :-2, 1:-1]
    row_place = lax.broadcasted_iota(jnp.int32, (1, 1, 1, lat_local), 3)
    northern = jnp.where((lat_index == 0) & (row_place == 0), 0.0, padded[:, :, 1:-1, :-2])
    southern = jnp.where(
        (lat_index == lat_count - 1) & (row_place == lat_local - 1), 0.0, padded[:, :, 1:-1, 2:]
    )
    blended = jnp.einsum("lfg,glij->flij", coupling, model_state, precision=top_wavenumber_kept)
    updated = (
        model_state
        + diffusion[0] * (east_west - 2.0 * model_state)
        + diffusion[1] * (northern + southern - 2.0 * model_state)
        + blended
    )
    is_south = lat_index == lat_count - 1
    is_polar = (lat_index == 0) | is_south
    start = jnp.where(is_south, lat_local - POLAR, 0).astype(jnp.int32)
    band_base = jnp.where(lat_index < lat_count // 2, 0, POLAR).astype(jnp.int32)
    block_rows = lax.dynamic_slice_in_dim(updated, start, POLAR, 3)
    polar_rows = jnp.transpose(block_rows, (0, 1, 3, 2))
    filtered = polar_pass(polar_rows, band_base, cutoff)
    new_rows = jnp.where(is_polar, jnp.transpose(filtered, (0, 1, 3, 2)), block_rows)
    advanced_state = lax.dynamic_update_slice_in_dim(updated, new_rows, start, 3)
    slots = strip_list.shape[0]
    owners = strip_list[:, 0]
    columns = strip_list[:, 1]
    offsets = strip_list[:, 2]
    lengths = strip_list[:, 3]
    zero = jnp.zeros((), jnp.int32)

    def cut_strip(column, offset):
        return lax.dynamic_slice(
            updated, (zero, zero, column, offset), (fields, levels, 1, STRIP)
        ).reshape(fields * levels, STRIP)

    boundary_strips = jax.vmap(cut_strip)(columns, offsets)
    inside = lax.broadcasted_iota(jnp.int32, (1, 1, STRIP), 2) < lengths[:, None, None]
    boundary_strips = jnp.where(inside, boundary_strips, 0.0).reshape(
        slots, fields * levels * STRIP
    )
    slot_ids = jnp.arange(slots, dtype=jnp.int32)
    earlier = slot_ids[None, :] < slot_ids[:, None]
    same = owners[:, None] == owners[None, :]
    rank = jnp.sum((same & earlier).astype(jnp.int32), axis=1)
    target = owners * CAP + rank
    routing = (jnp.arange(lon_count * CAP, dtype=jnp.int32)[:, None] == target[None, :]).astype(
        jnp.float32
    )
    outgoing = jnp.dot(
        routing, boundary_strips, precision=top_wavenumber_kept, preferred_element_type=jnp.float32
    ).reshape(lon_count, CAP, fields * levels * STRIP)
    arrived = lax.all_to_all(outgoing, "lon", split_axis=0, concat_axis=0, tiled=True)
    total = lon_count * CAP
    group = math.gcd(total, 16)
    pieces = arrived.reshape(total // group, group, fields * levels, STRIP)
    starts = nest_place.reshape(total // group, group)
    point = lax.broadcasted_iota(jnp.int32, (1, 1, NB), 2)
    row_step = lax.broadcasted_iota(jnp.int32, (1, STRIP, 1), 1) * RATIO

    def accumulate(carry, item):
        piece, begin = item
        offset = point - begin[:, None, None]
        hat = jnp.maximum(RATIO - jnp.abs(offset - row_step), 0)
        hat = (
            jnp.where((offset >= 0) & (offset < STRIP * RATIO), hat, 0).astype(jnp.float32) / RATIO
        )
        return (carry + jnp.einsum("gat,gtp->ap", piece, hat, precision=top_wavenumber_kept), None)

    boundary = lax.scan(
        accumulate, jnp.zeros((fields * levels, NB), jnp.float32), (pieces, starts)
    )[0]
    return (advanced_state, boundary.reshape(1, fields, levels, NB))


def local(model_state, *others):
    columns = model_state.shape[2]
    fits = lax.axis_size("lon") * STRIP == POLAR and model_state.shape[3] == 2 * POLAR
    if fits and columns % STEP == 0 and columns >= 2 * HELD:
        return compressed(model_state, *others)
    return transposed(model_state, *others)


def solution(mesh):
    return jax.shard_map(
        local,
        mesh=mesh,
        in_specs=(
            P(None, None, "lon", "lat"),
            P(None, "lat"),
            P(),
            P(),
            P(("lat", "lon"), None),
            P(("lat", "lon"), None, None),
        ),
        out_specs=(P(None, None, "lon", "lat"), P(("lat", "lon"), None, None, None)),
        check_vma=False,
    )
```

```python
import functools
import math

import jax
import jax.numpy as jnp
import numpy as np
from jax import lax
from jax.experimental import pallas as pl
from jax.experimental.pallas import tpu as pltpu
from jax.sharding import PartitionSpec as P

POLAR = 128
CAP = 2
STRIP = 16
RATIO = 11
NB = 2048
KC = 896
RANKS = (14, 5, 4, 4)
SPLIT_RANK = 14
STEP = 16
HELD = 80
EARLY_LISTS = 11
LATE = 2
VMEM_LIMIT = 48 * 1024 * 1024
F32 = jnp.float32
BF16 = jnp.bfloat16


def ceil8(value):
    return -(-value // 8) * 8


def shift_ranks(count):
    shifts = []
    for step in range(1, count // 2 + 1):
        for shift in (step, -step):
            if shift != -count // 2:
                shifts.append((shift, RANKS[min(step, len(RANKS)) - 1]))
    return shifts


def is_second(place, step, count):
    return lax.rem(lax.div(place, math.gcd(step, count)), 2) == 1


def swaps(pairs):
    return [pair for a, b in pairs for pair in ((a, b), (b, a))]


def ring_swaps(step, count):
    if 2 * step == count:
        return [swaps([(i, i + step) for i in range(step)])]
    groups = [[], []]
    for i in range(count):
        groups[i // math.gcd(step, count) % 2].append((i, (i + step) % count))
    return [swaps(group) for group in groups]


def split_table(table):
    high = table.astype(jnp.bfloat16)
    low = (table - high.astype(np.float64)).astype(jnp.bfloat16)
    return high, low


def factored(block, rank):
    left, values, right = np.linalg.svd(block)
    root = np.sqrt(values[:rank])
    return right[:rank] * root[:, None], left[:, :rank] * root[None, :]


@functools.lru_cache(maxsize=None)
def filter_tables(count, width):
    total = count * width
    half = width // 2

    def block(size, shift):
        place = np.arange(size)
        angle = np.pi * (shift + place[:, None] - place[None, :]) / total
        with np.errstate(divide="ignore"):
            return np.where(angle == 0, 0.0, 1.0 / (np.sin(angle) * total))

    senders, receivers = [], []
    for shift, rank in shift_ranks(count):
        sender, receiver = factored(block(width, shift * width), rank)
        senders.append(np.pad(sender, ((0, ceil8(rank) - rank), (0, 0))))
        receivers.append(receiver)
    nears = []
    for part, shift in enumerate((half, -half)):
        sender, receiver = factored(block(half, shift), SPLIT_RANK)
        rows = np.concatenate([block(half, 0), sender], axis=0)
        nears.append(np.pad(rows, ((0, 16 - SPLIT_RANK), (0, 0))))
        beyond = ((half, 0), (0, 0)) if part == 0 else ((0, half), (0, 0))
        receivers.append(np.pad(receiver, beyond))
    receivers = np.concatenate(receivers, axis=1)
    receivers = np.pad(receivers, ((0, 0), (0, HELD - receivers.shape[1])))
    near_high, near_low = split_table(np.concatenate(nears, axis=0))
    send_high, send_low = split_table(np.concatenate(senders, axis=0))
    far_high, far_low = split_table(receivers)
    return (
        np.concatenate([near_high, near_high, near_low], axis=1),
        np.concatenate([send_high, send_low], axis=0),
        np.concatenate([far_high, far_high, far_low], axis=1),
    )


def split_value(value):
    high = value.astype(BF16)
    return high, (value - high.astype(F32)).astype(BF16)


def modulated(row, cosine, sine):
    return jnp.concatenate([row * cosine[...], row * sine[...]], axis=1)


def stacked(value):
    high, low = split_value(value)
    return jnp.concatenate([high, low, high], axis=0)


def strip_rows(slots):
    return slots // 2


def payload_rows(rank, slots):
    return ceil8(slots * rank + strip_rows(slots))


def edge_kernel(meta, state, lon_pair, lon_cross, lat_pair, lat_cross, held, sems):
    fields, levels, columns, rows = state.shape
    copies = [
        [
            pltpu.make_async_copy(state.at[f, l], held.at[l, f], sems.at[l, f])
            for f in range(fields)
        ]
        for l in range(levels)
    ]
    for l in range(levels):
        for f in range(fields):
            copies[l][f].start()
    lane = lax.broadcasted_iota(jnp.int32, (columns, 128), 1)
    lon_odd = lax.rem(meta[2], 2) == 1
    lat_odd = lax.rem(meta[3], 2) == 1
    lon_pair[...] = jnp.zeros(lon_pair.shape, F32)
    lon_cross[...] = jnp.zeros(lon_cross.shape, F32)
    for l in range(levels):
        edges = jnp.zeros((columns, 128), F32)
        for f in range(fields):
            copies[l][f].wait()
            first = held[l, f, 0:1, :]
            last = held[l, f, columns - 1 : columns, :]
            lon_pair[l, f : f + 1, :] = jnp.where(lon_odd, first, last)
            lon_cross[l, f : f + 1, :] = jnp.where(lon_odd, last, first)
            edges = jnp.where(lane == f, held[l, f, :, 0:1], edges)
            edges = jnp.where(lane == 8 + f, held[l, f, :, rows - 1 : rows], edges)
        turned = edges.T
        north, south = turned[0:8], turned[8:16]
        lat_pair[l] = jnp.where(lat_odd, north, south)
        lat_cross[l] = jnp.where(lat_odd, south, north)


def stencil_kernel(
    count,
    meta,
    coupling,
    strips,
    lon_pair,
    lon_cross,
    lat_pair,
    lat_cross,
    diffusion,
    cosine,
    sine,
    send,
    state,
    updated,
    own,
    *rest,
):
    ranks = shift_ranks(count)
    payloads = rest[: len(ranks)]
    held, made, factors, placed, rows_cut, in_sems, out_sems = rest[len(ranks) :]
    fields, levels, columns, rows = state.shape
    tiles = rows // POLAR

    def copy_in(l, f):
        return pltpu.make_async_copy(state.at[f, l], held.at[l, f], in_sems.at[l, f])

    def copy_out(l, f):
        return pltpu.make_async_copy(made.at[l, f], updated.at[f, l], out_sems.at[l, f])

    for l in range(levels):
        for f in range(fields):
            copy_in(l, f).start()

    lane = lax.broadcasted_iota(jnp.int32, (STEP, POLAR), 1)
    lowest, highest = lane == 0, lane == POLAR - 1
    spans = [slice(tile * POLAR, (tile + 1) * POLAR) for tile in range(tiles)]
    along = [jnp.broadcast_to(diffusion[0:1, span], (STEP, POLAR)) for span in spans]
    across = [jnp.broadcast_to(diffusion[1:2, span], (STEP, POLAR)) for span in spans]
    centre = [1.0 - 2.0 * along[t] - 2.0 * across[t] for t in range(tiles)]
    start = pl.multiple_of(meta[0] * POLAR, POLAR)
    lon_odd = lax.rem(meta[2], 2) == 1
    lat_odd = lax.rem(meta[3], 2) == 1
    half = send.shape[0] // 2

    def one_level(l, carry):
        for f in range(fields):
            copy_in(l, f).wait()
        weights = [
            [coupling[l, f * fields + g] for g in range(fields)] for f in range(fields)
        ]
        west_halo = jnp.where(lon_odd, lon_pair[l], lon_cross[l])
        east_halo = jnp.where(lon_odd, lon_cross[l], lon_pair[l])
        north_halo = jnp.where(lat_odd, lat_pair[l], lat_cross[l])
        south_halo = jnp.where(lat_odd, lat_cross[l], lat_pair[l])
        halo = jnp.concatenate(
            [north_halo, south_halo, jnp.zeros((112, columns), F32)], axis=0
        ).T
        for begin in range(0, columns, STEP):
            end = begin + STEP
            here = [[held[l, f, begin:end, span] for span in spans] for f in range(fields)]
            for f in range(fields):
                down = [pltpu.roll(here[f][t], 1, 1) for t in range(tiles)]
                up = [pltpu.roll(here[f][t], POLAR - 1, 1) for t in range(tiles)]
                north_edge = [halo[begin:end, f : f + 1]] + down[:-1]
                south_edge = up[1:] + [halo[begin:end, 8 + f : 9 + f]]
                for t, span in enumerate(spans):
                    if begin == 0:
                        west = jnp.concatenate(
                            [west_halo[f : f + 1, span], held[l, f, 0 : STEP - 1, span]], axis=0
                        )
                    else:
                        west = held[l, f, begin - 1 : end - 1, span]
                    if end == columns:
                        east = jnp.concatenate(
                            [held[l, f, begin + 1 : end, span], east_halo[f : f + 1, span]],
                            axis=0,
                        )
                    else:
                        east = held[l, f, begin + 1 : end + 1, span]
                    north = jnp.where(lowest, north_edge[t], down[t])
                    south = jnp.where(highest, south_edge[t], up[t])
                    result = (centre[t] + weights[f][f]) * here[f][t]
                    result = result + along[t] * (east + west) + across[t] * (north + south)
                    for g in range(fields):
                        if g != f:
                            result = result + weights[f][g] * here[g][t]
                    made[l, f, begin:end, span] = result
        for f in range(fields):
            copy_out(l, f).start()
        for f in range(fields):
            row = made[l, f, :, pl.ds(start, POLAR)]
            high, low = split_value(modulated(row, cosine, sine))
            both = jnp.dot(send[...], high, preferred_element_type=F32)
            cross = jnp.dot(send[0:half, :], low, preferred_element_type=F32)
            factors[l * fields + f] = both[:half] + both[half:] + cross
        return carry

    lax.fori_loop(0, levels, one_level, 0)

    lon_index = meta[2]
    slots = strips.shape[0]
    lists = fields * levels
    each = strip_rows(lists)
    placed[...] = jnp.zeros(placed.shape, F32)
    rows_cut[...] = jnp.zeros(rows_cut.shape, F32)
    strip_lane = lax.broadcasted_iota(jnp.int32, (16, rows), 1)
    owners = [strips[s, 0] for s in range(slots)]
    for s in range(slots):
        column, offset, length = strips[s, 1], strips[s, 2], strips[s, 3]
        rank = jnp.int32(0)
        for earlier in range(s):
            rank = rank + (owners[earlier] == owners[s]).astype(jnp.int32)
        for l in range(levels):
            for f in range(fields):
                side, place = divmod(l * fields + f, each)
                rows_cut[s, side, place : place + 1, :] = made[l, f, pl.ds(column, 1), :]
        base = lax.rem(lon_index * CAP + rank, POLAR // STRIP) * STRIP
        shift = lax.rem(owners[s] - lon_index + count, count)
        for side in range(2):
            where = side * POLAR + base
            moved = pltpu.roll(rows_cut[s, side], lax.rem(where - offset + rows, rows), 1)
            inside = (strip_lane >= where) & (strip_lane < where + length)
            placed[shift] = placed[shift] + jnp.where(inside, moved, 0.0)
    own[...] = placed[0]

    place = 0
    index = 0
    while index < len(ranks):
        step, rank = ranks[index]
        padded = ceil8(rank)
        paired = 2 if 2 * step < count else 1
        second = is_second(lon_index, step, count)
        targets = payloads[index : index + paired]
        for item in range(lists):
            span = slice(item * rank, (item + 1) * rank)
            plus = factors[item, place : place + rank, :]
            if paired == 1:
                targets[0][span, :] = plus
            else:
                minus = factors[item, place + padded : place + padded + rank, :]
                targets[0][span, :] = jnp.where(second, minus, plus)
                targets[1][span, :] = jnp.where(second, plus, minus)
        plus, minus = placed[step][0:each, :], placed[count - step][0:each, :]
        targets[0][lists * rank : lists * rank + each, :] = jnp.where(second, minus, plus)
        if paired == 2:
            targets[1][lists * rank : lists * rank + each, :] = jnp.where(second, plus, minus)
        for target in targets:
            unused = target.shape[0] - lists * rank - each
            if unused:
                target[lists * rank + each :, :] = jnp.zeros((unused, rows), F32)
        place += paired * padded
        index += paired
    for l in range(levels):
        for f in range(fields):
            copy_out(l, f).wait()


def hat_kernel(begins, hats):
    point = lax.broadcasted_iota(jnp.int32, hats.shape, 1)
    place = lax.broadcasted_iota(jnp.int32, hats.shape, 0) % STRIP
    offset = point - begins[:, 0:1]
    hat = jnp.maximum(RATIO - jnp.abs(offset - place * RATIO), 0)
    hat = jnp.where((offset >= 0) & (offset < STRIP * RATIO), hat, 0)
    hats[...] = hat.astype(F32).astype(BF16)


def near_kernel(begin, passed, meta, cosine, sine, middle, near, rows, *rest):
    filtered, moments = rest[passed], rest[passed + 1]
    held, sems = rest[2 * passed + 2 :]
    fields = rows.shape[0]
    lists, columns, _ = filtered.shape
    half = columns // 2
    each = near.shape[0] // 2
    mine = pl.ds(pl.multiple_of(meta[0] * POLAR, POLAR), POLAR)

    def copy_in(item):
        l, f = (begin + item) // fields, (begin + item) % fields
        return pltpu.make_async_copy(rows.at[f, l, :, mine], held.at[item], sems.at[item])

    @pl.when(meta[1] == 1)
    def _():
        for item in range(lists):
            copy_in(item).start()

        def one(item, carry):
            copy_in(item).wait()
            for part in range(2):
                span = slice(part * half, (part + 1) * half)
                row = held[item, span, :]
                turn_cos, turn_sin = cosine[span, :], sine[span, :]
                value = jnp.concatenate([row * turn_cos, row * turn_sin], axis=1)
                table = near[part * each : (part + 1) * each, :]
                total = jnp.dot(table, stacked(value), preferred_element_type=F32)
                filtered[item, span, :] = (
                    turn_sin * total[:half, :POLAR]
                    - turn_cos * total[:half, POLAR:]
                    + middle[0:1, :] * row
                )
                moments[item, part * 16 : (part + 1) * 16, :] = total[half:, :]
            return carry

        lax.fori_loop(0, lists, one, 0)


def far_kernel(count, meta, cosine, sine, turn, far, hats, own, *rest):
    ranks = shift_ranks(count)
    payloads = rest[: len(ranks)]
    near_parts = (rest[len(ranks) : len(ranks) + 2], rest[len(ranks) + 2 : len(ranks) + 4])
    _, out, boundary, filtered, arrived, sems = rest[len(ranks) + 4 :]
    fields, levels = out.shape[0:2]
    lists = fields * levels
    each = strip_rows(lists)
    lon_index = meta[2]
    mine = pl.ds(pl.multiple_of(meta[0] * POLAR, POLAR), POLAR)

    def copy_out(item):
        l, f = item // fields, item % fields
        return pltpu.make_async_copy(filtered.at[item], out.at[f, l, :, mine], sems.at[item])

    def received(index, span):
        step = abs(ranks[index][0])
        if 2 * step == count:
            return payloads[index][span, :]
        base = index - index % 2
        first, last = payloads[base][span, :], payloads[base + 1][span, :]
        takes_first = is_second(lon_index, step, count)
        if index != base:
            takes_first = jnp.logical_not(takes_first)
        return jnp.where(takes_first, first, last)

    @pl.when(meta[1] == 1)
    def _():
        place = 0
        for index, (_, rank) in enumerate(ranks):
            turn_cos = turn[index : index + 1, :POLAR]
            turn_sin = turn[index : index + 1, POLAR:]
            for item in range(lists):
                value = received(index, slice(item * rank, (item + 1) * rank))
                cosines, sines = value[:, :POLAR], value[:, POLAR:]
                arrived[item, place : place + rank, :POLAR] = (
                    turn_cos * cosines + turn_sin * sines
                )
                arrived[item, place : place + rank, POLAR:] = (
                    turn_cos * sines - turn_sin * cosines
                )
            place += rank
        begin = 0
        for near, moments in near_parts:
            for item in range(near.shape[0]):
                for part in range(2):
                    at = place + part * SPLIT_RANK
                    arrived[begin + item, at : at + SPLIT_RANK, :] = moments[
                        item, part * 16 : part * 16 + SPLIT_RANK, :
                    ]
            begin += near.shape[0]
        place += 2 * SPLIT_RANK
        for item in range(lists):
            arrived[item, place:, :] = jnp.zeros((HELD - place, 2 * POLAR), F32)

        begin = 0
        for near, _ in near_parts:

            def one(item, carry, near=near, begin=begin):
                at = begin + item
                total = jnp.dot(far[...], stacked(arrived[at]), preferred_element_type=F32)
                filtered[at] = (
                    near[item] + sine[...] * total[:, :POLAR] - cosine[...] * total[:, POLAR:]
                )
                copy_out(at).start()
                return carry

            lax.fori_loop(0, near.shape[0], one, 0)
            begin += near.shape[0]

    groups = count * CAP * STRIP // POLAR
    sides = [[jnp.zeros((each, POLAR), F32)] * groups for _ in range(2)]
    for index in range(-1, len(ranks)):
        if index < 0:
            shift, arrival = 0, own[0:each, :]
        else:
            shift, rank = ranks[index]
            arrival = received(index, slice(lists * rank, lists * rank + each))
        source = lax.rem(lon_index - shift + count, count)
        group_at = lax.div(source, POLAR // (CAP * STRIP))
        for side in range(2):
            part = arrival[:, side * POLAR : (side + 1) * POLAR]
            for group in range(groups):
                sides[side][group] = sides[side][group] + jnp.where(group_at == group, part, 0.0)
    pieces = jnp.concatenate([jnp.concatenate(side, axis=1) for side in sides], axis=0)
    high = pieces.astype(BF16)
    middle, low = split_value(pieces - high.astype(F32))
    total = jnp.dot(high, hats[...], preferred_element_type=F32)
    total = total + jnp.dot(middle, hats[...], preferred_element_type=F32)
    total = total + jnp.dot(low, hats[...], preferred_element_type=F32)
    total = total * (1.0 / RATIO)
    for l in range(levels):
        for f in range(fields):
            item = l * fields + f
            boundary[0, f, l : l + 1, :] = total[item : item + 1, :]

    @pl.when(meta[1] == 1)
    def _():
        for item in range(lists):
            copy_out(item).wait()


def phase_table(kept, steps, period):
    phase = (2 * kept - 1)[None, :] * steps[:, None] % (2 * period)
    angle = phase.astype(F32) * (math.pi / period)
    return jnp.cos(angle), jnp.sin(angle)


def cost(flops, bytes_accessed):
    return pl.CostEstimate(flops=flops, bytes_accessed=bytes_accessed, transcendentals=0)


def compressed(model_state, diffusion, coupling, cutoff, strip_list, nest_place):
    lat_index = lax.axis_index("lat")
    lon_index = lax.axis_index("lon")
    lat_count = lax.axis_size("lat")
    lon_count = lax.axis_size("lon")
    fields, levels, columns, rows = model_state.shape
    lists = fields * levels
    total_columns = columns * lon_count
    ranks = shift_ranks(lon_count)
    near, send, far = [jnp.asarray(table) for table in filter_tables(lon_count, columns)]
    params = pltpu.CompilerParams(vmem_limit_bytes=VMEM_LIMIT)
    shape = lambda *sizes: jax.ShapeDtypeStruct(sizes, F32)
    whole_state = shape(*model_state.shape)

    is_south = lat_index == lat_count - 1
    is_polar = (lat_index == 0) | is_south
    part = jnp.where(is_south, rows // POLAR - 1, 0)
    meta = jnp.stack([part, is_polar.astype(jnp.int32), lon_index, lat_index]).astype(jnp.int32)
    kept = jnp.where(lat_index < lat_count // 2, cutoff[:POLAR], cutoff[POLAR:])
    cosine, sine = phase_table(kept, jnp.arange(columns, dtype=jnp.int32), total_columns)
    steps = jnp.array([abs(shift) for shift, _ in ranks], jnp.int32)
    sign = np.array([[1.0 if shift > 0 else -1.0] for shift, _ in ranks], np.float32)
    turn_cos, turn_sin = phase_table(kept, steps, lon_count)
    turn = jnp.concatenate([turn_cos, turn_sin * sign], axis=1)
    turn = jnp.pad(turn, ((0, ceil8(len(ranks)) - len(ranks)), (0, 0)))
    middle = ((2 * kept - 1).astype(F32) / total_columns)[None, :]
    begins = jnp.broadcast_to(
        jnp.repeat(nest_place.reshape(-1), STRIP)[:, None], (lon_count * CAP * STRIP, 128)
    )

    smem = pl.BlockSpec(memory_space=pltpu.SMEM)
    vmem = pl.BlockSpec(memory_space=pltpu.VMEM)
    hbm = pl.BlockSpec(memory_space=pl.ANY)
    level_sems = pltpu.SemaphoreType.DMA((levels, fields))
    state_scratch = pltpu.VMEM((levels, fields, columns, rows), F32)

    with jax.named_scope("edges"):
        edges = pl.pallas_call(
            edge_kernel,
            in_specs=[smem, hbm],
            out_specs=[vmem] * 4,
            out_shape=[shape(levels, 8, rows)] * 2 + [shape(levels, 8, columns)] * 2,
            scratch_shapes=[state_scratch, level_sems],
            compiler_params=params,
        )(meta, model_state)

    with jax.named_scope("halo"):
        lon_pairs, lon_crosses = ring_swaps(1, lon_count)
        lat_pairs = [(i, i + 1) for i in range(0, lat_count, 2)]
        lat_crosses = [(i, i + 1) for i in range(1, lat_count - 1, 2)]
        halos = [
            lax.ppermute(edges[0], "lon", lon_pairs),
            lax.ppermute(edges[1], "lon", lon_crosses),
            lax.ppermute(edges[2], "lat", swaps(lat_pairs)),
            lax.ppermute(edges[3], "lat", swaps(lat_crosses)),
        ]

    with jax.named_scope("hats"):
        hats = pl.pallas_call(
            hat_kernel,
            in_specs=[vmem],
            out_specs=vmem,
            out_shape=jax.ShapeDtypeStruct((begins.shape[0], NB), BF16),
            compiler_params=params,
            cost_estimate=cost(10 * begins.shape[0] * NB, 2 * begins.shape[0] * NB),
        )(begins)

    sizes = [payload_rows(rank, lists) for _, rank in ranks]
    with jax.named_scope("stencil"):
        updated, own, *outgoing = pl.pallas_call(
            functools.partial(stencil_kernel, lon_count),
            in_specs=[smem] * 3 + [vmem] * 8 + [hbm],
            out_specs=[hbm] + [vmem] * (1 + len(ranks)),
            out_shape=[whole_state, shape(16, rows)] + [shape(size, rows) for size in sizes],
            scratch_shapes=[
                state_scratch,
                state_scratch,
                pltpu.VMEM((lists, send.shape[0] // 2, rows), F32),
                pltpu.VMEM((lon_count, 16, rows), F32),
                pltpu.VMEM((strip_list.shape[0], 2, 16, rows), F32),
                level_sems,
                level_sems,
            ],
            compiler_params=params,
        )(
            meta,
            coupling.reshape(levels, fields * fields),
            strip_list,
            *halos,
            diffusion,
            cosine,
            sine,
            send,
            model_state,
        )

    def exchange(index, payload):
        step = abs(ranks[index][0])
        swap = index % 2 if 2 * step < lon_count else 0
        return lax.ppermute(payload, "lon", ring_swaps(step, lon_count)[swap])

    late = [index for index, (shift, _) in enumerate(ranks) if abs(shift) == LATE]
    early = [index for index in range(len(ranks)) if index not in late]
    with jax.named_scope("exchange"):
        incoming = {index: exchange(index, outgoing[index]) for index in early}

    def near_part(begin, end, passed):
        results = pl.pallas_call(
            functools.partial(near_kernel, begin, len(passed)),
            in_specs=[smem] + [vmem] * 4 + [hbm] * (1 + len(passed)),
            out_specs=[vmem] * 2 + [hbm] * len(passed),
            out_shape=[shape(end - begin, columns, POLAR), shape(end - begin, 32, rows)]
            + [shape(*payload.shape) for payload in passed],
            input_output_aliases={6 + index: 2 + index for index in range(len(passed))},
            scratch_shapes=[
                pltpu.VMEM((end - begin, columns, POLAR), F32),
                pltpu.SemaphoreType.DMA((end - begin,)),
            ],
            compiler_params=params,
            cost_estimate=cost(
                12 * (end - begin) * columns * columns * POLAR, 8 * (end - begin) * columns * POLAR
            ),
        )(meta, cosine, sine, middle, near, updated, *passed)
        return results[:2], results[2:]

    with jax.named_scope("near"):
        near_first, passed = near_part(0, EARLY_LISTS, [outgoing[index] for index in late])
    with jax.named_scope("late_exchange"):
        for index, payload in zip(late, passed):
            incoming[index] = exchange(index, payload)
    with jax.named_scope("near_rest"):
        near_last, passed = near_part(EARLY_LISTS, lists, [incoming[index] for index in early])
        incoming.update(zip(early, passed))

    with jax.named_scope("far"):
        advanced, boundary = pl.pallas_call(
            functools.partial(far_kernel, lon_count),
            in_specs=[smem] + [vmem] * (10 + len(ranks)) + [hbm],
            out_specs=[hbm, vmem],
            out_shape=[whole_state, shape(1, fields, levels, NB)],
            input_output_aliases={11 + len(ranks): 0},
            scratch_shapes=[
                pltpu.VMEM((lists, columns, POLAR), F32),
                pltpu.VMEM((lists, HELD, rows), F32),
                pltpu.SemaphoreType.DMA((lists,)),
            ],
            compiler_params=pltpu.CompilerParams(vmem_limit_bytes=VMEM_LIMIT // 2),
        )(
            meta,
            cosine,
            sine,
            turn,
            far,
            hats,
            own,
            *[incoming[index] for index in range(len(ranks))],
            *near_first,
            *near_last,
            updated,
        )
    return advanced, boundary


def padded_2(block, sides, width):
    for axis, dim in sides:
        count = lax.axis_size(axis)
        forward = [(i, i + 1) for i in range(count - 1)]
        forward.append((count - 1, 0))
        backward = [(target, source) for source, target in forward]
        low = lax.ppermute(
            lax.slice_in_dim(block, block.shape[dim] - width, None, axis=dim), axis, forward
        )
        high = lax.ppermute(lax.slice_in_dim(block, 0, width, axis=dim), axis, backward)
        block = jnp.concatenate([low, block, high], axis=dim)
    return block


def spectral_filter(rows, kept):
    top_wavenumber_kept = lax.Precision.HIGHEST
    length = rows.shape[3]
    width = math.gcd(KC, 128)
    column_grid = lax.broadcasted_iota(jnp.int32, (length, width), 0)
    step_output = jnp.zeros_like(rows)
    for block_index in range(KC // width):
        wavenumber = block_index * width + lax.broadcasted_iota(jnp.int32, (length, width), 1)
        phase = column_grid * wavenumber % length
        angle = phase.astype(jnp.float32) * (2.0 * math.pi / length)
        cosine = jnp.cos(angle)
        sine = jnp.sin(angle)
        along = block_index * width + jnp.arange(width, dtype=jnp.int32)
        scale = jnp.where(along == 0, 1.0 / length, 2.0 / length)
        weight = jnp.where(along[None, :] < kept[:, None], scale[None, :], 0.0)
        real_part = (
            jnp.einsum("flrn,nk->flrk", rows, cosine, precision=top_wavenumber_kept) * weight
        )
        imaginary_component = (
            jnp.einsum("flrn,nk->flrk", rows, sine, precision=top_wavenumber_kept) * weight
        )
        step_output = (
            step_output
            + jnp.einsum("flrk,nk->flrn", real_part, cosine, precision=top_wavenumber_kept)
            + jnp.einsum("flrk,nk->flrn", imaginary_component, sine, precision=top_wavenumber_kept)
        )
    return step_output


def polar_pass(work_rows, kept_start, kept_table):
    count = work_rows.shape[2] // lax.axis_size("lon")
    kept = lax.dynamic_slice_in_dim(kept_table, kept_start + lax.axis_index("lon") * count, count)
    return lax.all_to_all(
        spectral_filter(
            lax.all_to_all(work_rows, "lon", split_axis=2, concat_axis=3, tiled=True), kept
        ),
        "lon",
        split_axis=3,
        concat_axis=2,
        tiled=True,
    )


def transposed(model_state, diffusion, coupling, cutoff, strip_list, nest_place):
    top_wavenumber_kept = lax.Precision.HIGHEST
    lat_index = lax.axis_index("lat")
    lat_count = lax.axis_size("lat")
    lon_count = lax.axis_size("lon")
    fields, levels, lon_local, lat_local = model_state.shape
    padded = padded_2(model_state, (("lat", 3), ("lon", 2)), 1)
    east_west = padded[:, :, 2:, 1:-1] + padded[:, :, :-2, 1:-1]
    row_place = lax.broadcasted_iota(jnp.int32, (1, 1, 1, lat_local), 3)
    northern = jnp.where((lat_index == 0) & (row_place == 0), 0.0, padded[:, :, 1:-1, :-2])
    southern = jnp.where(
        (lat_index == lat_count - 1) & (row_place == lat_local - 1), 0.0, padded[:, :, 1:-1, 2:]
    )
    blended = jnp.einsum("lfg,glij->flij", coupling, model_state, precision=top_wavenumber_kept)
    updated = (
        model_state
        + diffusion[0] * (east_west - 2.0 * model_state)
        + diffusion[1] * (northern + southern - 2.0 * model_state)
        + blended
    )
    is_south = lat_index == lat_count - 1
    is_polar = (lat_index == 0) | is_south
    start = jnp.where(is_south, lat_local - POLAR, 0).astype(jnp.int32)
    band_base = jnp.where(lat_index < lat_count // 2, 0, POLAR).astype(jnp.int32)
    block_rows = lax.dynamic_slice_in_dim(updated, start, POLAR, 3)
    polar_rows = jnp.transpose(block_rows, (0, 1, 3, 2))
    filtered = polar_pass(polar_rows, band_base, cutoff)
    new_rows = jnp.where(is_polar, jnp.transpose(filtered, (0, 1, 3, 2)), block_rows)
    advanced_state = lax.dynamic_update_slice_in_dim(updated, new_rows, start, 3)
    slots = strip_list.shape[0]
    owners = strip_list[:, 0]
    columns = strip_list[:, 1]
    offsets = strip_list[:, 2]
    lengths = strip_list[:, 3]
    zero = jnp.zeros((), jnp.int32)

    def cut_strip(column, offset):
        return lax.dynamic_slice(
            updated, (zero, zero, column, offset), (fields, levels, 1, STRIP)
        ).reshape(fields * levels, STRIP)

    boundary_strips = jax.vmap(cut_strip)(columns, offsets)
    inside = lax.broadcasted_iota(jnp.int32, (1, 1, STRIP), 2) < lengths[:, None, None]
    boundary_strips = jnp.where(inside, boundary_strips, 0.0).reshape(
        slots, fields * levels * STRIP
    )
    slot_ids = jnp.arange(slots, dtype=jnp.int32)
    earlier = slot_ids[None, :] < slot_ids[:, None]
    same = owners[:, None] == owners[None, :]
    rank = jnp.sum((same & earlier).astype(jnp.int32), axis=1)
    target = owners * CAP + rank
    routing = (jnp.arange(lon_count * CAP, dtype=jnp.int32)[:, None] == target[None, :]).astype(
        jnp.float32
    )
    outgoing = jnp.dot(
        routing, boundary_strips, precision=top_wavenumber_kept, preferred_element_type=jnp.float32
    ).reshape(lon_count, CAP, fields * levels * STRIP)
    arrived = lax.all_to_all(outgoing, "lon", split_axis=0, concat_axis=0, tiled=True)
    total = lon_count * CAP
    group = math.gcd(total, 16)
    pieces = arrived.reshape(total // group, group, fields * levels, STRIP)
    starts = nest_place.reshape(total // group, group)
    point = lax.broadcasted_iota(jnp.int32, (1, 1, NB), 2)
    row_step = lax.broadcasted_iota(jnp.int32, (1, STRIP, 1), 1) * RATIO

    def accumulate(carry, item):
        piece, begin = item
        offset = point - begin[:, None, None]
        hat = jnp.maximum(RATIO - jnp.abs(offset - row_step), 0)
        hat = (
            jnp.where((offset >= 0) & (offset < STRIP * RATIO), hat, 0).astype(jnp.float32) / RATIO
        )
        return (carry + jnp.einsum("gat,gtp->ap", piece, hat, precision=top_wavenumber_kept), None)

    boundary = lax.scan(
        accumulate, jnp.zeros((fields * levels, NB), jnp.float32), (pieces, starts)
    )[0]
    return (advanced_state, boundary.reshape(1, fields, levels, NB))


def local(model_state, *others):
    columns = model_state.shape[2]
    fits = lax.axis_size("lon") * STRIP == POLAR and model_state.shape[3] == 2 * POLAR
    if fits and columns % STEP == 0 and columns >= 2 * HELD:
        return compressed(model_state, *others)
    return transposed(model_state, *others)


def solution(mesh):
    return jax.shard_map(
        local,
        mesh=mesh,
        in_specs=(
            P(None, None, "lon", "lat"),
            P(None, "lat"),
            P(),
            P(),
            P(("lat", "lon"), None),
            P(("lat", "lon"), None, None),
        ),
        out_specs=(P(None, None, "lon", "lat"), P(("lat", "lon"), None, None, None)),
        check_vma=False,
    )
```

```python
import functools
import math

import jax
import jax.numpy as jnp
import numpy as np
from jax import lax
from jax.experimental import pallas as pl
from jax.experimental.pallas import tpu as pltpu
from jax.sharding import PartitionSpec as P

POLAR = 128
CAP = 2
STRIP = 16
RATIO = 11
NB = 2048
KC = 896
RANKS = (14, 5, 4, 4)
SPLIT_RANK = 14
STEP = 16
HELD = 80
EARLY_LISTS = 12
LATE = 2
VMEM_LIMIT = 48 * 1024 * 1024
F32 = jnp.float32
BF16 = jnp.bfloat16


def ceil8(value):
    return -(-value // 8) * 8


def shift_ranks(count):
    shifts = []
    for step in range(1, count // 2 + 1):
        for shift in (step, -step):
            if shift != -count // 2:
                shifts.append((shift, RANKS[min(step, len(RANKS)) - 1]))
    return shifts


def is_second(place, step, count):
    return lax.rem(lax.div(place, math.gcd(step, count)), 2) == 1


def swaps(pairs):
    return [pair for a, b in pairs for pair in ((a, b), (b, a))]


def ring_swaps(step, count):
    if 2 * step == count:
        return [swaps([(i, i + step) for i in range(step)])]
    groups = [[], []]
    for i in range(count):
        groups[i // math.gcd(step, count) % 2].append((i, (i + step) % count))
    return [swaps(group) for group in groups]


def split_table(table):
    high = table.astype(jnp.bfloat16)
    low = (table - high.astype(np.float64)).astype(jnp.bfloat16)
    return high, low


def factored(block, rank):
    left, values, right = np.linalg.svd(block)
    root = np.sqrt(values[:rank])
    return right[:rank] * root[:, None], left[:, :rank] * root[None, :]


@functools.lru_cache(maxsize=None)
def filter_tables(count, width):
    total = count * width
    half = width // 2

    def block(size, shift):
        place = np.arange(size)
        angle = np.pi * (shift + place[:, None] - place[None, :]) / total
        with np.errstate(divide="ignore"):
            return np.where(angle == 0, 0.0, 1.0 / (np.sin(angle) * total))

    senders, receivers = [], []
    for shift, rank in shift_ranks(count):
        sender, receiver = factored(block(width, shift * width), rank)
        senders.append(np.pad(sender, ((0, ceil8(rank) - rank), (0, 0))))
        receivers.append(receiver)
    nears = []
    for part, shift in enumerate((half, -half)):
        sender, receiver = factored(block(half, shift), SPLIT_RANK)
        rows = np.concatenate([block(half, 0), sender], axis=0)
        nears.append(np.pad(rows, ((0, 16 - SPLIT_RANK), (0, 0))))
        beyond = ((half, 0), (0, 0)) if part == 0 else ((0, half), (0, 0))
        receivers.append(np.pad(receiver, beyond))
    receivers = np.concatenate(receivers, axis=1)
    receivers = np.pad(receivers, ((0, 0), (0, HELD - receivers.shape[1])))
    nears = [table for rows in nears for table in split_table(rows)]
    send_high, send_low = split_table(np.concatenate(senders, axis=0))
    far_high, far_low = split_table(receivers)
    return (
        np.concatenate(nears, axis=0),
        np.concatenate([send_high, send_low], axis=0),
        np.concatenate([far_high, far_high, far_low], axis=1),
    )


def hat_table():
    width = -(-STRIP * RATIO // POLAR) * POLAR
    point = np.arange(width)
    table = np.zeros((POLAR, CAP * width), np.float32)
    for rank in range(CAP):
        for row in range(STRIP):
            hat = np.maximum(RATIO - np.abs(point - row * RATIO), 0) * (point < STRIP * RATIO)
            table[rank * STRIP + row, rank * width : (rank + 1) * width] = hat
    return table.astype(jnp.bfloat16)


def split_value(value):
    high = value.astype(BF16)
    return high, (value - high.astype(F32)).astype(BF16)


def modulated(row, cosine, sine):
    return jnp.concatenate([row * cosine[...], row * sine[...]], axis=1)


def stacked(value):
    high, low = split_value(value)
    return jnp.concatenate([high, low, high], axis=0)


def strip_rows(slots):
    return slots // 2


def payload_rows(rank, slots):
    return ceil8(slots * rank + strip_rows(slots))


def edge_kernel(meta, state, lon_pair, lon_cross, lat_pair, lat_cross, held, sems):
    fields, levels, columns, rows = state.shape
    copies = [
        [
            pltpu.make_async_copy(state.at[f, l], held.at[l, f], sems.at[l, f])
            for f in range(fields)
        ]
        for l in range(levels)
    ]
    for l in range(levels):
        for f in range(fields):
            copies[l][f].start()
    lane = lax.broadcasted_iota(jnp.int32, (columns, 128), 1)
    lon_odd = lax.rem(meta[2], 2) == 1
    lat_odd = lax.rem(meta[3], 2) == 1
    lon_pair[...] = jnp.zeros(lon_pair.shape, F32)
    lon_cross[...] = jnp.zeros(lon_cross.shape, F32)
    for l in range(levels):
        edges = jnp.zeros((columns, 128), F32)
        for f in range(fields):
            copies[l][f].wait()
            first = held[l, f, 0:1, :]
            last = held[l, f, columns - 1 : columns, :]
            lon_pair[l, f : f + 1, :] = jnp.where(lon_odd, first, last)
            lon_cross[l, f : f + 1, :] = jnp.where(lon_odd, last, first)
            edges = jnp.where(lane == f, held[l, f, :, 0:1], edges)
            edges = jnp.where(lane == 8 + f, held[l, f, :, rows - 1 : rows], edges)
        turned = edges.T
        north, south = turned[0:8], turned[8:16]
        lat_pair[l] = jnp.where(lat_odd, north, south)
        lat_cross[l] = jnp.where(lat_odd, south, north)


def stencil_kernel(
    count,
    meta,
    coupling,
    strips,
    lon_pair,
    lon_cross,
    lat_pair,
    lat_cross,
    diffusion,
    cosine,
    sine,
    send,
    state,
    updated,
    own,
    *rest,
):
    ranks = shift_ranks(count)
    payloads = rest[: len(ranks)]
    held, made, factors, placed, rows_cut, in_sems, out_sems = rest[len(ranks) :]
    fields, levels, columns, rows = state.shape
    tiles = rows // POLAR
    spans = [slice(tile * POLAR, (tile + 1) * POLAR) for tile in range(tiles)]

    def copy_in(l, f, t):
        return pltpu.make_async_copy(
            state.at[f, l, :, spans[t]], held.at[l, f, t], in_sems.at[l, f, t]
        )

    def copy_out(l, f, t):
        return pltpu.make_async_copy(
            made.at[l, f, t], updated.at[f, l, :, spans[t]], out_sems.at[l, f, t]
        )

    for l in range(levels):
        for f in range(fields):
            for t in range(tiles):
                copy_in(l, f, t).start()

    lane = lax.broadcasted_iota(jnp.int32, (STEP, POLAR), 1)
    lowest, highest = lane == 0, lane == POLAR - 1
    along = [jnp.broadcast_to(diffusion[0:1, span], (STEP, POLAR)) for span in spans]
    across = [jnp.broadcast_to(diffusion[1:2, span], (STEP, POLAR)) for span in spans]
    centre = [1.0 - 2.0 * along[t] - 2.0 * across[t] for t in range(tiles)]
    lon_odd = lax.rem(meta[2], 2) == 1
    lat_odd = lax.rem(meta[3], 2) == 1
    half = send.shape[0] // 2

    def one_level(l, carry):
        for f in range(fields):
            for t in range(tiles):
                copy_in(l, f, t).wait()
        weights = [
            [coupling[l, f * fields + g] for g in range(fields)] for f in range(fields)
        ]
        west_halo = jnp.where(lon_odd, lon_pair[l], lon_cross[l])
        east_halo = jnp.where(lon_odd, lon_cross[l], lon_pair[l])
        north_halo = jnp.where(lat_odd, lat_pair[l], lat_cross[l])
        south_halo = jnp.where(lat_odd, lat_cross[l], lat_pair[l])
        halo = jnp.concatenate(
            [north_halo, south_halo, jnp.zeros((112, columns), F32)], axis=0
        ).T
        for begin in range(0, columns, STEP):
            end = begin + STEP
            here = [[held[l, f, t, begin:end, :] for t in range(tiles)] for f in range(fields)]
            for f in range(fields):
                down = [pltpu.roll(here[f][t], 1, 1) for t in range(tiles)]
                up = [pltpu.roll(here[f][t], POLAR - 1, 1) for t in range(tiles)]
                north_edge = [halo[begin:end, f : f + 1]] + down[:-1]
                south_edge = up[1:] + [halo[begin:end, 8 + f : 9 + f]]
                for t, span in enumerate(spans):
                    if begin == 0:
                        west = jnp.concatenate(
                            [west_halo[f : f + 1, span], held[l, f, t, 0 : STEP - 1, :]], axis=0
                        )
                    else:
                        west = held[l, f, t, begin - 1 : end - 1, :]
                    if end == columns:
                        east = jnp.concatenate(
                            [held[l, f, t, begin + 1 : end, :], east_halo[f : f + 1, span]],
                            axis=0,
                        )
                    else:
                        east = held[l, f, t, begin + 1 : end + 1, :]
                    north = jnp.where(lowest, north_edge[t], down[t])
                    south = jnp.where(highest, south_edge[t], up[t])
                    result = (centre[t] + weights[f][f]) * here[f][t]
                    result = result + along[t] * (east + west) + across[t] * (north + south)
                    for g in range(fields):
                        if g != f:
                            result = result + weights[f][g] * here[g][t]
                    made[l, f, t, begin:end, :] = result
        for f in range(fields):
            for t in range(tiles):
                copy_out(l, f, t).start()
        for f in range(fields):
            row = made[l, f, meta[0]]
            high, low = split_value(modulated(row, cosine, sine))
            both = jnp.dot(send[...], high, preferred_element_type=F32)
            cross = jnp.dot(send[0:half, :], low, preferred_element_type=F32)
            factors[l * fields + f] = both[:half] + both[half:] + cross
        return carry

    lax.fori_loop(0, levels, one_level, 0)

    lon_index = meta[2]
    slots = strips.shape[0]
    lists = fields * levels
    each = strip_rows(lists)
    placed[...] = jnp.zeros(placed.shape, F32)
    rows_cut[...] = jnp.zeros(rows_cut.shape, F32)
    strip_lane = lax.broadcasted_iota(jnp.int32, (16, rows), 1)
    owners = [strips[s, 0] for s in range(slots)]
    for s in range(slots):
        column, offset, length = strips[s, 1], strips[s, 2], strips[s, 3]
        rank = jnp.int32(0)
        for earlier in range(s):
            rank = rank + (owners[earlier] == owners[s]).astype(jnp.int32)
        for l in range(levels):
            for f in range(fields):
                side, place = divmod(l * fields + f, each)
                for t, span in enumerate(spans):
                    rows_cut[s, side, place : place + 1, span] = made[l, f, t, pl.ds(column, 1), :]
        base = rank * STRIP
        shift = lax.rem(owners[s] - lon_index + count, count)
        for side in range(2):
            where = side * POLAR + base
            moved = pltpu.roll(rows_cut[s, side], lax.rem(where - offset + rows, rows), 1)
            inside = (strip_lane >= where) & (strip_lane < where + length)
            placed[shift] = placed[shift] + jnp.where(inside, moved, 0.0)
    own[...] = placed[0]

    place = 0
    index = 0
    while index < len(ranks):
        step, rank = ranks[index]
        padded = ceil8(rank)
        paired = 2 if 2 * step < count else 1
        second = is_second(lon_index, step, count)
        targets = payloads[index : index + paired]
        for item in range(lists):
            span = slice(item * rank, (item + 1) * rank)
            plus = factors[item, place : place + rank, :]
            if paired == 1:
                targets[0][span, :] = plus
            else:
                minus = factors[item, place + padded : place + padded + rank, :]
                targets[0][span, :] = jnp.where(second, minus, plus)
                targets[1][span, :] = jnp.where(second, plus, minus)
        plus, minus = placed[step][0:each, :], placed[count - step][0:each, :]
        targets[0][lists * rank : lists * rank + each, :] = jnp.where(second, minus, plus)
        if paired == 2:
            targets[1][lists * rank : lists * rank + each, :] = jnp.where(second, plus, minus)
        for target in targets:
            unused = target.shape[0] - lists * rank - each
            if unused:
                target[lists * rank + each :, :] = jnp.zeros((unused, rows), F32)
        place += paired * padded
        index += paired
    for l in range(levels):
        for f in range(fields):
            for t in range(tiles):
                copy_out(l, f, t).wait()


def near_kernel(begin, passed, meta, cosine, sine, middle, near, rows, *rest):
    filtered, moments = rest[passed], rest[passed + 1]
    held, sems = rest[2 * passed + 2 :]
    fields = rows.shape[0]
    lists, columns, _ = filtered.shape
    half = columns // 2
    each = near.shape[0] // 4
    mine = pl.ds(pl.multiple_of(meta[0] * POLAR, POLAR), POLAR)

    def copy_in(item):
        l, f = (begin + item) // fields, (begin + item) % fields
        return pltpu.make_async_copy(rows.at[f, l, :, mine], held.at[item], sems.at[item])

    @pl.when(meta[1] == 1)
    def _():
        for item in range(lists):
            copy_in(item).start()

        def one(item, carry):
            copy_in(item).wait()
            for part in range(2):
                span = slice(part * half, (part + 1) * half)
                row = held[item, span, :]
                turn_cos, turn_sin = cosine[span, :], sine[span, :]
                value = jnp.concatenate([row * turn_cos, row * turn_sin], axis=1)
                table = near[2 * part * each : 2 * (part + 1) * each, :]
                high, low = split_value(value)
                both = jnp.dot(table, high, preferred_element_type=F32)
                cross = jnp.dot(table[:each], low, preferred_element_type=F32)
                total = both[:each] + both[each:] + cross
                filtered[item, span, :] = (
                    turn_sin * total[:half, :POLAR]
                    - turn_cos * total[:half, POLAR:]
                    + middle[0:1, :] * row
                )
                moments[item, part * 16 : (part + 1) * 16, :] = total[half:, :]
            return carry

        lax.fori_loop(0, lists, one, 0, unroll=4)


def far_kernel(count, meta, begins, cosine, sine, turn, far, hats, own, *rest):
    ranks = shift_ranks(count)
    payloads = rest[: len(ranks)]
    near_parts = (rest[len(ranks) : len(ranks) + 2], rest[len(ranks) + 2 : len(ranks) + 4])
    _, out, boundary, filtered, arrived, sums, sems = rest[len(ranks) + 4 :]
    fields, levels = out.shape[0:2]
    lists = fields * levels
    each = strip_rows(lists)
    lon_index = meta[2]
    mine = pl.ds(pl.multiple_of(meta[0] * POLAR, POLAR), POLAR)

    def copy_out(item):
        l, f = item // fields, item % fields
        return pltpu.make_async_copy(filtered.at[item], out.at[f, l, :, mine], sems.at[item])

    def received(index, span):
        step = abs(ranks[index][0])
        if 2 * step == count:
            return payloads[index][span, :]
        base = index - index % 2
        first, last = payloads[base][span, :], payloads[base + 1][span, :]
        takes_first = is_second(lon_index, step, count)
        if index != base:
            takes_first = jnp.logical_not(takes_first)
        return jnp.where(takes_first, first, last)

    @pl.when(meta[1] == 1)
    def _():
        place = 0
        for index, (_, rank) in enumerate(ranks):
            turn_cos = turn[index : index + 1, :POLAR]
            turn_sin = turn[index : index + 1, POLAR:]
            for item in range(lists):
                value = received(index, slice(item * rank, (item + 1) * rank))
                cosines, sines = value[:, :POLAR], value[:, POLAR:]
                arrived[item, place : place + rank, :POLAR] = (
                    turn_cos * cosines + turn_sin * sines
                )
                arrived[item, place : place + rank, POLAR:] = (
                    turn_cos * sines - turn_sin * cosines
                )
            place += rank
        begin = 0
        for near, moments in near_parts:
            for item in range(near.shape[0]):
                for part in range(2):
                    at = place + part * SPLIT_RANK
                    arrived[begin + item, at : at + SPLIT_RANK, :] = moments[
                        item, part * 16 : part * 16 + SPLIT_RANK, :
                    ]
            begin += near.shape[0]
        place += 2 * SPLIT_RANK
        for item in range(lists):
            arrived[item, place:, :] = jnp.zeros((HELD - place, 2 * POLAR), F32)

        begin = 0
        for near, _ in near_parts:

            def one(item, carry, near=near, begin=begin):
                at = begin + item
                total = jnp.dot(far[...], stacked(arrived[at]), preferred_element_type=F32)
                filtered[at] = (
                    near[item] + sine[...] * total[:, :POLAR] - cosine[...] * total[:, POLAR:]
                )
                copy_out(at).start()
                return carry

            lax.fori_loop(0, near.shape[0], one, 0, unroll=4)
            begin += near.shape[0]

    sums[...] = jnp.zeros(sums.shape, F32)
    pieces, sources = [], []
    blank = jnp.zeros((16 - each, POLAR), F32)
    for index in range(-1, len(ranks)):
        if index < 0:
            shift, arrival = 0, own[0:each, :]
        else:
            shift, rank = ranks[index]
            arrival = received(index, slice(lists * rank, lists * rank + each))
        sources.append(lax.rem(lon_index - shift + count, count))
        pieces += [arrival[:, :POLAR], blank, arrival[:, POLAR:], blank]
    pieces = jnp.concatenate(pieces, axis=0)
    high = pieces.astype(BF16)
    middle, low = split_value(pieces - high.astype(F32))
    points = jnp.dot(high, hats[...], preferred_element_type=F32)
    points = points + jnp.dot(middle, hats[...], preferred_element_type=F32)
    points = points + jnp.dot(low, hats[...], preferred_element_type=F32)
    width = hats.shape[1] // CAP
    beyond = jnp.zeros((32, POLAR), F32)
    for index, source in enumerate(sources):
        for rank in range(CAP):
            place = begins[source, rank]
            offset = lax.rem(place, POLAR)
            span = points[index * 32 : (index + 1) * 32, rank * width : (rank + 1) * width]
            moved = pltpu.roll(jnp.concatenate([span, beyond], axis=1), offset, 1)
            at = pl.ds(pl.multiple_of(place - offset, POLAR), width + POLAR)
            sums[:, at] = sums[:, at] + moved
    for l in range(levels):
        for f in range(fields):
            side, row = divmod(l * fields + f, each)
            row = side * 16 + row
            boundary[0, f, l : l + 1, :] = sums[row : row + 1, 0:NB] * (1.0 / RATIO)

    @pl.when(meta[1] == 1)
    def _():
        for item in range(lists):
            copy_out(item).wait()


def phase_table(kept, steps, period):
    phase = (2 * kept - 1)[None, :] * steps[:, None] % (2 * period)
    angle = phase.astype(F32) * (math.pi / period)
    return jnp.cos(angle), jnp.sin(angle)


def cost(flops, bytes_accessed):
    return pl.CostEstimate(flops=flops, bytes_accessed=bytes_accessed, transcendentals=0)


def compressed(model_state, diffusion, coupling, cutoff, strip_list, nest_place):
    lat_index = lax.axis_index("lat")
    lon_index = lax.axis_index("lon")
    lat_count = lax.axis_size("lat")
    lon_count = lax.axis_size("lon")
    fields, levels, columns, rows = model_state.shape
    lists = fields * levels
    total_columns = columns * lon_count
    ranks = shift_ranks(lon_count)
    near, send, far = [jnp.asarray(table) for table in filter_tables(lon_count, columns)]
    params = pltpu.CompilerParams(vmem_limit_bytes=VMEM_LIMIT)
    shape = lambda *sizes: jax.ShapeDtypeStruct(sizes, F32)
    whole_state = shape(*model_state.shape)

    is_south = lat_index == lat_count - 1
    is_polar = (lat_index == 0) | is_south
    part = jnp.where(is_south, rows // POLAR - 1, 0)
    meta = jnp.stack([part, is_polar.astype(jnp.int32), lon_index, lat_index]).astype(jnp.int32)
    kept = jnp.where(lat_index < lat_count // 2, cutoff[:POLAR], cutoff[POLAR:])
    cosine, sine = phase_table(kept, jnp.arange(columns, dtype=jnp.int32), total_columns)
    steps = jnp.array([abs(shift) for shift, _ in ranks], jnp.int32)
    sign = np.array([[1.0 if shift > 0 else -1.0] for shift, _ in ranks], np.float32)
    turn_cos, turn_sin = phase_table(kept, steps, lon_count)
    turn = jnp.concatenate([turn_cos, turn_sin * sign], axis=1)
    turn = jnp.pad(turn, ((0, ceil8(len(ranks)) - len(ranks)), (0, 0)))
    middle = ((2 * kept - 1).astype(F32) / total_columns)[None, :]
    hats = jnp.asarray(hat_table())

    smem = pl.BlockSpec(memory_space=pltpu.SMEM)
    vmem = pl.BlockSpec(memory_space=pltpu.VMEM)
    hbm = pl.BlockSpec(memory_space=pl.ANY)
    tiles = rows // POLAR
    tile_sems = pltpu.SemaphoreType.DMA((levels, fields, tiles))
    tile_scratch = pltpu.VMEM((levels, fields, tiles, columns, POLAR), F32)

    with jax.named_scope("edges"):
        edges = pl.pallas_call(
            edge_kernel,
            in_specs=[smem, hbm],
            out_specs=[vmem] * 4,
            out_shape=[shape(levels, 8, rows)] * 2 + [shape(levels, 8, columns)] * 2,
            scratch_shapes=[
                pltpu.VMEM((levels, fields, columns, rows), F32),
                pltpu.SemaphoreType.DMA((levels, fields)),
            ],
            compiler_params=params,
        )(meta, model_state)

    with jax.named_scope("halo"):
        lon_pairs, lon_crosses = ring_swaps(1, lon_count)
        lat_pairs = [(i, i + 1) for i in range(0, lat_count, 2)]
        lat_crosses = [(i, i + 1) for i in range(1, lat_count - 1, 2)]
        halos = [
            lax.ppermute(edges[0], "lon", lon_pairs),
            lax.ppermute(edges[1], "lon", lon_crosses),
            lax.ppermute(edges[2], "lat", swaps(lat_pairs)),
            lax.ppermute(edges[3], "lat", swaps(lat_crosses)),
        ]

    sizes = [payload_rows(rank, lists) for _, rank in ranks]
    with jax.named_scope("stencil"):
        updated, own, *outgoing = pl.pallas_call(
            functools.partial(stencil_kernel, lon_count),
            in_specs=[smem] * 3 + [vmem] * 8 + [hbm],
            out_specs=[hbm] + [vmem] * (1 + len(ranks)),
            out_shape=[whole_state, shape(16, rows)] + [shape(size, rows) for size in sizes],
            scratch_shapes=[
                tile_scratch,
                tile_scratch,
                pltpu.VMEM((lists, send.shape[0] // 2, rows), F32),
                pltpu.VMEM((lon_count, 16, rows), F32),
                pltpu.VMEM((strip_list.shape[0], 2, 16, rows), F32),
                tile_sems,
                tile_sems,
            ],
            compiler_params=params,
        )(
            meta,
            coupling.reshape(levels, fields * fields),
            strip_list,
            *halos,
            diffusion,
            cosine,
            sine,
            send,
            model_state,
        )

    def exchange(index, payload):
        step = abs(ranks[index][0])
        swap = index % 2 if 2 * step < lon_count else 0
        return lax.ppermute(payload, "lon", ring_swaps(step, lon_count)[swap])

    late = [index for index, (shift, _) in enumerate(ranks) if abs(shift) == LATE]
    early = [index for index in range(len(ranks)) if index not in late]
    with jax.named_scope("exchange"):
        incoming = {index: exchange(index, outgoing[index]) for index in early}

    def near_part(begin, end, passed):
        results = pl.pallas_call(
            functools.partial(near_kernel, begin, len(passed)),
            in_specs=[smem] + [vmem] * 4 + [hbm] * (1 + len(passed)),
            out_specs=[vmem] * 2 + [hbm] * len(passed),
            out_shape=[shape(end - begin, columns, POLAR), shape(end - begin, 32, rows)]
            + [shape(*payload.shape) for payload in passed],
            input_output_aliases={6 + index: 2 + index for index in range(len(passed))},
            scratch_shapes=[
                pltpu.VMEM((end - begin, columns, POLAR), F32),
                pltpu.SemaphoreType.DMA((end - begin,)),
            ],
            compiler_params=params,
            cost_estimate=cost(
                12 * (end - begin) * columns * columns * POLAR, 8 * (end - begin) * columns * POLAR
            ),
        )(meta, cosine, sine, middle, near, updated, *passed)
        return results[:2], results[2:]

    with jax.named_scope("near"):
        near_first, passed = near_part(0, EARLY_LISTS, [outgoing[index] for index in late])
    with jax.named_scope("late_exchange"):
        for index, payload in zip(late, passed):
            incoming[index] = exchange(index, payload)
    with jax.named_scope("near_rest"):
        near_last, passed = near_part(EARLY_LISTS, lists, [incoming[index] for index in early])
        incoming.update(zip(early, passed))

    with jax.named_scope("far"):
        advanced, boundary = pl.pallas_call(
            functools.partial(far_kernel, lon_count),
            in_specs=[smem] * 2 + [vmem] * (10 + len(ranks)) + [hbm],
            out_specs=[hbm, vmem],
            out_shape=[whole_state, shape(1, fields, levels, NB)],
            input_output_aliases={12 + len(ranks): 0},
            scratch_shapes=[
                pltpu.VMEM((lists, columns, POLAR), F32),
                pltpu.VMEM((lists, HELD, rows), F32),
                pltpu.VMEM((32, NB + 2 * POLAR), F32),
                pltpu.SemaphoreType.DMA((lists,)),
            ],
            compiler_params=pltpu.CompilerParams(vmem_limit_bytes=VMEM_LIMIT // 2),
        )(
            meta,
            nest_place.reshape(lon_count, CAP),
            cosine,
            sine,
            turn,
            far,
            hats,
            own,
            *[incoming[index] for index in range(len(ranks))],
            *near_first,
            *near_last,
            updated,
        )
    return advanced, boundary


def padded_2(block, sides, width):
    for axis, dim in sides:
        count = lax.axis_size(axis)
        forward = [(i, i + 1) for i in range(count - 1)]
        forward.append((count - 1, 0))
        backward = [(target, source) for source, target in forward]
        low = lax.ppermute(
            lax.slice_in_dim(block, block.shape[dim] - width, None, axis=dim), axis, forward
        )
        high = lax.ppermute(lax.slice_in_dim(block, 0, width, axis=dim), axis, backward)
        block = jnp.concatenate([low, block, high], axis=dim)
    return block


def spectral_filter(rows, kept):
    top_wavenumber_kept = lax.Precision.HIGHEST
    length = rows.shape[3]
    width = math.gcd(KC, 128)
    column_grid = lax.broadcasted_iota(jnp.int32, (length, width), 0)
    step_output = jnp.zeros_like(rows)
    for block_index in range(KC // width):
        wavenumber = block_index * width + lax.broadcasted_iota(jnp.int32, (length, width), 1)
        phase = column_grid * wavenumber % length
        angle = phase.astype(jnp.float32) * (2.0 * math.pi / length)
        cosine = jnp.cos(angle)
        sine = jnp.sin(angle)
        along = block_index * width + jnp.arange(width, dtype=jnp.int32)
        scale = jnp.where(along == 0, 1.0 / length, 2.0 / length)
        weight = jnp.where(along[None, :] < kept[:, None], scale[None, :], 0.0)
        real_part = (
            jnp.einsum("flrn,nk->flrk", rows, cosine, precision=top_wavenumber_kept) * weight
        )
        imaginary_component = (
            jnp.einsum("flrn,nk->flrk", rows, sine, precision=top_wavenumber_kept) * weight
        )
        step_output = (
            step_output
            + jnp.einsum("flrk,nk->flrn", real_part, cosine, precision=top_wavenumber_kept)
            + jnp.einsum("flrk,nk->flrn", imaginary_component, sine, precision=top_wavenumber_kept)
        )
    return step_output


def polar_pass(work_rows, kept_start, kept_table):
    count = work_rows.shape[2] // lax.axis_size("lon")
    kept = lax.dynamic_slice_in_dim(kept_table, kept_start + lax.axis_index("lon") * count, count)
    return lax.all_to_all(
        spectral_filter(
            lax.all_to_all(work_rows, "lon", split_axis=2, concat_axis=3, tiled=True), kept
        ),
        "lon",
        split_axis=3,
        concat_axis=2,
        tiled=True,
    )


def transposed(model_state, diffusion, coupling, cutoff, strip_list, nest_place):
    top_wavenumber_kept = lax.Precision.HIGHEST
    lat_index = lax.axis_index("lat")
    lat_count = lax.axis_size("lat")
    lon_count = lax.axis_size("lon")
    fields, levels, lon_local, lat_local = model_state.shape
    padded = padded_2(model_state, (("lat", 3), ("lon", 2)), 1)
    east_west = padded[:, :, 2:, 1:-1] + padded[:, :, :-2, 1:-1]
    row_place = lax.broadcasted_iota(jnp.int32, (1, 1, 1, lat_local), 3)
    northern = jnp.where((lat_index == 0) & (row_place == 0), 0.0, padded[:, :, 1:-1, :-2])
    southern = jnp.where(
        (lat_index == lat_count - 1) & (row_place == lat_local - 1), 0.0, padded[:, :, 1:-1, 2:]
    )
    blended = jnp.einsum("lfg,glij->flij", coupling, model_state, precision=top_wavenumber_kept)
    updated = (
        model_state
        + diffusion[0] * (east_west - 2.0 * model_state)
        + diffusion[1] * (northern + southern - 2.0 * model_state)
        + blended
    )
    is_south = lat_index == lat_count - 1
    is_polar = (lat_index == 0) | is_south
    start = jnp.where(is_south, lat_local - POLAR, 0).astype(jnp.int32)
    band_base = jnp.where(lat_index < lat_count // 2, 0, POLAR).astype(jnp.int32)
    block_rows = lax.dynamic_slice_in_dim(updated, start, POLAR, 3)
    polar_rows = jnp.transpose(block_rows, (0, 1, 3, 2))
    filtered = polar_pass(polar_rows, band_base, cutoff)
    new_rows = jnp.where(is_polar, jnp.transpose(filtered, (0, 1, 3, 2)), block_rows)
    advanced_state = lax.dynamic_update_slice_in_dim(updated, new_rows, start, 3)
    slots = strip_list.shape[0]
    owners = strip_list[:, 0]
    columns = strip_list[:, 1]
    offsets = strip_list[:, 2]
    lengths = strip_list[:, 3]
    zero = jnp.zeros((), jnp.int32)

    def cut_strip(column, offset):
        return lax.dynamic_slice(
            updated, (zero, zero, column, offset), (fields, levels, 1, STRIP)
        ).reshape(fields * levels, STRIP)

    boundary_strips = jax.vmap(cut_strip)(columns, offsets)
    inside = lax.broadcasted_iota(jnp.int32, (1, 1, STRIP), 2) < lengths[:, None, None]
    boundary_strips = jnp.where(inside, boundary_strips, 0.0).reshape(
        slots, fields * levels * STRIP
    )
    slot_ids = jnp.arange(slots, dtype=jnp.int32)
    earlier = slot_ids[None, :] < slot_ids[:, None]
    same = owners[:, None] == owners[None, :]
    rank = jnp.sum((same & earlier).astype(jnp.int32), axis=1)
    target = owners * CAP + rank
    routing = (jnp.arange(lon_count * CAP, dtype=jnp.int32)[:, None] == target[None, :]).astype(
        jnp.float32
    )
    outgoing = jnp.dot(
        routing, boundary_strips, precision=top_wavenumber_kept, preferred_element_type=jnp.float32
    ).reshape(lon_count, CAP, fields * levels * STRIP)
    arrived = lax.all_to_all(outgoing, "lon", split_axis=0, concat_axis=0, tiled=True)
    total = lon_count * CAP
    group = math.gcd(total, 16)
    pieces = arrived.reshape(total // group, group, fields * levels, STRIP)
    starts = nest_place.reshape(total // group, group)
    point = lax.broadcasted_iota(jnp.int32, (1, 1, NB), 2)
    row_step = lax.broadcasted_iota(jnp.int32, (1, STRIP, 1), 1) * RATIO

    def accumulate(carry, item):
        piece, begin = item
        offset = point - begin[:, None, None]
        hat = jnp.maximum(RATIO - jnp.abs(offset - row_step), 0)
        hat = (
            jnp.where((offset >= 0) & (offset < STRIP * RATIO), hat, 0).astype(jnp.float32) / RATIO
        )
        return (carry + jnp.einsum("gat,gtp->ap", piece, hat, precision=top_wavenumber_kept), None)

    boundary = lax.scan(
        accumulate, jnp.zeros((fields * levels, NB), jnp.float32), (pieces, starts)
    )[0]
    return (advanced_state, boundary.reshape(1, fields, levels, NB))


def local(model_state, *others):
    columns = model_state.shape[2]
    fits = lax.axis_size("lon") * STRIP == POLAR and model_state.shape[3] == 2 * POLAR
    if fits and columns % STEP == 0 and columns >= 2 * HELD:
        return compressed(model_state, *others)
    return transposed(model_state, *others)


def solution(mesh):
    return jax.shard_map(
        local,
        mesh=mesh,
        in_specs=(
            P(None, None, "lon", "lat"),
            P(None, "lat"),
            P(),
            P(),
            P(("lat", "lon"), None),
            P(("lat", "lon"), None, None),
        ),
        out_specs=(P(None, None, "lon", "lat"), P(("lat", "lon"), None, None, None)),
        check_vma=False,
    )
```

```python
import functools
import math

import jax
import jax.numpy as jnp
import numpy as np
from jax import lax
from jax.experimental import pallas as pl
from jax.experimental.pallas import tpu as pltpu
from jax.sharding import PartitionSpec as P

POLAR = 128
CAP = 2
STRIP = 16
RATIO = 11
NB = 2048
KC = 896
RANKS = (14, 5, 4, 4)
SPLIT_RANK = 14
STEP = 16
HELD = 80
EARLY_LISTS = 12
LATE = 2
VMEM_LIMIT = 48 * 1024 * 1024
F32 = jnp.float32
BF16 = jnp.bfloat16


def ceil8(value):
    return -(-value // 8) * 8


def shift_ranks(count):
    shifts = []
    for step in range(1, count // 2 + 1):
        for shift in (step, -step):
            if shift != -count // 2:
                shifts.append((shift, RANKS[min(step, len(RANKS)) - 1]))
    return shifts


def is_second(place, step, count):
    return lax.rem(lax.div(place, math.gcd(step, count)), 2) == 1


def swaps(pairs):
    return [pair for a, b in pairs for pair in ((a, b), (b, a))]


def ring_swaps(step, count):
    if 2 * step == count:
        return [swaps([(i, i + step) for i in range(step)])]
    groups = [[], []]
    for i in range(count):
        groups[i // math.gcd(step, count) % 2].append((i, (i + step) % count))
    return [swaps(group) for group in groups]


def split_table(table):
    high = table.astype(jnp.bfloat16)
    low = (table - high.astype(np.float64)).astype(jnp.bfloat16)
    return high, low


def factored(block, rank):
    left, values, right = np.linalg.svd(block)
    root = np.sqrt(values[:rank])
    return right[:rank] * root[:, None], left[:, :rank] * root[None, :]


@functools.lru_cache(maxsize=None)
def filter_tables(count, width):
    total = count * width
    half = width // 2

    def block(size, shift):
        place = np.arange(size)
        angle = np.pi * (shift + place[:, None] - place[None, :]) / total
        with np.errstate(divide="ignore"):
            return np.where(angle == 0, 0.0, 1.0 / (np.sin(angle) * total))

    senders, receivers = [], []
    for shift, rank in shift_ranks(count):
        sender, receiver = factored(block(width, shift * width), rank)
        senders.append(np.pad(sender, ((0, ceil8(rank) - rank), (0, 0))))
        receivers.append(receiver)
    nears = []
    for part, shift in enumerate((half, -half)):
        sender, receiver = factored(block(half, shift), SPLIT_RANK)
        rows = np.concatenate([block(half, 0), sender], axis=0)
        nears.append(np.pad(rows, ((0, 16 - SPLIT_RANK), (0, 0))))
        beyond = ((half, 0), (0, 0)) if part == 0 else ((0, half), (0, 0))
        receivers.append(np.pad(receiver, beyond))
    receivers = np.concatenate(receivers, axis=1)
    receivers = np.pad(receivers, ((0, 0), (0, HELD - receivers.shape[1])))
    nears = [table for rows in nears for table in split_table(rows)]
    send_high, send_low = split_table(np.concatenate(senders, axis=0))
    far_high, far_low = split_table(receivers)
    return (
        np.concatenate(nears, axis=0),
        np.concatenate([send_high, send_low], axis=0),
        np.concatenate([far_high, far_high, far_low], axis=1),
    )


def hat_table():
    width = -(-STRIP * RATIO // POLAR) * POLAR
    point = np.arange(width)
    table = np.zeros((POLAR, CAP * width), np.float32)
    for rank in range(CAP):
        for row in range(STRIP):
            hat = np.maximum(RATIO - np.abs(point - row * RATIO), 0) * (point < STRIP * RATIO)
            table[rank * STRIP + row, rank * width : (rank + 1) * width] = hat
    return table.astype(jnp.bfloat16)


def split_value(value):
    high = value.astype(BF16)
    return high, (value - high.astype(F32)).astype(BF16)


def modulated(row, cosine, sine):
    return jnp.concatenate([row * cosine[...], row * sine[...]], axis=1)


def stacked(value):
    high, low = split_value(value)
    return jnp.concatenate([high, low, high], axis=0)


def strip_rows(slots):
    return slots // 2


def payload_rows(rank, slots):
    return ceil8(slots * rank + strip_rows(slots))


def edge_kernel(meta, state, lon_pair, lon_cross, lat_pair, lat_cross, held, sems):
    fields, levels, columns, rows = state.shape
    copies = [
        [
            pltpu.make_async_copy(state.at[f, l], held.at[l, f], sems.at[l, f])
            for f in range(fields)
        ]
        for l in range(levels)
    ]
    for l in range(levels):
        for f in range(fields):
            copies[l][f].start()
    lane = lax.broadcasted_iota(jnp.int32, (columns, 128), 1)
    lon_odd = lax.rem(meta[2], 2) == 1
    lat_odd = lax.rem(meta[3], 2) == 1
    lon_pair[...] = jnp.zeros(lon_pair.shape, F32)
    lon_cross[...] = jnp.zeros(lon_cross.shape, F32)
    for l in range(levels):
        edges = jnp.zeros((columns, 128), F32)
        for f in range(fields):
            copies[l][f].wait()
            first = held[l, f, 0:1, :]
            last = held[l, f, columns - 1 : columns, :]
            lon_pair[l, f : f + 1, :] = jnp.where(lon_odd, first, last)
            lon_cross[l, f : f + 1, :] = jnp.where(lon_odd, last, first)
            edges = jnp.where(lane == f, held[l, f, :, 0:1], edges)
            edges = jnp.where(lane == 8 + f, held[l, f, :, rows - 1 : rows], edges)
        turned = edges.T
        north, south = turned[0:8], turned[8:16]
        lat_pair[l] = jnp.where(lat_odd, north, south)
        lat_cross[l] = jnp.where(lat_odd, south, north)


def stencil_kernel(
    count,
    meta,
    coupling,
    strips,
    lon_pair,
    lon_cross,
    lat_pair,
    lat_cross,
    diffusion,
    cosine,
    sine,
    send,
    state,
    updated,
    own,
    *rest,
):
    ranks = shift_ranks(count)
    payloads = rest[: len(ranks)]
    held, made, halo, factors, placed, rows_cut, in_sems, out_sems = rest[len(ranks) :]
    fields, levels, columns, rows = state.shape
    tiles = rows // POLAR
    spans = [slice(tile * POLAR, (tile + 1) * POLAR) for tile in range(tiles)]

    def copy_in(l, f, t):
        return pltpu.make_async_copy(
            state.at[f, l, :, spans[t]],
            held.at[l, f, t, pl.ds(8, columns)],
            in_sems.at[l, f, t],
        )

    def copy_out(l, f, t):
        return pltpu.make_async_copy(
            made.at[l, f, t], updated.at[f, l, :, spans[t]], out_sems.at[l, f, t]
        )

    for l in range(levels):
        for f in range(fields):
            for t in range(tiles):
                copy_in(l, f, t).start()

    lane = lax.broadcasted_iota(jnp.int32, (STEP // 2, POLAR), 1)
    lowest, highest = lane == 0, lane == POLAR - 1
    along = [jnp.broadcast_to(diffusion[0:1, span], (STEP // 2, POLAR)) for span in spans]
    across = [jnp.broadcast_to(diffusion[1:2, span], (STEP // 2, POLAR)) for span in spans]
    centre = [1.0 - 2.0 * along[t] - 2.0 * across[t] for t in range(tiles)]
    lon_odd = lax.rem(meta[2], 2) == 1
    lat_odd = lax.rem(meta[3], 2) == 1
    half = send.shape[0] // 2

    def one_level(l, carry):
        for f in range(fields):
            for t in range(tiles):
                copy_in(l, f, t).wait()
        weights = [
            [coupling[l, f * fields + g] for g in range(fields)] for f in range(fields)
        ]
        west_halo = jnp.where(lon_odd, lon_pair[l], lon_cross[l])
        east_halo = jnp.where(lon_odd, lon_cross[l], lon_pair[l])
        north_halo = jnp.where(lat_odd, lat_pair[l], lat_cross[l])
        south_halo = jnp.where(lat_odd, lat_cross[l], lat_pair[l])
        halo[...] = jnp.concatenate(
            [north_halo, south_halo, jnp.zeros((112, columns), F32)], axis=0
        ).T
        for f in range(fields):
            for t, span in enumerate(spans):
                held[l, f, t, 7:8, :] = west_halo[f : f + 1, span]
                held[l, f, t, columns + 8 : columns + 9, :] = east_halo[f : f + 1, span]
        for begin in range(0, columns, STEP):
            strided = lambda f, t, start: held[l, f, t, pl.ds(start + 8, STEP // 2, stride=2), :]
            both = [
                [[strided(f, t, begin + odd) for odd in range(2)] for t in range(tiles)]
                for f in range(fields)
            ]
            for odd in range(2):
                place = pl.ds(begin + odd, STEP // 2, stride=2)
                edges = halo[place, :]
                for f in range(fields):
                    here = [both[f][t][odd] for t in range(tiles)]
                    down = [pltpu.roll(here[t], 1, 1) for t in range(tiles)]
                    up = [pltpu.roll(here[t], POLAR - 1, 1) for t in range(tiles)]
                    north_edge = [edges[:, f : f + 1]] + down[:-1]
                    south_edge = up[1:] + [edges[:, 8 + f : 9 + f]]
                    for t in range(tiles):
                        beyond = strided(f, t, begin + 2 if odd else begin - 1)
                        north = jnp.where(lowest, north_edge[t], down[t])
                        south = jnp.where(highest, south_edge[t], up[t])
                        result = (centre[t] + weights[f][f]) * here[t]
                        result = result + along[t] * (both[f][t][1 - odd] + beyond)
                        result = result + across[t] * (north + south)
                        for g in range(fields):
                            if g != f:
                                result = result + weights[f][g] * both[g][t][odd]
                        made[l, f, t, place, :] = result
        for f in range(fields):
            for t in range(tiles):
                copy_out(l, f, t).start()
        for f in range(fields):
            row = made[l, f, meta[0]]
            high, low = split_value(modulated(row, cosine, sine))
            both = jnp.dot(send[...], high, preferred_element_type=F32)
            cross = jnp.dot(send[0:half, :], low, preferred_element_type=F32)
            factors[l * fields + f] = both[:half] + both[half:] + cross
        return carry

    lax.fori_loop(0, levels, one_level, 0)

    lon_index = meta[2]
    slots = strips.shape[0]
    lists = fields * levels
    each = strip_rows(lists)
    placed[...] = jnp.zeros(placed.shape, F32)
    rows_cut[...] = jnp.zeros(rows_cut.shape, F32)
    strip_lane = lax.broadcasted_iota(jnp.int32, (16, rows), 1)
    owners = [strips[s, 0] for s in range(slots)]
    for s in range(slots):
        column, offset, length = strips[s, 1], strips[s, 2], strips[s, 3]
        rank = jnp.int32(0)
        for earlier in range(s):
            rank = rank + (owners[earlier] == owners[s]).astype(jnp.int32)
        for l in range(levels):
            for f in range(fields):
                side, place = divmod(l * fields + f, each)
                for t, span in enumerate(spans):
                    rows_cut[s, side, place : place + 1, span] = made[l, f, t, pl.ds(column, 1), :]
        base = rank * STRIP
        shift = lax.rem(owners[s] - lon_index + count, count)
        for side in range(2):
            where = side * POLAR + base
            moved = pltpu.roll(rows_cut[s, side], lax.rem(where - offset + rows, rows), 1)
            inside = (strip_lane >= where) & (strip_lane < where + length)
            placed[shift] = placed[shift] + jnp.where(inside, moved, 0.0)
    own[...] = placed[0]

    place = 0
    index = 0
    while index < len(ranks):
        step, rank = ranks[index]
        padded = ceil8(rank)
        paired = 2 if 2 * step < count else 1
        second = is_second(lon_index, step, count)
        targets = payloads[index : index + paired]
        for item in range(lists):
            span = slice(item * rank, (item + 1) * rank)
            plus = factors[item, place : place + rank, :]
            if paired == 1:
                targets[0][span, :] = plus
            else:
                minus = factors[item, place + padded : place + padded + rank, :]
                targets[0][span, :] = jnp.where(second, minus, plus)
                targets[1][span, :] = jnp.where(second, plus, minus)
        plus, minus = placed[step][0:each, :], placed[count - step][0:each, :]
        targets[0][lists * rank : lists * rank + each, :] = jnp.where(second, minus, plus)
        if paired == 2:
            targets[1][lists * rank : lists * rank + each, :] = jnp.where(second, plus, minus)
        for target in targets:
            unused = target.shape[0] - lists * rank - each
            if unused:
                target[lists * rank + each :, :] = jnp.zeros((unused, rows), F32)
        place += paired * padded
        index += paired
    for l in range(levels):
        for f in range(fields):
            for t in range(tiles):
                copy_out(l, f, t).wait()


def near_kernel(begin, passed, meta, cosine, sine, middle, near, rows, *rest):
    filtered, moments = rest[passed], rest[passed + 1]
    held, sems = rest[2 * passed + 2 :]
    fields = rows.shape[0]
    lists, columns, _ = filtered.shape
    half = columns // 2
    each = near.shape[0] // 4
    mine = pl.ds(pl.multiple_of(meta[0] * POLAR, POLAR), POLAR)

    def copy_in(item):
        l, f = (begin + item) // fields, (begin + item) % fields
        return pltpu.make_async_copy(rows.at[f, l, :, mine], held.at[item], sems.at[item])

    @pl.when(meta[1] == 1)
    def _():
        for item in range(lists):
            copy_in(item).start()

        def one(item, carry):
            copy_in(item).wait()
            for part in range(2):
                span = slice(part * half, (part + 1) * half)
                row = held[item, span, :]
                turn_cos, turn_sin = cosine[span, :], sine[span, :]
                value = jnp.concatenate([row * turn_cos, row * turn_sin], axis=1)
                table = near[2 * part * each : 2 * (part + 1) * each, :]
                high, low = split_value(value)
                both = jnp.dot(table, high, preferred_element_type=F32)
                cross = jnp.dot(table[:each], low, preferred_element_type=F32)
                total = both[:each] + both[each:] + cross
                filtered[item, span, :] = (
                    turn_sin * total[:half, :POLAR]
                    - turn_cos * total[:half, POLAR:]
                    + middle[0:1, :] * row
                )
                moments[item, part * 16 : (part + 1) * 16, :] = total[half:, :]
            return carry

        lax.fori_loop(0, lists, one, 0, unroll=4)


def far_kernel(count, meta, begins, cosine, sine, turn, far, hats, own, *rest):
    ranks = shift_ranks(count)
    payloads = rest[: len(ranks)]
    near_parts = (rest[len(ranks) : len(ranks) + 2], rest[len(ranks) + 2 : len(ranks) + 4])
    _, out, boundary, filtered, arrived, sums, sems = rest[len(ranks) + 4 :]
    fields, levels = out.shape[0:2]
    lists = fields * levels
    each = strip_rows(lists)
    lon_index = meta[2]
    mine = pl.ds(pl.multiple_of(meta[0] * POLAR, POLAR), POLAR)

    def copy_out(item):
        l, f = item // fields, item % fields
        return pltpu.make_async_copy(filtered.at[item], out.at[f, l, :, mine], sems.at[item])

    def received(index, span):
        step = abs(ranks[index][0])
        if 2 * step == count:
            return payloads[index][span, :]
        base = index - index % 2
        first, last = payloads[base][span, :], payloads[base + 1][span, :]
        takes_first = is_second(lon_index, step, count)
        if index != base:
            takes_first = jnp.logical_not(takes_first)
        return jnp.where(takes_first, first, last)

    @pl.when(meta[1] == 1)
    def _():
        place = 0
        for index, (_, rank) in enumerate(ranks):
            turn_cos = turn[index : index + 1, :POLAR]
            turn_sin = turn[index : index + 1, POLAR:]
            for item in range(lists):
                value = received(index, slice(item * rank, (item + 1) * rank))
                cosines, sines = value[:, :POLAR], value[:, POLAR:]
                arrived[item, place : place + rank, :POLAR] = (
                    turn_cos * cosines + turn_sin * sines
                )
                arrived[item, place : place + rank, POLAR:] = (
                    turn_cos * sines - turn_sin * cosines
                )
            place += rank
        begin = 0
        for near, moments in near_parts:
            for item in range(near.shape[0]):
                for part in range(2):
                    at = place + part * SPLIT_RANK
                    arrived[begin + item, at : at + SPLIT_RANK, :] = moments[
                        item, part * 16 : part * 16 + SPLIT_RANK, :
                    ]
            begin += near.shape[0]
        place += 2 * SPLIT_RANK
        for item in range(lists):
            arrived[item, place:, :] = jnp.zeros((HELD - place, 2 * POLAR), F32)

        begin = 0
        for near, _ in near_parts:

            def one(item, carry, near=near, begin=begin):
                at = begin + item
                total = jnp.dot(far[...], stacked(arrived[at]), preferred_element_type=F32)
                filtered[at] = (
                    near[item] + sine[...] * total[:, :POLAR] - cosine[...] * total[:, POLAR:]
                )
                copy_out(at).start()
                return carry

            lax.fori_loop(0, near.shape[0], one, 0, unroll=4)
            begin += near.shape[0]

    sums[...] = jnp.zeros(sums.shape, F32)
    pieces, sources = [], []
    blank = jnp.zeros((16 - each, POLAR), F32)
    for index in range(-1, len(ranks)):
        if index < 0:
            shift, arrival = 0, own[0:each, :]
        else:
            shift, rank = ranks[index]
            arrival = received(index, slice(lists * rank, lists * rank + each))
        sources.append(lax.rem(lon_index - shift + count, count))
        pieces += [arrival[:, :POLAR], blank, arrival[:, POLAR:], blank]
    pieces = jnp.concatenate(pieces, axis=0)
    high = pieces.astype(BF16)
    middle, low = split_value(pieces - high.astype(F32))
    points = jnp.dot(high, hats[...], preferred_element_type=F32)
    points = points + jnp.dot(middle, hats[...], preferred_element_type=F32)
    points = points + jnp.dot(low, hats[...], preferred_element_type=F32)
    width = hats.shape[1] // CAP
    beyond = jnp.zeros((32, POLAR), F32)
    for index, source in enumerate(sources):
        for rank in range(CAP):
            place = begins[source, rank]
            offset = lax.rem(place, POLAR)
            span = points[index * 32 : (index + 1) * 32, rank * width : (rank + 1) * width]
            moved = pltpu.roll(jnp.concatenate([span, beyond], axis=1), offset, 1)
            at = pl.ds(pl.multiple_of(place - offset, POLAR), width + POLAR)
            sums[:, at] = sums[:, at] + moved
    for l in range(levels):
        for f in range(fields):
            side, row = divmod(l * fields + f, each)
            row = side * 16 + row
            boundary[0, f, l : l + 1, :] = sums[row : row + 1, 0:NB] * (1.0 / RATIO)

    @pl.when(meta[1] == 1)
    def _():
        for item in range(lists):
            copy_out(item).wait()


def phase_table(kept, steps, period):
    phase = (2 * kept - 1)[None, :] * steps[:, None] % (2 * period)
    angle = phase.astype(F32) * (math.pi / period)
    return jnp.cos(angle), jnp.sin(angle)


def cost(flops, bytes_accessed):
    return pl.CostEstimate(flops=flops, bytes_accessed=bytes_accessed, transcendentals=0)


def compressed(model_state, diffusion, coupling, cutoff, strip_list, nest_place):
    lat_index = lax.axis_index("lat")
    lon_index = lax.axis_index("lon")
    lat_count = lax.axis_size("lat")
    lon_count = lax.axis_size("lon")
    fields, levels, columns, rows = model_state.shape
    lists = fields * levels
    total_columns = columns * lon_count
    ranks = shift_ranks(lon_count)
    near, send, far = [jnp.asarray(table) for table in filter_tables(lon_count, columns)]
    params = pltpu.CompilerParams(vmem_limit_bytes=VMEM_LIMIT)
    shape = lambda *sizes: jax.ShapeDtypeStruct(sizes, F32)
    whole_state = shape(*model_state.shape)

    is_south = lat_index == lat_count - 1
    is_polar = (lat_index == 0) | is_south
    part = jnp.where(is_south, rows // POLAR - 1, 0)
    meta = jnp.stack([part, is_polar.astype(jnp.int32), lon_index, lat_index]).astype(jnp.int32)
    kept = jnp.where(lat_index < lat_count // 2, cutoff[:POLAR], cutoff[POLAR:])
    cosine, sine = phase_table(kept, jnp.arange(columns, dtype=jnp.int32), total_columns)
    steps = jnp.array([abs(shift) for shift, _ in ranks], jnp.int32)
    sign = np.array([[1.0 if shift > 0 else -1.0] for shift, _ in ranks], np.float32)
    turn_cos, turn_sin = phase_table(kept, steps, lon_count)
    turn = jnp.concatenate([turn_cos, turn_sin * sign], axis=1)
    turn = jnp.pad(turn, ((0, ceil8(len(ranks)) - len(ranks)), (0, 0)))
    middle = ((2 * kept - 1).astype(F32) / total_columns)[None, :]
    hats = jnp.asarray(hat_table())

    smem = pl.BlockSpec(memory_space=pltpu.SMEM)
    vmem = pl.BlockSpec(memory_space=pltpu.VMEM)
    hbm = pl.BlockSpec(memory_space=pl.ANY)
    tiles = rows // POLAR
    tile_sems = pltpu.SemaphoreType.DMA((levels, fields, tiles))

    with jax.named_scope("edges"):
        edges = pl.pallas_call(
            edge_kernel,
            in_specs=[smem, hbm],
            out_specs=[vmem] * 4,
            out_shape=[shape(levels, 8, rows)] * 2 + [shape(levels, 8, columns)] * 2,
            scratch_shapes=[
                pltpu.VMEM((levels, fields, columns, rows), F32),
                pltpu.SemaphoreType.DMA((levels, fields)),
            ],
            compiler_params=params,
        )(meta, model_state)

    with jax.named_scope("halo"):
        lon_pairs, lon_crosses = ring_swaps(1, lon_count)
        lat_pairs = [(i, i + 1) for i in range(0, lat_count, 2)]
        lat_crosses = [(i, i + 1) for i in range(1, lat_count - 1, 2)]
        halos = [
            lax.ppermute(edges[0], "lon", lon_pairs),
            lax.ppermute(edges[1], "lon", lon_crosses),
            lax.ppermute(edges[2], "lat", swaps(lat_pairs)),
            lax.ppermute(edges[3], "lat", swaps(lat_crosses)),
        ]

    sizes = [payload_rows(rank, lists) for _, rank in ranks]
    with jax.named_scope("stencil"):
        updated, own, *outgoing = pl.pallas_call(
            functools.partial(stencil_kernel, lon_count),
            in_specs=[smem] * 3 + [vmem] * 8 + [hbm],
            out_specs=[hbm] + [vmem] * (1 + len(ranks)),
            out_shape=[whole_state, shape(16, rows)] + [shape(size, rows) for size in sizes],
            scratch_shapes=[
                pltpu.VMEM((levels, fields, tiles, columns + 16, POLAR), F32),
                pltpu.VMEM((levels, fields, tiles, columns, POLAR), F32),
                pltpu.VMEM((columns, POLAR), F32),
                pltpu.VMEM((lists, send.shape[0] // 2, rows), F32),
                pltpu.VMEM((lon_count, 16, rows), F32),
                pltpu.VMEM((strip_list.shape[0], 2, 16, rows), F32),
                tile_sems,
                tile_sems,
            ],
            compiler_params=params,
        )(
            meta,
            coupling.reshape(levels, fields * fields),
            strip_list,
            *halos,
            diffusion,
            cosine,
            sine,
            send,
            model_state,
        )

    def exchange(index, payload):
        step = abs(ranks[index][0])
        swap = index % 2 if 2 * step < lon_count else 0
        return lax.ppermute(payload, "lon", ring_swaps(step, lon_count)[swap])

    late = [index for index, (shift, _) in enumerate(ranks) if abs(shift) == LATE]
    early = [index for index in range(len(ranks)) if index not in late]
    with jax.named_scope("exchange"):
        incoming = {index: exchange(index, outgoing[index]) for index in early}

    def near_part(begin, end, passed):
        results = pl.pallas_call(
            functools.partial(near_kernel, begin, len(passed)),
            in_specs=[smem] + [vmem] * 4 + [hbm] * (1 + len(passed)),
            out_specs=[vmem] * 2 + [hbm] * len(passed),
            out_shape=[shape(end - begin, columns, POLAR), shape(end - begin, 32, rows)]
            + [shape(*payload.shape) for payload in passed],
            input_output_aliases={6 + index: 2 + index for index in range(len(passed))},
            scratch_shapes=[
                pltpu.VMEM((end - begin, columns, POLAR), F32),
                pltpu.SemaphoreType.DMA((end - begin,)),
            ],
            compiler_params=params,
            cost_estimate=cost(
                12 * (end - begin) * columns * columns * POLAR, 8 * (end - begin) * columns * POLAR
            ),
        )(meta, cosine, sine, middle, near, updated, *passed)
        return results[:2], results[2:]

    with jax.named_scope("near"):
        near_first, passed = near_part(0, EARLY_LISTS, [outgoing[index] for index in late])
    with jax.named_scope("late_exchange"):
        for index, payload in zip(late, passed):
            incoming[index] = exchange(index, payload)
    with jax.named_scope("near_rest"):
        near_last, passed = near_part(EARLY_LISTS, lists, [incoming[index] for index in early])
        incoming.update(zip(early, passed))

    with jax.named_scope("far"):
        advanced, boundary = pl.pallas_call(
            functools.partial(far_kernel, lon_count),
            in_specs=[smem] * 2 + [vmem] * (10 + len(ranks)) + [hbm],
            out_specs=[hbm, vmem],
            out_shape=[whole_state, shape(1, fields, levels, NB)],
            input_output_aliases={12 + len(ranks): 0},
            scratch_shapes=[
                pltpu.VMEM((lists, columns, POLAR), F32),
                pltpu.VMEM((lists, HELD, rows), F32),
                pltpu.VMEM((32, NB + 2 * POLAR), F32),
                pltpu.SemaphoreType.DMA((lists,)),
            ],
            compiler_params=pltpu.CompilerParams(vmem_limit_bytes=VMEM_LIMIT // 2),
        )(
            meta,
            nest_place.reshape(lon_count, CAP),
            cosine,
            sine,
            turn,
            far,
            hats,
            own,
            *[incoming[index] for index in range(len(ranks))],
            *near_first,
            *near_last,
            updated,
        )
    return advanced, boundary


def padded_2(block, sides, width):
    for axis, dim in sides:
        count = lax.axis_size(axis)
        forward = [(i, i + 1) for i in range(count - 1)]
        forward.append((count - 1, 0))
        backward = [(target, source) for source, target in forward]
        low = lax.ppermute(
            lax.slice_in_dim(block, block.shape[dim] - width, None, axis=dim), axis, forward
        )
        high = lax.ppermute(lax.slice_in_dim(block, 0, width, axis=dim), axis, backward)
        block = jnp.concatenate([low, block, high], axis=dim)
    return block


def spectral_filter(rows, kept):
    top_wavenumber_kept = lax.Precision.HIGHEST
    length = rows.shape[3]
    width = math.gcd(KC, 128)
    column_grid = lax.broadcasted_iota(jnp.int32, (length, width), 0)
    step_output = jnp.zeros_like(rows)
    for block_index in range(KC // width):
        wavenumber = block_index * width + lax.broadcasted_iota(jnp.int32, (length, width), 1)
        phase = column_grid * wavenumber % length
        angle = phase.astype(jnp.float32) * (2.0 * math.pi / length)
        cosine = jnp.cos(angle)
        sine = jnp.sin(angle)
        along = block_index * width + jnp.arange(width, dtype=jnp.int32)
        scale = jnp.where(along == 0, 1.0 / length, 2.0 / length)
        weight = jnp.where(along[None, :] < kept[:, None], scale[None, :], 0.0)
        real_part = (
            jnp.einsum("flrn,nk->flrk", rows, cosine, precision=top_wavenumber_kept) * weight
        )
        imaginary_component = (
            jnp.einsum("flrn,nk->flrk", rows, sine, precision=top_wavenumber_kept) * weight
        )
        step_output = (
            step_output
            + jnp.einsum("flrk,nk->flrn", real_part, cosine, precision=top_wavenumber_kept)
            + jnp.einsum("flrk,nk->flrn", imaginary_component, sine, precision=top_wavenumber_kept)
        )
    return step_output


def polar_pass(work_rows, kept_start, kept_table):
    count = work_rows.shape[2] // lax.axis_size("lon")
    kept = lax.dynamic_slice_in_dim(kept_table, kept_start + lax.axis_index("lon") * count, count)
    return lax.all_to_all(
        spectral_filter(
            lax.all_to_all(work_rows, "lon", split_axis=2, concat_axis=3, tiled=True), kept
        ),
        "lon",
        split_axis=3,
        concat_axis=2,
        tiled=True,
    )


def transposed(model_state, diffusion, coupling, cutoff, strip_list, nest_place):
    top_wavenumber_kept = lax.Precision.HIGHEST
    lat_index = lax.axis_index("lat")
    lat_count = lax.axis_size("lat")
    lon_count = lax.axis_size("lon")
    fields, levels, lon_local, lat_local = model_state.shape
    padded = padded_2(model_state, (("lat", 3), ("lon", 2)), 1)
    east_west = padded[:, :, 2:, 1:-1] + padded[:, :, :-2, 1:-1]
    row_place = lax.broadcasted_iota(jnp.int32, (1, 1, 1, lat_local), 3)
    northern = jnp.where((lat_index == 0) & (row_place == 0), 0.0, padded[:, :, 1:-1, :-2])
    southern = jnp.where(
        (lat_index == lat_count - 1) & (row_place == lat_local - 1), 0.0, padded[:, :, 1:-1, 2:]
    )
    blended = jnp.einsum("lfg,glij->flij", coupling, model_state, precision=top_wavenumber_kept)
    updated = (
        model_state
        + diffusion[0] * (east_west - 2.0 * model_state)
        + diffusion[1] * (northern + southern - 2.0 * model_state)
        + blended
    )
    is_south = lat_index == lat_count - 1
    is_polar = (lat_index == 0) | is_south
    start = jnp.where(is_south, lat_local - POLAR, 0).astype(jnp.int32)
    band_base = jnp.where(lat_index < lat_count // 2, 0, POLAR).astype(jnp.int32)
    block_rows = lax.dynamic_slice_in_dim(updated, start, POLAR, 3)
    polar_rows = jnp.transpose(block_rows, (0, 1, 3, 2))
    filtered = polar_pass(polar_rows, band_base, cutoff)
    new_rows = jnp.where(is_polar, jnp.transpose(filtered, (0, 1, 3, 2)), block_rows)
    advanced_state = lax.dynamic_update_slice_in_dim(updated, new_rows, start, 3)
    slots = strip_list.shape[0]
    owners = strip_list[:, 0]
    columns = strip_list[:, 1]
    offsets = strip_list[:, 2]
    lengths = strip_list[:, 3]
    zero = jnp.zeros((), jnp.int32)

    def cut_strip(column, offset):
        return lax.dynamic_slice(
            updated, (zero, zero, column, offset), (fields, levels, 1, STRIP)
        ).reshape(fields * levels, STRIP)

    boundary_strips = jax.vmap(cut_strip)(columns, offsets)
    inside = lax.broadcasted_iota(jnp.int32, (1, 1, STRIP), 2) < lengths[:, None, None]
    boundary_strips = jnp.where(inside, boundary_strips, 0.0).reshape(
        slots, fields * levels * STRIP
    )
    slot_ids = jnp.arange(slots, dtype=jnp.int32)
    earlier = slot_ids[None, :] < slot_ids[:, None]
    same = owners[:, None] == owners[None, :]
    rank = jnp.sum((same & earlier).astype(jnp.int32), axis=1)
    target = owners * CAP + rank
    routing = (jnp.arange(lon_count * CAP, dtype=jnp.int32)[:, None] == target[None, :]).astype(
        jnp.float32
    )
    outgoing = jnp.dot(
        routing, boundary_strips, precision=top_wavenumber_kept, preferred_element_type=jnp.float32
    ).reshape(lon_count, CAP, fields * levels * STRIP)
    arrived = lax.all_to_all(outgoing, "lon", split_axis=0, concat_axis=0, tiled=True)
    total = lon_count * CAP
    group = math.gcd(total, 16)
    pieces = arrived.reshape(total // group, group, fields * levels, STRIP)
    starts = nest_place.reshape(total // group, group)
    point = lax.broadcasted_iota(jnp.int32, (1, 1, NB), 2)
    row_step = lax.broadcasted_iota(jnp.int32, (1, STRIP, 1), 1) * RATIO

    def accumulate(carry, item):
        piece, begin = item
        offset = point - begin[:, None, None]
        hat = jnp.maximum(RATIO - jnp.abs(offset - row_step), 0)
        hat = (
            jnp.where((offset >= 0) & (offset < STRIP * RATIO), hat, 0).astype(jnp.float32) / RATIO
        )
        return (carry + jnp.einsum("gat,gtp->ap", piece, hat, precision=top_wavenumber_kept), None)

    boundary = lax.scan(
        accumulate, jnp.zeros((fields * levels, NB), jnp.float32), (pieces, starts)
    )[0]
    return (advanced_state, boundary.reshape(1, fields, levels, NB))


def local(model_state, *others):
    columns = model_state.shape[2]
    fits = lax.axis_size("lon") * STRIP == POLAR and model_state.shape[3] == 2 * POLAR
    if fits and columns % STEP == 0 and columns >= 2 * HELD:
        return compressed(model_state, *others)
    return transposed(model_state, *others)


def solution(mesh):
    return jax.shard_map(
        local,
        mesh=mesh,
        in_specs=(
            P(None, None, "lon", "lat"),
            P(None, "lat"),
            P(),
            P(),
            P(("lat", "lon"), None),
            P(("lat", "lon"), None, None),
        ),
        out_specs=(P(None, None, "lon", "lat"), P(("lat", "lon"), None, None, None)),
        check_vma=False,
    )
```

```python
import functools
import math

import jax
import jax.numpy as jnp
import numpy as np
from jax import lax
from jax.experimental import pallas as pl
from jax.experimental.pallas import tpu as pltpu
from jax.sharding import PartitionSpec as P

POLAR = 128
CAP = 2
STRIP = 16
RATIO = 11
NB = 2048
KC = 896
RANKS = (14, 5, 4, 4)
SPLIT_RANK = 14
STEP = 16
HELD = 80
EARLY_LISTS = 12
LATE = 2
SOUTH = 64
VMEM_LIMIT = 48 * 1024 * 1024
F32 = jnp.float32
BF16 = jnp.bfloat16


def ceil8(value):
    return -(-value // 8) * 8


def shift_ranks(count):
    shifts = []
    for step in range(1, count // 2 + 1):
        for shift in (step, -step):
            if shift != -count // 2:
                shifts.append((shift, RANKS[min(step, len(RANKS)) - 1]))
    return shifts


def is_second(place, step, count):
    return lax.rem(lax.div(place, math.gcd(step, count)), 2) == 1


def swaps(pairs):
    return [pair for a, b in pairs for pair in ((a, b), (b, a))]


def ring_swaps(step, count):
    if 2 * step == count:
        return [swaps([(i, i + step) for i in range(step)])]
    groups = [[], []]
    for i in range(count):
        groups[i // math.gcd(step, count) % 2].append((i, (i + step) % count))
    return [swaps(group) for group in groups]


def split_table(table):
    high = table.astype(jnp.bfloat16)
    low = (table - high.astype(np.float64)).astype(jnp.bfloat16)
    return high, low


def factored(block, rank):
    left, values, right = np.linalg.svd(block)
    root = np.sqrt(values[:rank])
    return right[:rank] * root[:, None], left[:, :rank] * root[None, :]


@functools.lru_cache(maxsize=None)
def filter_tables(count, width):
    total = count * width
    half = width // 2

    def block(size, shift):
        place = np.arange(size)
        angle = np.pi * (shift + place[:, None] - place[None, :]) / total
        with np.errstate(divide="ignore"):
            return np.where(angle == 0, 0.0, 1.0 / (np.sin(angle) * total))

    senders, receivers = [], []
    for shift, rank in shift_ranks(count):
        sender, receiver = factored(block(width, shift * width), rank)
        senders.append(np.pad(sender, ((0, ceil8(rank) - rank), (0, 0))))
        receivers.append(receiver)
    nears = []
    for part, shift in enumerate((half, -half)):
        sender, receiver = factored(block(half, shift), SPLIT_RANK)
        rows = np.concatenate([block(half, 0), sender], axis=0)
        nears.append(np.pad(rows, ((0, 16 - SPLIT_RANK), (0, 0))))
        beyond = ((half, 0), (0, 0)) if part == 0 else ((0, half), (0, 0))
        receivers.append(np.pad(receiver, beyond))
    receivers = np.concatenate(receivers, axis=1)
    receivers = np.pad(receivers, ((0, 0), (0, HELD - receivers.shape[1])))
    nears = [table for rows in nears for table in split_table(rows)]
    send_high, send_low = split_table(np.concatenate(senders, axis=0))
    far_high, far_low = split_table(receivers)
    return (
        np.concatenate(nears, axis=0),
        np.concatenate([send_high, send_low], axis=0),
        np.concatenate([far_high, far_high, far_low], axis=1),
    )


def hat_table():
    width = -(-STRIP * RATIO // POLAR) * POLAR
    point = np.arange(width)
    table = np.zeros((POLAR, CAP * width), np.float32)
    for rank in range(CAP):
        for row in range(STRIP):
            hat = np.maximum(RATIO - np.abs(point - row * RATIO), 0) * (point < STRIP * RATIO)
            table[rank * STRIP + row, rank * width : (rank + 1) * width] = hat
    return table.astype(jnp.bfloat16)


def split_value(value):
    high = value.astype(BF16)
    return high, (value - high.astype(F32)).astype(BF16)


def modulated(row, cosine, sine):
    return jnp.concatenate([row * cosine[...], row * sine[...]], axis=1)


def stacked(value):
    high, low = split_value(value)
    return jnp.concatenate([high, low, high], axis=0)


def strip_rows(slots):
    return slots // 2


def payload_rows(rank, slots):
    return ceil8(slots * rank + strip_rows(slots))


def edge_kernel(
    meta, state, lon_pair, lon_cross, lat_pair, lat_cross, held, edges, in_sems
):
    fields, levels, columns, rows = state.shape
    lists = fields * levels

    def copy_in(item):
        l, f = item // fields, item % fields
        return pltpu.make_async_copy(state.at[f, l], held.at[item], in_sems.at[item])

    def start(item, carry):
        copy_in(item).start()
        return carry

    lax.fori_loop(0, lists, start, 0)
    lane = lax.broadcasted_iota(jnp.int32, (columns, POLAR), 1)
    lon_odd = lax.rem(meta[2], 2) == 1
    lat_odd = lax.rem(meta[3], 2) == 1
    edges[...] = jnp.zeros(edges.shape, F32)

    def one(item, carry):
        copy_in(item).wait()
        first = held[item, 0:1, :]
        last = held[item, columns - 1 : columns, :]
        lon_pair[pl.ds(item, 1), :] = jnp.where(lon_odd, first, last)
        lon_cross[pl.ds(item, 1), :] = jnp.where(lon_odd, last, first)
        north = pltpu.roll(held[item, :, 0:POLAR], item, 1)
        south = pltpu.roll(held[item, :, rows - POLAR :], item + SOUTH + 1, 1)
        value = jnp.where(lane == item, north, edges[...])
        edges[...] = jnp.where(lane == SOUTH + item, south, value)
        return carry

    lax.fori_loop(0, lists, one, 0)
    turned = edges[...].T
    size = lat_pair.shape[0]
    north, south = turned[0:size], turned[SOUTH : SOUTH + size]
    lat_pair[...] = jnp.where(lat_odd, north, south)
    lat_cross[...] = jnp.where(lat_odd, south, north)


def stencil_kernel(
    count,
    meta,
    coupling,
    strips,
    lon_pair,
    lon_cross,
    lat_pair,
    lat_cross,
    diffusion,
    cosine,
    sine,
    send,
    state,
    updated,
    own,
    *rest,
):
    ranks = shift_ranks(count)
    payloads = rest[: len(ranks)]
    held, made, halos, halo, factors, placed, rows_cut, in_sems, out_sems = rest[len(ranks) :]
    fields, levels, columns, rows = state.shape
    tiles = rows // POLAR
    spans = [slice(tile * POLAR, (tile + 1) * POLAR) for tile in range(tiles)]

    def copy_in(l, f, t):
        return pltpu.make_async_copy(
            state.at[f, l, :, spans[t]],
            held.at[l, f, t, pl.ds(8, columns)],
            in_sems.at[l, f, t],
        )

    def copy_out(l, f, t):
        return pltpu.make_async_copy(
            made.at[l, f, t], updated.at[f, l, :, spans[t]], out_sems.at[l, f, t]
        )

    for l in range(levels):
        for f in range(fields):
            for t in range(tiles):
                copy_in(l, f, t).start()

    lane = lax.broadcasted_iota(jnp.int32, (STEP // 2, POLAR), 1)
    lowest, highest = lane == 0, lane == POLAR - 1
    along = [jnp.broadcast_to(diffusion[0:1, span], (STEP // 2, POLAR)) for span in spans]
    across = [jnp.broadcast_to(diffusion[1:2, span], (STEP // 2, POLAR)) for span in spans]
    centre = [1.0 - 2.0 * along[t] - 2.0 * across[t] for t in range(tiles)]
    lon_odd = lax.rem(meta[2], 2) == 1
    lat_odd = lax.rem(meta[3], 2) == 1
    half = send.shape[0] // 2
    size = lat_pair.shape[0]
    blank = jnp.zeros((SOUTH - size, columns), F32)
    north_halo = jnp.where(lat_odd, lat_pair[...], lat_cross[...])
    south_halo = jnp.where(lat_odd, lat_cross[...], lat_pair[...])
    halos[...] = jnp.concatenate([north_halo, blank, south_halo, blank], axis=0).T

    def one_level(l, carry):
        for f in range(fields):
            for t in range(tiles):
                copy_in(l, f, t).wait()
        weights = [
            [coupling[l, f * fields + g] for g in range(fields)] for f in range(fields)
        ]
        halo[...] = pltpu.roll(halos[...], lax.rem(POLAR - l * fields, POLAR), 1)
        for f in range(fields):
            item = pl.ds(l * fields + f, 1)
            pair, cross = lon_pair[item, :], lon_cross[item, :]
            west, east = jnp.where(lon_odd, pair, cross), jnp.where(lon_odd, cross, pair)
            for t, span in enumerate(spans):
                held[l, f, t, 7:8, :] = west[:, span]
                held[l, f, t, columns + 8 : columns + 9, :] = east[:, span]
        def one_step(index, carry):
            begin = index * STEP
            strided = lambda f, t, start: held[l, f, t, pl.ds(start + 8, STEP // 2, stride=2), :]
            both = [
                [[strided(f, t, begin + odd) for odd in range(2)] for t in range(tiles)]
                for f in range(fields)
            ]
            for odd in range(2):
                place = pl.ds(begin + odd, STEP // 2, stride=2)
                edges = halo[place, :]
                for f in range(fields):
                    here = [both[f][t][odd] for t in range(tiles)]
                    down = [pltpu.roll(here[t], 1, 1) for t in range(tiles)]
                    up = [pltpu.roll(here[t], POLAR - 1, 1) for t in range(tiles)]
                    north_edge = [pltpu.roll(edges, POLAR - f, 1) if f else edges] + down[:-1]
                    south_edge = up[1:] + [pltpu.roll(edges, POLAR - 1 - SOUTH - f, 1)]
                    for t in range(tiles):
                        beyond = strided(f, t, begin + 2 if odd else begin - 1)
                        north = jnp.where(lowest, north_edge[t], down[t])
                        south = jnp.where(highest, south_edge[t], up[t])
                        result = (centre[t] + weights[f][f]) * here[t]
                        result = result + along[t] * (both[f][t][1 - odd] + beyond)
                        result = result + across[t] * (north + south)
                        for g in range(fields):
                            if g != f:
                                result = result + weights[f][g] * both[g][t][odd]
                        made[l, f, t, place, :] = result
            return carry

        lax.fori_loop(0, columns // STEP, one_step, 0)
        for f in range(fields):
            for t in range(tiles):
                copy_out(l, f, t).start()
        for f in range(fields):
            row = made[l, f, meta[0]]
            high, low = split_value(modulated(row, cosine, sine))
            both = jnp.dot(send[...], high, preferred_element_type=F32)
            cross = jnp.dot(send[0:half, :], low, preferred_element_type=F32)
            factors[l * fields + f] = both[:half] + both[half:] + cross
        return carry

    lax.fori_loop(0, levels, one_level, 0)

    lon_index = meta[2]
    slots = strips.shape[0]
    lists = fields * levels
    each = strip_rows(lists)
    placed[...] = jnp.zeros(placed.shape, F32)
    rows_cut[...] = jnp.zeros(rows_cut.shape, F32)
    strip_lane = lax.broadcasted_iota(jnp.int32, (16, rows), 1)

    def one_slot(s, carry):
        owner, column = strips[s, 0], strips[s, 1]
        offset, length = strips[s, 2], strips[s, 3]
        rank = lax.fori_loop(
            0, s, lambda other, total: total + (strips[other, 0] == owner).astype(jnp.int32), 0
        )
        for l in range(levels):
            for f in range(fields):
                side, place = divmod(l * fields + f, each)
                for t, span in enumerate(spans):
                    rows_cut[side, place : place + 1, span] = made[l, f, t, pl.ds(column, 1), :]
        base = rank * STRIP
        shift = lax.rem(owner - lon_index + count, count)
        for side in range(2):
            where = side * POLAR + base
            moved = pltpu.roll(rows_cut[side], lax.rem(where - offset + rows, rows), 1)
            inside = (strip_lane >= where) & (strip_lane < where + length)
            placed[shift] = placed[shift] + jnp.where(inside, moved, 0.0)
        return carry

    lax.fori_loop(0, slots, one_slot, 0)
    own[...] = placed[0]

    place = 0
    index = 0
    while index < len(ranks):
        step, rank = ranks[index]
        padded = ceil8(rank)
        paired = 2 if 2 * step < count else 1
        second = is_second(lon_index, step, count)
        targets = payloads[index : index + paired]
        for item in range(lists):
            span = slice(item * rank, (item + 1) * rank)
            plus = factors[item, place : place + rank, :]
            if paired == 1:
                targets[0][span, :] = plus
            else:
                minus = factors[item, place + padded : place + padded + rank, :]
                targets[0][span, :] = jnp.where(second, minus, plus)
                targets[1][span, :] = jnp.where(second, plus, minus)
        plus, minus = placed[step][0:each, :], placed[count - step][0:each, :]
        targets[0][lists * rank : lists * rank + each, :] = jnp.where(second, minus, plus)
        if paired == 2:
            targets[1][lists * rank : lists * rank + each, :] = jnp.where(second, plus, minus)
        for target in targets:
            unused = target.shape[0] - lists * rank - each
            if unused:
                target[lists * rank + each :, :] = jnp.zeros((unused, rows), F32)
        place += paired * padded
        index += paired
    for l in range(levels):
        for f in range(fields):
            for t in range(tiles):
                copy_out(l, f, t).wait()


def near_kernel(begin, passed, meta, cosine, sine, middle, near, rows, *rest):
    filtered, moments = rest[passed], rest[passed + 1]
    held, sems = rest[2 * passed + 2 :]
    fields = rows.shape[0]
    lists, columns, _ = filtered.shape
    half = columns // 2
    each = near.shape[0] // 4
    mine = pl.ds(pl.multiple_of(meta[0] * POLAR, POLAR), POLAR)

    def copy_in(item):
        l, f = (begin + item) // fields, (begin + item) % fields
        return pltpu.make_async_copy(rows.at[f, l, :, mine], held.at[item], sems.at[item])

    @pl.when(meta[1] == 1)
    def _():
        for item in range(lists):
            copy_in(item).start()

        def one(item, carry):
            copy_in(item).wait()
            for part in range(2):
                span = slice(part * half, (part + 1) * half)
                row = held[item, span, :]
                turn_cos, turn_sin = cosine[span, :], sine[span, :]
                value = jnp.concatenate([row * turn_cos, row * turn_sin], axis=1)
                table = near[2 * part * each : 2 * (part + 1) * each, :]
                high, low = split_value(value)
                both = jnp.dot(table, high, preferred_element_type=F32)
                cross = jnp.dot(table[:each], low, preferred_element_type=F32)
                total = both[:each] + both[each:] + cross
                filtered[item, span, :] = (
                    turn_sin * total[:half, :POLAR]
                    - turn_cos * total[:half, POLAR:]
                    + middle[0:1, :] * row
                )
                moments[item, part * 16 : (part + 1) * 16, :] = total[half:, :]
            return carry

        lax.fori_loop(0, lists, one, 0, unroll=4)


def far_kernel(count, meta, begins, cosine, sine, turn, far, hats, own, *rest):
    ranks = shift_ranks(count)
    payloads = rest[: len(ranks)]
    near_parts = (rest[len(ranks) : len(ranks) + 2], rest[len(ranks) + 2 : len(ranks) + 4])
    _, out, boundary, filtered, arrived, sums, sems = rest[len(ranks) + 4 :]
    fields, levels = out.shape[0:2]
    lists = fields * levels
    each = strip_rows(lists)
    lon_index = meta[2]
    mine = pl.ds(pl.multiple_of(meta[0] * POLAR, POLAR), POLAR)

    def copy_out(item):
        l, f = item // fields, item % fields
        return pltpu.make_async_copy(filtered.at[item], out.at[f, l, :, mine], sems.at[item])

    def received(index, span):
        step = abs(ranks[index][0])
        if 2 * step == count:
            return payloads[index][span, :]
        base = index - index % 2
        first, last = payloads[base][span, :], payloads[base + 1][span, :]
        takes_first = is_second(lon_index, step, count)
        if index != base:
            takes_first = jnp.logical_not(takes_first)
        return jnp.where(takes_first, first, last)

    @pl.when(meta[1] == 1)
    def _():
        place = 0
        for index, (_, rank) in enumerate(ranks):
            turn_cos = turn[index : index + 1, :POLAR]
            turn_sin = turn[index : index + 1, POLAR:]
            for item in range(lists):
                value = received(index, slice(item * rank, (item + 1) * rank))
                cosines, sines = value[:, :POLAR], value[:, POLAR:]
                arrived[item, place : place + rank, :POLAR] = (
                    turn_cos * cosines + turn_sin * sines
                )
                arrived[item, place : place + rank, POLAR:] = (
                    turn_cos * sines - turn_sin * cosines
                )
            place += rank
        begin = 0
        for near, moments in near_parts:
            for item in range(near.shape[0]):
                for part in range(2):
                    at = place + part * SPLIT_RANK
                    arrived[begin + item, at : at + SPLIT_RANK, :] = moments[
                        item, part * 16 : part * 16 + SPLIT_RANK, :
                    ]
            begin += near.shape[0]
        place += 2 * SPLIT_RANK
        for item in range(lists):
            arrived[item, place:, :] = jnp.zeros((HELD - place, 2 * POLAR), F32)

        begin = 0
        for near, _ in near_parts:

            def one(item, carry, near=near, begin=begin):
                at = begin + item
                total = jnp.dot(far[...], stacked(arrived[at]), preferred_element_type=F32)
                filtered[at] = (
                    near[item] + sine[...] * total[:, :POLAR] - cosine[...] * total[:, POLAR:]
                )
                copy_out(at).start()
                return carry

            lax.fori_loop(0, near.shape[0], one, 0, unroll=4)
            begin += near.shape[0]

    sums[...] = jnp.zeros(sums.shape, F32)
    pieces, sources = [], []
    blank = jnp.zeros((16 - each, POLAR), F32)
    for index in range(-1, len(ranks)):
        if index < 0:
            shift, arrival = 0, own[0:each, :]
        else:
            shift, rank = ranks[index]
            arrival = received(index, slice(lists * rank, lists * rank + each))
        sources.append(lax.rem(lon_index - shift + count, count))
        pieces += [arrival[:, :POLAR], blank, arrival[:, POLAR:], blank]
    pieces = jnp.concatenate(pieces, axis=0)
    high = pieces.astype(BF16)
    middle, low = split_value(pieces - high.astype(F32))
    points = jnp.dot(high, hats[...], preferred_element_type=F32)
    points = points + jnp.dot(middle, hats[...], preferred_element_type=F32)
    points = points + jnp.dot(low, hats[...], preferred_element_type=F32)
    width = hats.shape[1] // CAP
    beyond = jnp.zeros((32, POLAR), F32)
    for index, source in enumerate(sources):
        for rank in range(CAP):
            place = begins[source, rank]
            offset = lax.rem(place, POLAR)
            span = points[index * 32 : (index + 1) * 32, rank * width : (rank + 1) * width]
            moved = pltpu.roll(jnp.concatenate([span, beyond], axis=1), offset, 1)
            at = pl.ds(pl.multiple_of(place - offset, POLAR), width + POLAR)
            sums[:, at] = sums[:, at] + moved
    for l in range(levels):
        for f in range(fields):
            side, row = divmod(l * fields + f, each)
            row = side * 16 + row
            boundary[0, f, l : l + 1, :] = sums[row : row + 1, 0:NB] * (1.0 / RATIO)

    @pl.when(meta[1] == 1)
    def _():
        for item in range(lists):
            copy_out(item).wait()


def phase_table(kept, steps, period):
    phase = (2 * kept - 1)[None, :] * steps[:, None] % (2 * period)
    angle = phase.astype(F32) * (math.pi / period)
    return jnp.cos(angle), jnp.sin(angle)


def cost(flops, bytes_accessed):
    return pl.CostEstimate(flops=flops, bytes_accessed=bytes_accessed, transcendentals=0)


def compressed(model_state, diffusion, coupling, cutoff, strip_list, nest_place):
    lat_index = lax.axis_index("lat")
    lon_index = lax.axis_index("lon")
    lat_count = lax.axis_size("lat")
    lon_count = lax.axis_size("lon")
    fields, levels, columns, rows = model_state.shape
    lists = fields * levels
    total_columns = columns * lon_count
    ranks = shift_ranks(lon_count)
    near, send, far = [jnp.asarray(table) for table in filter_tables(lon_count, columns)]
    params = pltpu.CompilerParams(vmem_limit_bytes=VMEM_LIMIT)
    shape = lambda *sizes: jax.ShapeDtypeStruct(sizes, F32)
    whole_state = shape(*model_state.shape)

    is_south = lat_index == lat_count - 1
    is_polar = (lat_index == 0) | is_south
    part = jnp.where(is_south, rows // POLAR - 1, 0)
    meta = jnp.stack([part, is_polar.astype(jnp.int32), lon_index, lat_index]).astype(jnp.int32)
    kept = jnp.where(lat_index < lat_count // 2, cutoff[:POLAR], cutoff[POLAR:])
    cosine, sine = phase_table(kept, jnp.arange(columns, dtype=jnp.int32), total_columns)
    steps = jnp.array([abs(shift) for shift, _ in ranks], jnp.int32)
    sign = np.array([[1.0 if shift > 0 else -1.0] for shift, _ in ranks], np.float32)
    turn_cos, turn_sin = phase_table(kept, steps, lon_count)
    turn = jnp.concatenate([turn_cos, turn_sin * sign], axis=1)
    turn = jnp.pad(turn, ((0, ceil8(len(ranks)) - len(ranks)), (0, 0)))
    middle = ((2 * kept - 1).astype(F32) / total_columns)[None, :]
    hats = jnp.asarray(hat_table())

    smem = pl.BlockSpec(memory_space=pltpu.SMEM)
    vmem = pl.BlockSpec(memory_space=pltpu.VMEM)
    hbm = pl.BlockSpec(memory_space=pl.ANY)
    tiles = rows // POLAR
    tile_sems = pltpu.SemaphoreType.DMA((levels, fields, tiles))

    with jax.named_scope("edges"):
        edges = pl.pallas_call(
            edge_kernel,
            in_specs=[smem, hbm],
            out_specs=[vmem] * 4,
            out_shape=[shape(ceil8(lists), rows)] * 2 + [shape(ceil8(lists), columns)] * 2,
            scratch_shapes=[
                pltpu.VMEM((lists, columns, rows), F32),
                pltpu.VMEM((columns, POLAR), F32),
                pltpu.SemaphoreType.DMA((lists,)),
            ],
            compiler_params=params,
        )(meta, model_state)

    with jax.named_scope("halo"):
        lon_pairs, lon_crosses = ring_swaps(1, lon_count)
        lat_pairs = [(i, i + 1) for i in range(0, lat_count, 2)]
        lat_crosses = [(i, i + 1) for i in range(1, lat_count - 1, 2)]
        halos = [
            lax.ppermute(edges[0], "lon", lon_pairs),
            lax.ppermute(edges[1], "lon", lon_crosses),
            lax.ppermute(edges[2], "lat", swaps(lat_pairs)),
            lax.ppermute(edges[3], "lat", swaps(lat_crosses)),
        ]

    sizes = [payload_rows(rank, lists) for _, rank in ranks]
    with jax.named_scope("stencil"):
        updated, own, *outgoing = pl.pallas_call(
            functools.partial(stencil_kernel, lon_count),
            in_specs=[smem] * 3 + [vmem] * 8 + [hbm],
            out_specs=[hbm] + [vmem] * (1 + len(ranks)),
            out_shape=[whole_state, shape(16, rows)] + [shape(size, rows) for size in sizes],
            scratch_shapes=[
                pltpu.VMEM((levels, fields, tiles, columns + 16, POLAR), F32),
                pltpu.VMEM((levels, fields, tiles, columns, POLAR), F32),
                pltpu.VMEM((columns, POLAR), F32),
                pltpu.VMEM((columns, POLAR), F32),
                pltpu.VMEM((lists, send.shape[0] // 2, rows), F32),
                pltpu.VMEM((lon_count, 16, rows), F32),
                pltpu.VMEM((2, 16, rows), F32),
                tile_sems,
                tile_sems,
            ],
            compiler_params=params,
        )(
            meta,
            coupling.reshape(levels, fields * fields),
            strip_list,
            *halos,
            diffusion,
            cosine,
            sine,
            send,
            model_state,
        )

    def exchange(index, payload):
        step = abs(ranks[index][0])
        swap = index % 2 if 2 * step < lon_count else 0
        return lax.ppermute(payload, "lon", ring_swaps(step, lon_count)[swap])

    late = [index for index, (shift, _) in enumerate(ranks) if abs(shift) == LATE]
    early = [index for index in range(len(ranks)) if index not in late]
    with jax.named_scope("exchange"):
        incoming = {index: exchange(index, outgoing[index]) for index in early}

    def near_part(begin, end, passed):
        results = pl.pallas_call(
            functools.partial(near_kernel, begin, len(passed)),
            in_specs=[smem] + [vmem] * 4 + [hbm] * (1 + len(passed)),
            out_specs=[vmem] * 2 + [hbm] * len(passed),
            out_shape=[shape(end - begin, columns, POLAR), shape(end - begin, 32, rows)]
            + [shape(*payload.shape) for payload in passed],
            input_output_aliases={6 + index: 2 + index for index in range(len(passed))},
            scratch_shapes=[
                pltpu.VMEM((end - begin, columns, POLAR), F32),
                pltpu.SemaphoreType.DMA((end - begin,)),
            ],
            compiler_params=params,
            cost_estimate=cost(
                12 * (end - begin) * columns * columns * POLAR, 8 * (end - begin) * columns * POLAR
            ),
        )(meta, cosine, sine, middle, near, updated, *passed)
        return results[:2], results[2:]

    with jax.named_scope("near"):
        near_first, passed = near_part(0, EARLY_LISTS, [outgoing[index] for index in late])
    with jax.named_scope("late_exchange"):
        for index, payload in zip(late, passed):
            incoming[index] = exchange(index, payload)
    with jax.named_scope("near_rest"):
        near_last, passed = near_part(EARLY_LISTS, lists, [incoming[index] for index in early])
        incoming.update(zip(early, passed))

    with jax.named_scope("far"):
        advanced, boundary = pl.pallas_call(
            functools.partial(far_kernel, lon_count),
            in_specs=[smem] * 2 + [vmem] * (10 + len(ranks)) + [hbm],
            out_specs=[hbm, vmem],
            out_shape=[whole_state, shape(1, fields, levels, NB)],
            input_output_aliases={12 + len(ranks): 0},
            scratch_shapes=[
                pltpu.VMEM((lists, columns, POLAR), F32),
                pltpu.VMEM((lists, HELD, rows), F32),
                pltpu.VMEM((32, NB + 2 * POLAR), F32),
                pltpu.SemaphoreType.DMA((lists,)),
            ],
            compiler_params=pltpu.CompilerParams(vmem_limit_bytes=VMEM_LIMIT // 2),
        )(
            meta,
            nest_place.reshape(lon_count, CAP),
            cosine,
            sine,
            turn,
            far,
            hats,
            own,
            *[incoming[index] for index in range(len(ranks))],
            *near_first,
            *near_last,
            updated,
        )
    return advanced, boundary


def padded_2(block, sides, width):
    for axis, dim in sides:
        count = lax.axis_size(axis)
        forward = [(i, i + 1) for i in range(count - 1)]
        forward.append((count - 1, 0))
        backward = [(target, source) for source, target in forward]
        low = lax.ppermute(
            lax.slice_in_dim(block, block.shape[dim] - width, None, axis=dim), axis, forward
        )
        high = lax.ppermute(lax.slice_in_dim(block, 0, width, axis=dim), axis, backward)
        block = jnp.concatenate([low, block, high], axis=dim)
    return block


def spectral_filter(rows, kept):
    top_wavenumber_kept = lax.Precision.HIGHEST
    length = rows.shape[3]
    width = math.gcd(KC, 128)
    column_grid = lax.broadcasted_iota(jnp.int32, (length, width), 0)
    step_output = jnp.zeros_like(rows)
    for block_index in range(KC // width):
        wavenumber = block_index * width + lax.broadcasted_iota(jnp.int32, (length, width), 1)
        phase = column_grid * wavenumber % length
        angle = phase.astype(jnp.float32) * (2.0 * math.pi / length)
        cosine = jnp.cos(angle)
        sine = jnp.sin(angle)
        along = block_index * width + jnp.arange(width, dtype=jnp.int32)
        scale = jnp.where(along == 0, 1.0 / length, 2.0 / length)
        weight = jnp.where(along[None, :] < kept[:, None], scale[None, :], 0.0)
        real_part = (
            jnp.einsum("flrn,nk->flrk", rows, cosine, precision=top_wavenumber_kept) * weight
        )
        imaginary_component = (
            jnp.einsum("flrn,nk->flrk", rows, sine, precision=top_wavenumber_kept) * weight
        )
        step_output = (
            step_output
            + jnp.einsum("flrk,nk->flrn", real_part, cosine, precision=top_wavenumber_kept)
            + jnp.einsum("flrk,nk->flrn", imaginary_component, sine, precision=top_wavenumber_kept)
        )
    return step_output


def polar_pass(work_rows, kept_start, kept_table):
    count = work_rows.shape[2] // lax.axis_size("lon")
    kept = lax.dynamic_slice_in_dim(kept_table, kept_start + lax.axis_index("lon") * count, count)
    return lax.all_to_all(
        spectral_filter(
            lax.all_to_all(work_rows, "lon", split_axis=2, concat_axis=3, tiled=True), kept
        ),
        "lon",
        split_axis=3,
        concat_axis=2,
        tiled=True,
    )


def transposed(model_state, diffusion, coupling, cutoff, strip_list, nest_place):
    top_wavenumber_kept = lax.Precision.HIGHEST
    lat_index = lax.axis_index("lat")
    lat_count = lax.axis_size("lat")
    lon_count = lax.axis_size("lon")
    fields, levels, lon_local, lat_local = model_state.shape
    padded = padded_2(model_state, (("lat", 3), ("lon", 2)), 1)
    east_west = padded[:, :, 2:, 1:-1] + padded[:, :, :-2, 1:-1]
    row_place = lax.broadcasted_iota(jnp.int32, (1, 1, 1, lat_local), 3)
    northern = jnp.where((lat_index == 0) & (row_place == 0), 0.0, padded[:, :, 1:-1, :-2])
    southern = jnp.where(
        (lat_index == lat_count - 1) & (row_place == lat_local - 1), 0.0, padded[:, :, 1:-1, 2:]
    )
    blended = jnp.einsum("lfg,glij->flij", coupling, model_state, precision=top_wavenumber_kept)
    updated = (
        model_state
        + diffusion[0] * (east_west - 2.0 * model_state)
        + diffusion[1] * (northern + southern - 2.0 * model_state)
        + blended
    )
    is_south = lat_index == lat_count - 1
    is_polar = (lat_index == 0) | is_south
    start = jnp.where(is_south, lat_local - POLAR, 0).astype(jnp.int32)
    band_base = jnp.where(lat_index < lat_count // 2, 0, POLAR).astype(jnp.int32)
    block_rows = lax.dynamic_slice_in_dim(updated, start, POLAR, 3)
    polar_rows = jnp.transpose(block_rows, (0, 1, 3, 2))
    filtered = polar_pass(polar_rows, band_base, cutoff)
    new_rows = jnp.where(is_polar, jnp.transpose(filtered, (0, 1, 3, 2)), block_rows)
    advanced_state = lax.dynamic_update_slice_in_dim(updated, new_rows, start, 3)
    slots = strip_list.shape[0]
    owners = strip_list[:, 0]
    columns = strip_list[:, 1]
    offsets = strip_list[:, 2]
    lengths = strip_list[:, 3]
    zero = jnp.zeros((), jnp.int32)

    def cut_strip(column, offset):
        return lax.dynamic_slice(
            updated, (zero, zero, column, offset), (fields, levels, 1, STRIP)
        ).reshape(fields * levels, STRIP)

    boundary_strips = jax.vmap(cut_strip)(columns, offsets)
    inside = lax.broadcasted_iota(jnp.int32, (1, 1, STRIP), 2) < lengths[:, None, None]
    boundary_strips = jnp.where(inside, boundary_strips, 0.0).reshape(
        slots, fields * levels * STRIP
    )
    slot_ids = jnp.arange(slots, dtype=jnp.int32)
    earlier = slot_ids[None, :] < slot_ids[:, None]
    same = owners[:, None] == owners[None, :]
    rank = jnp.sum((same & earlier).astype(jnp.int32), axis=1)
    target = owners * CAP + rank
    routing = (jnp.arange(lon_count * CAP, dtype=jnp.int32)[:, None] == target[None, :]).astype(
        jnp.float32
    )
    outgoing = jnp.dot(
        routing, boundary_strips, precision=top_wavenumber_kept, preferred_element_type=jnp.float32
    ).reshape(lon_count, CAP, fields * levels * STRIP)
    arrived = lax.all_to_all(outgoing, "lon", split_axis=0, concat_axis=0, tiled=True)
    total = lon_count * CAP
    group = math.gcd(total, 16)
    pieces = arrived.reshape(total // group, group, fields * levels, STRIP)
    starts = nest_place.reshape(total // group, group)
    point = lax.broadcasted_iota(jnp.int32, (1, 1, NB), 2)
    row_step = lax.broadcasted_iota(jnp.int32, (1, STRIP, 1), 1) * RATIO

    def accumulate(carry, item):
        piece, begin = item
        offset = point - begin[:, None, None]
        hat = jnp.maximum(RATIO - jnp.abs(offset - row_step), 0)
        hat = (
            jnp.where((offset >= 0) & (offset < STRIP * RATIO), hat, 0).astype(jnp.float32) / RATIO
        )
        return (carry + jnp.einsum("gat,gtp->ap", piece, hat, precision=top_wavenumber_kept), None)

    boundary = lax.scan(
        accumulate, jnp.zeros((fields * levels, NB), jnp.float32), (pieces, starts)
    )[0]
    return (advanced_state, boundary.reshape(1, fields, levels, NB))


def local(model_state, *others):
    columns = model_state.shape[2]
    fits = lax.axis_size("lon") * STRIP == POLAR and model_state.shape[3] == 2 * POLAR
    if fits and columns % STEP == 0 and columns >= 2 * HELD:
        return compressed(model_state, *others)
    return transposed(model_state, *others)


def solution(mesh):
    return jax.shard_map(
        local,
        mesh=mesh,
        in_specs=(
            P(None, None, "lon", "lat"),
            P(None, "lat"),
            P(),
            P(),
            P(("lat", "lon"), None),
            P(("lat", "lon"), None, None),
        ),
        out_specs=(P(None, None, "lon", "lat"), P(("lat", "lon"), None, None, None)),
        check_vma=False,
    )
```

```python
import functools
import math

import jax
import jax.numpy as jnp
import numpy as np
from jax import lax
from jax.experimental import pallas as pl
from jax.experimental.pallas import tpu as pltpu
from jax.sharding import PartitionSpec as P

POLAR = 128
CAP = 2
STRIP = 16
RATIO = 11
NB = 2048
KC = 896
RANKS = (14, 5, 4, 4)
SPLIT_RANK = 14
STEP = 16
HELD = 80
EARLY_LISTS = 12
LATE = 2
SOUTH = 64
VMEM_LIMIT = 48 * 1024 * 1024
F32 = jnp.float32
BF16 = jnp.bfloat16


def ceil8(value):
    return -(-value // 8) * 8


def shift_ranks(count):
    shifts = []
    for step in range(1, count // 2 + 1):
        for shift in (step, -step):
            if shift != -count // 2:
                shifts.append((shift, RANKS[min(step, len(RANKS)) - 1]))
    return shifts


def is_second(place, step, count):
    return lax.rem(lax.div(place, math.gcd(step, count)), 2) == 1


def swaps(pairs):
    return [pair for a, b in pairs for pair in ((a, b), (b, a))]


def ring_swaps(step, count):
    if 2 * step == count:
        return [swaps([(i, i + step) for i in range(step)])]
    groups = [[], []]
    for i in range(count):
        groups[i // math.gcd(step, count) % 2].append((i, (i + step) % count))
    return [swaps(group) for group in groups]


def split_table(table):
    high = table.astype(jnp.bfloat16)
    low = (table - high.astype(np.float64)).astype(jnp.bfloat16)
    return high, low


def factored(block, rank):
    left, values, right = np.linalg.svd(block)
    root = np.sqrt(values[:rank])
    return right[:rank] * root[:, None], left[:, :rank] * root[None, :]


@functools.lru_cache(maxsize=None)
def filter_tables(count, width):
    total = count * width
    half = width // 2

    def block(size, shift):
        place = np.arange(size)
        angle = np.pi * (shift + place[:, None] - place[None, :]) / total
        with np.errstate(divide="ignore"):
            return np.where(angle == 0, 0.0, 1.0 / (np.sin(angle) * total))

    senders, receivers = [], []
    for shift, rank in shift_ranks(count):
        sender, receiver = factored(block(width, shift * width), rank)
        senders.append(np.pad(sender, ((0, ceil8(rank) - rank), (0, 0))))
        receivers.append(receiver)
    nears = []
    for part, shift in enumerate((half, -half)):
        sender, receiver = factored(block(half, shift), SPLIT_RANK)
        rows = np.concatenate([block(half, 0), sender], axis=0)
        nears.append(np.pad(rows, ((0, 16 - SPLIT_RANK), (0, 0))))
        beyond = ((half, 0), (0, 0)) if part == 0 else ((0, half), (0, 0))
        receivers.append(np.pad(receiver, beyond))
    receivers = np.concatenate(receivers, axis=1)
    receivers = np.pad(receivers, ((0, 0), (0, HELD - receivers.shape[1])))
    nears = [table for rows in nears for table in split_table(rows)]
    send_high, send_low = split_table(np.concatenate(senders, axis=0))
    far_high, far_low = split_table(receivers)
    return (
        np.concatenate(nears, axis=0),
        np.concatenate([send_high, send_low], axis=0),
        np.concatenate([far_high, far_high, far_low], axis=1),
    )


def hat_table():
    width = -(-STRIP * RATIO // POLAR) * POLAR
    point = np.arange(width)
    table = np.zeros((POLAR, CAP * width), np.float32)
    for rank in range(CAP):
        for row in range(STRIP):
            hat = np.maximum(RATIO - np.abs(point - row * RATIO), 0) * (point < STRIP * RATIO)
            table[rank * STRIP + row, rank * width : (rank + 1) * width] = hat
    return table.astype(jnp.bfloat16)


def split_value(value):
    high = value.astype(BF16)
    return high, (value - high.astype(F32)).astype(BF16)


def modulated(row, cosine, sine):
    return jnp.concatenate([row * cosine[...], row * sine[...]], axis=1)


def stacked(value):
    high, low = split_value(value)
    return jnp.concatenate([high, low, high], axis=0)


def strip_rows(slots):
    return slots // 2


def payload_rows(rank, slots):
    return ceil8(slots * rank + strip_rows(slots))


def edge_kernel(
    meta, state, lon_pair, lon_cross, lat_pair, lat_cross, held, edges, in_sems
):
    fields, levels, columns, rows = state.shape
    lists = fields * levels

    def copy_in(item):
        l, f = item // fields, item % fields
        return pltpu.make_async_copy(state.at[f, l], held.at[item], in_sems.at[item])

    def start(item, carry):
        copy_in(item).start()
        return carry

    lax.fori_loop(0, lists, start, 0)
    lane = lax.broadcasted_iota(jnp.int32, (columns, POLAR), 1)
    lon_odd = lax.rem(meta[2], 2) == 1
    lat_odd = lax.rem(meta[3], 2) == 1
    edges[...] = jnp.zeros(edges.shape, F32)

    def one(item, carry):
        copy_in(item).wait()
        first = held[item, 0:1, :]
        last = held[item, columns - 1 : columns, :]
        lon_pair[pl.ds(item, 1), :] = jnp.where(lon_odd, first, last)
        lon_cross[pl.ds(item, 1), :] = jnp.where(lon_odd, last, first)
        north = pltpu.roll(held[item, :, 0:POLAR], item, 1)
        south = pltpu.roll(held[item, :, rows - POLAR :], item + SOUTH + 1, 1)
        value = jnp.where(lane == item, north, edges[...])
        edges[...] = jnp.where(lane == SOUTH + item, south, value)
        return carry

    lax.fori_loop(0, lists, one, 0)
    turned = edges[...].T
    size = lat_pair.shape[0]
    north, south = turned[0:size], turned[SOUTH : SOUTH + size]
    lat_pair[...] = jnp.where(lat_odd, north, south)
    lat_cross[...] = jnp.where(lat_odd, south, north)


def stencil_kernel(
    count,
    meta,
    coupling,
    strips,
    lon_pair,
    lon_cross,
    lat_pair,
    lat_cross,
    diffusion,
    cosine,
    sine,
    send,
    state,
    updated,
    own,
    *rest,
):
    ranks = shift_ranks(count)
    payloads = rest[: len(ranks)]
    held, made, halos, halo, factors, placed, rows_cut, in_sems, out_sems = rest[len(ranks) :]
    fields, levels, columns, rows = state.shape
    tiles = rows // POLAR
    spans = [slice(tile * POLAR, (tile + 1) * POLAR) for tile in range(tiles)]

    def copy_in(l, f):
        return pltpu.make_async_copy(
            state.at[f, l], held.at[l, f, pl.ds(8, columns)], in_sems.at[l, f]
        )

    def copy_out(l, f):
        return pltpu.make_async_copy(made.at[l, f], updated.at[f, l], out_sems.at[l, f])

    for l in range(levels):
        for f in range(fields):
            copy_in(l, f).start()

    lane = lax.broadcasted_iota(jnp.int32, (STEP, POLAR), 1)
    lowest, highest = lane == 0, lane == POLAR - 1
    along = [jnp.broadcast_to(diffusion[0:1, span], (STEP, POLAR)) for span in spans]
    across = [jnp.broadcast_to(diffusion[1:2, span], (STEP, POLAR)) for span in spans]
    centre = [1.0 - 2.0 * along[t] - 2.0 * across[t] for t in range(tiles)]
    lon_odd = lax.rem(meta[2], 2) == 1
    lat_odd = lax.rem(meta[3], 2) == 1
    half = send.shape[0] // 2
    start = pl.multiple_of(meta[0] * POLAR, POLAR)
    size = lat_pair.shape[0]
    blank = jnp.zeros((SOUTH - size, columns), F32)
    north_halo = jnp.where(lat_odd, lat_pair[...], lat_cross[...])
    south_halo = jnp.where(lat_odd, lat_cross[...], lat_pair[...])
    halos[...] = jnp.concatenate([north_halo, blank, south_halo, blank], axis=0).T

    def one_level(l, carry):
        for f in range(fields):
            copy_in(l, f).wait()
        weights = [
            [coupling[l, f * fields + g] for g in range(fields)] for f in range(fields)
        ]
        halo[...] = pltpu.roll(halos[...], lax.rem(POLAR - l * fields, POLAR), 1)
        for f in range(fields):
            item = pl.ds(l * fields + f, 1)
            pair, cross = lon_pair[item, :], lon_cross[item, :]
            held[l, f, 7:8, :] = jnp.where(lon_odd, pair, cross)
            held[l, f, columns + 8 : columns + 9, :] = jnp.where(lon_odd, cross, pair)
        for begin in range(0, columns, STEP):
            end = begin + STEP
            shifted = lambda f, t, by: held[l, f, begin + 8 + by : end + 8 + by, spans[t]]
            here = [[shifted(f, t, 0) for t in range(tiles)] for f in range(fields)]
            edges = halo[begin:end, :]
            for f in range(fields):
                down = [pltpu.roll(here[f][t], 1, 1) for t in range(tiles)]
                up = [pltpu.roll(here[f][t], POLAR - 1, 1) for t in range(tiles)]
                north_edge = [pltpu.roll(edges, POLAR - f, 1) if f else edges] + down[:-1]
                south_edge = up[1:] + [pltpu.roll(edges, POLAR - 1 - SOUTH - f, 1)]
                for t in range(tiles):
                    north = jnp.where(lowest, north_edge[t], down[t])
                    south = jnp.where(highest, south_edge[t], up[t])
                    result = (centre[t] + weights[f][f]) * here[f][t]
                    result = result + along[t] * (shifted(f, t, 1) + shifted(f, t, -1))
                    result = result + across[t] * (north + south)
                    for g in range(fields):
                        if g != f:
                            result = result + weights[f][g] * here[g][t]
                    made[l, f, begin:end, spans[t]] = result
        for f in range(fields):
            copy_out(l, f).start()
        for f in range(fields):
            row = made[l, f, :, pl.ds(start, POLAR)]
            high, low = split_value(modulated(row, cosine, sine))
            both = jnp.dot(send[...], high, preferred_element_type=F32)
            cross = jnp.dot(send[0:half, :], low, preferred_element_type=F32)
            factors[l * fields + f] = both[:half] + both[half:] + cross
        return carry

    lax.fori_loop(0, levels, one_level, 0)

    lon_index = meta[2]
    slots = strips.shape[0]
    lists = fields * levels
    each = strip_rows(lists)
    placed[...] = jnp.zeros(placed.shape, F32)
    rows_cut[...] = jnp.zeros(rows_cut.shape, F32)
    strip_lane = lax.broadcasted_iota(jnp.int32, (16, rows), 1)

    def one_slot(s):
        owner, column = strips[s, 0], strips[s, 1]
        offset, length = strips[s, 2], strips[s, 3]
        rank = jnp.int32(0)
        for other in range(s):
            rank = rank + (strips[other, 0] == owner).astype(jnp.int32)
        for l in range(levels):
            for f in range(fields):
                side, place = divmod(l * fields + f, each)
                rows_cut[s, side, place : place + 1, :] = made[l, f, pl.ds(column, 1), :]
        base = rank * STRIP
        shift = lax.rem(owner - lon_index + count, count)
        for side in range(2):
            where = side * POLAR + base
            moved = pltpu.roll(rows_cut[s, side], lax.rem(where - offset + rows, rows), 1)
            inside = (strip_lane >= where) & (strip_lane < where + length)
            placed[shift] = placed[shift] + jnp.where(inside, moved, 0.0)

    for s in range(slots):
        one_slot(s)
    own[...] = placed[0]

    place = 0
    index = 0
    while index < len(ranks):
        step, rank = ranks[index]
        padded = ceil8(rank)
        paired = 2 if 2 * step < count else 1
        second = is_second(lon_index, step, count)
        targets = payloads[index : index + paired]
        for item in range(lists):
            span = slice(item * rank, (item + 1) * rank)
            plus = factors[item, place : place + rank, :]
            if paired == 1:
                targets[0][span, :] = plus
            else:
                minus = factors[item, place + padded : place + padded + rank, :]
                targets[0][span, :] = jnp.where(second, minus, plus)
                targets[1][span, :] = jnp.where(second, plus, minus)
        plus, minus = placed[step][0:each, :], placed[count - step][0:each, :]
        targets[0][lists * rank : lists * rank + each, :] = jnp.where(second, minus, plus)
        if paired == 2:
            targets[1][lists * rank : lists * rank + each, :] = jnp.where(second, plus, minus)
        for target in targets:
            unused = target.shape[0] - lists * rank - each
            if unused:
                target[lists * rank + each :, :] = jnp.zeros((unused, rows), F32)
        place += paired * padded
        index += paired
    for l in range(levels):
        for f in range(fields):
            copy_out(l, f).wait()


def near_kernel(begin, passed, meta, cosine, sine, middle, near, rows, *rest):
    filtered, moments = rest[passed], rest[passed + 1]
    held, sems = rest[2 * passed + 2 :]
    fields = rows.shape[0]
    lists, columns, _ = filtered.shape
    half = columns // 2
    each = near.shape[0] // 4
    mine = pl.ds(pl.multiple_of(meta[0] * POLAR, POLAR), POLAR)

    def copy_in(item):
        l, f = (begin + item) // fields, (begin + item) % fields
        return pltpu.make_async_copy(rows.at[f, l, :, mine], held.at[item], sems.at[item])

    @pl.when(meta[1] == 1)
    def _():
        for item in range(lists):
            copy_in(item).start()

        def one(item, carry):
            copy_in(item).wait()
            for part in range(2):
                span = slice(part * half, (part + 1) * half)
                row = held[item, span, :]
                turn_cos, turn_sin = cosine[span, :], sine[span, :]
                value = jnp.concatenate([row * turn_cos, row * turn_sin], axis=1)
                table = near[2 * part * each : 2 * (part + 1) * each, :]
                high, low = split_value(value)
                both = jnp.dot(table, high, preferred_element_type=F32)
                cross = jnp.dot(table[:each], low, preferred_element_type=F32)
                total = both[:each] + both[each:] + cross
                filtered[item, span, :] = (
                    turn_sin * total[:half, :POLAR]
                    - turn_cos * total[:half, POLAR:]
                    + middle[0:1, :] * row
                )
                moments[item, part * 16 : (part + 1) * 16, :] = total[half:, :]
            return carry

        lax.fori_loop(0, lists, one, 0, unroll=4)


def far_kernel(count, meta, begins, cosine, sine, turn, far, hats, own, *rest):
    ranks = shift_ranks(count)
    payloads = rest[: len(ranks)]
    near_parts = (rest[len(ranks) : len(ranks) + 2], rest[len(ranks) + 2 : len(ranks) + 4])
    _, out, boundary, filtered, arrived, sums, sems = rest[len(ranks) + 4 :]
    fields, levels = out.shape[0:2]
    lists = fields * levels
    each = strip_rows(lists)
    lon_index = meta[2]
    mine = pl.ds(pl.multiple_of(meta[0] * POLAR, POLAR), POLAR)

    def copy_out(item):
        l, f = item // fields, item % fields
        return pltpu.make_async_copy(filtered.at[item], out.at[f, l, :, mine], sems.at[item])

    def received(index, span):
        step = abs(ranks[index][0])
        if 2 * step == count:
            return payloads[index][span, :]
        base = index - index % 2
        first, last = payloads[base][span, :], payloads[base + 1][span, :]
        takes_first = is_second(lon_index, step, count)
        if index != base:
            takes_first = jnp.logical_not(takes_first)
        return jnp.where(takes_first, first, last)

    @pl.when(meta[1] == 1)
    def _():
        place = 0
        for index, (_, rank) in enumerate(ranks):
            turn_cos = turn[index : index + 1, :POLAR]
            turn_sin = turn[index : index + 1, POLAR:]
            for item in range(lists):
                value = received(index, slice(item * rank, (item + 1) * rank))
                cosines, sines = value[:, :POLAR], value[:, POLAR:]
                arrived[item, place : place + rank, :POLAR] = (
                    turn_cos * cosines + turn_sin * sines
                )
                arrived[item, place : place + rank, POLAR:] = (
                    turn_cos * sines - turn_sin * cosines
                )
            place += rank
        begin = 0
        for near, moments in near_parts:
            for item in range(near.shape[0]):
                for part in range(2):
                    at = place + part * SPLIT_RANK
                    arrived[begin + item, at : at + SPLIT_RANK, :] = moments[
                        item, part * 16 : part * 16 + SPLIT_RANK, :
                    ]
            begin += near.shape[0]
        place += 2 * SPLIT_RANK
        for item in range(lists):
            arrived[item, place:, :] = jnp.zeros((HELD - place, 2 * POLAR), F32)

        begin = 0
        for near, _ in near_parts:

            def one(item, carry, near=near, begin=begin):
                at = begin + item
                total = jnp.dot(far[...], stacked(arrived[at]), preferred_element_type=F32)
                filtered[at] = (
                    near[item] + sine[...] * total[:, :POLAR] - cosine[...] * total[:, POLAR:]
                )
                copy_out(at).start()
                return carry

            lax.fori_loop(0, near.shape[0], one, 0, unroll=4)
            begin += near.shape[0]

    sums[...] = jnp.zeros(sums.shape, F32)
    pieces, sources = [], []
    blank = jnp.zeros((16 - each, POLAR), F32)
    for index in range(-1, len(ranks)):
        if index < 0:
            shift, arrival = 0, own[0:each, :]
        else:
            shift, rank = ranks[index]
            arrival = received(index, slice(lists * rank, lists * rank + each))
        sources.append(lax.rem(lon_index - shift + count, count))
        pieces += [arrival[:, :POLAR], blank, arrival[:, POLAR:], blank]
    pieces = jnp.concatenate(pieces, axis=0)
    high = pieces.astype(BF16)
    middle, low = split_value(pieces - high.astype(F32))
    points = jnp.dot(high, hats[...], preferred_element_type=F32)
    points = points + jnp.dot(middle, hats[...], preferred_element_type=F32)
    points = points + jnp.dot(low, hats[...], preferred_element_type=F32)
    width = hats.shape[1] // CAP
    beyond = jnp.zeros((32, POLAR), F32)
    for index, source in enumerate(sources):
        for rank in range(CAP):
            place = begins[source, rank]
            offset = lax.rem(place, POLAR)
            span = points[index * 32 : (index + 1) * 32, rank * width : (rank + 1) * width]
            moved = pltpu.roll(jnp.concatenate([span, beyond], axis=1), offset, 1)
            at = pl.ds(pl.multiple_of(place - offset, POLAR), width + POLAR)
            sums[:, at] = sums[:, at] + moved
    for l in range(levels):
        for f in range(fields):
            side, row = divmod(l * fields + f, each)
            row = side * 16 + row
            boundary[0, f, l : l + 1, :] = sums[row : row + 1, 0:NB] * (1.0 / RATIO)

    @pl.when(meta[1] == 1)
    def _():
        for item in range(lists):
            copy_out(item).wait()


def phase_table(kept, steps, period):
    phase = (2 * kept - 1)[None, :] * steps[:, None] % (2 * period)
    angle = phase.astype(F32) * (math.pi / period)
    return jnp.cos(angle), jnp.sin(angle)


def cost(flops, bytes_accessed):
    return pl.CostEstimate(flops=flops, bytes_accessed=bytes_accessed, transcendentals=0)


def compressed(model_state, diffusion, coupling, cutoff, strip_list, nest_place):
    lat_index = lax.axis_index("lat")
    lon_index = lax.axis_index("lon")
    lat_count = lax.axis_size("lat")
    lon_count = lax.axis_size("lon")
    fields, levels, columns, rows = model_state.shape
    lists = fields * levels
    total_columns = columns * lon_count
    ranks = shift_ranks(lon_count)
    near, send, far = [jnp.asarray(table) for table in filter_tables(lon_count, columns)]
    params = pltpu.CompilerParams(vmem_limit_bytes=VMEM_LIMIT)
    shape = lambda *sizes: jax.ShapeDtypeStruct(sizes, F32)
    whole_state = shape(*model_state.shape)

    is_south = lat_index == lat_count - 1
    is_polar = (lat_index == 0) | is_south
    part = jnp.where(is_south, rows // POLAR - 1, 0)
    meta = jnp.stack([part, is_polar.astype(jnp.int32), lon_index, lat_index]).astype(jnp.int32)
    kept = jnp.where(lat_index < lat_count // 2, cutoff[:POLAR], cutoff[POLAR:])
    cosine, sine = phase_table(kept, jnp.arange(columns, dtype=jnp.int32), total_columns)
    steps = jnp.array([abs(shift) for shift, _ in ranks], jnp.int32)
    sign = np.array([[1.0 if shift > 0 else -1.0] for shift, _ in ranks], np.float32)
    turn_cos, turn_sin = phase_table(kept, steps, lon_count)
    turn = jnp.concatenate([turn_cos, turn_sin * sign], axis=1)
    turn = jnp.pad(turn, ((0, ceil8(len(ranks)) - len(ranks)), (0, 0)))
    middle = ((2 * kept - 1).astype(F32) / total_columns)[None, :]
    hats = jnp.asarray(hat_table())

    smem = pl.BlockSpec(memory_space=pltpu.SMEM)
    vmem = pl.BlockSpec(memory_space=pltpu.VMEM)
    hbm = pl.BlockSpec(memory_space=pl.ANY)
    level_sems = pltpu.SemaphoreType.DMA((levels, fields))

    with jax.named_scope("edges"):
        edges = pl.pallas_call(
            edge_kernel,
            in_specs=[smem, hbm],
            out_specs=[vmem] * 4,
            out_shape=[shape(ceil8(lists), rows)] * 2 + [shape(ceil8(lists), columns)] * 2,
            scratch_shapes=[
                pltpu.VMEM((lists, columns, rows), F32),
                pltpu.VMEM((columns, POLAR), F32),
                pltpu.SemaphoreType.DMA((lists,)),
            ],
            compiler_params=params,
        )(meta, model_state)

    with jax.named_scope("halo"):
        lon_pairs, lon_crosses = ring_swaps(1, lon_count)
        lat_pairs = [(i, i + 1) for i in range(0, lat_count, 2)]
        lat_crosses = [(i, i + 1) for i in range(1, lat_count - 1, 2)]
        halos = [
            lax.ppermute(edges[0], "lon", lon_pairs),
            lax.ppermute(edges[1], "lon", lon_crosses),
            lax.ppermute(edges[2], "lat", swaps(lat_pairs)),
            lax.ppermute(edges[3], "lat", swaps(lat_crosses)),
        ]

    sizes = [payload_rows(rank, lists) for _, rank in ranks]
    with jax.named_scope("stencil"):
        updated, own, *outgoing = pl.pallas_call(
            functools.partial(stencil_kernel, lon_count),
            in_specs=[smem] * 3 + [vmem] * 8 + [hbm],
            out_specs=[hbm] + [vmem] * (1 + len(ranks)),
            out_shape=[whole_state, shape(16, rows)] + [shape(size, rows) for size in sizes],
            scratch_shapes=[
                pltpu.VMEM((levels, fields, columns + 16, rows), F32),
                pltpu.VMEM((levels, fields, columns, rows), F32),
                pltpu.VMEM((columns, POLAR), F32),
                pltpu.VMEM((columns, POLAR), F32),
                pltpu.VMEM((lists, send.shape[0] // 2, rows), F32),
                pltpu.VMEM((lon_count, 16, rows), F32),
                pltpu.VMEM((strip_list.shape[0], 2, 16, rows), F32),
                level_sems,
                level_sems,
            ],
            compiler_params=params,
        )(
            meta,
            coupling.reshape(levels, fields * fields),
            strip_list,
            *halos,
            diffusion,
            cosine,
            sine,
            send,
            model_state,
        )

    def exchange(index, payload):
        step = abs(ranks[index][0])
        swap = index % 2 if 2 * step < lon_count else 0
        return lax.ppermute(payload, "lon", ring_swaps(step, lon_count)[swap])

    late = [index for index, (shift, _) in enumerate(ranks) if abs(shift) == LATE]
    early = [index for index in range(len(ranks)) if index not in late]
    with jax.named_scope("exchange"):
        incoming = {index: exchange(index, outgoing[index]) for index in early}

    def near_part(begin, end, passed):
        results = pl.pallas_call(
            functools.partial(near_kernel, begin, len(passed)),
            in_specs=[smem] + [vmem] * 4 + [hbm] * (1 + len(passed)),
            out_specs=[vmem] * 2 + [hbm] * len(passed),
            out_shape=[shape(end - begin, columns, POLAR), shape(end - begin, 32, rows)]
            + [shape(*payload.shape) for payload in passed],
            input_output_aliases={6 + index: 2 + index for index in range(len(passed))},
            scratch_shapes=[
                pltpu.VMEM((end - begin, columns, POLAR), F32),
                pltpu.SemaphoreType.DMA((end - begin,)),
            ],
            compiler_params=params,
            cost_estimate=cost(
                12 * (end - begin) * columns * columns * POLAR, 8 * (end - begin) * columns * POLAR
            ),
        )(meta, cosine, sine, middle, near, updated, *passed)
        return results[:2], results[2:]

    with jax.named_scope("near"):
        near_first, passed = near_part(0, EARLY_LISTS, [outgoing[index] for index in late])
    with jax.named_scope("late_exchange"):
        for index, payload in zip(late, passed):
            incoming[index] = exchange(index, payload)
    with jax.named_scope("near_rest"):
        near_last, passed = near_part(EARLY_LISTS, lists, [incoming[index] for index in early])
        incoming.update(zip(early, passed))

    with jax.named_scope("far"):
        advanced, boundary = pl.pallas_call(
            functools.partial(far_kernel, lon_count),
            in_specs=[smem] * 2 + [vmem] * (10 + len(ranks)) + [hbm],
            out_specs=[hbm, vmem],
            out_shape=[whole_state, shape(1, fields, levels, NB)],
            input_output_aliases={12 + len(ranks): 0},
            scratch_shapes=[
                pltpu.VMEM((lists, columns, POLAR), F32),
                pltpu.VMEM((lists, HELD, rows), F32),
                pltpu.VMEM((32, NB + 2 * POLAR), F32),
                pltpu.SemaphoreType.DMA((lists,)),
            ],
            compiler_params=pltpu.CompilerParams(vmem_limit_bytes=VMEM_LIMIT // 2),
        )(
            meta,
            nest_place.reshape(lon_count, CAP),
            cosine,
            sine,
            turn,
            far,
            hats,
            own,
            *[incoming[index] for index in range(len(ranks))],
            *near_first,
            *near_last,
            updated,
        )
    return advanced, boundary


def padded_2(block, sides, width):
    for axis, dim in sides:
        count = lax.axis_size(axis)
        forward = [(i, i + 1) for i in range(count - 1)]
        forward.append((count - 1, 0))
        backward = [(target, source) for source, target in forward]
        low = lax.ppermute(
            lax.slice_in_dim(block, block.shape[dim] - width, None, axis=dim), axis, forward
        )
        high = lax.ppermute(lax.slice_in_dim(block, 0, width, axis=dim), axis, backward)
        block = jnp.concatenate([low, block, high], axis=dim)
    return block


def spectral_filter(rows, kept):
    top_wavenumber_kept = lax.Precision.HIGHEST
    length = rows.shape[3]
    width = math.gcd(KC, 128)
    column_grid = lax.broadcasted_iota(jnp.int32, (length, width), 0)
    step_output = jnp.zeros_like(rows)
    for block_index in range(KC // width):
        wavenumber = block_index * width + lax.broadcasted_iota(jnp.int32, (length, width), 1)
        phase = column_grid * wavenumber % length
        angle = phase.astype(jnp.float32) * (2.0 * math.pi / length)
        cosine = jnp.cos(angle)
        sine = jnp.sin(angle)
        along = block_index * width + jnp.arange(width, dtype=jnp.int32)
        scale = jnp.where(along == 0, 1.0 / length, 2.0 / length)
        weight = jnp.where(along[None, :] < kept[:, None], scale[None, :], 0.0)
        real_part = (
            jnp.einsum("flrn,nk->flrk", rows, cosine, precision=top_wavenumber_kept) * weight
        )
        imaginary_component = (
            jnp.einsum("flrn,nk->flrk", rows, sine, precision=top_wavenumber_kept) * weight
        )
        step_output = (
            step_output
            + jnp.einsum("flrk,nk->flrn", real_part, cosine, precision=top_wavenumber_kept)
            + jnp.einsum("flrk,nk->flrn", imaginary_component, sine, precision=top_wavenumber_kept)
        )
    return step_output


def polar_pass(work_rows, kept_start, kept_table):
    count = work_rows.shape[2] // lax.axis_size("lon")
    kept = lax.dynamic_slice_in_dim(kept_table, kept_start + lax.axis_index("lon") * count, count)
    return lax.all_to_all(
        spectral_filter(
            lax.all_to_all(work_rows, "lon", split_axis=2, concat_axis=3, tiled=True), kept
        ),
        "lon",
        split_axis=3,
        concat_axis=2,
        tiled=True,
    )


def transposed(model_state, diffusion, coupling, cutoff, strip_list, nest_place):
    top_wavenumber_kept = lax.Precision.HIGHEST
    lat_index = lax.axis_index("lat")
    lat_count = lax.axis_size("lat")
    lon_count = lax.axis_size("lon")
    fields, levels, lon_local, lat_local = model_state.shape
    padded = padded_2(model_state, (("lat", 3), ("lon", 2)), 1)
    east_west = padded[:, :, 2:, 1:-1] + padded[:, :, :-2, 1:-1]
    row_place = lax.broadcasted_iota(jnp.int32, (1, 1, 1, lat_local), 3)
    northern = jnp.where((lat_index == 0) & (row_place == 0), 0.0, padded[:, :, 1:-1, :-2])
    southern = jnp.where(
        (lat_index == lat_count - 1) & (row_place == lat_local - 1), 0.0, padded[:, :, 1:-1, 2:]
    )
    blended = jnp.einsum("lfg,glij->flij", coupling, model_state, precision=top_wavenumber_kept)
    updated = (
        model_state
        + diffusion[0] * (east_west - 2.0 * model_state)
        + diffusion[1] * (northern + southern - 2.0 * model_state)
        + blended
    )
    is_south = lat_index == lat_count - 1
    is_polar = (lat_index == 0) | is_south
    start = jnp.where(is_south, lat_local - POLAR, 0).astype(jnp.int32)
    band_base = jnp.where(lat_index < lat_count // 2, 0, POLAR).astype(jnp.int32)
    block_rows = lax.dynamic_slice_in_dim(updated, start, POLAR, 3)
    polar_rows = jnp.transpose(block_rows, (0, 1, 3, 2))
    filtered = polar_pass(polar_rows, band_base, cutoff)
    new_rows = jnp.where(is_polar, jnp.transpose(filtered, (0, 1, 3, 2)), block_rows)
    advanced_state = lax.dynamic_update_slice_in_dim(updated, new_rows, start, 3)
    slots = strip_list.shape[0]
    owners = strip_list[:, 0]
    columns = strip_list[:, 1]
    offsets = strip_list[:, 2]
    lengths = strip_list[:, 3]
    zero = jnp.zeros((), jnp.int32)

    def cut_strip(column, offset):
        return lax.dynamic_slice(
            updated, (zero, zero, column, offset), (fields, levels, 1, STRIP)
        ).reshape(fields * levels, STRIP)

    boundary_strips = jax.vmap(cut_strip)(columns, offsets)
    inside = lax.broadcasted_iota(jnp.int32, (1, 1, STRIP), 2) < lengths[:, None, None]
    boundary_strips = jnp.where(inside, boundary_strips, 0.0).reshape(
        slots, fields * levels * STRIP
    )
    slot_ids = jnp.arange(slots, dtype=jnp.int32)
    earlier = slot_ids[None, :] < slot_ids[:, None]
    same = owners[:, None] == owners[None, :]
    rank = jnp.sum((same & earlier).astype(jnp.int32), axis=1)
    target = owners * CAP + rank
    routing = (jnp.arange(lon_count * CAP, dtype=jnp.int32)[:, None] == target[None, :]).astype(
        jnp.float32
    )
    outgoing = jnp.dot(
        routing, boundary_strips, precision=top_wavenumber_kept, preferred_element_type=jnp.float32
    ).reshape(lon_count, CAP, fields * levels * STRIP)
    arrived = lax.all_to_all(outgoing, "lon", split_axis=0, concat_axis=0, tiled=True)
    total = lon_count * CAP
    group = math.gcd(total, 16)
    pieces = arrived.reshape(total // group, group, fields * levels, STRIP)
    starts = nest_place.reshape(total // group, group)
    point = lax.broadcasted_iota(jnp.int32, (1, 1, NB), 2)
    row_step = lax.broadcasted_iota(jnp.int32, (1, STRIP, 1), 1) * RATIO

    def accumulate(carry, item):
        piece, begin = item
        offset = point - begin[:, None, None]
        hat = jnp.maximum(RATIO - jnp.abs(offset - row_step), 0)
        hat = (
            jnp.where((offset >= 0) & (offset < STRIP * RATIO), hat, 0).astype(jnp.float32) / RATIO
        )
        return (carry + jnp.einsum("gat,gtp->ap", piece, hat, precision=top_wavenumber_kept), None)

    boundary = lax.scan(
        accumulate, jnp.zeros((fields * levels, NB), jnp.float32), (pieces, starts)
    )[0]
    return (advanced_state, boundary.reshape(1, fields, levels, NB))


def local(model_state, *others):
    columns = model_state.shape[2]
    fits = lax.axis_size("lon") * STRIP == POLAR and model_state.shape[3] == 2 * POLAR
    if fits and columns % STEP == 0 and columns >= 2 * HELD:
        return compressed(model_state, *others)
    return transposed(model_state, *others)


def solution(mesh):
    return jax.shard_map(
        local,
        mesh=mesh,
        in_specs=(
            P(None, None, "lon", "lat"),
            P(None, "lat"),
            P(),
            P(),
            P(("lat", "lon"), None),
            P(("lat", "lon"), None, None),
        ),
        out_specs=(P(None, None, "lon", "lat"), P(("lat", "lon"), None, None, None)),
        check_vma=False,
    )
```

```python
import functools
import math

import jax
import jax.numpy as jnp
import numpy as np
from jax import lax
from jax.experimental import pallas as pl
from jax.experimental.pallas import tpu as pltpu
from jax.sharding import PartitionSpec as P

POLAR = 128
CAP = 2
STRIP = 16
RATIO = 11
NB = 2048
KC = 896
RANKS = (14, 5, 4, 4)
SPLIT_RANK = 14
STEP = 16
HELD = 80
EARLY_LISTS = 8
QUICK = (0, 2)
LATE = (3, 4)
SOUTH = 64
VMEM_LIMIT = 48 * 1024 * 1024
F32 = jnp.float32
BF16 = jnp.bfloat16


def ceil8(value):
    return -(-value // 8) * 8


def shift_ranks(count):
    shifts = []
    for step in range(1, count // 2 + 1):
        for shift in (step, -step):
            if shift != -count // 2:
                shifts.append((shift, RANKS[min(step, len(RANKS)) - 1]))
    return shifts


def is_second(place, step, count):
    return lax.rem(lax.div(place, math.gcd(step, count)), 2) == 1


def swaps(pairs):
    return [pair for a, b in pairs for pair in ((a, b), (b, a))]


def ring_swaps(step, count):
    if 2 * step == count:
        return [swaps([(i, i + step) for i in range(step)])]
    groups = [[], []]
    for i in range(count):
        groups[i // math.gcd(step, count) % 2].append((i, (i + step) % count))
    return [swaps(group) for group in groups]


def split_table(table):
    high = table.astype(jnp.bfloat16)
    low = (table - high.astype(np.float64)).astype(jnp.bfloat16)
    return high, low


def factored(block, rank):
    left, values, right = np.linalg.svd(block)
    root = np.sqrt(values[:rank])
    return right[:rank] * root[:, None], left[:, :rank] * root[None, :]


@functools.lru_cache(maxsize=None)
def filter_tables(count, width):
    total = count * width
    half = width // 2

    def block(size, shift):
        place = np.arange(size)
        angle = np.pi * (shift + place[:, None] - place[None, :]) / total
        with np.errstate(divide="ignore"):
            return np.where(angle == 0, 0.0, 1.0 / (np.sin(angle) * total))

    senders, receivers = [], []
    for shift, rank in shift_ranks(count):
        sender, receiver = factored(block(width, shift * width), rank)
        senders.append(np.pad(sender, ((0, ceil8(rank) - rank), (0, 0))))
        receivers.append(receiver)
    nears = []
    for part, shift in enumerate((half, -half)):
        sender, receiver = factored(block(half, shift), SPLIT_RANK)
        rows = np.concatenate([block(half, 0), sender], axis=0)
        nears.append(np.pad(rows, ((0, 16 - SPLIT_RANK), (0, 0))))
        beyond = ((half, 0), (0, 0)) if part == 0 else ((0, half), (0, 0))
        receivers.append(np.pad(receiver, beyond))
    receivers = np.concatenate(receivers, axis=1)
    receivers = np.pad(receivers, ((0, 0), (0, HELD - receivers.shape[1])))
    nears = [table for rows in nears for table in split_table(rows)]
    send_high, send_low = split_table(np.concatenate(senders, axis=0))
    far_high, far_low = split_table(receivers)
    return (
        np.concatenate(nears, axis=0),
        np.concatenate([send_high, send_low], axis=0),
        np.concatenate([far_high, far_high, far_low], axis=1),
    )


def hat_table():
    width = -(-STRIP * RATIO // POLAR) * POLAR
    point = np.arange(width)
    table = np.zeros((POLAR, CAP * width), np.float32)
    for rank in range(CAP):
        for row in range(STRIP):
            hat = np.maximum(RATIO - np.abs(point - row * RATIO), 0) * (point < STRIP * RATIO)
            table[rank * STRIP + row, rank * width : (rank + 1) * width] = hat
    return table.astype(jnp.bfloat16)


def split_value(value):
    high = value.astype(BF16)
    return high, (value - high.astype(F32)).astype(BF16)


def modulated(row, cosine, sine):
    return jnp.concatenate([row * cosine[...], row * sine[...]], axis=1)


def stacked(value):
    high, low = split_value(value)
    return jnp.concatenate([high, low, high], axis=0)


def strip_rows(slots):
    return slots // 2


def payload_rows(rank, slots):
    return ceil8(slots * rank + strip_rows(slots))


def edge_kernel(
    meta, state, lon_pair, lon_cross, lat_pair, lat_cross, held, edges, in_sems
):
    fields, levels, columns, rows = state.shape
    lists = fields * levels

    def copy_in(item):
        l, f = item // fields, item % fields
        return pltpu.make_async_copy(state.at[f, l], held.at[item], in_sems.at[item])

    def start(item, carry):
        copy_in(item).start()
        return carry

    lax.fori_loop(0, lists, start, 0)
    lane = lax.broadcasted_iota(jnp.int32, (columns, POLAR), 1)
    lon_odd = lax.rem(meta[2], 2) == 1
    lat_odd = lax.rem(meta[3], 2) == 1
    edges[...] = jnp.zeros(edges.shape, F32)

    def one(item, carry):
        copy_in(item).wait()
        first = held[item, 0:1, :]
        last = held[item, columns - 1 : columns, :]
        lon_pair[pl.ds(item, 1), :] = jnp.where(lon_odd, first, last)
        lon_cross[pl.ds(item, 1), :] = jnp.where(lon_odd, last, first)
        north = pltpu.roll(held[item, :, 0:POLAR], item, 1)
        south = pltpu.roll(held[item, :, rows - POLAR :], item + SOUTH + 1, 1)
        value = jnp.where(lane == item, north, edges[...])
        edges[...] = jnp.where(lane == SOUTH + item, south, value)
        return carry

    lax.fori_loop(0, lists, one, 0, unroll=5)
    turned = edges[...].T
    size = lat_pair.shape[0]
    north, south = turned[0:size], turned[SOUTH : SOUTH + size]
    lat_pair[...] = jnp.where(lat_odd, north, south)
    lat_cross[...] = jnp.where(lat_odd, south, north)


def stencil_kernel(
    count,
    meta,
    coupling,
    strips,
    lon_pair,
    lon_cross,
    lat_pair,
    lat_cross,
    diffusion,
    cosine,
    sine,
    send,
    state,
    updated,
    own,
    *rest,
):
    ranks = shift_ranks(count)
    payloads = rest[: len(ranks)]
    held, made, halos, halo, factors, placed, rows_cut, in_sems, out_sems = rest[len(ranks) :]
    fields, levels, columns, rows = state.shape
    tiles = rows // POLAR
    spans = [slice(tile * POLAR, (tile + 1) * POLAR) for tile in range(tiles)]

    def copy_in(l, f):
        return pltpu.make_async_copy(
            state.at[f, l], held.at[l, f, pl.ds(8, columns)], in_sems.at[l, f]
        )

    def copy_out(l, f):
        return pltpu.make_async_copy(made.at[l, f], updated.at[f, l], out_sems.at[l, f])

    for l in range(levels):
        for f in range(fields):
            copy_in(l, f).start()

    lane = lax.broadcasted_iota(jnp.int32, (STEP, POLAR), 1)
    lowest, highest = lane == 0, lane == POLAR - 1
    along = [jnp.broadcast_to(diffusion[0:1, span], (STEP, POLAR)) for span in spans]
    across = [jnp.broadcast_to(diffusion[1:2, span], (STEP, POLAR)) for span in spans]
    centre = [1.0 - 2.0 * along[t] - 2.0 * across[t] for t in range(tiles)]
    lon_odd = lax.rem(meta[2], 2) == 1
    lat_odd = lax.rem(meta[3], 2) == 1
    half = send.shape[0] // 2
    start = pl.multiple_of(meta[0] * POLAR, POLAR)
    size = lat_pair.shape[0]
    blank = jnp.zeros((SOUTH - size, columns), F32)
    north_halo = jnp.where(lat_odd, lat_pair[...], lat_cross[...])
    south_halo = jnp.where(lat_odd, lat_cross[...], lat_pair[...])
    halos[...] = jnp.concatenate([north_halo, blank, south_halo, blank], axis=0).T

    def one_level(l, carry):
        for f in range(fields):
            copy_in(l, f).wait()
        weights = [
            [coupling[l, f * fields + g] for g in range(fields)] for f in range(fields)
        ]
        halo[...] = pltpu.roll(halos[...], lax.rem(POLAR - l * fields, POLAR), 1)
        for f in range(fields):
            item = pl.ds(l * fields + f, 1)
            pair, cross = lon_pair[item, :], lon_cross[item, :]
            held[l, f, 7:8, :] = jnp.where(lon_odd, pair, cross)
            held[l, f, columns + 8 : columns + 9, :] = jnp.where(lon_odd, cross, pair)
        for begin in range(0, columns, STEP):
            end = begin + STEP
            shifted = lambda f, t, by: held[l, f, begin + 8 + by : end + 8 + by, spans[t]]
            here = [[shifted(f, t, 0) for t in range(tiles)] for f in range(fields)]
            edges = halo[begin:end, :]
            for f in range(fields):
                down = [pltpu.roll(here[f][t], 1, 1) for t in range(tiles)]
                up = [pltpu.roll(here[f][t], POLAR - 1, 1) for t in range(tiles)]
                north_edge = [pltpu.roll(edges, POLAR - f, 1) if f else edges] + down[:-1]
                south_edge = up[1:] + [pltpu.roll(edges, POLAR - 1 - SOUTH - f, 1)]
                for t in range(tiles):
                    north = jnp.where(lowest, north_edge[t], down[t])
                    south = jnp.where(highest, south_edge[t], up[t])
                    result = (centre[t] + weights[f][f]) * here[f][t]
                    result = result + along[t] * (shifted(f, t, 1) + shifted(f, t, -1))
                    result = result + across[t] * (north + south)
                    for g in range(fields):
                        if g != f:
                            result = result + weights[f][g] * here[g][t]
                    made[l, f, begin:end, spans[t]] = result
        for f in range(fields):
            copy_out(l, f).start()
        for f in range(fields):
            row = made[l, f, :, pl.ds(start, POLAR)]
            high, low = split_value(modulated(row, cosine, sine))
            both = jnp.dot(send[...], high, preferred_element_type=F32)
            cross = jnp.dot(send[0:half, :], low, preferred_element_type=F32)
            factors[l * fields + f] = both[:half] + both[half:] + cross
        return carry

    lax.fori_loop(0, levels, one_level, 0)

    lon_index = meta[2]
    slots = strips.shape[0]
    lists = fields * levels
    each = strip_rows(lists)
    placed[...] = jnp.zeros(placed.shape, F32)
    rows_cut[...] = jnp.zeros(rows_cut.shape, F32)
    strip_lane = lax.broadcasted_iota(jnp.int32, (16, rows), 1)

    def one_slot(s):
        owner, column = strips[s, 0], strips[s, 1]
        offset, length = strips[s, 2], strips[s, 3]
        rank = jnp.int32(0)
        for other in range(s):
            rank = rank + (strips[other, 0] == owner).astype(jnp.int32)
        for l in range(levels):
            for f in range(fields):
                side, place = divmod(l * fields + f, each)
                rows_cut[s, side, place : place + 1, :] = made[l, f, pl.ds(column, 1), :]
        base = rank * STRIP
        shift = lax.rem(owner - lon_index + count, count)
        for side in range(2):
            where = side * POLAR + base
            moved = pltpu.roll(rows_cut[s, side], lax.rem(where - offset + rows, rows), 1)
            inside = (strip_lane >= where) & (strip_lane < where + length)
            placed[shift] = placed[shift] + jnp.where(inside, moved, 0.0)

    for s in range(slots):
        one_slot(s)
    own[...] = placed[0]

    place = 0
    index = 0
    while index < len(ranks):
        step, rank = ranks[index]
        padded = ceil8(rank)
        paired = 2 if 2 * step < count else 1
        second = is_second(lon_index, step, count)
        targets = payloads[index : index + paired]
        for item in range(lists):
            span = slice(item * rank, (item + 1) * rank)
            plus = factors[item, place : place + rank, :]
            if paired == 1:
                targets[0][span, :] = plus
            else:
                minus = factors[item, place + padded : place + padded + rank, :]
                targets[0][span, :] = jnp.where(second, minus, plus)
                targets[1][span, :] = jnp.where(second, plus, minus)
        plus, minus = placed[step][0:each, :], placed[count - step][0:each, :]
        targets[0][lists * rank : lists * rank + each, :] = jnp.where(second, minus, plus)
        if paired == 2:
            targets[1][lists * rank : lists * rank + each, :] = jnp.where(second, plus, minus)
        for target in targets:
            unused = target.shape[0] - lists * rank - each
            if unused:
                target[lists * rank + each :, :] = jnp.zeros((unused, rows), F32)
        place += paired * padded
        index += paired
    for l in range(levels):
        for f in range(fields):
            copy_out(l, f).wait()


def near_kernel(begin, passed, meta, cosine, sine, middle, near, rows, *rest):
    filtered, moments = rest[passed], rest[passed + 1]
    held, sems = rest[2 * passed + 2 :]
    fields = rows.shape[0]
    lists, columns, _ = filtered.shape
    half = columns // 2
    each = near.shape[0] // 4
    mine = pl.ds(pl.multiple_of(meta[0] * POLAR, POLAR), POLAR)

    def copy_in(item):
        l, f = (begin + item) // fields, (begin + item) % fields
        return pltpu.make_async_copy(rows.at[f, l, :, mine], held.at[item], sems.at[item])

    @pl.when(meta[1] == 1)
    def _():
        for item in range(lists):
            copy_in(item).start()

        def one(item, carry):
            copy_in(item).wait()
            for part in range(2):
                span = slice(part * half, (part + 1) * half)
                row = held[item, span, :]
                turn_cos, turn_sin = cosine[span, :], sine[span, :]
                value = jnp.concatenate([row * turn_cos, row * turn_sin], axis=1)
                table = near[2 * part * each : 2 * (part + 1) * each, :]
                high, low = split_value(value)
                both = jnp.dot(table, high, preferred_element_type=F32)
                cross = jnp.dot(table[:each], low, preferred_element_type=F32)
                total = both[:each] + both[each:] + cross
                filtered[item, span, :] = (
                    turn_sin * total[:half, :POLAR]
                    - turn_cos * total[:half, POLAR:]
                    + middle[0:1, :] * row
                )
                moments[item, part * 16 : (part + 1) * 16, :] = total[half:, :]
            return carry

        lax.fori_loop(0, lists, one, 0, unroll=4)


def far_kernel(count, meta, begins, cosine, sine, turn, far, hats, own, *rest):
    ranks = shift_ranks(count)
    payloads = rest[: len(ranks)]
    near_parts = (rest[len(ranks) : len(ranks) + 2], rest[len(ranks) + 2 : len(ranks) + 4])
    _, out, boundary, filtered, arrived, sums, sems = rest[len(ranks) + 4 :]
    fields, levels = out.shape[0:2]
    lists = fields * levels
    each = strip_rows(lists)
    lon_index = meta[2]
    mine = pl.ds(pl.multiple_of(meta[0] * POLAR, POLAR), POLAR)

    def copy_out(item):
        l, f = item // fields, item % fields
        return pltpu.make_async_copy(filtered.at[item], out.at[f, l, :, mine], sems.at[item])

    def received(index, span):
        step = abs(ranks[index][0])
        if 2 * step == count:
            return payloads[index][span, :]
        base = index - index % 2
        first, last = payloads[base][span, :], payloads[base + 1][span, :]
        takes_first = is_second(lon_index, step, count)
        if index != base:
            takes_first = jnp.logical_not(takes_first)
        return jnp.where(takes_first, first, last)

    @pl.when(meta[1] == 1)
    def _():
        place = 0
        for index, (_, rank) in enumerate(ranks):
            turn_cos = turn[index : index + 1, :POLAR]
            turn_sin = turn[index : index + 1, POLAR:]
            for item in range(lists):
                value = received(index, slice(item * rank, (item + 1) * rank))
                cosines, sines = value[:, :POLAR], value[:, POLAR:]
                arrived[item, place : place + rank, :POLAR] = (
                    turn_cos * cosines + turn_sin * sines
                )
                arrived[item, place : place + rank, POLAR:] = (
                    turn_cos * sines - turn_sin * cosines
                )
            place += rank
        begin = 0
        for near, moments in near_parts:
            for item in range(near.shape[0]):
                for part in range(2):
                    at = place + part * SPLIT_RANK
                    arrived[begin + item, at : at + SPLIT_RANK, :] = moments[
                        item, part * 16 : part * 16 + SPLIT_RANK, :
                    ]
            begin += near.shape[0]
        place += 2 * SPLIT_RANK
        for item in range(lists):
            arrived[item, place:, :] = jnp.zeros((HELD - place, 2 * POLAR), F32)

        begin = 0
        for near, _ in near_parts:

            def one(item, carry, near=near, begin=begin):
                at = begin + item
                total = jnp.dot(far[...], stacked(arrived[at]), preferred_element_type=F32)
                filtered[at] = (
                    near[item] + sine[...] * total[:, :POLAR] - cosine[...] * total[:, POLAR:]
                )
                copy_out(at).start()
                return carry

            lax.fori_loop(0, near.shape[0], one, 0, unroll=4)
            begin += near.shape[0]

    sums[...] = jnp.zeros(sums.shape, F32)
    pieces, sources = [], []
    blank = jnp.zeros((16 - each, POLAR), F32)
    for index in range(-1, len(ranks)):
        if index < 0:
            shift, arrival = 0, own[0:each, :]
        else:
            shift, rank = ranks[index]
            arrival = received(index, slice(lists * rank, lists * rank + each))
        sources.append(lax.rem(lon_index - shift + count, count))
        pieces += [arrival[:, :POLAR], blank, arrival[:, POLAR:], blank]
    pieces = jnp.concatenate(pieces, axis=0)
    high = pieces.astype(BF16)
    middle, low = split_value(pieces - high.astype(F32))
    points = jnp.dot(high, hats[...], preferred_element_type=F32)
    points = points + jnp.dot(middle, hats[...], preferred_element_type=F32)
    points = points + jnp.dot(low, hats[...], preferred_element_type=F32)
    width = hats.shape[1] // CAP
    beyond = jnp.zeros((32, POLAR), F32)
    for index, source in enumerate(sources):
        for rank in range(CAP):
            place = begins[source, rank]
            offset = lax.rem(place, POLAR)
            span = points[index * 32 : (index + 1) * 32, rank * width : (rank + 1) * width]
            moved = pltpu.roll(jnp.concatenate([span, beyond], axis=1), offset, 1)
            at = pl.ds(pl.multiple_of(place - offset, POLAR), width + POLAR)
            sums[:, at] = sums[:, at] + moved
    for l in range(levels):
        for f in range(fields):
            side, row = divmod(l * fields + f, each)
            row = side * 16 + row
            boundary[0, f, l : l + 1, :] = sums[row : row + 1, 0:NB] * (1.0 / RATIO)

    @pl.when(meta[1] == 1)
    def _():
        for item in range(lists):
            copy_out(item).wait()


def phase_table(kept, steps, period):
    phase = (2 * kept - 1)[None, :] * steps[:, None] % (2 * period)
    angle = phase.astype(F32) * (math.pi / period)
    return jnp.cos(angle), jnp.sin(angle)


def cost(flops, bytes_accessed):
    return pl.CostEstimate(flops=flops, bytes_accessed=bytes_accessed, transcendentals=0)


def compressed(model_state, diffusion, coupling, cutoff, strip_list, nest_place):
    lat_index = lax.axis_index("lat")
    lon_index = lax.axis_index("lon")
    lat_count = lax.axis_size("lat")
    lon_count = lax.axis_size("lon")
    fields, levels, columns, rows = model_state.shape
    lists = fields * levels
    total_columns = columns * lon_count
    ranks = shift_ranks(lon_count)
    near, send, far = [jnp.asarray(table) for table in filter_tables(lon_count, columns)]
    params = pltpu.CompilerParams(vmem_limit_bytes=VMEM_LIMIT)
    shape = lambda *sizes: jax.ShapeDtypeStruct(sizes, F32)
    whole_state = shape(*model_state.shape)

    is_south = lat_index == lat_count - 1
    is_polar = (lat_index == 0) | is_south
    part = jnp.where(is_south, rows // POLAR - 1, 0)
    meta = jnp.stack([part, is_polar.astype(jnp.int32), lon_index, lat_index]).astype(jnp.int32)
    kept = jnp.where(lat_index < lat_count // 2, cutoff[:POLAR], cutoff[POLAR:])
    cosine, sine = phase_table(kept, jnp.arange(columns, dtype=jnp.int32), total_columns)
    steps = jnp.array([abs(shift) for shift, _ in ranks], jnp.int32)
    sign = np.array([[1.0 if shift > 0 else -1.0] for shift, _ in ranks], np.float32)
    turn_cos, turn_sin = phase_table(kept, steps, lon_count)
    turn = jnp.concatenate([turn_cos, turn_sin * sign], axis=1)
    turn = jnp.pad(turn, ((0, ceil8(len(ranks)) - len(ranks)), (0, 0)))
    middle = ((2 * kept - 1).astype(F32) / total_columns)[None, :]
    hats = jnp.asarray(hat_table())

    smem = pl.BlockSpec(memory_space=pltpu.SMEM)
    vmem = pl.BlockSpec(memory_space=pltpu.VMEM)
    hbm = pl.BlockSpec(memory_space=pl.ANY)
    level_sems = pltpu.SemaphoreType.DMA((levels, fields))

    with jax.named_scope("edges"):
        edges = pl.pallas_call(
            edge_kernel,
            in_specs=[smem, hbm],
            out_specs=[vmem] * 4,
            out_shape=[shape(ceil8(lists), rows)] * 2 + [shape(ceil8(lists), columns)] * 2,
            scratch_shapes=[
                pltpu.VMEM((lists, columns, rows), F32),
                pltpu.VMEM((columns, POLAR), F32),
                pltpu.SemaphoreType.DMA((lists,)),
            ],
            compiler_params=params,
        )(meta, model_state)

    with jax.named_scope("halo"):
        lon_pairs, lon_crosses = ring_swaps(1, lon_count)
        lat_pairs = [(i, i + 1) for i in range(0, lat_count, 2)]
        lat_crosses = [(i, i + 1) for i in range(1, lat_count - 1, 2)]
        halos = [
            lax.ppermute(edges[0], "lon", lon_pairs),
            lax.ppermute(edges[1], "lon", lon_crosses),
            lax.ppermute(edges[2], "lat", swaps(lat_pairs)),
            lax.ppermute(edges[3], "lat", swaps(lat_crosses)),
        ]

    sizes = [payload_rows(rank, lists) for _, rank in ranks]
    with jax.named_scope("stencil"):
        updated, own, *outgoing = pl.pallas_call(
            functools.partial(stencil_kernel, lon_count),
            in_specs=[smem] * 3 + [vmem] * 8 + [hbm],
            out_specs=[hbm] + [vmem] * (1 + len(ranks)),
            out_shape=[whole_state, shape(16, rows)] + [shape(size, rows) for size in sizes],
            scratch_shapes=[
                pltpu.VMEM((levels, fields, columns + 16, rows), F32),
                pltpu.VMEM((levels, fields, columns, rows), F32),
                pltpu.VMEM((columns, POLAR), F32),
                pltpu.VMEM((columns, POLAR), F32),
                pltpu.VMEM((lists, send.shape[0] // 2, rows), F32),
                pltpu.VMEM((lon_count, 16, rows), F32),
                pltpu.VMEM((strip_list.shape[0], 2, 16, rows), F32),
                level_sems,
                level_sems,
            ],
            compiler_params=params,
        )(
            meta,
            coupling.reshape(levels, fields * fields),
            strip_list,
            *halos,
            diffusion,
            cosine,
            sine,
            send,
            model_state,
        )

    def exchange(index, payload):
        step = abs(ranks[index][0])
        swap = index % 2 if 2 * step < lon_count else 0
        return lax.ppermute(payload, "lon", ring_swaps(step, lon_count)[swap])

    with jax.named_scope("exchange"):
        incoming = {
            index: exchange(index, outgoing[index])
            for index in range(len(ranks))
            if index not in LATE
        }

    def near_part(begin, end, passed):
        results = pl.pallas_call(
            functools.partial(near_kernel, begin, len(passed)),
            in_specs=[smem] + [vmem] * 4 + [hbm] * (1 + len(passed)),
            out_specs=[vmem] * 2 + [hbm] * len(passed),
            out_shape=[shape(end - begin, columns, POLAR), shape(end - begin, 32, rows)]
            + [shape(*payload.shape) for payload in passed],
            input_output_aliases={6 + index: 2 + index for index in range(len(passed))},
            scratch_shapes=[
                pltpu.VMEM((end - begin, columns, POLAR), F32),
                pltpu.SemaphoreType.DMA((end - begin,)),
            ],
            compiler_params=params,
            cost_estimate=cost(
                12 * (end - begin) * columns * columns * POLAR, 8 * (end - begin) * columns * POLAR
            ),
        )(meta, cosine, sine, middle, near, updated, *passed)
        return results[:2], results[2:]

    with jax.named_scope("near"):
        near_first, passed = near_part(0, EARLY_LISTS, [outgoing[index] for index in LATE])
    with jax.named_scope("late_exchange"):
        for index, payload in zip(LATE, passed):
            incoming[index] = exchange(index, payload)
    with jax.named_scope("near_rest"):
        near_last, passed = near_part(EARLY_LISTS, lists, [incoming[index] for index in QUICK])
        incoming.update(zip(QUICK, passed))

    with jax.named_scope("far"):
        advanced, boundary = pl.pallas_call(
            functools.partial(far_kernel, lon_count),
            in_specs=[smem] * 2 + [vmem] * (10 + len(ranks)) + [hbm],
            out_specs=[hbm, vmem],
            out_shape=[whole_state, shape(1, fields, levels, NB)],
            input_output_aliases={12 + len(ranks): 0},
            scratch_shapes=[
                pltpu.VMEM((lists, columns, POLAR), F32),
                pltpu.VMEM((lists, HELD, rows), F32),
                pltpu.VMEM((32, NB + 2 * POLAR), F32),
                pltpu.SemaphoreType.DMA((lists,)),
            ],
            compiler_params=pltpu.CompilerParams(vmem_limit_bytes=VMEM_LIMIT // 2),
        )(
            meta,
            nest_place.reshape(lon_count, CAP),
            cosine,
            sine,
            turn,
            far,
            hats,
            own,
            *[incoming[index] for index in range(len(ranks))],
            *near_first,
            *near_last,
            updated,
        )
    return advanced, boundary


def padded_2(block, sides, width):
    for axis, dim in sides:
        count = lax.axis_size(axis)
        forward = [(i, i + 1) for i in range(count - 1)]
        forward.append((count - 1, 0))
        backward = [(target, source) for source, target in forward]
        low = lax.ppermute(
            lax.slice_in_dim(block, block.shape[dim] - width, None, axis=dim), axis, forward
        )
        high = lax.ppermute(lax.slice_in_dim(block, 0, width, axis=dim), axis, backward)
        block = jnp.concatenate([low, block, high], axis=dim)
    return block


def spectral_filter(rows, kept):
    top_wavenumber_kept = lax.Precision.HIGHEST
    length = rows.shape[3]
    width = math.gcd(KC, 128)
    column_grid = lax.broadcasted_iota(jnp.int32, (length, width), 0)
    step_output = jnp.zeros_like(rows)
    for block_index in range(KC // width):
        wavenumber = block_index * width + lax.broadcasted_iota(jnp.int32, (length, width), 1)
        phase = column_grid * wavenumber % length
        angle = phase.astype(jnp.float32) * (2.0 * math.pi / length)
        cosine = jnp.cos(angle)
        sine = jnp.sin(angle)
        along = block_index * width + jnp.arange(width, dtype=jnp.int32)
        scale = jnp.where(along == 0, 1.0 / length, 2.0 / length)
        weight = jnp.where(along[None, :] < kept[:, None], scale[None, :], 0.0)
        real_part = (
            jnp.einsum("flrn,nk->flrk", rows, cosine, precision=top_wavenumber_kept) * weight
        )
        imaginary_component = (
            jnp.einsum("flrn,nk->flrk", rows, sine, precision=top_wavenumber_kept) * weight
        )
        step_output = (
            step_output
            + jnp.einsum("flrk,nk->flrn", real_part, cosine, precision=top_wavenumber_kept)
            + jnp.einsum("flrk,nk->flrn", imaginary_component, sine, precision=top_wavenumber_kept)
        )
    return step_output


def polar_pass(work_rows, kept_start, kept_table):
    count = work_rows.shape[2] // lax.axis_size("lon")
    kept = lax.dynamic_slice_in_dim(kept_table, kept_start + lax.axis_index("lon") * count, count)
    return lax.all_to_all(
        spectral_filter(
            lax.all_to_all(work_rows, "lon", split_axis=2, concat_axis=3, tiled=True), kept
        ),
        "lon",
        split_axis=3,
        concat_axis=2,
        tiled=True,
    )


def transposed(model_state, diffusion, coupling, cutoff, strip_list, nest_place):
    top_wavenumber_kept = lax.Precision.HIGHEST
    lat_index = lax.axis_index("lat")
    lat_count = lax.axis_size("lat")
    lon_count = lax.axis_size("lon")
    fields, levels, lon_local, lat_local = model_state.shape
    padded = padded_2(model_state, (("lat", 3), ("lon", 2)), 1)
    east_west = padded[:, :, 2:, 1:-1] + padded[:, :, :-2, 1:-1]
    row_place = lax.broadcasted_iota(jnp.int32, (1, 1, 1, lat_local), 3)
    northern = jnp.where((lat_index == 0) & (row_place == 0), 0.0, padded[:, :, 1:-1, :-2])
    southern = jnp.where(
        (lat_index == lat_count - 1) & (row_place == lat_local - 1), 0.0, padded[:, :, 1:-1, 2:]
    )
    blended = jnp.einsum("lfg,glij->flij", coupling, model_state, precision=top_wavenumber_kept)
    updated = (
        model_state
        + diffusion[0] * (east_west - 2.0 * model_state)
        + diffusion[1] * (northern + southern - 2.0 * model_state)
        + blended
    )
    is_south = lat_index == lat_count - 1
    is_polar = (lat_index == 0) | is_south
    start = jnp.where(is_south, lat_local - POLAR, 0).astype(jnp.int32)
    band_base = jnp.where(lat_index < lat_count // 2, 0, POLAR).astype(jnp.int32)
    block_rows = lax.dynamic_slice_in_dim(updated, start, POLAR, 3)
    polar_rows = jnp.transpose(block_rows, (0, 1, 3, 2))
    filtered = polar_pass(polar_rows, band_base, cutoff)
    new_rows = jnp.where(is_polar, jnp.transpose(filtered, (0, 1, 3, 2)), block_rows)
    advanced_state = lax.dynamic_update_slice_in_dim(updated, new_rows, start, 3)
    slots = strip_list.shape[0]
    owners = strip_list[:, 0]
    columns = strip_list[:, 1]
    offsets = strip_list[:, 2]
    lengths = strip_list[:, 3]
    zero = jnp.zeros((), jnp.int32)

    def cut_strip(column, offset):
        return lax.dynamic_slice(
            updated, (zero, zero, column, offset), (fields, levels, 1, STRIP)
        ).reshape(fields * levels, STRIP)

    boundary_strips = jax.vmap(cut_strip)(columns, offsets)
    inside = lax.broadcasted_iota(jnp.int32, (1, 1, STRIP), 2) < lengths[:, None, None]
    boundary_strips = jnp.where(inside, boundary_strips, 0.0).reshape(
        slots, fields * levels * STRIP
    )
    slot_ids = jnp.arange(slots, dtype=jnp.int32)
    earlier = slot_ids[None, :] < slot_ids[:, None]
    same = owners[:, None] == owners[None, :]
    rank = jnp.sum((same & earlier).astype(jnp.int32), axis=1)
    target = owners * CAP + rank
    routing = (jnp.arange(lon_count * CAP, dtype=jnp.int32)[:, None] == target[None, :]).astype(
        jnp.float32
    )
    outgoing = jnp.dot(
        routing, boundary_strips, precision=top_wavenumber_kept, preferred_element_type=jnp.float32
    ).reshape(lon_count, CAP, fields * levels * STRIP)
    arrived = lax.all_to_all(outgoing, "lon", split_axis=0, concat_axis=0, tiled=True)
    total = lon_count * CAP
    group = math.gcd(total, 16)
    pieces = arrived.reshape(total // group, group, fields * levels, STRIP)
    starts = nest_place.reshape(total // group, group)
    point = lax.broadcasted_iota(jnp.int32, (1, 1, NB), 2)
    row_step = lax.broadcasted_iota(jnp.int32, (1, STRIP, 1), 1) * RATIO

    def accumulate(carry, item):
        piece, begin = item
        offset = point - begin[:, None, None]
        hat = jnp.maximum(RATIO - jnp.abs(offset - row_step), 0)
        hat = (
            jnp.where((offset >= 0) & (offset < STRIP * RATIO), hat, 0).astype(jnp.float32) / RATIO
        )
        return (carry + jnp.einsum("gat,gtp->ap", piece, hat, precision=top_wavenumber_kept), None)

    boundary = lax.scan(
        accumulate, jnp.zeros((fields * levels, NB), jnp.float32), (pieces, starts)
    )[0]
    return (advanced_state, boundary.reshape(1, fields, levels, NB))


def local(model_state, *others):
    columns = model_state.shape[2]
    fits = lax.axis_size("lon") * STRIP == POLAR and model_state.shape[3] == 2 * POLAR
    if fits and columns % STEP == 0 and columns >= 2 * HELD:
        return compressed(model_state, *others)
    return transposed(model_state, *others)


def solution(mesh):
    return jax.shard_map(
        local,
        mesh=mesh,
        in_specs=(
            P(None, None, "lon", "lat"),
            P(None, "lat"),
            P(),
            P(),
            P(("lat", "lon"), None),
            P(("lat", "lon"), None, None),
        ),
        out_specs=(P(None, None, "lon", "lat"), P(("lat", "lon"), None, None, None)),
        check_vma=False,
    )
```

```python
import functools
import math

import jax
import jax.numpy as jnp
import numpy as np
from jax import lax
from jax.experimental import pallas as pl
from jax.experimental.pallas import tpu as pltpu
from jax.sharding import PartitionSpec as P

POLAR = 128
CAP = 2
STRIP = 16
RATIO = 11
NB = 2048
KC = 896
RANKS = (14, 5, 4, 4)
SPLIT_RANK = 14
STEP = 16
HELD = 80
EARLY_LISTS = 8
QUICK = (0, 2)
LATE = (3, 4)
SOUTH = 64
VMEM_LIMIT = 48 * 1024 * 1024
F32 = jnp.float32
BF16 = jnp.bfloat16


def ceil8(value):
    return -(-value // 8) * 8


def shift_ranks(count):
    shifts = []
    for step in range(1, count // 2 + 1):
        for shift in (step, -step):
            if shift != -count // 2:
                shifts.append((shift, RANKS[min(step, len(RANKS)) - 1]))
    return shifts


def is_second(place, step, count):
    return lax.rem(lax.div(place, math.gcd(step, count)), 2) == 1


def swaps(pairs):
    return [pair for a, b in pairs for pair in ((a, b), (b, a))]


def ring_swaps(step, count):
    if 2 * step == count:
        return [swaps([(i, i + step) for i in range(step)])]
    groups = [[], []]
    for i in range(count):
        groups[i // math.gcd(step, count) % 2].append((i, (i + step) % count))
    return [swaps(group) for group in groups]


def split_table(table):
    high = table.astype(jnp.bfloat16)
    low = (table - high.astype(np.float64)).astype(jnp.bfloat16)
    return high, low


def factored(block, rank):
    left, values, right = np.linalg.svd(block)
    root = np.sqrt(values[:rank])
    return right[:rank] * root[:, None], left[:, :rank] * root[None, :]


@functools.lru_cache(maxsize=None)
def filter_tables(count, width):
    total = count * width
    half = width // 2

    def block(size, shift):
        place = np.arange(size)
        angle = np.pi * (shift + place[:, None] - place[None, :]) / total
        with np.errstate(divide="ignore"):
            return np.where(angle == 0, 0.0, 1.0 / (np.sin(angle) * total))

    senders, receivers = [], []
    for shift, rank in shift_ranks(count):
        sender, receiver = factored(block(width, shift * width), rank)
        senders.append(np.pad(sender, ((0, ceil8(rank) - rank), (0, 0))))
        receivers.append(receiver)
    nears = []
    for part, shift in enumerate((half, -half)):
        sender, receiver = factored(block(half, shift), SPLIT_RANK)
        rows = np.concatenate([block(half, 0), sender], axis=0)
        nears.append(np.pad(rows, ((0, 16 - SPLIT_RANK), (0, 0))))
        beyond = ((half, 0), (0, 0)) if part == 0 else ((0, half), (0, 0))
        receivers.append(np.pad(receiver, beyond))
    receivers = np.concatenate(receivers, axis=1)
    receivers = np.pad(receivers, ((0, 0), (0, HELD - receivers.shape[1])))
    nears = [table for rows in nears for table in split_table(rows)]
    send_high, send_low = split_table(np.concatenate(senders, axis=0))
    far_high, far_low = split_table(receivers)
    return (
        np.concatenate(nears, axis=0),
        np.concatenate([send_high, send_low], axis=0),
        np.concatenate([far_high, far_high, far_low], axis=1),
    )


def hat_table():
    width = -(-STRIP * RATIO // POLAR) * POLAR
    point = np.arange(width)
    table = np.zeros((POLAR, CAP * width), np.float32)
    for rank in range(CAP):
        for row in range(STRIP):
            hat = np.maximum(RATIO - np.abs(point - row * RATIO), 0) * (point < STRIP * RATIO)
            table[rank * STRIP + row, rank * width : (rank + 1) * width] = hat
    return table.astype(jnp.bfloat16)


def split_value(value):
    high = value.astype(BF16)
    return high, (value - high.astype(F32)).astype(BF16)


def modulated(row, cosine, sine):
    return jnp.concatenate([row * cosine[...], row * sine[...]], axis=1)


def stacked(value):
    high, low = split_value(value)
    return jnp.concatenate([high, low, high], axis=0)


def strip_rows(slots):
    return slots // 2


def payload_rows(rank, slots):
    return ceil8(slots * rank + strip_rows(slots))


def edge_columns(is_north, state, out, held, edges, sems):
    fields, levels, columns, rows = state.shape
    lists = fields * levels
    tile = pl.ds(pl.multiple_of(jnp.where(is_north, 0, rows - POLAR), POLAR), POLAR)

    def copy_in(item):
        l, f = item // fields, item % fields
        return pltpu.make_async_copy(state.at[f, l, :, tile], held.at[item], sems.at[item])

    def start(item, carry):
        copy_in(item).start()
        return carry

    lax.fori_loop(0, lists, start, 0)
    lane = lax.broadcasted_iota(jnp.int32, (columns, POLAR), 1)
    edges[...] = jnp.zeros(edges.shape, F32)

    def one(item, carry):
        copy_in(item).wait()
        row = pltpu.roll(held[item], jnp.where(is_north, item, item + 1), 1)
        edges[...] = jnp.where(lane == item, row, edges[...])
        return carry

    lax.fori_loop(0, lists, one, 0, unroll=5)
    out[...] = edges[...].T[0 : out.shape[0]]


def first_edge_kernel(
    meta, state, lon_pair, lon_cross, lat_pair, ends, held, edges, end_sems, sems
):
    fields, levels, columns, _ = state.shape
    lists = fields * levels

    def copy_end(item, side):
        l, f = item // fields, item % fields
        return pltpu.make_async_copy(
            state.at[f, l, pl.ds(side * (columns - 8), 8), :],
            ends.at[item, side],
            end_sems.at[item, side],
        )

    for item in range(lists):
        for side in range(2):
            copy_end(item, side).start()
    edge_columns(lax.rem(meta[3], 2) == 1, state, lat_pair, held, edges, sems)
    lon_odd = lax.rem(meta[2], 2) == 1
    lon_pair[...] = jnp.zeros(lon_pair.shape, F32)
    lon_cross[...] = jnp.zeros(lon_cross.shape, F32)
    for item in range(lists):
        for side in range(2):
            copy_end(item, side).wait()
        first, last = ends[item, 0, 0:1, :], ends[item, 1, 7:8, :]
        lon_pair[item : item + 1, :] = jnp.where(lon_odd, first, last)
        lon_cross[item : item + 1, :] = jnp.where(lon_odd, last, first)


def second_edge_kernel(meta, state, before, lat_cross, held, edges, sems):
    del before

    @pl.when(meta[4] == 1)
    def _():
        edge_columns(lax.rem(meta[3], 2) == 0, state, lat_cross, held, edges, sems)

    @pl.when(meta[4] == 0)
    def _():
        lat_cross[...] = jnp.zeros(lat_cross.shape, F32)


def stencil_kernel(
    count,
    meta,
    coupling,
    strips,
    lon_pair,
    lon_cross,
    lat_pair,
    lat_cross,
    diffusion,
    angle_cos,
    angle_sin,
    send,
    state,
    updated,
    cosine,
    sine,
    own,
    *rest,
):
    ranks = shift_ranks(count)
    payloads = rest[: len(ranks)]
    held, made, halos, halo, factors, placed, rows_cut, in_sems, out_sems = rest[len(ranks) :]
    fields, levels, columns, rows = state.shape
    tiles = rows // POLAR
    spans = [slice(tile * POLAR, (tile + 1) * POLAR) for tile in range(tiles)]

    def copy_in(l, f):
        return pltpu.make_async_copy(
            state.at[f, l], held.at[l, f, pl.ds(8, columns)], in_sems.at[l, f]
        )

    def copy_out(l, f):
        return pltpu.make_async_copy(made.at[l, f], updated.at[f, l], out_sems.at[l, f])

    for l in range(levels):
        for f in range(fields):
            copy_in(l, f).start()

    steps = columns // STEP
    fine_cos, fine_sin = angle_cos[steps:, :], angle_sin[steps:, :]
    for step in range(steps):
        span = slice(step * STEP, (step + 1) * STEP)
        coarse_cos, coarse_sin = angle_cos[step : step + 1, :], angle_sin[step : step + 1, :]
        cosine[span, :] = coarse_cos * fine_cos - coarse_sin * fine_sin
        sine[span, :] = coarse_sin * fine_cos + coarse_cos * fine_sin

    lane = lax.broadcasted_iota(jnp.int32, (STEP, POLAR), 1)
    lowest, highest = lane == 0, lane == POLAR - 1
    along = [jnp.broadcast_to(diffusion[0:1, span], (STEP, POLAR)) for span in spans]
    across = [jnp.broadcast_to(diffusion[1:2, span], (STEP, POLAR)) for span in spans]
    centre = [1.0 - 2.0 * along[t] - 2.0 * across[t] for t in range(tiles)]
    lon_odd = lax.rem(meta[2], 2) == 1
    lat_odd = lax.rem(meta[3], 2) == 1
    half = send.shape[0] // 2
    start = pl.multiple_of(meta[0] * POLAR, POLAR)
    size = lat_pair.shape[0]
    blank = jnp.zeros((SOUTH - size, columns), F32)
    north_halo = jnp.where(lat_odd, lat_pair[...], lat_cross[...])
    south_halo = jnp.where(lat_odd, lat_cross[...], lat_pair[...])
    halos[...] = jnp.concatenate([north_halo, blank, south_halo, blank], axis=0).T

    def one_level(l, carry):
        for f in range(fields):
            copy_in(l, f).wait()
        weights = [
            [coupling[l, f * fields + g] for g in range(fields)] for f in range(fields)
        ]
        halo[...] = pltpu.roll(halos[...], lax.rem(POLAR - l * fields, POLAR), 1)
        for f in range(fields):
            item = pl.ds(l * fields + f, 1)
            pair, cross = lon_pair[item, :], lon_cross[item, :]
            held[l, f, 7:8, :] = jnp.where(lon_odd, pair, cross)
            held[l, f, columns + 8 : columns + 9, :] = jnp.where(lon_odd, cross, pair)
        for begin in range(0, columns, STEP):
            end = begin + STEP
            shifted = lambda f, t, by: held[l, f, begin + 8 + by : end + 8 + by, spans[t]]
            here = [[shifted(f, t, 0) for t in range(tiles)] for f in range(fields)]
            edges = halo[begin:end, :]
            for f in range(fields):
                down = [pltpu.roll(here[f][t], 1, 1) for t in range(tiles)]
                up = [pltpu.roll(here[f][t], POLAR - 1, 1) for t in range(tiles)]
                north_edge = [pltpu.roll(edges, POLAR - f, 1) if f else edges] + down[:-1]
                south_edge = up[1:] + [pltpu.roll(edges, POLAR - 1 - SOUTH - f, 1)]
                for t in range(tiles):
                    north = jnp.where(lowest, north_edge[t], down[t])
                    south = jnp.where(highest, south_edge[t], up[t])
                    result = (centre[t] + weights[f][f]) * here[f][t]
                    result = result + along[t] * (shifted(f, t, 1) + shifted(f, t, -1))
                    result = result + across[t] * (north + south)
                    for g in range(fields):
                        if g != f:
                            result = result + weights[f][g] * here[g][t]
                    made[l, f, begin:end, spans[t]] = result
        for f in range(fields):
            copy_out(l, f).start()
        for f in range(fields):
            row = made[l, f, :, pl.ds(start, POLAR)]
            high, low = split_value(modulated(row, cosine, sine))
            both = jnp.dot(send[...], high, preferred_element_type=F32)
            cross = jnp.dot(send[0:half, :], low, preferred_element_type=F32)
            factors[l * fields + f] = both[:half] + both[half:] + cross
        return carry

    lax.fori_loop(0, levels, one_level, 0)

    lon_index = meta[2]
    slots = strips.shape[0]
    lists = fields * levels
    each = strip_rows(lists)
    placed[...] = jnp.zeros(placed.shape, F32)
    rows_cut[...] = jnp.zeros(rows_cut.shape, F32)
    strip_lane = lax.broadcasted_iota(jnp.int32, (16, rows), 1)

    def one_slot(s):
        owner, column = strips[s, 0], strips[s, 1]
        offset, length = strips[s, 2], strips[s, 3]
        rank = jnp.int32(0)
        for other in range(s):
            rank = rank + (strips[other, 0] == owner).astype(jnp.int32)
        for l in range(levels):
            for f in range(fields):
                side, place = divmod(l * fields + f, each)
                rows_cut[s, side, place : place + 1, :] = made[l, f, pl.ds(column, 1), :]
        base = rank * STRIP
        shift = lax.rem(owner - lon_index + count, count)
        for side in range(2):
            where = side * POLAR + base
            moved = pltpu.roll(rows_cut[s, side], lax.rem(where - offset + rows, rows), 1)
            inside = (strip_lane >= where) & (strip_lane < where + length)
            placed[shift] = placed[shift] + jnp.where(inside, moved, 0.0)

    for s in range(slots):
        one_slot(s)
    own[...] = placed[0]

    place = 0
    index = 0
    while index < len(ranks):
        step, rank = ranks[index]
        padded = ceil8(rank)
        paired = 2 if 2 * step < count else 1
        second = is_second(lon_index, step, count)
        targets = payloads[index : index + paired]
        for item in range(lists):
            span = slice(item * rank, (item + 1) * rank)
            plus = factors[item, place : place + rank, :]
            if paired == 1:
                targets[0][span, :] = plus
            else:
                minus = factors[item, place + padded : place + padded + rank, :]
                targets[0][span, :] = jnp.where(second, minus, plus)
                targets[1][span, :] = jnp.where(second, plus, minus)
        plus, minus = placed[step][0:each, :], placed[count - step][0:each, :]
        targets[0][lists * rank : lists * rank + each, :] = jnp.where(second, minus, plus)
        if paired == 2:
            targets[1][lists * rank : lists * rank + each, :] = jnp.where(second, plus, minus)
        for target in targets:
            unused = target.shape[0] - lists * rank - each
            if unused:
                target[lists * rank + each :, :] = jnp.zeros((unused, rows), F32)
        place += paired * padded
        index += paired
    for l in range(levels):
        for f in range(fields):
            copy_out(l, f).wait()


def near_kernel(begin, passed, meta, cosine, sine, middle, near, rows, *rest):
    filtered, moments = rest[passed], rest[passed + 1]
    held, sems = rest[2 * passed + 2 :]
    fields = rows.shape[0]
    lists, columns, _ = filtered.shape
    half = columns // 2
    each = near.shape[0] // 4
    mine = pl.ds(pl.multiple_of(meta[0] * POLAR, POLAR), POLAR)

    def copy_in(item):
        l, f = (begin + item) // fields, (begin + item) % fields
        return pltpu.make_async_copy(rows.at[f, l, :, mine], held.at[item], sems.at[item])

    @pl.when(meta[1] == 1)
    def _():
        for item in range(lists):
            copy_in(item).start()

        def one(item, carry):
            copy_in(item).wait()
            for part in range(2):
                span = slice(part * half, (part + 1) * half)
                row = held[item, span, :]
                turn_cos, turn_sin = cosine[span, :], sine[span, :]
                value = jnp.concatenate([row * turn_cos, row * turn_sin], axis=1)
                table = near[2 * part * each : 2 * (part + 1) * each, :]
                high, low = split_value(value)
                both = jnp.dot(table, high, preferred_element_type=F32)
                cross = jnp.dot(table[:each], low, preferred_element_type=F32)
                total = both[:each] + both[each:] + cross
                filtered[item, span, :] = (
                    turn_sin * total[:half, :POLAR]
                    - turn_cos * total[:half, POLAR:]
                    + middle[0:1, :] * row
                )
                moments[item, part * 16 : (part + 1) * 16, :] = total[half:, :]
            return carry

        lax.fori_loop(0, lists, one, 0, unroll=4)


def far_kernel(count, meta, begins, cosine, sine, turn, far, hats, own, *rest):
    ranks = shift_ranks(count)
    payloads = rest[: len(ranks)]
    near_parts = (rest[len(ranks) : len(ranks) + 2], rest[len(ranks) + 2 : len(ranks) + 4])
    _, out, boundary, filtered, arrived, sums, sems = rest[len(ranks) + 4 :]
    fields, levels = out.shape[0:2]
    lists = fields * levels
    each = strip_rows(lists)
    lon_index = meta[2]
    mine = pl.ds(pl.multiple_of(meta[0] * POLAR, POLAR), POLAR)

    def copy_out(item):
        l, f = item // fields, item % fields
        return pltpu.make_async_copy(filtered.at[item], out.at[f, l, :, mine], sems.at[item])

    def received(index, span):
        step = abs(ranks[index][0])
        if 2 * step == count:
            return payloads[index][span, :]
        base = index - index % 2
        first, last = payloads[base][span, :], payloads[base + 1][span, :]
        takes_first = is_second(lon_index, step, count)
        if index != base:
            takes_first = jnp.logical_not(takes_first)
        return jnp.where(takes_first, first, last)

    @pl.when(meta[1] == 1)
    def _():
        place = 0
        for index, (_, rank) in enumerate(ranks):
            turn_cos = turn[index : index + 1, :POLAR]
            turn_sin = turn[index : index + 1, POLAR:]
            for item in range(lists):
                value = received(index, slice(item * rank, (item + 1) * rank))
                cosines, sines = value[:, :POLAR], value[:, POLAR:]
                arrived[item, place : place + rank, :POLAR] = (
                    turn_cos * cosines + turn_sin * sines
                )
                arrived[item, place : place + rank, POLAR:] = (
                    turn_cos * sines - turn_sin * cosines
                )
            place += rank
        begin = 0
        for near, moments in near_parts:
            for item in range(near.shape[0]):
                for part in range(2):
                    at = place + part * SPLIT_RANK
                    arrived[begin + item, at : at + SPLIT_RANK, :] = moments[
                        item, part * 16 : part * 16 + SPLIT_RANK, :
                    ]
            begin += near.shape[0]
        place += 2 * SPLIT_RANK
        for item in range(lists):
            arrived[item, place:, :] = jnp.zeros((HELD - place, 2 * POLAR), F32)

        begin = 0
        for near, _ in near_parts:

            def one(item, carry, near=near, begin=begin):
                at = begin + item
                total = jnp.dot(far[...], stacked(arrived[at]), preferred_element_type=F32)
                filtered[at] = (
                    near[item] + sine[...] * total[:, :POLAR] - cosine[...] * total[:, POLAR:]
                )
                copy_out(at).start()
                return carry

            lax.fori_loop(0, near.shape[0], one, 0, unroll=4)
            begin += near.shape[0]

    sums[...] = jnp.zeros(sums.shape, F32)
    pieces, sources = [], []
    blank = jnp.zeros((16 - each, POLAR), F32)
    for index in range(-1, len(ranks)):
        if index < 0:
            shift, arrival = 0, own[0:each, :]
        else:
            shift, rank = ranks[index]
            arrival = received(index, slice(lists * rank, lists * rank + each))
        sources.append(lax.rem(lon_index - shift + count, count))
        pieces += [arrival[:, :POLAR], blank, arrival[:, POLAR:], blank]
    pieces = jnp.concatenate(pieces, axis=0)
    high = pieces.astype(BF16)
    middle, low = split_value(pieces - high.astype(F32))
    points = jnp.dot(high, hats[...], preferred_element_type=F32)
    points = points + jnp.dot(middle, hats[...], preferred_element_type=F32)
    points = points + jnp.dot(low, hats[...], preferred_element_type=F32)
    width = hats.shape[1] // CAP
    beyond = jnp.zeros((32, POLAR), F32)
    for index, source in enumerate(sources):
        for rank in range(CAP):
            place = begins[source, rank]
            offset = lax.rem(place, POLAR)
            span = points[index * 32 : (index + 1) * 32, rank * width : (rank + 1) * width]
            moved = pltpu.roll(jnp.concatenate([span, beyond], axis=1), offset, 1)
            at = pl.ds(pl.multiple_of(place - offset, POLAR), width + POLAR)
            sums[:, at] = sums[:, at] + moved
    for l in range(levels):
        for f in range(fields):
            side, row = divmod(l * fields + f, each)
            row = side * 16 + row
            boundary[0, f, l : l + 1, :] = sums[row : row + 1, 0:NB] * (1.0 / RATIO)

    @pl.when(meta[1] == 1)
    def _():
        for item in range(lists):
            copy_out(item).wait()


def phase_table(kept, steps, period):
    phase = (2 * kept - 1)[None, :] * steps[:, None] % (2 * period)
    angle = phase.astype(F32) * (math.pi / period)
    return jnp.cos(angle), jnp.sin(angle)


def cost(flops, bytes_accessed):
    return pl.CostEstimate(flops=flops, bytes_accessed=bytes_accessed, transcendentals=0)


def compressed(model_state, diffusion, coupling, cutoff, strip_list, nest_place):
    lat_index = lax.axis_index("lat")
    lon_index = lax.axis_index("lon")
    lat_count = lax.axis_size("lat")
    lon_count = lax.axis_size("lon")
    fields, levels, columns, rows = model_state.shape
    lists = fields * levels
    total_columns = columns * lon_count
    ranks = shift_ranks(lon_count)
    near, send, far = [jnp.asarray(table) for table in filter_tables(lon_count, columns)]
    params = pltpu.CompilerParams(vmem_limit_bytes=VMEM_LIMIT)
    shape = lambda *sizes: jax.ShapeDtypeStruct(sizes, F32)
    whole_state = shape(*model_state.shape)

    is_south = lat_index == lat_count - 1
    is_polar = (lat_index == 0) | is_south
    part = jnp.where(is_south, rows // POLAR - 1, 0)
    is_crossed = jnp.where(lat_index % 2 == 1, lat_index < lat_count - 1, lat_index > 0)
    meta = [part, is_polar, lon_index, lat_index, is_crossed]
    meta = jnp.stack([value.astype(jnp.int32) for value in meta])
    kept = jnp.where(lat_index < lat_count // 2, cutoff[:POLAR], cutoff[POLAR:])
    places = np.concatenate([np.arange(0, columns, STEP), np.arange(STEP)]).astype(np.int32)
    angles = phase_table(kept, jnp.asarray(places), total_columns)
    steps = jnp.array([abs(shift) for shift, _ in ranks], jnp.int32)
    sign = np.array([[1.0 if shift > 0 else -1.0] for shift, _ in ranks], np.float32)
    turn_cos, turn_sin = phase_table(kept, steps, lon_count)
    turn = jnp.concatenate([turn_cos, turn_sin * sign], axis=1)
    turn = jnp.pad(turn, ((0, ceil8(len(ranks)) - len(ranks)), (0, 0)))
    middle = ((2 * kept - 1).astype(F32) / total_columns)[None, :]
    hats = jnp.asarray(hat_table())

    smem = pl.BlockSpec(memory_space=pltpu.SMEM)
    vmem = pl.BlockSpec(memory_space=pltpu.VMEM)
    hbm = pl.BlockSpec(memory_space=pl.ANY)
    level_sems = pltpu.SemaphoreType.DMA((levels, fields))

    edge_scratch = [
        pltpu.VMEM((lists, columns, POLAR), F32),
        pltpu.VMEM((columns, POLAR), F32),
    ]
    list_sems = pltpu.SemaphoreType.DMA((lists,))
    with jax.named_scope("edges"):
        edges = pl.pallas_call(
            first_edge_kernel,
            in_specs=[smem, hbm],
            out_specs=[vmem] * 3,
            out_shape=[shape(ceil8(lists), rows)] * 2 + [shape(ceil8(lists), columns)],
            scratch_shapes=[pltpu.VMEM((lists, 2, 8, rows), F32)]
            + edge_scratch
            + [pltpu.SemaphoreType.DMA((lists, 2)), list_sems],
            compiler_params=params,
        )(meta, model_state)
    with jax.named_scope("second_edges"):
        second_edge = pl.pallas_call(
            second_edge_kernel,
            in_specs=[smem, hbm, hbm],
            out_specs=vmem,
            out_shape=shape(ceil8(lists), columns),
            scratch_shapes=edge_scratch + [list_sems],
            compiler_params=params,
            cost_estimate=cost(0, 4 * lists * columns * POLAR),
        )(meta, model_state, edges[2])

    with jax.named_scope("halo"):
        lon_pairs, lon_crosses = ring_swaps(1, lon_count)
        lat_pairs = [(i, i + 1) for i in range(0, lat_count, 2)]
        lat_crosses = [(i, i + 1) for i in range(1, lat_count - 1, 2)]
        halos = [
            lax.ppermute(edges[0], "lon", lon_pairs),
            lax.ppermute(edges[1], "lon", lon_crosses),
            lax.ppermute(edges[2], "lat", swaps(lat_pairs)),
            lax.ppermute(second_edge, "lat", swaps(lat_crosses)),
        ]

    sizes = [payload_rows(rank, lists) for _, rank in ranks]
    with jax.named_scope("stencil"):
        updated, cosine, sine, own, *outgoing = pl.pallas_call(
            functools.partial(stencil_kernel, lon_count),
            in_specs=[smem] * 3 + [vmem] * 8 + [hbm],
            out_specs=[hbm] + [vmem] * (3 + len(ranks)),
            out_shape=[whole_state]
            + [shape(columns, POLAR)] * 2
            + [shape(16, rows)]
            + [shape(size, rows) for size in sizes],
            scratch_shapes=[
                pltpu.VMEM((levels, fields, columns + 16, rows), F32),
                pltpu.VMEM((levels, fields, columns, rows), F32),
                pltpu.VMEM((columns, POLAR), F32),
                pltpu.VMEM((columns, POLAR), F32),
                pltpu.VMEM((lists, send.shape[0] // 2, rows), F32),
                pltpu.VMEM((lon_count, 16, rows), F32),
                pltpu.VMEM((strip_list.shape[0], 2, 16, rows), F32),
                level_sems,
                level_sems,
            ],
            compiler_params=params,
        )(
            meta,
            coupling.reshape(levels, fields * fields),
            strip_list,
            *halos,
            diffusion,
            *angles,
            send,
            model_state,
        )

    def exchange(index, payload):
        step = abs(ranks[index][0])
        swap = index % 2 if 2 * step < lon_count else 0
        return lax.ppermute(payload, "lon", ring_swaps(step, lon_count)[swap])

    with jax.named_scope("exchange"):
        incoming = {
            index: exchange(index, outgoing[index])
            for index in range(len(ranks))
            if index not in LATE
        }

    def near_part(begin, end, passed):
        results = pl.pallas_call(
            functools.partial(near_kernel, begin, len(passed)),
            in_specs=[smem] + [vmem] * 4 + [hbm] * (1 + len(passed)),
            out_specs=[vmem] * 2 + [hbm] * len(passed),
            out_shape=[shape(end - begin, columns, POLAR), shape(end - begin, 32, rows)]
            + [shape(*payload.shape) for payload in passed],
            input_output_aliases={6 + index: 2 + index for index in range(len(passed))},
            scratch_shapes=[
                pltpu.VMEM((end - begin, columns, POLAR), F32),
                pltpu.SemaphoreType.DMA((end - begin,)),
            ],
            compiler_params=params,
            cost_estimate=cost(
                12 * (end - begin) * columns * columns * POLAR, 8 * (end - begin) * columns * POLAR
            ),
        )(meta, cosine, sine, middle, near, updated, *passed)
        return results[:2], results[2:]

    with jax.named_scope("near"):
        near_first, passed = near_part(0, EARLY_LISTS, [outgoing[index] for index in LATE])
    with jax.named_scope("late_exchange"):
        for index, payload in zip(LATE, passed):
            incoming[index] = exchange(index, payload)
    with jax.named_scope("near_rest"):
        near_last, passed = near_part(EARLY_LISTS, lists, [incoming[index] for index in QUICK])
        incoming.update(zip(QUICK, passed))

    with jax.named_scope("far"):
        advanced, boundary = pl.pallas_call(
            functools.partial(far_kernel, lon_count),
            in_specs=[smem] * 2 + [vmem] * (10 + len(ranks)) + [hbm],
            out_specs=[hbm, vmem],
            out_shape=[whole_state, shape(1, fields, levels, NB)],
            input_output_aliases={12 + len(ranks): 0},
            scratch_shapes=[
                pltpu.VMEM((lists, columns, POLAR), F32),
                pltpu.VMEM((lists, HELD, rows), F32),
                pltpu.VMEM((32, NB + 2 * POLAR), F32),
                pltpu.SemaphoreType.DMA((lists,)),
            ],
            compiler_params=pltpu.CompilerParams(vmem_limit_bytes=VMEM_LIMIT // 2),
        )(
            meta,
            nest_place.reshape(lon_count, CAP),
            cosine,
            sine,
            turn,
            far,
            hats,
            own,
            *[incoming[index] for index in range(len(ranks))],
            *near_first,
            *near_last,
            updated,
        )
    return advanced, boundary


def padded_2(block, sides, width):
    for axis, dim in sides:
        count = lax.axis_size(axis)
        forward = [(i, i + 1) for i in range(count - 1)]
        forward.append((count - 1, 0))
        backward = [(target, source) for source, target in forward]
        low = lax.ppermute(
            lax.slice_in_dim(block, block.shape[dim] - width, None, axis=dim), axis, forward
        )
        high = lax.ppermute(lax.slice_in_dim(block, 0, width, axis=dim), axis, backward)
        block = jnp.concatenate([low, block, high], axis=dim)
    return block


def spectral_filter(rows, kept):
    top_wavenumber_kept = lax.Precision.HIGHEST
    length = rows.shape[3]
    width = math.gcd(KC, 128)
    column_grid = lax.broadcasted_iota(jnp.int32, (length, width), 0)
    step_output = jnp.zeros_like(rows)
    for block_index in range(KC // width):
        wavenumber = block_index * width + lax.broadcasted_iota(jnp.int32, (length, width), 1)
        phase = column_grid * wavenumber % length
        angle = phase.astype(jnp.float32) * (2.0 * math.pi / length)
        cosine = jnp.cos(angle)
        sine = jnp.sin(angle)
        along = block_index * width + jnp.arange(width, dtype=jnp.int32)
        scale = jnp.where(along == 0, 1.0 / length, 2.0 / length)
        weight = jnp.where(along[None, :] < kept[:, None], scale[None, :], 0.0)
        real_part = (
            jnp.einsum("flrn,nk->flrk", rows, cosine, precision=top_wavenumber_kept) * weight
        )
        imaginary_component = (
            jnp.einsum("flrn,nk->flrk", rows, sine, precision=top_wavenumber_kept) * weight
        )
        step_output = (
            step_output
            + jnp.einsum("flrk,nk->flrn", real_part, cosine, precision=top_wavenumber_kept)
            + jnp.einsum("flrk,nk->flrn", imaginary_component, sine, precision=top_wavenumber_kept)
        )
    return step_output


def polar_pass(work_rows, kept_start, kept_table):
    count = work_rows.shape[2] // lax.axis_size("lon")
    kept = lax.dynamic_slice_in_dim(kept_table, kept_start + lax.axis_index("lon") * count, count)
    return lax.all_to_all(
        spectral_filter(
            lax.all_to_all(work_rows, "lon", split_axis=2, concat_axis=3, tiled=True), kept
        ),
        "lon",
        split_axis=3,
        concat_axis=2,
        tiled=True,
    )


def transposed(model_state, diffusion, coupling, cutoff, strip_list, nest_place):
    top_wavenumber_kept = lax.Precision.HIGHEST
    lat_index = lax.axis_index("lat")
    lat_count = lax.axis_size("lat")
    lon_count = lax.axis_size("lon")
    fields, levels, lon_local, lat_local = model_state.shape
    padded = padded_2(model_state, (("lat", 3), ("lon", 2)), 1)
    east_west = padded[:, :, 2:, 1:-1] + padded[:, :, :-2, 1:-1]
    row_place = lax.broadcasted_iota(jnp.int32, (1, 1, 1, lat_local), 3)
    northern = jnp.where((lat_index == 0) & (row_place == 0), 0.0, padded[:, :, 1:-1, :-2])
    southern = jnp.where(
        (lat_index == lat_count - 1) & (row_place == lat_local - 1), 0.0, padded[:, :, 1:-1, 2:]
    )
    blended = jnp.einsum("lfg,glij->flij", coupling, model_state, precision=top_wavenumber_kept)
    updated = (
        model_state
        + diffusion[0] * (east_west - 2.0 * model_state)
        + diffusion[1] * (northern + southern - 2.0 * model_state)
        + blended
    )
    is_south = lat_index == lat_count - 1
    is_polar = (lat_index == 0) | is_south
    start = jnp.where(is_south, lat_local - POLAR, 0).astype(jnp.int32)
    band_base = jnp.where(lat_index < lat_count // 2, 0, POLAR).astype(jnp.int32)
    block_rows = lax.dynamic_slice_in_dim(updated, start, POLAR, 3)
    polar_rows = jnp.transpose(block_rows, (0, 1, 3, 2))
    filtered = polar_pass(polar_rows, band_base, cutoff)
    new_rows = jnp.where(is_polar, jnp.transpose(filtered, (0, 1, 3, 2)), block_rows)
    advanced_state = lax.dynamic_update_slice_in_dim(updated, new_rows, start, 3)
    slots = strip_list.shape[0]
    owners = strip_list[:, 0]
    columns = strip_list[:, 1]
    offsets = strip_list[:, 2]
    lengths = strip_list[:, 3]
    zero = jnp.zeros((), jnp.int32)

    def cut_strip(column, offset):
        return lax.dynamic_slice(
            updated, (zero, zero, column, offset), (fields, levels, 1, STRIP)
        ).reshape(fields * levels, STRIP)

    boundary_strips = jax.vmap(cut_strip)(columns, offsets)
    inside = lax.broadcasted_iota(jnp.int32, (1, 1, STRIP), 2) < lengths[:, None, None]
    boundary_strips = jnp.where(inside, boundary_strips, 0.0).reshape(
        slots, fields * levels * STRIP
    )
    slot_ids = jnp.arange(slots, dtype=jnp.int32)
    earlier = slot_ids[None, :] < slot_ids[:, None]
    same = owners[:, None] == owners[None, :]
    rank = jnp.sum((same & earlier).astype(jnp.int32), axis=1)
    target = owners * CAP + rank
    routing = (jnp.arange(lon_count * CAP, dtype=jnp.int32)[:, None] == target[None, :]).astype(
        jnp.float32
    )
    outgoing = jnp.dot(
        routing, boundary_strips, precision=top_wavenumber_kept, preferred_element_type=jnp.float32
    ).reshape(lon_count, CAP, fields * levels * STRIP)
    arrived = lax.all_to_all(outgoing, "lon", split_axis=0, concat_axis=0, tiled=True)
    total = lon_count * CAP
    group = math.gcd(total, 16)
    pieces = arrived.reshape(total // group, group, fields * levels, STRIP)
    starts = nest_place.reshape(total // group, group)
    point = lax.broadcasted_iota(jnp.int32, (1, 1, NB), 2)
    row_step = lax.broadcasted_iota(jnp.int32, (1, STRIP, 1), 1) * RATIO

    def accumulate(carry, item):
        piece, begin = item
        offset = point - begin[:, None, None]
        hat = jnp.maximum(RATIO - jnp.abs(offset - row_step), 0)
        hat = (
            jnp.where((offset >= 0) & (offset < STRIP * RATIO), hat, 0).astype(jnp.float32) / RATIO
        )
        return (carry + jnp.einsum("gat,gtp->ap", piece, hat, precision=top_wavenumber_kept), None)

    boundary = lax.scan(
        accumulate, jnp.zeros((fields * levels, NB), jnp.float32), (pieces, starts)
    )[0]
    return (advanced_state, boundary.reshape(1, fields, levels, NB))


def local(model_state, *others):
    columns = model_state.shape[2]
    fits = lax.axis_size("lon") * STRIP == POLAR and model_state.shape[3] == 2 * POLAR
    if fits and columns % STEP == 0 and columns >= 2 * HELD:
        return compressed(model_state, *others)
    return transposed(model_state, *others)


def solution(mesh):
    return jax.shard_map(
        local,
        mesh=mesh,
        in_specs=(
            P(None, None, "lon", "lat"),
            P(None, "lat"),
            P(),
            P(),
            P(("lat", "lon"), None),
            P(("lat", "lon"), None, None),
        ),
        out_specs=(P(None, None, "lon", "lat"), P(("lat", "lon"), None, None, None)),
        check_vma=False,
    )
```

```python
import functools
import math

import jax
import jax.numpy as jnp
import numpy as np
from jax import lax
from jax.experimental import pallas as pl
from jax.experimental.pallas import tpu as pltpu
from jax.sharding import PartitionSpec as P

POLAR = 128
CAP = 2
STRIP = 16
RATIO = 11
NB = 2048
KC = 896
RANKS = (14, 5, 4, 4)
SPLIT_RANK = 14
STEP = 16
HELD = 80
NEAR_LISTS = (6, 6, 8)
QUICK = (0, 2)
LATE = (3, 4)
SOUTH = 64
VMEM_LIMIT = 48 * 1024 * 1024
F32 = jnp.float32
BF16 = jnp.bfloat16


def ceil8(value):
    return -(-value // 8) * 8


def shift_ranks(count):
    shifts = []
    for step in range(1, count // 2 + 1):
        for shift in (step, -step):
            if shift != -count // 2:
                shifts.append((shift, RANKS[min(step, len(RANKS)) - 1]))
    return shifts


def is_second(place, step, count):
    return lax.rem(lax.div(place, math.gcd(step, count)), 2) == 1


def swaps(pairs):
    return [pair for a, b in pairs for pair in ((a, b), (b, a))]


def ring_swaps(step, count):
    if 2 * step == count:
        return [swaps([(i, i + step) for i in range(step)])]
    groups = [[], []]
    for i in range(count):
        groups[i // math.gcd(step, count) % 2].append((i, (i + step) % count))
    return [swaps(group) for group in groups]


def split_table(table):
    high = table.astype(jnp.bfloat16)
    low = (table - high.astype(np.float64)).astype(jnp.bfloat16)
    return high, low


def factored(block, rank):
    left, values, right = np.linalg.svd(block)
    root = np.sqrt(values[:rank])
    return right[:rank] * root[:, None], left[:, :rank] * root[None, :]


@functools.lru_cache(maxsize=None)
def filter_tables(count, width):
    total = count * width
    half = width // 2

    def block(size, shift):
        place = np.arange(size)
        angle = np.pi * (shift + place[:, None] - place[None, :]) / total
        with np.errstate(divide="ignore"):
            return np.where(angle == 0, 0.0, 1.0 / (np.sin(angle) * total))

    senders, receivers = [], []
    for shift, rank in shift_ranks(count):
        sender, receiver = factored(block(width, shift * width), rank)
        senders.append(np.pad(sender, ((0, ceil8(rank) - rank), (0, 0))))
        receivers.append(receiver)
    nears = []
    for part, shift in enumerate((half, -half)):
        sender, receiver = factored(block(half, shift), SPLIT_RANK)
        rows = np.concatenate([block(half, 0), sender], axis=0)
        nears.append(np.pad(rows, ((0, 16 - SPLIT_RANK), (0, 0))))
        beyond = ((half, 0), (0, 0)) if part == 0 else ((0, half), (0, 0))
        receivers.append(np.pad(receiver, beyond))
    receivers = np.concatenate(receivers, axis=1)
    receivers = np.pad(receivers, ((0, 0), (0, HELD - receivers.shape[1])))
    nears = [table for rows in nears for table in split_table(rows)]
    send_high, send_low = split_table(np.concatenate(senders, axis=0))
    far_high, far_low = split_table(receivers)
    return (
        np.concatenate(nears, axis=0),
        np.concatenate([send_high, send_low], axis=0),
        np.concatenate([far_high, far_high, far_low], axis=1),
    )


def hat_table():
    width = -(-STRIP * RATIO // POLAR) * POLAR
    point = np.arange(width)
    table = np.zeros((POLAR, CAP * width), np.float32)
    for rank in range(CAP):
        for row in range(STRIP):
            hat = np.maximum(RATIO - np.abs(point - row * RATIO), 0) * (point < STRIP * RATIO)
            table[rank * STRIP + row, rank * width : (rank + 1) * width] = hat
    return table.astype(jnp.bfloat16)


def split_value(value):
    high = value.astype(BF16)
    return high, (value - high.astype(F32)).astype(BF16)


def modulated(row, cosine, sine):
    return jnp.concatenate([row * cosine[...], row * sine[...]], axis=1)


def stacked(value):
    high, low = split_value(value)
    return jnp.concatenate([high, low, high], axis=0)


def strip_rows(slots):
    return slots // 2


def payload_rows(rank, slots):
    return ceil8(slots * rank + strip_rows(slots))


def edge_kernel(
    meta, state, lon_pair, lon_cross, lat_pair, lat_cross, held, edges, in_sems
):
    fields, levels, columns, rows = state.shape
    copies = [
        pltpu.make_async_copy(state.at[f], held.at[f], in_sems.at[f]) for f in range(fields)
    ]
    for copy in copies:
        copy.start()
    lane = lax.broadcasted_iota(jnp.int32, (columns, POLAR), 1)
    lon_odd = lax.rem(meta[2], 2) == 1
    lat_odd = lax.rem(meta[3], 2) == 1
    edges[...] = jnp.zeros(edges.shape, F32)

    for f, copy in enumerate(copies):
        copy.wait()
        for l in range(levels):
            item = l * fields + f
            first = held[f, l, 0:1, :]
            last = held[f, l, columns - 1 : columns, :]
            lon_pair[item : item + 1, :] = jnp.where(lon_odd, first, last)
            lon_cross[item : item + 1, :] = jnp.where(lon_odd, last, first)
            north = held[f, l, :, 0:POLAR]
            north = pltpu.roll(north, item, 1) if item else north
            south = pltpu.roll(held[f, l, :, rows - POLAR :], item + SOUTH + 1, 1)
            value = jnp.where(lane == item, north, edges[...])
            edges[...] = jnp.where(lane == SOUTH + item, south, value)
    turned = edges[...].T
    size = lat_pair.shape[0]
    north, south = turned[0:size], turned[SOUTH : SOUTH + size]
    lat_pair[...] = jnp.where(lat_odd, north, south)
    lat_cross[...] = jnp.where(lat_odd, south, north)


def stencil_kernel(
    count,
    meta,
    coupling,
    strips,
    lon_pair,
    lon_cross,
    lat_pair,
    lat_cross,
    diffusion,
    angle_cos,
    angle_sin,
    send,
    state,
    updated,
    cosine,
    sine,
    own,
    *rest,
):
    ranks = shift_ranks(count)
    payloads = rest[: len(ranks)]
    held, made, halos, halo, factors, placed, rows_cut, in_sems, out_sems = rest[len(ranks) :]
    fields, levels, columns, rows = state.shape
    tiles = rows // POLAR
    spans = [slice(tile * POLAR, (tile + 1) * POLAR) for tile in range(tiles)]

    def copy_in(l, f):
        return pltpu.make_async_copy(
            state.at[f, l], held.at[l, f, pl.ds(8, columns)], in_sems.at[l, f]
        )

    def copy_out(l, f):
        return pltpu.make_async_copy(made.at[l, f], updated.at[f, l], out_sems.at[l, f])

    for l in range(levels):
        for f in range(fields):
            copy_in(l, f).start()

    steps = columns // STEP
    fine_cos, fine_sin = angle_cos[steps:, :], angle_sin[steps:, :]
    for step in range(steps):
        span = slice(step * STEP, (step + 1) * STEP)
        coarse_cos, coarse_sin = angle_cos[step : step + 1, :], angle_sin[step : step + 1, :]
        cosine[span, :] = coarse_cos * fine_cos - coarse_sin * fine_sin
        sine[span, :] = coarse_sin * fine_cos + coarse_cos * fine_sin

    lane = lax.broadcasted_iota(jnp.int32, (STEP, POLAR), 1)
    lowest, highest = lane == 0, lane == POLAR - 1
    along = [jnp.broadcast_to(diffusion[0:1, span], (STEP, POLAR)) for span in spans]
    across = [jnp.broadcast_to(diffusion[1:2, span], (STEP, POLAR)) for span in spans]
    centre = [1.0 - 2.0 * along[t] - 2.0 * across[t] for t in range(tiles)]
    lon_odd = lax.rem(meta[2], 2) == 1
    lat_odd = lax.rem(meta[3], 2) == 1
    half = send.shape[0] // 2
    start = pl.multiple_of(meta[0] * POLAR, POLAR)
    size = lat_pair.shape[0]
    blank = jnp.zeros((SOUTH - size, columns), F32)
    north_halo = jnp.where(lat_odd, lat_pair[...], lat_cross[...])
    south_halo = jnp.where(lat_odd, lat_cross[...], lat_pair[...])
    halos[...] = jnp.concatenate([north_halo, blank, south_halo, blank], axis=0).T

    def one_level(l, carry):
        for f in range(fields):
            copy_in(l, f).wait()
        weights = [
            [coupling[l, f * fields + g] for g in range(fields)] for f in range(fields)
        ]
        halo[...] = pltpu.roll(halos[...], lax.rem(POLAR - l * fields, POLAR), 1)
        for f in range(fields):
            item = pl.ds(l * fields + f, 1)
            pair, cross = lon_pair[item, :], lon_cross[item, :]
            held[l, f, 7:8, :] = jnp.where(lon_odd, pair, cross)
            held[l, f, columns + 8 : columns + 9, :] = jnp.where(lon_odd, cross, pair)
        for begin in range(0, columns, STEP):
            end = begin + STEP
            shifted = lambda f, t, by: held[l, f, begin + 8 + by : end + 8 + by, spans[t]]
            here = [[shifted(f, t, 0) for t in range(tiles)] for f in range(fields)]
            edges = halo[begin:end, :]
            for f in range(fields):
                down = [pltpu.roll(here[f][t], 1, 1) for t in range(tiles)]
                up = [pltpu.roll(here[f][t], POLAR - 1, 1) for t in range(tiles)]
                north_edge = [pltpu.roll(edges, POLAR - f, 1) if f else edges] + down[:-1]
                south_edge = up[1:] + [pltpu.roll(edges, POLAR - 1 - SOUTH - f, 1)]
                for t in range(tiles):
                    north = jnp.where(lowest, north_edge[t], down[t])
                    south = jnp.where(highest, south_edge[t], up[t])
                    result = (centre[t] + weights[f][f]) * here[f][t]
                    result = result + along[t] * (shifted(f, t, 1) + shifted(f, t, -1))
                    result = result + across[t] * (north + south)
                    for g in range(fields):
                        if g != f:
                            result = result + weights[f][g] * here[g][t]
                    made[l, f, begin:end, spans[t]] = result
        for f in range(fields):
            copy_out(l, f).start()
        for f in range(fields):
            row = made[l, f, :, pl.ds(start, POLAR)]
            high, low = split_value(modulated(row, cosine, sine))
            both = jnp.dot(send[...], high, preferred_element_type=F32)
            cross = jnp.dot(send[0:half, :], low, preferred_element_type=F32)
            factors[l * fields + f] = both[:half] + both[half:] + cross
        return carry

    lax.fori_loop(0, levels, one_level, 0)

    lon_index = meta[2]
    slots = strips.shape[0]
    lists = fields * levels
    each = strip_rows(lists)
    placed[...] = jnp.zeros(placed.shape, F32)
    rows_cut[...] = jnp.zeros(rows_cut.shape, F32)
    strip_lane = lax.broadcasted_iota(jnp.int32, (16, rows), 1)

    def one_slot(s):
        owner, column = strips[s, 0], strips[s, 1]
        offset, length = strips[s, 2], strips[s, 3]
        rank = jnp.int32(0)
        for other in range(s):
            rank = rank + (strips[other, 0] == owner).astype(jnp.int32)
        for l in range(levels):
            for f in range(fields):
                side, place = divmod(l * fields + f, each)
                rows_cut[s, side, place : place + 1, :] = made[l, f, pl.ds(column, 1), :]
        base = rank * STRIP
        shift = lax.rem(owner - lon_index + count, count)
        for side in range(2):
            where = side * POLAR + base
            moved = pltpu.roll(rows_cut[s, side], lax.rem(where - offset + rows, rows), 1)
            inside = (strip_lane >= where) & (strip_lane < where + length)
            placed[shift] = placed[shift] + jnp.where(inside, moved, 0.0)

    for s in range(slots):
        one_slot(s)
    own[...] = placed[0]

    place = 0
    index = 0
    while index < len(ranks):
        step, rank = ranks[index]
        padded = ceil8(rank)
        paired = 2 if 2 * step < count else 1
        second = is_second(lon_index, step, count)
        targets = payloads[index : index + paired]
        for item in range(lists):
            span = slice(item * rank, (item + 1) * rank)
            plus = factors[item, place : place + rank, :]
            if paired == 1:
                targets[0][span, :] = plus
            else:
                minus = factors[item, place + padded : place + padded + rank, :]
                targets[0][span, :] = jnp.where(second, minus, plus)
                targets[1][span, :] = jnp.where(second, plus, minus)
        plus, minus = placed[step][0:each, :], placed[count - step][0:each, :]
        targets[0][lists * rank : lists * rank + each, :] = jnp.where(second, minus, plus)
        if paired == 2:
            targets[1][lists * rank : lists * rank + each, :] = jnp.where(second, plus, minus)
        for target in targets:
            unused = target.shape[0] - lists * rank - each
            if unused:
                target[lists * rank + each :, :] = jnp.zeros((unused, rows), F32)
        place += paired * padded
        index += paired
    for l in range(levels):
        for f in range(fields):
            copy_out(l, f).wait()


def near_kernel(begin, passed, meta, cosine, sine, middle, near, rows, *rest):
    filtered, moments = rest[passed], rest[passed + 1]
    held, sems = rest[2 * passed + 2 :]
    fields = rows.shape[0]
    lists, columns, _ = filtered.shape
    half = columns // 2
    each = near.shape[0] // 4
    mine = pl.ds(pl.multiple_of(meta[0] * POLAR, POLAR), POLAR)

    def copy_in(item):
        l, f = (begin + item) // fields, (begin + item) % fields
        return pltpu.make_async_copy(rows.at[f, l, :, mine], held.at[item], sems.at[item])

    @pl.when(meta[1] == 1)
    def _():
        for item in range(lists):
            copy_in(item).start()

        def one(item, carry):
            copy_in(item).wait()
            for part in range(2):
                span = slice(part * half, (part + 1) * half)
                row = held[item, span, :]
                turn_cos, turn_sin = cosine[span, :], sine[span, :]
                value = jnp.concatenate([row * turn_cos, row * turn_sin], axis=1)
                table = near[2 * part * each : 2 * (part + 1) * each, :]
                high, low = split_value(value)
                both = jnp.dot(table, high, preferred_element_type=F32)
                cross = jnp.dot(table[:each], low, preferred_element_type=F32)
                total = both[:each] + both[each:] + cross
                filtered[item, span, :] = (
                    turn_sin * total[:half, :POLAR]
                    - turn_cos * total[:half, POLAR:]
                    + middle[0:1, :] * row
                )
                moments[item, part * 16 : (part + 1) * 16, :] = total[half:, :]
            return carry

        lax.fori_loop(0, lists, one, 0, unroll=2)


def far_kernel(count, meta, begins, cosine, sine, turn, far, hats, own, *rest):
    ranks = shift_ranks(count)
    payloads = rest[: len(ranks)]
    after = len(ranks) + 2 * len(NEAR_LISTS)
    near_parts = [rest[at : at + 2] for at in range(len(ranks), after, 2)]
    _, out, boundary, filtered, arrived, sums, sems = rest[after:]
    fields, levels = out.shape[0:2]
    lists = fields * levels
    each = strip_rows(lists)
    lon_index = meta[2]
    mine = pl.ds(pl.multiple_of(meta[0] * POLAR, POLAR), POLAR)

    def copy_out(item):
        l, f = item // fields, item % fields
        return pltpu.make_async_copy(filtered.at[item], out.at[f, l, :, mine], sems.at[item])

    def received(index, span):
        step = abs(ranks[index][0])
        if 2 * step == count:
            return payloads[index][span, :]
        base = index - index % 2
        first, last = payloads[base][span, :], payloads[base + 1][span, :]
        takes_first = is_second(lon_index, step, count)
        if index != base:
            takes_first = jnp.logical_not(takes_first)
        return jnp.where(takes_first, first, last)

    @pl.when(meta[1] == 1)
    def _():
        place = 0
        for index, (_, rank) in enumerate(ranks):
            turn_cos = turn[index : index + 1, :POLAR]
            turn_sin = turn[index : index + 1, POLAR:]
            for item in range(lists):
                value = received(index, slice(item * rank, (item + 1) * rank))
                cosines, sines = value[:, :POLAR], value[:, POLAR:]
                arrived[item, place : place + rank, :POLAR] = (
                    turn_cos * cosines + turn_sin * sines
                )
                arrived[item, place : place + rank, POLAR:] = (
                    turn_cos * sines - turn_sin * cosines
                )
            place += rank
        begin = 0
        for near, moments in near_parts:
            for item in range(near.shape[0]):
                for part in range(2):
                    at = place + part * SPLIT_RANK
                    arrived[begin + item, at : at + SPLIT_RANK, :] = moments[
                        item, part * 16 : part * 16 + SPLIT_RANK, :
                    ]
            begin += near.shape[0]
        place += 2 * SPLIT_RANK
        for item in range(lists):
            arrived[item, place:, :] = jnp.zeros((HELD - place, 2 * POLAR), F32)

        begin = 0
        for near, _ in near_parts:

            def one(item, carry, near=near, begin=begin):
                at = begin + item
                total = jnp.dot(far[...], stacked(arrived[at]), preferred_element_type=F32)
                filtered[at] = (
                    near[item] + sine[...] * total[:, :POLAR] - cosine[...] * total[:, POLAR:]
                )
                copy_out(at).start()
                return carry

            lax.fori_loop(0, near.shape[0], one, 0, unroll=2)
            begin += near.shape[0]

    sums[...] = jnp.zeros(sums.shape, F32)
    pieces, sources = [], []
    blank = jnp.zeros((16 - each, POLAR), F32)
    for index in range(-1, len(ranks)):
        if index < 0:
            shift, arrival = 0, own[0:each, :]
        else:
            shift, rank = ranks[index]
            arrival = received(index, slice(lists * rank, lists * rank + each))
        sources.append(lax.rem(lon_index - shift + count, count))
        pieces += [arrival[:, :POLAR], blank, arrival[:, POLAR:], blank]
    pieces = jnp.concatenate(pieces, axis=0)
    high = pieces.astype(BF16)
    middle, low = split_value(pieces - high.astype(F32))
    points = jnp.dot(high, hats[...], preferred_element_type=F32)
    points = points + jnp.dot(middle, hats[...], preferred_element_type=F32)
    points = points + jnp.dot(low, hats[...], preferred_element_type=F32)
    width = hats.shape[1] // CAP
    beyond = jnp.zeros((32, POLAR), F32)
    for index, source in enumerate(sources):
        for rank in range(CAP):
            place = begins[source, rank]
            offset = lax.rem(place, POLAR)
            span = points[index * 32 : (index + 1) * 32, rank * width : (rank + 1) * width]
            moved = pltpu.roll(jnp.concatenate([span, beyond], axis=1), offset, 1)
            at = pl.ds(pl.multiple_of(place - offset, POLAR), width + POLAR)
            sums[:, at] = sums[:, at] + moved
    for l in range(levels):
        for f in range(fields):
            side, row = divmod(l * fields + f, each)
            row = side * 16 + row
            boundary[0, f, l : l + 1, :] = sums[row : row + 1, 0:NB] * (1.0 / RATIO)

    @pl.when(meta[1] == 1)
    def _():
        for item in range(lists):
            copy_out(item).wait()


def phase_table(kept, steps, period):
    phase = (2 * kept - 1)[None, :] * steps[:, None] % (2 * period)
    angle = phase.astype(F32) * (math.pi / period)
    return jnp.cos(angle), jnp.sin(angle)


def cost(flops, bytes_accessed):
    return pl.CostEstimate(flops=flops, bytes_accessed=bytes_accessed, transcendentals=0)


def compressed(model_state, diffusion, coupling, cutoff, strip_list, nest_place):
    lat_index = lax.axis_index("lat")
    lon_index = lax.axis_index("lon")
    lat_count = lax.axis_size("lat")
    lon_count = lax.axis_size("lon")
    fields, levels, columns, rows = model_state.shape
    lists = fields * levels
    total_columns = columns * lon_count
    ranks = shift_ranks(lon_count)
    near, send, far = [jnp.asarray(table) for table in filter_tables(lon_count, columns)]
    params = pltpu.CompilerParams(vmem_limit_bytes=VMEM_LIMIT)
    shape = lambda *sizes: jax.ShapeDtypeStruct(sizes, F32)
    whole_state = shape(*model_state.shape)

    is_south = lat_index == lat_count - 1
    is_polar = (lat_index == 0) | is_south
    part = jnp.where(is_south, rows // POLAR - 1, 0)
    meta = jnp.stack([part, is_polar.astype(jnp.int32), lon_index, lat_index]).astype(jnp.int32)
    kept = jnp.where(lat_index < lat_count // 2, cutoff[:POLAR], cutoff[POLAR:])
    places = np.concatenate([np.arange(0, columns, STEP), np.arange(STEP)]).astype(np.int32)
    angles = phase_table(kept, jnp.asarray(places), total_columns)
    steps = jnp.array([abs(shift) for shift, _ in ranks], jnp.int32)
    sign = np.array([[1.0 if shift > 0 else -1.0] for shift, _ in ranks], np.float32)
    turn_cos, turn_sin = phase_table(kept, steps, lon_count)
    turn = jnp.concatenate([turn_cos, turn_sin * sign], axis=1)
    turn = jnp.pad(turn, ((0, ceil8(len(ranks)) - len(ranks)), (0, 0)))
    middle = ((2 * kept - 1).astype(F32) / total_columns)[None, :]
    hats = jnp.asarray(hat_table())

    smem = pl.BlockSpec(memory_space=pltpu.SMEM)
    vmem = pl.BlockSpec(memory_space=pltpu.VMEM)
    hbm = pl.BlockSpec(memory_space=pl.ANY)
    level_sems = pltpu.SemaphoreType.DMA((levels, fields))

    with jax.named_scope("edges"):
        edges = pl.pallas_call(
            edge_kernel,
            in_specs=[smem, hbm],
            out_specs=[vmem] * 4,
            out_shape=[shape(ceil8(lists), rows)] * 2 + [shape(ceil8(lists), columns)] * 2,
            scratch_shapes=[
                pltpu.VMEM((fields, levels, columns, rows), F32),
                pltpu.VMEM((columns, POLAR), F32),
                pltpu.SemaphoreType.DMA((fields,)),
            ],
            compiler_params=params,
        )(meta, model_state)

    with jax.named_scope("halo"):
        lon_pairs, lon_crosses = ring_swaps(1, lon_count)
        lat_pairs = [(i, i + 1) for i in range(0, lat_count, 2)]
        lat_crosses = [(i, i + 1) for i in range(1, lat_count - 1, 2)]
        halos = [
            lax.ppermute(edges[0], "lon", lon_pairs),
            lax.ppermute(edges[1], "lon", lon_crosses),
            lax.ppermute(edges[2], "lat", swaps(lat_pairs)),
            lax.ppermute(edges[3], "lat", swaps(lat_crosses)),
        ]

    sizes = [payload_rows(rank, lists) for _, rank in ranks]
    with jax.named_scope("stencil"):
        updated, cosine, sine, own, *outgoing = pl.pallas_call(
            functools.partial(stencil_kernel, lon_count),
            in_specs=[smem] * 3 + [vmem] * 8 + [hbm],
            out_specs=[hbm] + [vmem] * (3 + len(ranks)),
            out_shape=[whole_state]
            + [shape(columns, POLAR)] * 2
            + [shape(16, rows)]
            + [shape(size, rows) for size in sizes],
            scratch_shapes=[
                pltpu.VMEM((levels, fields, columns + 16, rows), F32),
                pltpu.VMEM((levels, fields, columns, rows), F32),
                pltpu.VMEM((columns, POLAR), F32),
                pltpu.VMEM((columns, POLAR), F32),
                pltpu.VMEM((lists, send.shape[0] // 2, rows), F32),
                pltpu.VMEM((lon_count, 16, rows), F32),
                pltpu.VMEM((strip_list.shape[0], 2, 16, rows), F32),
                level_sems,
                level_sems,
            ],
            compiler_params=params,
        )(
            meta,
            coupling.reshape(levels, fields * fields),
            strip_list,
            *halos,
            diffusion,
            *angles,
            send,
            model_state,
        )

    def exchange(index, payload):
        step = abs(ranks[index][0])
        swap = index % 2 if 2 * step < lon_count else 0
        return lax.ppermute(payload, "lon", ring_swaps(step, lon_count)[swap])

    with jax.named_scope("exchange"):
        incoming = {
            index: exchange(index, outgoing[index])
            for index in range(len(ranks))
            if index not in LATE
        }

    def near_part(begin, end, passed):
        results = pl.pallas_call(
            functools.partial(near_kernel, begin, len(passed)),
            in_specs=[smem] + [vmem] * 4 + [hbm] * (1 + len(passed)),
            out_specs=[vmem] * 2 + [hbm] * len(passed),
            out_shape=[shape(end - begin, columns, POLAR), shape(end - begin, 32, rows)]
            + [shape(*payload.shape) for payload in passed],
            input_output_aliases={6 + index: 2 + index for index in range(len(passed))},
            scratch_shapes=[
                pltpu.VMEM((end - begin, columns, POLAR), F32),
                pltpu.SemaphoreType.DMA((end - begin,)),
            ],
            compiler_params=params,
            cost_estimate=cost(
                12 * (end - begin) * columns * columns * POLAR, 8 * (end - begin) * columns * POLAR
            ),
        )(meta, cosine, sine, middle, near, updated, *passed)
        return results[:2], results[2:]

    near_parts = []
    begin = 0
    for index, count in enumerate(NEAR_LISTS):
        late, quick = LATE[index : index + 1], QUICK[index - 1 : index] if index else ()
        with jax.named_scope("near"):
            results, passed = near_part(
                begin,
                begin + count,
                [outgoing[swap] for swap in late] + [incoming[swap] for swap in quick],
            )
        near_parts += results
        begin += count
        with jax.named_scope("late_exchange"):
            for swap, payload in zip(late, passed):
                incoming[swap] = exchange(swap, payload)
        incoming.update(zip(quick, passed[len(late) :]))

    with jax.named_scope("far"):
        advanced, boundary = pl.pallas_call(
            functools.partial(far_kernel, lon_count),
            in_specs=[smem] * 2 + [vmem] * (6 + len(ranks) + len(near_parts)) + [hbm],
            out_specs=[hbm, vmem],
            out_shape=[whole_state, shape(1, fields, levels, NB)],
            input_output_aliases={8 + len(ranks) + len(near_parts): 0},
            scratch_shapes=[
                pltpu.VMEM((lists, columns, POLAR), F32),
                pltpu.VMEM((lists, HELD, rows), F32),
                pltpu.VMEM((32, NB + 2 * POLAR), F32),
                pltpu.SemaphoreType.DMA((lists,)),
            ],
            compiler_params=pltpu.CompilerParams(vmem_limit_bytes=VMEM_LIMIT // 2),
        )(
            meta,
            nest_place.reshape(lon_count, CAP),
            cosine,
            sine,
            turn,
            far,
            hats,
            own,
            *[incoming[index] for index in range(len(ranks))],
            *near_parts,
            updated,
        )
    return advanced, boundary


def padded_2(block, sides, width):
    for axis, dim in sides:
        count = lax.axis_size(axis)
        forward = [(i, i + 1) for i in range(count - 1)]
        forward.append((count - 1, 0))
        backward = [(target, source) for source, target in forward]
        low = lax.ppermute(
            lax.slice_in_dim(block, block.shape[dim] - width, None, axis=dim), axis, forward
        )
        high = lax.ppermute(lax.slice_in_dim(block, 0, width, axis=dim), axis, backward)
        block = jnp.concatenate([low, block, high], axis=dim)
    return block


def spectral_filter(rows, kept):
    top_wavenumber_kept = lax.Precision.HIGHEST
    length = rows.shape[3]
    width = math.gcd(KC, 128)
    column_grid = lax.broadcasted_iota(jnp.int32, (length, width), 0)
    step_output = jnp.zeros_like(rows)
    for block_index in range(KC // width):
        wavenumber = block_index * width + lax.broadcasted_iota(jnp.int32, (length, width), 1)
        phase = column_grid * wavenumber % length
        angle = phase.astype(jnp.float32) * (2.0 * math.pi / length)
        cosine = jnp.cos(angle)
        sine = jnp.sin(angle)
        along = block_index * width + jnp.arange(width, dtype=jnp.int32)
        scale = jnp.where(along == 0, 1.0 / length, 2.0 / length)
        weight = jnp.where(along[None, :] < kept[:, None], scale[None, :], 0.0)
        real_part = (
            jnp.einsum("flrn,nk->flrk", rows, cosine, precision=top_wavenumber_kept) * weight
        )
        imaginary_component = (
            jnp.einsum("flrn,nk->flrk", rows, sine, precision=top_wavenumber_kept) * weight
        )
        step_output = (
            step_output
            + jnp.einsum("flrk,nk->flrn", real_part, cosine, precision=top_wavenumber_kept)
            + jnp.einsum("flrk,nk->flrn", imaginary_component, sine, precision=top_wavenumber_kept)
        )
    return step_output


def polar_pass(work_rows, kept_start, kept_table):
    count = work_rows.shape[2] // lax.axis_size("lon")
    kept = lax.dynamic_slice_in_dim(kept_table, kept_start + lax.axis_index("lon") * count, count)
    return lax.all_to_all(
        spectral_filter(
            lax.all_to_all(work_rows, "lon", split_axis=2, concat_axis=3, tiled=True), kept
        ),
        "lon",
        split_axis=3,
        concat_axis=2,
        tiled=True,
    )


def transposed(model_state, diffusion, coupling, cutoff, strip_list, nest_place):
    top_wavenumber_kept = lax.Precision.HIGHEST
    lat_index = lax.axis_index("lat")
    lat_count = lax.axis_size("lat")
    lon_count = lax.axis_size("lon")
    fields, levels, lon_local, lat_local = model_state.shape
    padded = padded_2(model_state, (("lat", 3), ("lon", 2)), 1)
    east_west = padded[:, :, 2:, 1:-1] + padded[:, :, :-2, 1:-1]
    row_place = lax.broadcasted_iota(jnp.int32, (1, 1, 1, lat_local), 3)
    northern = jnp.where((lat_index == 0) & (row_place == 0), 0.0, padded[:, :, 1:-1, :-2])
    southern = jnp.where(
        (lat_index == lat_count - 1) & (row_place == lat_local - 1), 0.0, padded[:, :, 1:-1, 2:]
    )
    blended = jnp.einsum("lfg,glij->flij", coupling, model_state, precision=top_wavenumber_kept)
    updated = (
        model_state
        + diffusion[0] * (east_west - 2.0 * model_state)
        + diffusion[1] * (northern + southern - 2.0 * model_state)
        + blended
    )
    is_south = lat_index == lat_count - 1
    is_polar = (lat_index == 0) | is_south
    start = jnp.where(is_south, lat_local - POLAR, 0).astype(jnp.int32)
    band_base = jnp.where(lat_index < lat_count // 2, 0, POLAR).astype(jnp.int32)
    block_rows = lax.dynamic_slice_in_dim(updated, start, POLAR, 3)
    polar_rows = jnp.transpose(block_rows, (0, 1, 3, 2))
    filtered = polar_pass(polar_rows, band_base, cutoff)
    new_rows = jnp.where(is_polar, jnp.transpose(filtered, (0, 1, 3, 2)), block_rows)
    advanced_state = lax.dynamic_update_slice_in_dim(updated, new_rows, start, 3)
    slots = strip_list.shape[0]
    owners = strip_list[:, 0]
    columns = strip_list[:, 1]
    offsets = strip_list[:, 2]
    lengths = strip_list[:, 3]
    zero = jnp.zeros((), jnp.int32)

    def cut_strip(column, offset):
        return lax.dynamic_slice(
            updated, (zero, zero, column, offset), (fields, levels, 1, STRIP)
        ).reshape(fields * levels, STRIP)

    boundary_strips = jax.vmap(cut_strip)(columns, offsets)
    inside = lax.broadcasted_iota(jnp.int32, (1, 1, STRIP), 2) < lengths[:, None, None]
    boundary_strips = jnp.where(inside, boundary_strips, 0.0).reshape(
        slots, fields * levels * STRIP
    )
    slot_ids = jnp.arange(slots, dtype=jnp.int32)
    earlier = slot_ids[None, :] < slot_ids[:, None]
    same = owners[:, None] == owners[None, :]
    rank = jnp.sum((same & earlier).astype(jnp.int32), axis=1)
    target = owners * CAP + rank
    routing = (jnp.arange(lon_count * CAP, dtype=jnp.int32)[:, None] == target[None, :]).astype(
        jnp.float32
    )
    outgoing = jnp.dot(
        routing, boundary_strips, precision=top_wavenumber_kept, preferred_element_type=jnp.float32
    ).reshape(lon_count, CAP, fields * levels * STRIP)
    arrived = lax.all_to_all(outgoing, "lon", split_axis=0, concat_axis=0, tiled=True)
    total = lon_count * CAP
    group = math.gcd(total, 16)
    pieces = arrived.reshape(total // group, group, fields * levels, STRIP)
    starts = nest_place.reshape(total // group, group)
    point = lax.broadcasted_iota(jnp.int32, (1, 1, NB), 2)
    row_step = lax.broadcasted_iota(jnp.int32, (1, STRIP, 1), 1) * RATIO

    def accumulate(carry, item):
        piece, begin = item
        offset = point - begin[:, None, None]
        hat = jnp.maximum(RATIO - jnp.abs(offset - row_step), 0)
        hat = (
            jnp.where((offset >= 0) & (offset < STRIP * RATIO), hat, 0).astype(jnp.float32) / RATIO
        )
        return (carry + jnp.einsum("gat,gtp->ap", piece, hat, precision=top_wavenumber_kept), None)

    boundary = lax.scan(
        accumulate, jnp.zeros((fields * levels, NB), jnp.float32), (pieces, starts)
    )[0]
    return (advanced_state, boundary.reshape(1, fields, levels, NB))


def local(model_state, *others):
    columns = model_state.shape[2]
    fits = lax.axis_size("lon") * STRIP == POLAR and model_state.shape[3] == 2 * POLAR
    if fits and columns % STEP == 0 and columns >= 2 * HELD:
        return compressed(model_state, *others)
    return transposed(model_state, *others)


def solution(mesh):
    return jax.shard_map(
        local,
        mesh=mesh,
        in_specs=(
            P(None, None, "lon", "lat"),
            P(None, "lat"),
            P(),
            P(),
            P(("lat", "lon"), None),
            P(("lat", "lon"), None, None),
        ),
        out_specs=(P(None, None, "lon", "lat"), P(("lat", "lon"), None, None, None)),
        check_vma=False,
    )
```

```python
import functools
import math

import jax
import jax.numpy as jnp
import numpy as np
from jax import lax
from jax.experimental import pallas as pl
from jax.experimental.pallas import tpu as pltpu
from jax.sharding import PartitionSpec as P

POLAR = 128
CAP = 2
STRIP = 16
RATIO = 11
NB = 2048
KC = 896
RANKS = (14, 5, 4, 4)
SPLIT_RANK = 14
STEP = 16
HELD = 80
NEAR_LISTS = (6, 6, 8)
QUICK = (0, 2)
LATE = (3, 4)
SOUTH = 64
VMEM_LIMIT = 48 * 1024 * 1024
F32 = jnp.float32
BF16 = jnp.bfloat16


def ceil8(value):
    return -(-value // 8) * 8


def shift_ranks(count):
    shifts = []
    for step in range(1, count // 2 + 1):
        for shift in (step, -step):
            if shift != -count // 2:
                shifts.append((shift, RANKS[min(step, len(RANKS)) - 1]))
    return shifts


def is_second(place, step, count):
    return lax.rem(lax.div(place, math.gcd(step, count)), 2) == 1


def swaps(pairs):
    return [pair for a, b in pairs for pair in ((a, b), (b, a))]


def ring_swaps(step, count):
    if 2 * step == count:
        return [swaps([(i, i + step) for i in range(step)])]
    groups = [[], []]
    for i in range(count):
        groups[i // math.gcd(step, count) % 2].append((i, (i + step) % count))
    return [swaps(group) for group in groups]


def split_table(table):
    high = table.astype(jnp.bfloat16)
    low = (table - high.astype(np.float64)).astype(jnp.bfloat16)
    return high, low


def factored(block, rank):
    left, values, right = np.linalg.svd(block)
    root = np.sqrt(values[:rank])
    return right[:rank] * root[:, None], left[:, :rank] * root[None, :]


@functools.lru_cache(maxsize=None)
def filter_tables(count, width):
    total = count * width
    half = width // 2

    def block(size, shift):
        place = np.arange(size)
        angle = np.pi * (shift + place[:, None] - place[None, :]) / total
        with np.errstate(divide="ignore"):
            return np.where(angle == 0, 0.0, 1.0 / (np.sin(angle) * total))

    senders, receivers = [], []
    for shift, rank in shift_ranks(count):
        sender, receiver = factored(block(width, shift * width), rank)
        senders.append(np.pad(sender, ((0, ceil8(rank) - rank), (0, 0))))
        receivers.append(receiver)
    nears = []
    for part, shift in enumerate((half, -half)):
        sender, receiver = factored(block(half, shift), SPLIT_RANK)
        rows = np.concatenate([block(half, 0), sender], axis=0)
        nears.append(np.pad(rows, ((0, 16 - SPLIT_RANK), (0, 0))))
        beyond = ((half, 0), (0, 0)) if part == 0 else ((0, half), (0, 0))
        receivers.append(np.pad(receiver, beyond))
    receivers = np.concatenate(receivers, axis=1)
    receivers = np.pad(receivers, ((0, 0), (0, HELD - receivers.shape[1])))
    nears = [table for rows in nears for table in split_table(rows)]
    send_high, send_low = split_table(np.concatenate(senders, axis=0))
    far_high, far_low = split_table(receivers)
    return (
        np.concatenate(nears, axis=0),
        np.concatenate([send_high, send_low], axis=0),
        np.concatenate([far_high, far_high, far_low], axis=1),
    )


def hat_table():
    width = -(-STRIP * RATIO // POLAR) * POLAR
    point = np.arange(width)
    table = np.zeros((POLAR, CAP * width), np.float32)
    for rank in range(CAP):
        for row in range(STRIP):
            hat = np.maximum(RATIO - np.abs(point - row * RATIO), 0) * (point < STRIP * RATIO)
            table[rank * STRIP + row, rank * width : (rank + 1) * width] = hat
    return table.astype(jnp.bfloat16)


def split_value(value):
    high = value.astype(BF16)
    return high, (value - high.astype(F32)).astype(BF16)


def modulated(row, cosine, sine):
    return jnp.concatenate([row * cosine[...], row * sine[...]], axis=1)


def stacked(value):
    high, low = split_value(value)
    return jnp.concatenate([high, low, high], axis=0)


def strip_rows(slots):
    return slots // 2


def payload_rows(rank, slots):
    return ceil8(slots * rank + strip_rows(slots))


def edge_kernel(
    meta, state, lon_pair, lon_cross, lat_pair, lat_cross, held, edges, in_sems
):
    fields, levels, columns, rows = state.shape
    copies = [
        pltpu.make_async_copy(state.at[f], held.at[f], in_sems.at[f]) for f in range(fields)
    ]
    for copy in copies:
        copy.start()
    lane = lax.broadcasted_iota(jnp.int32, (columns, POLAR), 1)
    lon_odd = lax.rem(meta[2], 2) == 1
    lat_odd = lax.rem(meta[3], 2) == 1
    edges[...] = jnp.zeros(edges.shape, F32)

    for f, copy in enumerate(copies):
        copy.wait()
        for l in range(levels):
            item = l * fields + f
            first = held[f, l, 0:1, :]
            last = held[f, l, columns - 1 : columns, :]
            lon_pair[item : item + 1, :] = jnp.where(lon_odd, first, last)
            lon_cross[item : item + 1, :] = jnp.where(lon_odd, last, first)
            north = held[f, l, :, 0:POLAR]
            north = pltpu.roll(north, item, 1) if item else north
            south = pltpu.roll(held[f, l, :, rows - POLAR :], item + SOUTH + 1, 1)
            value = jnp.where(lane == item, north, edges[...])
            edges[...] = jnp.where(lane == SOUTH + item, south, value)
    turned = edges[...].T
    size = lat_pair.shape[0]
    north, south = turned[0:size], turned[SOUTH : SOUTH + size]
    lat_pair[...] = jnp.where(lat_odd, north, south)
    lat_cross[...] = jnp.where(lat_odd, south, north)


def stencil_kernel(
    count,
    meta,
    coupling,
    strips,
    lon_pair,
    lon_cross,
    lat_pair,
    lat_cross,
    diffusion,
    angle_cos,
    angle_sin,
    send,
    state,
    updated,
    cosine,
    sine,
    own,
    *rest,
):
    ranks = shift_ranks(count)
    payloads = rest[: len(ranks)]
    held, made, halos, halo, factors, placed, rows_cut, in_sems, out_sems = rest[len(ranks) :]
    fields, levels, columns, rows = state.shape
    tiles = rows // POLAR
    spans = [slice(tile * POLAR, (tile + 1) * POLAR) for tile in range(tiles)]

    def copy_in(l):
        return pltpu.make_async_copy(
            state.at[:, l], held.at[l, :, pl.ds(8, columns)], in_sems.at[l]
        )

    def copy_out(l):
        return pltpu.make_async_copy(made.at[l], updated.at[:, l], out_sems.at[l])

    for l in range(levels):
        copy_in(l).start()

    steps = columns // STEP
    fine_cos, fine_sin = angle_cos[steps:, :], angle_sin[steps:, :]
    for step in range(steps):
        span = slice(step * STEP, (step + 1) * STEP)
        coarse_cos, coarse_sin = angle_cos[step : step + 1, :], angle_sin[step : step + 1, :]
        cosine[span, :] = coarse_cos * fine_cos - coarse_sin * fine_sin
        sine[span, :] = coarse_sin * fine_cos + coarse_cos * fine_sin

    lane = lax.broadcasted_iota(jnp.int32, (STEP, POLAR), 1)
    lowest, highest = lane == 0, lane == POLAR - 1
    along = [jnp.broadcast_to(diffusion[0:1, span], (STEP, POLAR)) for span in spans]
    across = [jnp.broadcast_to(diffusion[1:2, span], (STEP, POLAR)) for span in spans]
    centre = [1.0 - 2.0 * along[t] - 2.0 * across[t] for t in range(tiles)]
    lon_odd = lax.rem(meta[2], 2) == 1
    lat_odd = lax.rem(meta[3], 2) == 1
    half = send.shape[0] // 2
    start = pl.multiple_of(meta[0] * POLAR, POLAR)
    size = lat_pair.shape[0]
    blank = jnp.zeros((SOUTH - size, columns), F32)
    north_halo = jnp.where(lat_odd, lat_pair[...], lat_cross[...])
    south_halo = jnp.where(lat_odd, lat_cross[...], lat_pair[...])
    halos[...] = jnp.concatenate([north_halo, blank, south_halo, blank], axis=0).T

    def one_level(l, carry):
        copy_in(l).wait()
        weights = [
            [coupling[l, f * fields + g] for g in range(fields)] for f in range(fields)
        ]
        halo[...] = pltpu.roll(halos[...], lax.rem(POLAR - l * fields, POLAR), 1)
        for f in range(fields):
            item = pl.ds(l * fields + f, 1)
            pair, cross = lon_pair[item, :], lon_cross[item, :]
            held[l, f, 7:8, :] = jnp.where(lon_odd, pair, cross)
            held[l, f, columns + 8 : columns + 9, :] = jnp.where(lon_odd, cross, pair)
        for begin in range(0, columns, STEP):
            end = begin + STEP
            shifted = lambda f, t, by: held[l, f, begin + 8 + by : end + 8 + by, spans[t]]
            here = [[shifted(f, t, 0) for t in range(tiles)] for f in range(fields)]
            edges = halo[begin:end, :]
            for f in range(fields):
                down = [pltpu.roll(here[f][t], 1, 1) for t in range(tiles)]
                up = [pltpu.roll(here[f][t], POLAR - 1, 1) for t in range(tiles)]
                north_edge = [pltpu.roll(edges, POLAR - f, 1) if f else edges] + down[:-1]
                south_edge = up[1:] + [pltpu.roll(edges, POLAR - 1 - SOUTH - f, 1)]
                for t in range(tiles):
                    north = jnp.where(lowest, north_edge[t], down[t])
                    south = jnp.where(highest, south_edge[t], up[t])
                    result = (centre[t] + weights[f][f]) * here[f][t]
                    result = result + along[t] * (shifted(f, t, 1) + shifted(f, t, -1))
                    result = result + across[t] * (north + south)
                    for g in range(fields):
                        if g != f:
                            result = result + weights[f][g] * here[g][t]
                    made[l, f, begin:end, spans[t]] = result
        copy_out(l).start()
        for f in range(fields):
            row = made[l, f, :, pl.ds(start, POLAR)]
            high, low = split_value(modulated(row, cosine, sine))
            both = jnp.dot(send[...], high, preferred_element_type=F32)
            cross = jnp.dot(send[0:half, :], low, preferred_element_type=F32)
            factors[l * fields + f] = both[:half] + both[half:] + cross
        return carry

    lax.fori_loop(0, levels, one_level, 0)

    lon_index = meta[2]
    slots = strips.shape[0]
    lists = fields * levels
    each = strip_rows(lists)
    placed[...] = jnp.zeros(placed.shape, F32)
    rows_cut[...] = jnp.zeros(rows_cut.shape, F32)
    strip_lane = lax.broadcasted_iota(jnp.int32, (16, rows), 1)

    def one_slot(s):
        owner, column = strips[s, 0], strips[s, 1]
        offset, length = strips[s, 2], strips[s, 3]
        rank = jnp.int32(0)
        for other in range(s):
            rank = rank + (strips[other, 0] == owner).astype(jnp.int32)
        for l in range(levels):
            for f in range(fields):
                side, place = divmod(l * fields + f, each)
                rows_cut[s, side, place : place + 1, :] = made[l, f, pl.ds(column, 1), :]
        base = rank * STRIP
        shift = lax.rem(owner - lon_index + count, count)
        for side in range(2):
            where = side * POLAR + base
            moved = pltpu.roll(rows_cut[s, side], lax.rem(where - offset + rows, rows), 1)
            inside = (strip_lane >= where) & (strip_lane < where + length)
            placed[shift] = placed[shift] + jnp.where(inside, moved, 0.0)

    for s in range(slots):
        one_slot(s)
    own[...] = placed[0]

    place = 0
    index = 0
    while index < len(ranks):
        step, rank = ranks[index]
        padded = ceil8(rank)
        paired = 2 if 2 * step < count else 1
        second = is_second(lon_index, step, count)
        targets = payloads[index : index + paired]
        for item in range(lists):
            span = slice(item * rank, (item + 1) * rank)
            plus = factors[item, place : place + rank, :]
            if paired == 1:
                targets[0][span, :] = plus
            else:
                minus = factors[item, place + padded : place + padded + rank, :]
                targets[0][span, :] = jnp.where(second, minus, plus)
                targets[1][span, :] = jnp.where(second, plus, minus)
        plus, minus = placed[step][0:each, :], placed[count - step][0:each, :]
        targets[0][lists * rank : lists * rank + each, :] = jnp.where(second, minus, plus)
        if paired == 2:
            targets[1][lists * rank : lists * rank + each, :] = jnp.where(second, plus, minus)
        for target in targets:
            unused = target.shape[0] - lists * rank - each
            if unused:
                target[lists * rank + each :, :] = jnp.zeros((unused, rows), F32)
        place += paired * padded
        index += paired
    for l in range(levels):
        copy_out(l).wait()


def near_kernel(begin, passed, meta, cosine, sine, middle, near, rows, *rest):
    filtered, moments = rest[passed], rest[passed + 1]
    held, sems = rest[2 * passed + 2 :]
    fields = rows.shape[0]
    lists, columns, _ = filtered.shape
    half = columns // 2
    each = near.shape[0] // 4
    mine = pl.ds(pl.multiple_of(meta[0] * POLAR, POLAR), POLAR)

    def copy_in(item):
        l, f = (begin + item) // fields, (begin + item) % fields
        return pltpu.make_async_copy(rows.at[f, l, :, mine], held.at[item], sems.at[item])

    @pl.when(meta[1] == 1)
    def _():
        for item in range(lists):
            copy_in(item).start()

        for item in range(lists):
            copy_in(item).wait()
            for part in range(2):
                span = slice(part * half, (part + 1) * half)
                row = held[item, span, :]
                turn_cos, turn_sin = cosine[span, :], sine[span, :]
                value = jnp.concatenate([row * turn_cos, row * turn_sin], axis=1)
                table = near[2 * part * each : 2 * (part + 1) * each, :]
                high, low = split_value(value)
                both = jnp.dot(table, high, preferred_element_type=F32)
                cross = jnp.dot(table[:each], low, preferred_element_type=F32)
                total = both[:each] + both[each:] + cross
                filtered[item, span, :] = (
                    turn_sin * total[:half, :POLAR]
                    - turn_cos * total[:half, POLAR:]
                    + middle[0:1, :] * row
                )
                moments[item, part * 16 : (part + 1) * 16, :] = total[half:, :]


def far_kernel(count, meta, begins, cosine, sine, turn, far, hats, own, *rest):
    ranks = shift_ranks(count)
    payloads = rest[: len(ranks)]
    after = len(ranks) + 2 * len(NEAR_LISTS)
    near_parts = [rest[at : at + 2] for at in range(len(ranks), after, 2)]
    _, out, boundary, filtered, arrived, sums, sems = rest[after:]
    fields, levels = out.shape[0:2]
    lists = fields * levels
    each = strip_rows(lists)
    lon_index = meta[2]
    mine = pl.ds(pl.multiple_of(meta[0] * POLAR, POLAR), POLAR)

    def copy_out(item):
        l, f = item // fields, item % fields
        return pltpu.make_async_copy(filtered.at[item], out.at[f, l, :, mine], sems.at[item])

    def received(index, span):
        step = abs(ranks[index][0])
        if 2 * step == count:
            return payloads[index][span, :]
        base = index - index % 2
        first, last = payloads[base][span, :], payloads[base + 1][span, :]
        takes_first = is_second(lon_index, step, count)
        if index != base:
            takes_first = jnp.logical_not(takes_first)
        return jnp.where(takes_first, first, last)

    @pl.when(meta[1] == 1)
    def _():
        item = 0
        for near, moments in near_parts:
            for at in range(near.shape[0]):
                place = 0
                for index, (_, rank) in enumerate(ranks):
                    turn_cos = turn[index : index + 1, :POLAR]
                    turn_sin = turn[index : index + 1, POLAR:]
                    value = received(index, slice(item * rank, (item + 1) * rank))
                    cosines, sines = value[:, :POLAR], value[:, POLAR:]
                    arrived[item, place : place + rank, :POLAR] = (
                        turn_cos * cosines + turn_sin * sines
                    )
                    arrived[item, place : place + rank, POLAR:] = (
                        turn_cos * sines - turn_sin * cosines
                    )
                    place += rank
                for part in range(2):
                    arrived[item, place : place + SPLIT_RANK, :] = moments[
                        at, part * 16 : part * 16 + SPLIT_RANK, :
                    ]
                    place += SPLIT_RANK
                arrived[item, place:, :] = jnp.zeros((HELD - place, 2 * POLAR), F32)
                total = jnp.dot(far[...], stacked(arrived[item]), preferred_element_type=F32)
                filtered[item] = (
                    near[at] + sine[...] * total[:, :POLAR] - cosine[...] * total[:, POLAR:]
                )
                copy_out(item).start()
                item += 1

    sums[...] = jnp.zeros(sums.shape, F32)
    pieces, sources = [], []
    blank = jnp.zeros((16 - each, POLAR), F32)
    for index in range(-1, len(ranks)):
        if index < 0:
            shift, arrival = 0, own[0:each, :]
        else:
            shift, rank = ranks[index]
            arrival = received(index, slice(lists * rank, lists * rank + each))
        sources.append(lax.rem(lon_index - shift + count, count))
        pieces += [arrival[:, :POLAR], blank, arrival[:, POLAR:], blank]
    pieces = jnp.concatenate(pieces, axis=0)
    high = pieces.astype(BF16)
    middle, low = split_value(pieces - high.astype(F32))
    points = jnp.dot(high, hats[...], preferred_element_type=F32)
    points = points + jnp.dot(middle, hats[...], preferred_element_type=F32)
    points = points + jnp.dot(low, hats[...], preferred_element_type=F32)
    width = hats.shape[1] // CAP
    beyond = jnp.zeros((32, POLAR), F32)
    for index, source in enumerate(sources):
        for rank in range(CAP):
            place = begins[source, rank]
            offset = lax.rem(place, POLAR)
            span = points[index * 32 : (index + 1) * 32, rank * width : (rank + 1) * width]
            moved = pltpu.roll(jnp.concatenate([span, beyond], axis=1), offset, 1)
            at = pl.ds(pl.multiple_of(place - offset, POLAR), width + POLAR)
            sums[:, at] = sums[:, at] + moved
    for l in range(levels):
        for f in range(fields):
            side, row = divmod(l * fields + f, each)
            row = side * 16 + row
            boundary[0, f, l : l + 1, :] = sums[row : row + 1, 0:NB] * (1.0 / RATIO)

    @pl.when(meta[1] == 1)
    def _():
        for item in range(lists):
            copy_out(item).wait()


def phase_table(kept, steps, period):
    phase = (2 * kept - 1)[None, :] * steps[:, None] % (2 * period)
    angle = phase.astype(F32) * (math.pi / period)
    return jnp.cos(angle), jnp.sin(angle)


def cost(flops, bytes_accessed):
    return pl.CostEstimate(flops=flops, bytes_accessed=bytes_accessed, transcendentals=0)


def compressed(model_state, diffusion, coupling, cutoff, strip_list, nest_place):
    lat_index = lax.axis_index("lat")
    lon_index = lax.axis_index("lon")
    lat_count = lax.axis_size("lat")
    lon_count = lax.axis_size("lon")
    fields, levels, columns, rows = model_state.shape
    lists = fields * levels
    total_columns = columns * lon_count
    ranks = shift_ranks(lon_count)
    near, send, far = [jnp.asarray(table) for table in filter_tables(lon_count, columns)]
    params = pltpu.CompilerParams(vmem_limit_bytes=VMEM_LIMIT)
    shape = lambda *sizes: jax.ShapeDtypeStruct(sizes, F32)
    whole_state = shape(*model_state.shape)

    is_south = lat_index == lat_count - 1
    is_polar = (lat_index == 0) | is_south
    part = jnp.where(is_south, rows // POLAR - 1, 0)
    meta = jnp.stack([part, is_polar.astype(jnp.int32), lon_index, lat_index]).astype(jnp.int32)
    kept = jnp.where(lat_index < lat_count // 2, cutoff[:POLAR], cutoff[POLAR:])
    places = np.concatenate([np.arange(0, columns, STEP), np.arange(STEP)]).astype(np.int32)
    angles = phase_table(kept, jnp.asarray(places), total_columns)
    steps = jnp.array([abs(shift) for shift, _ in ranks], jnp.int32)
    sign = np.array([[1.0 if shift > 0 else -1.0] for shift, _ in ranks], np.float32)
    turn_cos, turn_sin = phase_table(kept, steps, lon_count)
    turn = jnp.concatenate([turn_cos, turn_sin * sign], axis=1)
    turn = jnp.pad(turn, ((0, ceil8(len(ranks)) - len(ranks)), (0, 0)))
    middle = ((2 * kept - 1).astype(F32) / total_columns)[None, :]
    hats = jnp.asarray(hat_table())

    smem = pl.BlockSpec(memory_space=pltpu.SMEM)
    vmem = pl.BlockSpec(memory_space=pltpu.VMEM)
    hbm = pl.BlockSpec(memory_space=pl.ANY)
    level_sems = pltpu.SemaphoreType.DMA((levels,))

    with jax.named_scope("edges"):
        edges = pl.pallas_call(
            edge_kernel,
            in_specs=[smem, hbm],
            out_specs=[vmem] * 4,
            out_shape=[shape(ceil8(lists), rows)] * 2 + [shape(ceil8(lists), columns)] * 2,
            scratch_shapes=[
                pltpu.VMEM((fields, levels, columns, rows), F32),
                pltpu.VMEM((columns, POLAR), F32),
                pltpu.SemaphoreType.DMA((fields,)),
            ],
            compiler_params=params,
        )(meta, model_state)

    with jax.named_scope("halo"):
        lon_pairs, lon_crosses = ring_swaps(1, lon_count)
        lat_pairs = [(i, i + 1) for i in range(0, lat_count, 2)]
        lat_crosses = [(i, i + 1) for i in range(1, lat_count - 1, 2)]
        halos = [
            lax.ppermute(edges[0], "lon", lon_pairs),
            lax.ppermute(edges[1], "lon", lon_crosses),
            lax.ppermute(edges[2], "lat", swaps(lat_pairs)),
            lax.ppermute(edges[3], "lat", swaps(lat_crosses)),
        ]

    sizes = [payload_rows(rank, lists) for _, rank in ranks]
    with jax.named_scope("stencil"):
        updated, cosine, sine, own, *outgoing = pl.pallas_call(
            functools.partial(stencil_kernel, lon_count),
            in_specs=[smem] * 3 + [vmem] * 8 + [hbm],
            out_specs=[hbm] + [vmem] * (3 + len(ranks)),
            out_shape=[whole_state]
            + [shape(columns, POLAR)] * 2
            + [shape(16, rows)]
            + [shape(size, rows) for size in sizes],
            scratch_shapes=[
                pltpu.VMEM((levels, fields, columns + 16, rows), F32),
                pltpu.VMEM((levels, fields, columns, rows), F32),
                pltpu.VMEM((columns, POLAR), F32),
                pltpu.VMEM((columns, POLAR), F32),
                pltpu.VMEM((lists, send.shape[0] // 2, rows), F32),
                pltpu.VMEM((lon_count, 16, rows), F32),
                pltpu.VMEM((strip_list.shape[0], 2, 16, rows), F32),
                level_sems,
                level_sems,
            ],
            compiler_params=params,
        )(
            meta,
            coupling.reshape(levels, fields * fields),
            strip_list,
            *halos,
            diffusion,
            *angles,
            send,
            model_state,
        )

    def exchange(index, payload):
        step = abs(ranks[index][0])
        swap = index % 2 if 2 * step < lon_count else 0
        return lax.ppermute(payload, "lon", ring_swaps(step, lon_count)[swap])

    with jax.named_scope("exchange"):
        incoming = {
            index: exchange(index, outgoing[index])
            for index in range(len(ranks))
            if index not in LATE
        }

    def near_part(begin, end, passed):
        results = pl.pallas_call(
            functools.partial(near_kernel, begin, len(passed)),
            in_specs=[smem] + [vmem] * 4 + [hbm] * (1 + len(passed)),
            out_specs=[vmem] * 2 + [hbm] * len(passed),
            out_shape=[shape(end - begin, columns, POLAR), shape(end - begin, 32, rows)]
            + [shape(*payload.shape) for payload in passed],
            input_output_aliases={6 + index: 2 + index for index in range(len(passed))},
            scratch_shapes=[
                pltpu.VMEM((end - begin, columns, POLAR), F32),
                pltpu.SemaphoreType.DMA((end - begin,)),
            ],
            compiler_params=params,
            cost_estimate=cost(
                12 * (end - begin) * columns * columns * POLAR, 8 * (end - begin) * columns * POLAR
            ),
        )(meta, cosine, sine, middle, near, updated, *passed)
        return results[:2], results[2:]

    near_parts = []
    begin = 0
    for index, count in enumerate(NEAR_LISTS):
        late, quick = LATE[index : index + 1], QUICK[index - 1 : index] if index else ()
        with jax.named_scope("near"):
            results, passed = near_part(
                begin,
                begin + count,
                [outgoing[swap] for swap in late] + [incoming[swap] for swap in quick],
            )
        near_parts += results
        begin += count
        with jax.named_scope("late_exchange"):
            for swap, payload in zip(late, passed):
                incoming[swap] = exchange(swap, payload)
        incoming.update(zip(quick, passed[len(late) :]))

    with jax.named_scope("far"):
        advanced, boundary = pl.pallas_call(
            functools.partial(far_kernel, lon_count),
            in_specs=[smem] * 2 + [vmem] * (6 + len(ranks) + len(near_parts)) + [hbm],
            out_specs=[hbm, vmem],
            out_shape=[whole_state, shape(1, fields, levels, NB)],
            input_output_aliases={8 + len(ranks) + len(near_parts): 0},
            scratch_shapes=[
                pltpu.VMEM((lists, columns, POLAR), F32),
                pltpu.VMEM((lists, HELD, rows), F32),
                pltpu.VMEM((32, NB + 2 * POLAR), F32),
                pltpu.SemaphoreType.DMA((lists,)),
            ],
            compiler_params=pltpu.CompilerParams(vmem_limit_bytes=VMEM_LIMIT // 2),
        )(
            meta,
            nest_place.reshape(lon_count, CAP),
            cosine,
            sine,
            turn,
            far,
            hats,
            own,
            *[incoming[index] for index in range(len(ranks))],
            *near_parts,
            updated,
        )
    return advanced, boundary


def padded_2(block, sides, width):
    for axis, dim in sides:
        count = lax.axis_size(axis)
        forward = [(i, i + 1) for i in range(count - 1)]
        forward.append((count - 1, 0))
        backward = [(target, source) for source, target in forward]
        low = lax.ppermute(
            lax.slice_in_dim(block, block.shape[dim] - width, None, axis=dim), axis, forward
        )
        high = lax.ppermute(lax.slice_in_dim(block, 0, width, axis=dim), axis, backward)
        block = jnp.concatenate([low, block, high], axis=dim)
    return block


def spectral_filter(rows, kept):
    top_wavenumber_kept = lax.Precision.HIGHEST
    length = rows.shape[3]
    width = math.gcd(KC, 128)
    column_grid = lax.broadcasted_iota(jnp.int32, (length, width), 0)
    step_output = jnp.zeros_like(rows)
    for block_index in range(KC // width):
        wavenumber = block_index * width + lax.broadcasted_iota(jnp.int32, (length, width), 1)
        phase = column_grid * wavenumber % length
        angle = phase.astype(jnp.float32) * (2.0 * math.pi / length)
        cosine = jnp.cos(angle)
        sine = jnp.sin(angle)
        along = block_index * width + jnp.arange(width, dtype=jnp.int32)
        scale = jnp.where(along == 0, 1.0 / length, 2.0 / length)
        weight = jnp.where(along[None, :] < kept[:, None], scale[None, :], 0.0)
        real_part = (
            jnp.einsum("flrn,nk->flrk", rows, cosine, precision=top_wavenumber_kept) * weight
        )
        imaginary_component = (
            jnp.einsum("flrn,nk->flrk", rows, sine, precision=top_wavenumber_kept) * weight
        )
        step_output = (
            step_output
            + jnp.einsum("flrk,nk->flrn", real_part, cosine, precision=top_wavenumber_kept)
            + jnp.einsum("flrk,nk->flrn", imaginary_component, sine, precision=top_wavenumber_kept)
        )
    return step_output


def polar_pass(work_rows, kept_start, kept_table):
    count = work_rows.shape[2] // lax.axis_size("lon")
    kept = lax.dynamic_slice_in_dim(kept_table, kept_start + lax.axis_index("lon") * count, count)
    return lax.all_to_all(
        spectral_filter(
            lax.all_to_all(work_rows, "lon", split_axis=2, concat_axis=3, tiled=True), kept
        ),
        "lon",
        split_axis=3,
        concat_axis=2,
        tiled=True,
    )


def transposed(model_state, diffusion, coupling, cutoff, strip_list, nest_place):
    top_wavenumber_kept = lax.Precision.HIGHEST
    lat_index = lax.axis_index("lat")
    lat_count = lax.axis_size("lat")
    lon_count = lax.axis_size("lon")
    fields, levels, lon_local, lat_local = model_state.shape
    padded = padded_2(model_state, (("lat", 3), ("lon", 2)), 1)
    east_west = padded[:, :, 2:, 1:-1] + padded[:, :, :-2, 1:-1]
    row_place = lax.broadcasted_iota(jnp.int32, (1, 1, 1, lat_local), 3)
    northern = jnp.where((lat_index == 0) & (row_place == 0), 0.0, padded[:, :, 1:-1, :-2])
    southern = jnp.where(
        (lat_index == lat_count - 1) & (row_place == lat_local - 1), 0.0, padded[:, :, 1:-1, 2:]
    )
    blended = jnp.einsum("lfg,glij->flij", coupling, model_state, precision=top_wavenumber_kept)
    updated = (
        model_state
        + diffusion[0] * (east_west - 2.0 * model_state)
        + diffusion[1] * (northern + southern - 2.0 * model_state)
        + blended
    )
    is_south = lat_index == lat_count - 1
    is_polar = (lat_index == 0) | is_south
    start = jnp.where(is_south, lat_local - POLAR, 0).astype(jnp.int32)
    band_base = jnp.where(lat_index < lat_count // 2, 0, POLAR).astype(jnp.int32)
    block_rows = lax.dynamic_slice_in_dim(updated, start, POLAR, 3)
    polar_rows = jnp.transpose(block_rows, (0, 1, 3, 2))
    filtered = polar_pass(polar_rows, band_base, cutoff)
    new_rows = jnp.where(is_polar, jnp.transpose(filtered, (0, 1, 3, 2)), block_rows)
    advanced_state = lax.dynamic_update_slice_in_dim(updated, new_rows, start, 3)
    slots = strip_list.shape[0]
    owners = strip_list[:, 0]
    columns = strip_list[:, 1]
    offsets = strip_list[:, 2]
    lengths = strip_list[:, 3]
    zero = jnp.zeros((), jnp.int32)

    def cut_strip(column, offset):
        return lax.dynamic_slice(
            updated, (zero, zero, column, offset), (fields, levels, 1, STRIP)
        ).reshape(fields * levels, STRIP)

    boundary_strips = jax.vmap(cut_strip)(columns, offsets)
    inside = lax.broadcasted_iota(jnp.int32, (1, 1, STRIP), 2) < lengths[:, None, None]
    boundary_strips = jnp.where(inside, boundary_strips, 0.0).reshape(
        slots, fields * levels * STRIP
    )
    slot_ids = jnp.arange(slots, dtype=jnp.int32)
    earlier = slot_ids[None, :] < slot_ids[:, None]
    same = owners[:, None] == owners[None, :]
    rank = jnp.sum((same & earlier).astype(jnp.int32), axis=1)
    target = owners * CAP + rank
    routing = (jnp.arange(lon_count * CAP, dtype=jnp.int32)[:, None] == target[None, :]).astype(
        jnp.float32
    )
    outgoing = jnp.dot(
        routing, boundary_strips, precision=top_wavenumber_kept, preferred_element_type=jnp.float32
    ).reshape(lon_count, CAP, fields * levels * STRIP)
    arrived = lax.all_to_all(outgoing, "lon", split_axis=0, concat_axis=0, tiled=True)
    total = lon_count * CAP
    group = math.gcd(total, 16)
    pieces = arrived.reshape(total // group, group, fields * levels, STRIP)
    starts = nest_place.reshape(total // group, group)
    point = lax.broadcasted_iota(jnp.int32, (1, 1, NB), 2)
    row_step = lax.broadcasted_iota(jnp.int32, (1, STRIP, 1), 1) * RATIO

    def accumulate(carry, item):
        piece, begin = item
        offset = point - begin[:, None, None]
        hat = jnp.maximum(RATIO - jnp.abs(offset - row_step), 0)
        hat = (
            jnp.where((offset >= 0) & (offset < STRIP * RATIO), hat, 0).astype(jnp.float32) / RATIO
        )
        return (carry + jnp.einsum("gat,gtp->ap", piece, hat, precision=top_wavenumber_kept), None)

    boundary = lax.scan(
        accumulate, jnp.zeros((fields * levels, NB), jnp.float32), (pieces, starts)
    )[0]
    return (advanced_state, boundary.reshape(1, fields, levels, NB))


def local(model_state, *others):
    columns = model_state.shape[2]
    fits = lax.axis_size("lon") * STRIP == POLAR and model_state.shape[3] == 2 * POLAR
    if fits and columns % STEP == 0 and columns >= 2 * HELD:
        return compressed(model_state, *others)
    return transposed(model_state, *others)


def solution(mesh):
    return jax.shard_map(
        local,
        mesh=mesh,
        in_specs=(
            P(None, None, "lon", "lat"),
            P(None, "lat"),
            P(),
            P(),
            P(("lat", "lon"), None),
            P(("lat", "lon"), None, None),
        ),
        out_specs=(P(None, None, "lon", "lat"), P(("lat", "lon"), None, None, None)),
        check_vma=False,
    )
```

```python
import functools
import math

import jax
import jax.numpy as jnp
import numpy as np
from jax import lax
from jax.experimental import pallas as pl
from jax.experimental.pallas import tpu as pltpu
from jax.sharding import PartitionSpec as P

POLAR = 128
CAP = 2
STRIP = 16
RATIO = 11
NB = 2048
KC = 896
RANKS = (14, 5, 4, 4)
SPLIT_RANK = 14
STEP = 16
HELD = 80
NEAR_LISTS = (6, 6, 8)
QUICK = (0, 2)
LATE = (3, 4)
SOUTH = 64
VMEM_LIMIT = 48 * 1024 * 1024
F32 = jnp.float32
BF16 = jnp.bfloat16


def ceil8(value):
    return -(-value // 8) * 8


def shift_ranks(count):
    shifts = []
    for step in range(1, count // 2 + 1):
        for shift in (step, -step):
            if shift != -count // 2:
                shifts.append((shift, RANKS[min(step, len(RANKS)) - 1]))
    return shifts


def is_second(place, step, count):
    return lax.rem(lax.div(place, math.gcd(step, count)), 2) == 1


def swaps(pairs):
    return [pair for a, b in pairs for pair in ((a, b), (b, a))]


def ring_swaps(step, count):
    if 2 * step == count:
        return [swaps([(i, i + step) for i in range(step)])]
    groups = [[], []]
    for i in range(count):
        groups[i // math.gcd(step, count) % 2].append((i, (i + step) % count))
    return [swaps(group) for group in groups]


def split_table(table):
    high = table.astype(jnp.bfloat16)
    low = (table - high.astype(np.float64)).astype(jnp.bfloat16)
    return high, low


def factored(block, rank):
    left, values, right = np.linalg.svd(block)
    root = np.sqrt(values[:rank])
    return right[:rank] * root[:, None], left[:, :rank] * root[None, :]


@functools.lru_cache(maxsize=None)
def filter_tables(count, width):
    total = count * width
    half = width // 2

    def block(size, shift):
        place = np.arange(size)
        angle = np.pi * (shift + place[:, None] - place[None, :]) / total
        with np.errstate(divide="ignore"):
            return np.where(angle == 0, 0.0, 1.0 / (np.sin(angle) * total))

    senders, receivers = [], []
    for shift, rank in shift_ranks(count):
        sender, receiver = factored(block(width, shift * width), rank)
        senders.append(np.pad(sender, ((0, ceil8(rank) - rank), (0, 0))))
        receivers.append(receiver)
    nears = []
    for part, shift in enumerate((half, -half)):
        sender, receiver = factored(block(half, shift), SPLIT_RANK)
        rows = np.concatenate([block(half, 0), sender], axis=0)
        nears.append(np.pad(rows, ((0, 16 - SPLIT_RANK), (0, 0))))
        beyond = ((half, 0), (0, 0)) if part == 0 else ((0, half), (0, 0))
        receivers.append(np.pad(receiver, beyond))
    receivers = np.concatenate(receivers, axis=1)
    receivers = np.pad(receivers, ((0, 0), (0, HELD - receivers.shape[1])))
    nears = [table for rows in nears for table in split_table(rows)]
    send_high, send_low = split_table(np.concatenate(senders, axis=0))
    far_high, far_low = split_table(receivers)
    return (
        np.concatenate(nears, axis=0),
        np.concatenate([send_high, send_low], axis=0),
        np.concatenate([far_high, far_high, far_low], axis=1),
    )


def hat_table():
    width = -(-STRIP * RATIO // POLAR) * POLAR
    point = np.arange(width)
    table = np.zeros((POLAR, CAP * width), np.float32)
    for rank in range(CAP):
        for row in range(STRIP):
            hat = np.maximum(RATIO - np.abs(point - row * RATIO), 0) * (point < STRIP * RATIO)
            table[rank * STRIP + row, rank * width : (rank + 1) * width] = hat
    return table.astype(jnp.bfloat16)


def split_value(value):
    high = value.astype(BF16)
    return high, (value - high.astype(F32)).astype(BF16)


def modulated(row, cosine, sine):
    return jnp.concatenate([row * cosine[...], row * sine[...]], axis=1)


def stacked(value):
    high, low = split_value(value)
    return jnp.concatenate([high, low, high], axis=0)


def strip_rows(slots):
    return slots // 2


def payload_rows(rank, slots):
    return ceil8(slots * rank + strip_rows(slots))


def edge_kernel(
    meta, state, lon_pair, lon_cross, lat_pair, lat_cross, held, edges, in_sems
):
    fields, levels, columns, rows = state.shape
    copies = [
        pltpu.make_async_copy(state.at[f], held.at[f], in_sems.at[f]) for f in range(fields - 1)
    ]
    f = fields - 1
    copies += [
        pltpu.make_async_copy(state.at[f, l], held.at[f, l], in_sems.at[f + l])
        for l in range(levels)
    ]
    for copy in copies:
        copy.start()
    lane = lax.broadcasted_iota(jnp.int32, (columns, POLAR), 1)
    lon_odd = lax.rem(meta[2], 2) == 1
    lat_odd = lax.rem(meta[3], 2) == 1
    edges[...] = jnp.zeros(edges.shape, F32)

    for f in range(fields):
        for l in range(levels):
            if f == fields - 1:
                copies[f + l].wait()
            elif l == 0:
                copies[f].wait()
            item = l * fields + f
            first = held[f, l, 0:1, :]
            last = held[f, l, columns - 1 : columns, :]
            lon_pair[item : item + 1, :] = jnp.where(lon_odd, first, last)
            lon_cross[item : item + 1, :] = jnp.where(lon_odd, last, first)
            north = held[f, l, :, 0:POLAR]
            north = pltpu.roll(north, item, 1) if item else north
            south = pltpu.roll(held[f, l, :, rows - POLAR :], item + SOUTH + 1, 1)
            value = jnp.where(lane == item, north, edges[...])
            edges[...] = jnp.where(lane == SOUTH + item, south, value)
    turned = edges[...].T
    size = lat_pair.shape[0]
    north, south = turned[0:size], turned[SOUTH : SOUTH + size]
    lat_pair[...] = jnp.where(lat_odd, north, south)
    lat_cross[...] = jnp.where(lat_odd, south, north)


def stencil_kernel(
    count,
    meta,
    coupling,
    strips,
    lon_pair,
    lon_cross,
    lat_pair,
    lat_cross,
    diffusion,
    angle_cos,
    angle_sin,
    send,
    state,
    updated,
    polar,
    cosine,
    sine,
    own,
    *rest,
):
    ranks = shift_ranks(count)
    payloads = rest[: len(ranks)]
    held, made, halos, halo, factors, placed, rows_cut, in_sems, out_sems = rest[len(ranks) :]
    fields, levels, columns, rows = state.shape
    tiles = rows // POLAR
    spans = [slice(tile * POLAR, (tile + 1) * POLAR) for tile in range(tiles)]

    def copy_in(l):
        return pltpu.make_async_copy(
            state.at[:, l], held.at[l, :, pl.ds(8, columns)], in_sems.at[l]
        )

    def copy_out(l):
        return pltpu.make_async_copy(made.at[l], updated.at[:, l], out_sems.at[l])

    for l in range(levels):
        copy_in(l).start()

    steps = columns // STEP
    fine_cos, fine_sin = angle_cos[steps:, :], angle_sin[steps:, :]
    for step in range(steps):
        span = slice(step * STEP, (step + 1) * STEP)
        coarse_cos, coarse_sin = angle_cos[step : step + 1, :], angle_sin[step : step + 1, :]
        cosine[span, :] = coarse_cos * fine_cos - coarse_sin * fine_sin
        sine[span, :] = coarse_sin * fine_cos + coarse_cos * fine_sin

    lane = lax.broadcasted_iota(jnp.int32, (STEP, POLAR), 1)
    lowest, highest = lane == 0, lane == POLAR - 1
    along = [jnp.broadcast_to(diffusion[0:1, span], (STEP, POLAR)) for span in spans]
    across = [jnp.broadcast_to(diffusion[1:2, span], (STEP, POLAR)) for span in spans]
    centre = [1.0 - 2.0 * along[t] - 2.0 * across[t] for t in range(tiles)]
    lon_odd = lax.rem(meta[2], 2) == 1
    lat_odd = lax.rem(meta[3], 2) == 1
    half = send.shape[0] // 2
    start = pl.multiple_of(meta[0] * POLAR, POLAR)
    size = lat_pair.shape[0]
    blank = jnp.zeros((SOUTH - size, columns), F32)
    north_halo = jnp.where(lat_odd, lat_pair[...], lat_cross[...])
    south_halo = jnp.where(lat_odd, lat_cross[...], lat_pair[...])
    halos[...] = jnp.concatenate([north_halo, blank, south_halo, blank], axis=0).T

    def one_level(l, carry):
        copy_in(l).wait()
        weights = [
            [coupling[l, f * fields + g] for g in range(fields)] for f in range(fields)
        ]
        halo[...] = pltpu.roll(halos[...], lax.rem(POLAR - l * fields, POLAR), 1)
        for f in range(fields):
            item = pl.ds(l * fields + f, 1)
            pair, cross = lon_pair[item, :], lon_cross[item, :]
            held[l, f, 7:8, :] = jnp.where(lon_odd, pair, cross)
            held[l, f, columns + 8 : columns + 9, :] = jnp.where(lon_odd, cross, pair)
        for begin in range(0, columns, STEP):
            end = begin + STEP
            shifted = lambda f, t, by: held[l, f, begin + 8 + by : end + 8 + by, spans[t]]
            here = [[shifted(f, t, 0) for t in range(tiles)] for f in range(fields)]
            edges = halo[begin:end, :]
            for f in range(fields):
                down = [pltpu.roll(here[f][t], 1, 1) for t in range(tiles)]
                up = [pltpu.roll(here[f][t], POLAR - 1, 1) for t in range(tiles)]
                north_edge = [pltpu.roll(edges, POLAR - f, 1) if f else edges] + down[:-1]
                south_edge = up[1:] + [pltpu.roll(edges, POLAR - 1 - SOUTH - f, 1)]
                for t in range(tiles):
                    north = jnp.where(lowest, north_edge[t], down[t])
                    south = jnp.where(highest, south_edge[t], up[t])
                    result = (centre[t] + weights[f][f]) * here[f][t]
                    result = result + along[t] * (shifted(f, t, 1) + shifted(f, t, -1))
                    result = result + across[t] * (north + south)
                    for g in range(fields):
                        if g != f:
                            result = result + weights[f][g] * here[g][t]
                    made[l, f, begin:end, spans[t]] = result
        copy_out(l).start()
        for f in range(fields):
            row = made[l, f, :, pl.ds(start, POLAR)]
            polar[l * fields + f] = row
            high, low = split_value(modulated(row, cosine, sine))
            both = jnp.dot(send[...], high, preferred_element_type=F32)
            cross = jnp.dot(send[0:half, :], low, preferred_element_type=F32)
            factors[l * fields + f] = both[:half] + both[half:] + cross
        return carry

    lax.fori_loop(0, levels, one_level, 0)

    lon_index = meta[2]
    slots = strips.shape[0]
    lists = fields * levels
    each = strip_rows(lists)
    placed[...] = jnp.zeros(placed.shape, F32)
    rows_cut[...] = jnp.zeros(rows_cut.shape, F32)
    strip_lane = lax.broadcasted_iota(jnp.int32, (16, rows), 1)

    def one_slot(s):
        owner, column = strips[s, 0], strips[s, 1]
        offset, length = strips[s, 2], strips[s, 3]
        rank = jnp.int32(0)
        for other in range(s):
            rank = rank + (strips[other, 0] == owner).astype(jnp.int32)
        for l in range(levels):
            for f in range(fields):
                side, place = divmod(l * fields + f, each)
                rows_cut[s, side, place : place + 1, :] = made[l, f, pl.ds(column, 1), :]
        base = rank * STRIP
        shift = lax.rem(owner - lon_index + count, count)
        for side in range(2):
            where = side * POLAR + base
            moved = pltpu.roll(rows_cut[s, side], lax.rem(where - offset + rows, rows), 1)
            inside = (strip_lane >= where) & (strip_lane < where + length)
            placed[shift] = placed[shift] + jnp.where(inside, moved, 0.0)

    for s in range(slots):
        one_slot(s)
    own[...] = placed[0]

    place = 0
    index = 0
    while index < len(ranks):
        step, rank = ranks[index]
        padded = ceil8(rank)
        paired = 2 if 2 * step < count else 1
        second = is_second(lon_index, step, count)
        targets = payloads[index : index + paired]
        for item in range(lists):
            span = slice(item * rank, (item + 1) * rank)
            plus = factors[item, place : place + rank, :]
            if paired == 1:
                targets[0][span, :] = plus
            else:
                minus = factors[item, place + padded : place + padded + rank, :]
                targets[0][span, :] = jnp.where(second, minus, plus)
                targets[1][span, :] = jnp.where(second, plus, minus)
        plus, minus = placed[step][0:each, :], placed[count - step][0:each, :]
        targets[0][lists * rank : lists * rank + each, :] = jnp.where(second, minus, plus)
        if paired == 2:
            targets[1][lists * rank : lists * rank + each, :] = jnp.where(second, plus, minus)
        for target in targets:
            unused = target.shape[0] - lists * rank - each
            if unused:
                target[lists * rank + each :, :] = jnp.zeros((unused, rows), F32)
        place += paired * padded
        index += paired
    for l in range(levels):
        copy_out(l).wait()


def near_kernel(begin, passed, meta, cosine, sine, middle, near, polar, *rest):
    filtered, moments = rest[passed], rest[passed + 1]
    lists, columns, _ = filtered.shape
    half = columns // 2
    each = near.shape[0] // 4

    @pl.when(meta[1] == 1)
    def _():
        for item in range(lists):
            for part in range(2):
                span = slice(part * half, (part + 1) * half)
                row = polar[begin + item, span, :]
                turn_cos, turn_sin = cosine[span, :], sine[span, :]
                value = jnp.concatenate([row * turn_cos, row * turn_sin], axis=1)
                table = near[2 * part * each : 2 * (part + 1) * each, :]
                high, low = split_value(value)
                both = jnp.dot(table, high, preferred_element_type=F32)
                cross = jnp.dot(table[:each], low, preferred_element_type=F32)
                total = both[:each] + both[each:] + cross
                filtered[item, span, :] = (
                    turn_sin * total[:half, :POLAR]
                    - turn_cos * total[:half, POLAR:]
                    + middle[0:1, :] * row
                )
                moments[item, part * 16 : (part + 1) * 16, :] = total[half:, :]


def far_kernel(count, meta, begins, cosine, sine, turn, far, hats, own, *rest):
    ranks = shift_ranks(count)
    payloads = rest[: len(ranks)]
    after = len(ranks) + 2 * len(NEAR_LISTS)
    near_parts = [rest[at : at + 2] for at in range(len(ranks), after, 2)]
    _, out, boundary, filtered, arrived, sums, sems = rest[after:]
    fields, levels = out.shape[0:2]
    lists = fields * levels
    each = strip_rows(lists)
    lon_index = meta[2]
    mine = pl.ds(pl.multiple_of(meta[0] * POLAR, POLAR), POLAR)

    def copy_out(item):
        l, f = item // fields, item % fields
        return pltpu.make_async_copy(filtered.at[item], out.at[f, l, :, mine], sems.at[item])

    def received(index, span):
        step = abs(ranks[index][0])
        if 2 * step == count:
            return payloads[index][span, :]
        base = index - index % 2
        first, last = payloads[base][span, :], payloads[base + 1][span, :]
        takes_first = is_second(lon_index, step, count)
        if index != base:
            takes_first = jnp.logical_not(takes_first)
        return jnp.where(takes_first, first, last)

    @pl.when(meta[1] == 1)
    def _():
        item = 0
        for near, moments in near_parts:
            for at in range(near.shape[0]):
                place = 0
                for index, (_, rank) in enumerate(ranks):
                    turn_cos = turn[index : index + 1, :POLAR]
                    turn_sin = turn[index : index + 1, POLAR:]
                    value = received(index, slice(item * rank, (item + 1) * rank))
                    cosines, sines = value[:, :POLAR], value[:, POLAR:]
                    arrived[item, place : place + rank, :POLAR] = (
                        turn_cos * cosines + turn_sin * sines
                    )
                    arrived[item, place : place + rank, POLAR:] = (
                        turn_cos * sines - turn_sin * cosines
                    )
                    place += rank
                for part in range(2):
                    arrived[item, place : place + SPLIT_RANK, :] = moments[
                        at, part * 16 : part * 16 + SPLIT_RANK, :
                    ]
                    place += SPLIT_RANK
                arrived[item, place:, :] = jnp.zeros((HELD - place, 2 * POLAR), F32)
                total = jnp.dot(far[...], stacked(arrived[item]), preferred_element_type=F32)
                filtered[item] = (
                    near[at] + sine[...] * total[:, :POLAR] - cosine[...] * total[:, POLAR:]
                )
                copy_out(item).start()
                item += 1

    sums[...] = jnp.zeros(sums.shape, F32)
    pieces, sources = [], []
    blank = jnp.zeros((16 - each, POLAR), F32)
    for index in range(-1, len(ranks)):
        if index < 0:
            shift, arrival = 0, own[0:each, :]
        else:
            shift, rank = ranks[index]
            arrival = received(index, slice(lists * rank, lists * rank + each))
        sources.append(lax.rem(lon_index - shift + count, count))
        pieces += [arrival[:, :POLAR], blank, arrival[:, POLAR:], blank]
    pieces = jnp.concatenate(pieces, axis=0)
    high = pieces.astype(BF16)
    middle, low = split_value(pieces - high.astype(F32))
    points = jnp.dot(high, hats[...], preferred_element_type=F32)
    points = points + jnp.dot(middle, hats[...], preferred_element_type=F32)
    points = points + jnp.dot(low, hats[...], preferred_element_type=F32)
    width = hats.shape[1] // CAP
    beyond = jnp.zeros((32, POLAR), F32)
    for index, source in enumerate(sources):
        for rank in range(CAP):
            place = begins[source, rank]
            offset = lax.rem(place, POLAR)
            span = points[index * 32 : (index + 1) * 32, rank * width : (rank + 1) * width]
            moved = pltpu.roll(jnp.concatenate([span, beyond], axis=1), offset, 1)
            at = pl.ds(pl.multiple_of(place - offset, POLAR), width + POLAR)
            sums[:, at] = sums[:, at] + moved
    for l in range(levels):
        for f in range(fields):
            side, row = divmod(l * fields + f, each)
            row = side * 16 + row
            boundary[0, f, l : l + 1, :] = sums[row : row + 1, 0:NB] * (1.0 / RATIO)

    @pl.when(meta[1] == 1)
    def _():
        for item in range(lists):
            copy_out(item).wait()


def phase_table(kept, steps, period):
    phase = (2 * kept - 1)[None, :] * steps[:, None] % (2 * period)
    angle = phase.astype(F32) * (math.pi / period)
    return jnp.cos(angle), jnp.sin(angle)


def cost(flops, bytes_accessed):
    return pl.CostEstimate(flops=flops, bytes_accessed=bytes_accessed, transcendentals=0)


def compressed(model_state, diffusion, coupling, cutoff, strip_list, nest_place):
    lat_index = lax.axis_index("lat")
    lon_index = lax.axis_index("lon")
    lat_count = lax.axis_size("lat")
    lon_count = lax.axis_size("lon")
    fields, levels, columns, rows = model_state.shape
    lists = fields * levels
    total_columns = columns * lon_count
    ranks = shift_ranks(lon_count)
    near, send, far = [jnp.asarray(table) for table in filter_tables(lon_count, columns)]
    params = pltpu.CompilerParams(vmem_limit_bytes=VMEM_LIMIT)
    shape = lambda *sizes: jax.ShapeDtypeStruct(sizes, F32)
    whole_state = shape(*model_state.shape)

    is_south = lat_index == lat_count - 1
    is_polar = (lat_index == 0) | is_south
    part = jnp.where(is_south, rows // POLAR - 1, 0)
    meta = jnp.stack([part, is_polar.astype(jnp.int32), lon_index, lat_index]).astype(jnp.int32)
    kept = jnp.where(lat_index < lat_count // 2, cutoff[:POLAR], cutoff[POLAR:])
    places = np.concatenate([np.arange(0, columns, STEP), np.arange(STEP)]).astype(np.int32)
    angles = phase_table(kept, jnp.asarray(places), total_columns)
    steps = jnp.array([abs(shift) for shift, _ in ranks], jnp.int32)
    sign = np.array([[1.0 if shift > 0 else -1.0] for shift, _ in ranks], np.float32)
    turn_cos, turn_sin = phase_table(kept, steps, lon_count)
    turn = jnp.concatenate([turn_cos, turn_sin * sign], axis=1)
    turn = jnp.pad(turn, ((0, ceil8(len(ranks)) - len(ranks)), (0, 0)))
    middle = ((2 * kept - 1).astype(F32) / total_columns)[None, :]
    hats = jnp.asarray(hat_table())

    smem = pl.BlockSpec(memory_space=pltpu.SMEM)
    vmem = pl.BlockSpec(memory_space=pltpu.VMEM)
    hbm = pl.BlockSpec(memory_space=pl.ANY)
    level_sems = pltpu.SemaphoreType.DMA((levels,))

    with jax.named_scope("edges"):
        edges = pl.pallas_call(
            edge_kernel,
            in_specs=[smem, hbm],
            out_specs=[vmem] * 4,
            out_shape=[shape(ceil8(lists), rows)] * 2 + [shape(ceil8(lists), columns)] * 2,
            scratch_shapes=[
                pltpu.VMEM((fields, levels, columns, rows), F32),
                pltpu.VMEM((columns, POLAR), F32),
                pltpu.SemaphoreType.DMA((fields - 1 + levels,)),
            ],
            compiler_params=params,
        )(meta, model_state)

    with jax.named_scope("halo"):
        lon_pairs, lon_crosses = ring_swaps(1, lon_count)
        lat_pairs = [(i, i + 1) for i in range(0, lat_count, 2)]
        lat_crosses = [(i, i + 1) for i in range(1, lat_count - 1, 2)]
        halos = [
            lax.ppermute(edges[0], "lon", lon_pairs),
            lax.ppermute(edges[1], "lon", lon_crosses),
            lax.ppermute(edges[2], "lat", swaps(lat_pairs)),
            lax.ppermute(edges[3], "lat", swaps(lat_crosses)),
        ]

    sizes = [payload_rows(rank, lists) for _, rank in ranks]
    with jax.named_scope("stencil"):
        updated, polar, cosine, sine, own, *outgoing = pl.pallas_call(
            functools.partial(stencil_kernel, lon_count),
            in_specs=[smem] * 3 + [vmem] * 8 + [hbm],
            out_specs=[hbm] + [vmem] * (4 + len(ranks)),
            out_shape=[whole_state, shape(lists, columns, POLAR)]
            + [shape(columns, POLAR)] * 2
            + [shape(16, rows)]
            + [shape(size, rows) for size in sizes],
            scratch_shapes=[
                pltpu.VMEM((levels, fields, columns + 16, rows), F32),
                pltpu.VMEM((levels, fields, columns, rows), F32),
                pltpu.VMEM((columns, POLAR), F32),
                pltpu.VMEM((columns, POLAR), F32),
                pltpu.VMEM((lists, send.shape[0] // 2, rows), F32),
                pltpu.VMEM((lon_count, 16, rows), F32),
                pltpu.VMEM((strip_list.shape[0], 2, 16, rows), F32),
                level_sems,
                level_sems,
            ],
            compiler_params=params,
        )(
            meta,
            coupling.reshape(levels, fields * fields),
            strip_list,
            *halos,
            diffusion,
            *angles,
            send,
            model_state,
        )

    def exchange(index, payload):
        step = abs(ranks[index][0])
        swap = index % 2 if 2 * step < lon_count else 0
        return lax.ppermute(payload, "lon", ring_swaps(step, lon_count)[swap])

    with jax.named_scope("exchange"):
        incoming = {
            index: exchange(index, outgoing[index])
            for index in range(len(ranks))
            if index not in LATE
        }

    def near_part(begin, end, passed):
        results = pl.pallas_call(
            functools.partial(near_kernel, begin, len(passed)),
            in_specs=[smem] + [vmem] * 5 + [hbm] * len(passed),
            out_specs=[vmem] * 2 + [hbm] * len(passed),
            out_shape=[shape(end - begin, columns, POLAR), shape(end - begin, 32, rows)]
            + [shape(*payload.shape) for payload in passed],
            input_output_aliases={6 + index: 2 + index for index in range(len(passed))},
            compiler_params=params,
            cost_estimate=cost(
                12 * (end - begin) * columns * columns * POLAR, 8 * (end - begin) * columns * POLAR
            ),
        )(meta, cosine, sine, middle, near, polar, *passed)
        return results[:2], results[2:]

    near_parts = []
    begin = 0
    for index, count in enumerate(NEAR_LISTS):
        late, quick = LATE[index : index + 1], QUICK[index - 1 : index] if index else ()
        with jax.named_scope("near"):
            results, passed = near_part(
                begin,
                begin + count,
                [outgoing[swap] for swap in late] + [incoming[swap] for swap in quick],
            )
        near_parts += results
        begin += count
        with jax.named_scope("late_exchange"):
            for swap, payload in zip(late, passed):
                incoming[swap] = exchange(swap, payload)
        incoming.update(zip(quick, passed[len(late) :]))

    with jax.named_scope("far"):
        advanced, boundary = pl.pallas_call(
            functools.partial(far_kernel, lon_count),
            in_specs=[smem] * 2 + [vmem] * (6 + len(ranks) + len(near_parts)) + [hbm],
            out_specs=[hbm, vmem],
            out_shape=[whole_state, shape(1, fields, levels, NB)],
            input_output_aliases={8 + len(ranks) + len(near_parts): 0},
            scratch_shapes=[
                pltpu.VMEM((lists, columns, POLAR), F32),
                pltpu.VMEM((lists, HELD, rows), F32),
                pltpu.VMEM((32, NB + 2 * POLAR), F32),
                pltpu.SemaphoreType.DMA((lists,)),
            ],
            compiler_params=pltpu.CompilerParams(vmem_limit_bytes=VMEM_LIMIT // 2),
        )(
            meta,
            nest_place.reshape(lon_count, CAP),
            cosine,
            sine,
            turn,
            far,
            hats,
            own,
            *[incoming[index] for index in range(len(ranks))],
            *near_parts,
            updated,
        )
    return advanced, boundary


def padded_2(block, sides, width):
    for axis, dim in sides:
        count = lax.axis_size(axis)
        forward = [(i, i + 1) for i in range(count - 1)]
        forward.append((count - 1, 0))
        backward = [(target, source) for source, target in forward]
        low = lax.ppermute(
            lax.slice_in_dim(block, block.shape[dim] - width, None, axis=dim), axis, forward
        )
        high = lax.ppermute(lax.slice_in_dim(block, 0, width, axis=dim), axis, backward)
        block = jnp.concatenate([low, block, high], axis=dim)
    return block


def spectral_filter(rows, kept):
    top_wavenumber_kept = lax.Precision.HIGHEST
    length = rows.shape[3]
    width = math.gcd(KC, 128)
    column_grid = lax.broadcasted_iota(jnp.int32, (length, width), 0)
    step_output = jnp.zeros_like(rows)
    for block_index in range(KC // width):
        wavenumber = block_index * width + lax.broadcasted_iota(jnp.int32, (length, width), 1)
        phase = column_grid * wavenumber % length
        angle = phase.astype(jnp.float32) * (2.0 * math.pi / length)
        cosine = jnp.cos(angle)
        sine = jnp.sin(angle)
        along = block_index * width + jnp.arange(width, dtype=jnp.int32)
        scale = jnp.where(along == 0, 1.0 / length, 2.0 / length)
        weight = jnp.where(along[None, :] < kept[:, None], scale[None, :], 0.0)
        real_part = (
            jnp.einsum("flrn,nk->flrk", rows, cosine, precision=top_wavenumber_kept) * weight
        )
        imaginary_component = (
            jnp.einsum("flrn,nk->flrk", rows, sine, precision=top_wavenumber_kept) * weight
        )
        step_output = (
            step_output
            + jnp.einsum("flrk,nk->flrn", real_part, cosine, precision=top_wavenumber_kept)
            + jnp.einsum("flrk,nk->flrn", imaginary_component, sine, precision=top_wavenumber_kept)
        )
    return step_output


def polar_pass(work_rows, kept_start, kept_table):
    count = work_rows.shape[2] // lax.axis_size("lon")
    kept = lax.dynamic_slice_in_dim(kept_table, kept_start + lax.axis_index("lon") * count, count)
    return lax.all_to_all(
        spectral_filter(
            lax.all_to_all(work_rows, "lon", split_axis=2, concat_axis=3, tiled=True), kept
        ),
        "lon",
        split_axis=3,
        concat_axis=2,
        tiled=True,
    )


def transposed(model_state, diffusion, coupling, cutoff, strip_list, nest_place):
    top_wavenumber_kept = lax.Precision.HIGHEST
    lat_index = lax.axis_index("lat")
    lat_count = lax.axis_size("lat")
    lon_count = lax.axis_size("lon")
    fields, levels, lon_local, lat_local = model_state.shape
    padded = padded_2(model_state, (("lat", 3), ("lon", 2)), 1)
    east_west = padded[:, :, 2:, 1:-1] + padded[:, :, :-2, 1:-1]
    row_place = lax.broadcasted_iota(jnp.int32, (1, 1, 1, lat_local), 3)
    northern = jnp.where((lat_index == 0) & (row_place == 0), 0.0, padded[:, :, 1:-1, :-2])
    southern = jnp.where(
        (lat_index == lat_count - 1) & (row_place == lat_local - 1), 0.0, padded[:, :, 1:-1, 2:]
    )
    blended = jnp.einsum("lfg,glij->flij", coupling, model_state, precision=top_wavenumber_kept)
    updated = (
        model_state
        + diffusion[0] * (east_west - 2.0 * model_state)
        + diffusion[1] * (northern + southern - 2.0 * model_state)
        + blended
    )
    is_south = lat_index == lat_count - 1
    is_polar = (lat_index == 0) | is_south
    start = jnp.where(is_south, lat_local - POLAR, 0).astype(jnp.int32)
    band_base = jnp.where(lat_index < lat_count // 2, 0, POLAR).astype(jnp.int32)
    block_rows = lax.dynamic_slice_in_dim(updated, start, POLAR, 3)
    polar_rows = jnp.transpose(block_rows, (0, 1, 3, 2))
    filtered = polar_pass(polar_rows, band_base, cutoff)
    new_rows = jnp.where(is_polar, jnp.transpose(filtered, (0, 1, 3, 2)), block_rows)
    advanced_state = lax.dynamic_update_slice_in_dim(updated, new_rows, start, 3)
    slots = strip_list.shape[0]
    owners = strip_list[:, 0]
    columns = strip_list[:, 1]
    offsets = strip_list[:, 2]
    lengths = strip_list[:, 3]
    zero = jnp.zeros((), jnp.int32)

    def cut_strip(column, offset):
        return lax.dynamic_slice(
            updated, (zero, zero, column, offset), (fields, levels, 1, STRIP)
        ).reshape(fields * levels, STRIP)

    boundary_strips = jax.vmap(cut_strip)(columns, offsets)
    inside = lax.broadcasted_iota(jnp.int32, (1, 1, STRIP), 2) < lengths[:, None, None]
    boundary_strips = jnp.where(inside, boundary_strips, 0.0).reshape(
        slots, fields * levels * STRIP
    )
    slot_ids = jnp.arange(slots, dtype=jnp.int32)
    earlier = slot_ids[None, :] < slot_ids[:, None]
    same = owners[:, None] == owners[None, :]
    rank = jnp.sum((same & earlier).astype(jnp.int32), axis=1)
    target = owners * CAP + rank
    routing = (jnp.arange(lon_count * CAP, dtype=jnp.int32)[:, None] == target[None, :]).astype(
        jnp.float32
    )
    outgoing = jnp.dot(
        routing, boundary_strips, precision=top_wavenumber_kept, preferred_element_type=jnp.float32
    ).reshape(lon_count, CAP, fields * levels * STRIP)
    arrived = lax.all_to_all(outgoing, "lon", split_axis=0, concat_axis=0, tiled=True)
    total = lon_count * CAP
    group = math.gcd(total, 16)
    pieces = arrived.reshape(total // group, group, fields * levels, STRIP)
    starts = nest_place.reshape(total // group, group)
    point = lax.broadcasted_iota(jnp.int32, (1, 1, NB), 2)
    row_step = lax.broadcasted_iota(jnp.int32, (1, STRIP, 1), 1) * RATIO

    def accumulate(carry, item):
        piece, begin = item
        offset = point - begin[:, None, None]
        hat = jnp.maximum(RATIO - jnp.abs(offset - row_step), 0)
        hat = (
            jnp.where((offset >= 0) & (offset < STRIP * RATIO), hat, 0).astype(jnp.float32) / RATIO
        )
        return (carry + jnp.einsum("gat,gtp->ap", piece, hat, precision=top_wavenumber_kept), None)

    boundary = lax.scan(
        accumulate, jnp.zeros((fields * levels, NB), jnp.float32), (pieces, starts)
    )[0]
    return (advanced_state, boundary.reshape(1, fields, levels, NB))


def local(model_state, *others):
    columns = model_state.shape[2]
    fits = lax.axis_size("lon") * STRIP == POLAR and model_state.shape[3] == 2 * POLAR
    if fits and columns % STEP == 0 and columns >= 2 * HELD:
        return compressed(model_state, *others)
    return transposed(model_state, *others)


def solution(mesh):
    return jax.shard_map(
        local,
        mesh=mesh,
        in_specs=(
            P(None, None, "lon", "lat"),
            P(None, "lat"),
            P(),
            P(),
            P(("lat", "lon"), None),
            P(("lat", "lon"), None, None),
        ),
        out_specs=(P(None, None, "lon", "lat"), P(("lat", "lon"), None, None, None)),
        check_vma=False,
    )
```

```python
import functools
import math

import jax
import jax.numpy as jnp
import numpy as np
from jax import lax
from jax.experimental import pallas as pl
from jax.experimental.pallas import tpu as pltpu
from jax.sharding import PartitionSpec as P

POLAR = 128
CAP = 2
STRIP = 16
RATIO = 11
NB = 2048
KC = 896
RANKS = (14, 5, 4, 4)
SPLIT_RANK = 14
STEP = 16
HELD = 80
NEAR_LISTS = (4, 8, 8)
QUICK = (0, 2)
LATE = (3, 4)
SOUTH = 64
VMEM_LIMIT = 48 * 1024 * 1024
F32 = jnp.float32
BF16 = jnp.bfloat16


def ceil8(value):
    return -(-value // 8) * 8


def shift_ranks(count):
    shifts = []
    for step in range(1, count // 2 + 1):
        for shift in (step, -step):
            if shift != -count // 2:
                shifts.append((shift, RANKS[min(step, len(RANKS)) - 1]))
    return shifts


def is_second(place, step, count):
    return lax.rem(lax.div(place, math.gcd(step, count)), 2) == 1


def swaps(pairs):
    return [pair for a, b in pairs for pair in ((a, b), (b, a))]


def ring_swaps(step, count):
    if 2 * step == count:
        return [swaps([(i, i + step) for i in range(step)])]
    groups = [[], []]
    for i in range(count):
        groups[i // math.gcd(step, count) % 2].append((i, (i + step) % count))
    return [swaps(group) for group in groups]


def split_table(table):
    high = table.astype(jnp.bfloat16)
    low = (table - high.astype(np.float64)).astype(jnp.bfloat16)
    return high, low


def factored(block, rank):
    left, values, right = np.linalg.svd(block)
    root = np.sqrt(values[:rank])
    return right[:rank] * root[:, None], left[:, :rank] * root[None, :]


@functools.lru_cache(maxsize=None)
def filter_tables(count, width):
    total = count * width
    half = width // 2

    def block(size, shift):
        place = np.arange(size)
        angle = np.pi * (shift + place[:, None] - place[None, :]) / total
        with np.errstate(divide="ignore"):
            return np.where(angle == 0, 0.0, 1.0 / (np.sin(angle) * total))

    senders, receivers = [], []
    for shift, rank in shift_ranks(count):
        sender, receiver = factored(block(width, shift * width), rank)
        senders.append(np.pad(sender, ((0, ceil8(rank) - rank), (0, 0))))
        receivers.append(receiver)
    nears = []
    for part, shift in enumerate((half, -half)):
        sender, receiver = factored(block(half, shift), SPLIT_RANK)
        rows = np.concatenate([block(half, 0), sender], axis=0)
        nears.append(np.pad(rows, ((0, 16 - SPLIT_RANK), (0, 0))))
        beyond = ((half, 0), (0, 0)) if part == 0 else ((0, half), (0, 0))
        receivers.append(np.pad(receiver, beyond))
    receivers = np.concatenate(receivers, axis=1)
    receivers = np.pad(receivers, ((0, 0), (0, HELD - receivers.shape[1])))
    nears = [table for rows in nears for table in split_table(rows)]
    send_high, send_low = split_table(np.concatenate(senders, axis=0))
    far_high, far_low = split_table(receivers)
    return (
        np.concatenate(nears, axis=0),
        np.concatenate([send_high, send_low], axis=0),
        np.concatenate([far_high, far_high, far_low], axis=1),
    )


def hat_table():
    width = -(-STRIP * RATIO // POLAR) * POLAR
    point = np.arange(width)
    table = np.zeros((POLAR, CAP * width), np.float32)
    for rank in range(CAP):
        for row in range(STRIP):
            hat = np.maximum(RATIO - np.abs(point - row * RATIO), 0) * (point < STRIP * RATIO)
            table[rank * STRIP + row, rank * width : (rank + 1) * width] = hat
    return table.astype(jnp.bfloat16)


def split_value(value):
    high = value.astype(BF16)
    return high, (value - high.astype(F32)).astype(BF16)


def modulated(row, cosine, sine):
    return jnp.concatenate([row * cosine[...], row * sine[...]], axis=1)


def stacked(value):
    high, low = split_value(value)
    return jnp.concatenate([high, low, high], axis=0)


def strip_rows(slots):
    return slots // 2


def payload_rows(rank, slots):
    return ceil8(slots * rank + strip_rows(slots))


def edge_kernel(
    meta, state, lon_pair, lon_cross, lat_pair, lat_cross, held, edges, in_sems
):
    fields, levels, columns, rows = state.shape
    copies = [
        pltpu.make_async_copy(state.at[f], held.at[f], in_sems.at[f]) for f in range(fields)
    ]
    for copy in copies:
        copy.start()
    lane = lax.broadcasted_iota(jnp.int32, (columns, POLAR), 1)
    lon_odd = lax.rem(meta[2], 2) == 1
    lat_odd = lax.rem(meta[3], 2) == 1
    edges[...] = jnp.zeros(edges.shape, F32)

    for f, copy in enumerate(copies):
        copy.wait()
        for l in range(levels):
            item = l * fields + f
            first = held[f, l, 0:1, :]
            last = held[f, l, columns - 1 : columns, :]
            lon_pair[item : item + 1, :] = jnp.where(lon_odd, first, last)
            lon_cross[item : item + 1, :] = jnp.where(lon_odd, last, first)
            north = held[f, l, :, 0:POLAR]
            north = pltpu.roll(north, item, 1) if item else north
            south = pltpu.roll(held[f, l, :, rows - POLAR :], item + SOUTH + 1, 1)
            value = jnp.where(lane == item, north, edges[...])
            edges[...] = jnp.where(lane == SOUTH + item, south, value)
    turned = edges[...].T
    size = lat_pair.shape[0]
    north, south = turned[0:size], turned[SOUTH : SOUTH + size]
    lat_pair[...] = jnp.where(lat_odd, north, south)
    lat_cross[...] = jnp.where(lat_odd, south, north)


def stencil_kernel(
    count,
    meta,
    coupling,
    strips,
    lon_pair,
    lon_cross,
    lat_pair,
    lat_cross,
    diffusion,
    angle_cos,
    angle_sin,
    send,
    state,
    updated,
    cosine,
    sine,
    own,
    *rest,
):
    ranks = shift_ranks(count)
    payloads = rest[: len(ranks)]
    held, made, halos, halo, factors, placed, rows_cut, in_sems, out_sems = rest[len(ranks) :]
    fields, levels, columns, rows = state.shape
    tiles = rows // POLAR
    spans = [slice(tile * POLAR, (tile + 1) * POLAR) for tile in range(tiles)]

    def copy_in(l):
        return pltpu.make_async_copy(
            state.at[:, l], held.at[l, :, pl.ds(8, columns)], in_sems.at[l]
        )

    def copy_out(l):
        return pltpu.make_async_copy(made.at[l], updated.at[:, l], out_sems.at[l])

    for l in range(levels):
        copy_in(l).start()

    steps = columns // STEP
    fine_cos, fine_sin = angle_cos[steps:, :], angle_sin[steps:, :]
    for step in range(steps):
        span = slice(step * STEP, (step + 1) * STEP)
        coarse_cos, coarse_sin = angle_cos[step : step + 1, :], angle_sin[step : step + 1, :]
        cosine[span, :] = coarse_cos * fine_cos - coarse_sin * fine_sin
        sine[span, :] = coarse_sin * fine_cos + coarse_cos * fine_sin

    lane = lax.broadcasted_iota(jnp.int32, (STEP, POLAR), 1)
    lowest, highest = lane == 0, lane == POLAR - 1
    along = [jnp.broadcast_to(diffusion[0:1, span], (STEP, POLAR)) for span in spans]
    across = [jnp.broadcast_to(diffusion[1:2, span], (STEP, POLAR)) for span in spans]
    centre = [1.0 - 2.0 * along[t] - 2.0 * across[t] for t in range(tiles)]
    lon_odd = lax.rem(meta[2], 2) == 1
    lat_odd = lax.rem(meta[3], 2) == 1
    half = send.shape[0] // 2
    start = pl.multiple_of(meta[0] * POLAR, POLAR)
    size = lat_pair.shape[0]
    blank = jnp.zeros((SOUTH - size, columns), F32)
    north_halo = jnp.where(lat_odd, lat_pair[...], lat_cross[...])
    south_halo = jnp.where(lat_odd, lat_cross[...], lat_pair[...])
    halos[...] = jnp.concatenate([north_halo, blank, south_halo, blank], axis=0).T

    def one_level(l, carry):
        copy_in(l).wait()
        weights = [
            [coupling[l, f * fields + g] for g in range(fields)] for f in range(fields)
        ]
        halo[...] = pltpu.roll(halos[...], lax.rem(POLAR - l * fields, POLAR), 1)
        for f in range(fields):
            item = pl.ds(l * fields + f, 1)
            pair, cross = lon_pair[item, :], lon_cross[item, :]
            held[l, f, 7:8, :] = jnp.where(lon_odd, pair, cross)
            held[l, f, columns + 8 : columns + 9, :] = jnp.where(lon_odd, cross, pair)
        for begin in range(0, columns, STEP):
            end = begin + STEP
            shifted = lambda f, t, by: held[l, f, begin + 8 + by : end + 8 + by, spans[t]]
            here = [[shifted(f, t, 0) for t in range(tiles)] for f in range(fields)]
            edges = halo[begin:end, :]
            for f in range(fields):
                down = [pltpu.roll(here[f][t], 1, 1) for t in range(tiles)]
                up = [pltpu.roll(here[f][t], POLAR - 1, 1) for t in range(tiles)]
                north_edge = [pltpu.roll(edges, POLAR - f, 1) if f else edges] + down[:-1]
                south_edge = up[1:] + [pltpu.roll(edges, POLAR - 1 - SOUTH - f, 1)]
                for t in range(tiles):
                    north = jnp.where(lowest, north_edge[t], down[t])
                    south = jnp.where(highest, south_edge[t], up[t])
                    result = (centre[t] + weights[f][f]) * here[f][t]
                    result = result + along[t] * (shifted(f, t, 1) + shifted(f, t, -1))
                    result = result + across[t] * (north + south)
                    for g in range(fields):
                        if g != f:
                            result = result + weights[f][g] * here[g][t]
                    made[l, f, begin:end, spans[t]] = result
        copy_out(l).start()
        for f in range(fields):
            row = made[l, f, :, pl.ds(start, POLAR)]
            high, low = split_value(modulated(row, cosine, sine))
            both = jnp.dot(send[...], high, preferred_element_type=F32)
            cross = jnp.dot(send[0:half, :], low, preferred_element_type=F32)
            factors[l * fields + f] = both[:half] + both[half:] + cross
        return carry

    lax.fori_loop(0, levels, one_level, 0)

    lon_index = meta[2]
    slots = strips.shape[0]
    lists = fields * levels
    each = strip_rows(lists)
    placed[...] = jnp.zeros(placed.shape, F32)
    rows_cut[...] = jnp.zeros(rows_cut.shape, F32)
    strip_lane = lax.broadcasted_iota(jnp.int32, (16, rows), 1)

    def one_slot(s):
        owner, column = strips[s, 0], strips[s, 1]
        offset, length = strips[s, 2], strips[s, 3]
        rank = jnp.int32(0)
        for other in range(s):
            rank = rank + (strips[other, 0] == owner).astype(jnp.int32)
        for l in range(levels):
            for f in range(fields):
                side, place = divmod(l * fields + f, each)
                rows_cut[s, side, place : place + 1, :] = made[l, f, pl.ds(column, 1), :]
        base = rank * STRIP
        shift = lax.rem(owner - lon_index + count, count)
        for side in range(2):
            where = side * POLAR + base
            moved = pltpu.roll(rows_cut[s, side], lax.rem(where - offset + rows, rows), 1)
            inside = (strip_lane >= where) & (strip_lane < where + length)
            placed[shift] = placed[shift] + jnp.where(inside, moved, 0.0)

    for s in range(slots):
        one_slot(s)
    own[...] = placed[0]

    place = 0
    index = 0
    while index < len(ranks):
        step, rank = ranks[index]
        padded = ceil8(rank)
        paired = 2 if 2 * step < count else 1
        second = is_second(lon_index, step, count)
        targets = payloads[index : index + paired]
        for item in range(lists):
            span = slice(item * rank, (item + 1) * rank)
            plus = factors[item, place : place + rank, :]
            if paired == 1:
                targets[0][span, :] = plus
            else:
                minus = factors[item, place + padded : place + padded + rank, :]
                targets[0][span, :] = jnp.where(second, minus, plus)
                targets[1][span, :] = jnp.where(second, plus, minus)
        plus, minus = placed[step][0:each, :], placed[count - step][0:each, :]
        targets[0][lists * rank : lists * rank + each, :] = jnp.where(second, minus, plus)
        if paired == 2:
            targets[1][lists * rank : lists * rank + each, :] = jnp.where(second, plus, minus)
        for target in targets:
            unused = target.shape[0] - lists * rank - each
            if unused:
                target[lists * rank + each :, :] = jnp.zeros((unused, rows), F32)
        place += paired * padded
        index += paired
    for l in range(levels):
        copy_out(l).wait()


def near_kernel(begin, passed, meta, cosine, sine, middle, near, rows, *rest):
    filtered, moments = rest[passed], rest[passed + 1]
    held, sems = rest[2 * passed + 2 :]
    fields = rows.shape[0]
    lists, columns, _ = filtered.shape
    half = columns // 2
    each = near.shape[0] // 4
    mine = pl.ds(pl.multiple_of(meta[0] * POLAR, POLAR), POLAR)

    def copy_in(item):
        l, f = (begin + item) // fields, (begin + item) % fields
        return pltpu.make_async_copy(rows.at[f, l, :, mine], held.at[item], sems.at[item])

    @pl.when(meta[1] == 1)
    def _():
        for item in range(lists):
            copy_in(item).start()

        for item in range(lists):
            copy_in(item).wait()
            for part in range(2):
                span = slice(part * half, (part + 1) * half)
                row = held[item, span, :]
                turn_cos, turn_sin = cosine[span, :], sine[span, :]
                value = jnp.concatenate([row * turn_cos, row * turn_sin], axis=1)
                table = near[2 * part * each : 2 * (part + 1) * each, :]
                high, low = split_value(value)
                both = jnp.dot(table, high, preferred_element_type=F32)
                cross = jnp.dot(table[:each], low, preferred_element_type=F32)
                total = both[:each] + both[each:] + cross
                filtered[item, span, :] = (
                    turn_sin * total[:half, :POLAR]
                    - turn_cos * total[:half, POLAR:]
                    + middle[0:1, :] * row
                )
                moments[item, part * 16 : (part + 1) * 16, :] = total[half:, :]


def far_kernel(count, meta, begins, cosine, sine, turn, far, hats, own, *rest):
    ranks = shift_ranks(count)
    payloads = rest[: len(ranks)]
    after = len(ranks) + 2 * len(NEAR_LISTS)
    near_parts = [rest[at : at + 2] for at in range(len(ranks), after, 2)]
    _, out, boundary, filtered, arrived, sums, sems = rest[after:]
    fields, levels = out.shape[0:2]
    lists = fields * levels
    each = strip_rows(lists)
    lon_index = meta[2]
    mine = pl.ds(pl.multiple_of(meta[0] * POLAR, POLAR), POLAR)

    def copy_out(item):
        l, f = item // fields, item % fields
        return pltpu.make_async_copy(filtered.at[item], out.at[f, l, :, mine], sems.at[item])

    def received(index, span):
        step = abs(ranks[index][0])
        if 2 * step == count:
            return payloads[index][span, :]
        base = index - index % 2
        first, last = payloads[base][span, :], payloads[base + 1][span, :]
        takes_first = is_second(lon_index, step, count)
        if index != base:
            takes_first = jnp.logical_not(takes_first)
        return jnp.where(takes_first, first, last)

    @pl.when(meta[1] == 1)
    def _():
        item = 0
        for near, moments in near_parts:
            for at in range(near.shape[0]):
                place = 0
                for index, (_, rank) in enumerate(ranks):
                    turn_cos = turn[index : index + 1, :POLAR]
                    turn_sin = turn[index : index + 1, POLAR:]
                    value = received(index, slice(item * rank, (item + 1) * rank))
                    cosines, sines = value[:, :POLAR], value[:, POLAR:]
                    arrived[item, place : place + rank, :POLAR] = (
                        turn_cos * cosines + turn_sin * sines
                    )
                    arrived[item, place : place + rank, POLAR:] = (
                        turn_cos * sines - turn_sin * cosines
                    )
                    place += rank
                for part in range(2):
                    arrived[item, place : place + SPLIT_RANK, :] = moments[
                        at, part * 16 : part * 16 + SPLIT_RANK, :
                    ]
                    place += SPLIT_RANK
                arrived[item, place:, :] = jnp.zeros((HELD - place, 2 * POLAR), F32)
                total = jnp.dot(far[...], stacked(arrived[item]), preferred_element_type=F32)
                filtered[item] = (
                    near[at] + sine[...] * total[:, :POLAR] - cosine[...] * total[:, POLAR:]
                )
                copy_out(item).start()
                item += 1

    sums[...] = jnp.zeros(sums.shape, F32)
    pieces, sources = [], []
    blank = jnp.zeros((16 - each, POLAR), F32)
    for index in range(-1, len(ranks)):
        if index < 0:
            shift, arrival = 0, own[0:each, :]
        else:
            shift, rank = ranks[index]
            arrival = received(index, slice(lists * rank, lists * rank + each))
        sources.append(lax.rem(lon_index - shift + count, count))
        pieces += [arrival[:, :POLAR], blank, arrival[:, POLAR:], blank]
    pieces = jnp.concatenate(pieces, axis=0)
    high = pieces.astype(BF16)
    middle, low = split_value(pieces - high.astype(F32))
    points = jnp.dot(high, hats[...], preferred_element_type=F32)
    points = points + jnp.dot(middle, hats[...], preferred_element_type=F32)
    points = points + jnp.dot(low, hats[...], preferred_element_type=F32)
    width = hats.shape[1] // CAP
    beyond = jnp.zeros((32, POLAR), F32)
    for index, source in enumerate(sources):
        for rank in range(CAP):
            place = begins[source, rank]
            offset = lax.rem(place, POLAR)
            span = points[index * 32 : (index + 1) * 32, rank * width : (rank + 1) * width]
            moved = pltpu.roll(jnp.concatenate([span, beyond], axis=1), offset, 1)
            at = pl.ds(pl.multiple_of(place - offset, POLAR), width + POLAR)
            sums[:, at] = sums[:, at] + moved
    for l in range(levels):
        for f in range(fields):
            side, row = divmod(l * fields + f, each)
            row = side * 16 + row
            boundary[0, f, l : l + 1, :] = sums[row : row + 1, 0:NB] * (1.0 / RATIO)

    @pl.when(meta[1] == 1)
    def _():
        for item in range(lists):
            copy_out(item).wait()


def phase_table(kept, steps, period):
    phase = (2 * kept - 1)[None, :] * steps[:, None] % (2 * period)
    angle = phase.astype(F32) * (math.pi / period)
    return jnp.cos(angle), jnp.sin(angle)


def cost(flops, bytes_accessed):
    return pl.CostEstimate(flops=flops, bytes_accessed=bytes_accessed, transcendentals=0)


def compressed(model_state, diffusion, coupling, cutoff, strip_list, nest_place):
    lat_index = lax.axis_index("lat")
    lon_index = lax.axis_index("lon")
    lat_count = lax.axis_size("lat")
    lon_count = lax.axis_size("lon")
    fields, levels, columns, rows = model_state.shape
    lists = fields * levels
    total_columns = columns * lon_count
    ranks = shift_ranks(lon_count)
    near, send, far = [jnp.asarray(table) for table in filter_tables(lon_count, columns)]
    params = pltpu.CompilerParams(vmem_limit_bytes=VMEM_LIMIT)
    shape = lambda *sizes: jax.ShapeDtypeStruct(sizes, F32)
    whole_state = shape(*model_state.shape)

    is_south = lat_index == lat_count - 1
    is_polar = (lat_index == 0) | is_south
    part = jnp.where(is_south, rows // POLAR - 1, 0)
    meta = jnp.stack([part, is_polar.astype(jnp.int32), lon_index, lat_index]).astype(jnp.int32)
    kept = jnp.where(lat_index < lat_count // 2, cutoff[:POLAR], cutoff[POLAR:])
    places = np.concatenate([np.arange(0, columns, STEP), np.arange(STEP)]).astype(np.int32)
    angles = phase_table(kept, jnp.asarray(places), total_columns)
    steps = jnp.array([abs(shift) for shift, _ in ranks], jnp.int32)
    sign = np.array([[1.0 if shift > 0 else -1.0] for shift, _ in ranks], np.float32)
    turn_cos, turn_sin = phase_table(kept, steps, lon_count)
    turn = jnp.concatenate([turn_cos, turn_sin * sign], axis=1)
    turn = jnp.pad(turn, ((0, ceil8(len(ranks)) - len(ranks)), (0, 0)))
    middle = ((2 * kept - 1).astype(F32) / total_columns)[None, :]
    hats = jnp.asarray(hat_table())

    smem = pl.BlockSpec(memory_space=pltpu.SMEM)
    vmem = pl.BlockSpec(memory_space=pltpu.VMEM)
    hbm = pl.BlockSpec(memory_space=pl.ANY)
    level_sems = pltpu.SemaphoreType.DMA((levels,))

    with jax.named_scope("edges"):
        edges = pl.pallas_call(
            edge_kernel,
            in_specs=[smem, hbm],
            out_specs=[vmem] * 4,
            out_shape=[shape(ceil8(lists), rows)] * 2 + [shape(ceil8(lists), columns)] * 2,
            scratch_shapes=[
                pltpu.VMEM((fields, levels, columns, rows), F32),
                pltpu.VMEM((columns, POLAR), F32),
                pltpu.SemaphoreType.DMA((fields,)),
            ],
            compiler_params=params,
        )(meta, model_state)

    with jax.named_scope("halo"):
        lon_pairs, lon_crosses = ring_swaps(1, lon_count)
        lat_pairs = [(i, i + 1) for i in range(0, lat_count, 2)]
        lat_crosses = [(i, i + 1) for i in range(1, lat_count - 1, 2)]
        halos = [
            lax.ppermute(edges[0], "lon", lon_pairs),
            lax.ppermute(edges[1], "lon", lon_crosses),
            lax.ppermute(edges[2], "lat", swaps(lat_pairs)),
            lax.ppermute(edges[3], "lat", swaps(lat_crosses)),
        ]

    sizes = [payload_rows(rank, lists) for _, rank in ranks]
    with jax.named_scope("stencil"):
        updated, cosine, sine, own, *outgoing = pl.pallas_call(
            functools.partial(stencil_kernel, lon_count),
            in_specs=[smem] * 3 + [vmem] * 8 + [hbm],
            out_specs=[hbm] + [vmem] * (3 + len(ranks)),
            out_shape=[whole_state]
            + [shape(columns, POLAR)] * 2
            + [shape(16, rows)]
            + [shape(size, rows) for size in sizes],
            scratch_shapes=[
                pltpu.VMEM((levels, fields, columns + 16, rows), F32),
                pltpu.VMEM((levels, fields, columns, rows), F32),
                pltpu.VMEM((columns, POLAR), F32),
                pltpu.VMEM((columns, POLAR), F32),
                pltpu.VMEM((lists, send.shape[0] // 2, rows), F32),
                pltpu.VMEM((lon_count, 16, rows), F32),
                pltpu.VMEM((strip_list.shape[0], 2, 16, rows), F32),
                level_sems,
                level_sems,
            ],
            compiler_params=params,
        )(
            meta,
            coupling.reshape(levels, fields * fields),
            strip_list,
            *halos,
            diffusion,
            *angles,
            send,
            model_state,
        )

    def exchange(index, payload):
        step = abs(ranks[index][0])
        swap = index % 2 if 2 * step < lon_count else 0
        return lax.ppermute(payload, "lon", ring_swaps(step, lon_count)[swap])

    with jax.named_scope("exchange"):
        incoming = {
            index: exchange(index, outgoing[index])
            for index in range(len(ranks))
            if index not in LATE
        }

    def near_part(begin, end, passed):
        results = pl.pallas_call(
            functools.partial(near_kernel, begin, len(passed)),
            in_specs=[smem] + [vmem] * 4 + [hbm] * (1 + len(passed)),
            out_specs=[vmem] * 2 + [hbm] * len(passed),
            out_shape=[shape(end - begin, columns, POLAR), shape(end - begin, 32, rows)]
            + [shape(*payload.shape) for payload in passed],
            input_output_aliases={6 + index: 2 + index for index in range(len(passed))},
            scratch_shapes=[
                pltpu.VMEM((end - begin, columns, POLAR), F32),
                pltpu.SemaphoreType.DMA((end - begin,)),
            ],
            compiler_params=params,
            cost_estimate=cost(
                12 * (end - begin) * columns * columns * POLAR, 8 * (end - begin) * columns * POLAR
            ),
        )(meta, cosine, sine, middle, near, updated, *passed)
        return results[:2], results[2:]

    near_parts = []
    begin = 0
    for index, count in enumerate(NEAR_LISTS):
        late, quick = LATE[index : index + 1], QUICK[index - 1 : index] if index else ()
        with jax.named_scope("near"):
            results, passed = near_part(
                begin,
                begin + count,
                [outgoing[swap] for swap in late] + [incoming[swap] for swap in quick],
            )
        near_parts += results
        begin += count
        with jax.named_scope("late_exchange"):
            for swap, payload in zip(late, passed):
                incoming[swap] = exchange(swap, payload)
        incoming.update(zip(quick, passed[len(late) :]))

    with jax.named_scope("far"):
        advanced, boundary = pl.pallas_call(
            functools.partial(far_kernel, lon_count),
            in_specs=[smem] * 2 + [vmem] * (6 + len(ranks) + len(near_parts)) + [hbm],
            out_specs=[hbm, vmem],
            out_shape=[whole_state, shape(1, fields, levels, NB)],
            input_output_aliases={8 + len(ranks) + len(near_parts): 0},
            scratch_shapes=[
                pltpu.VMEM((lists, columns, POLAR), F32),
                pltpu.VMEM((lists, HELD, rows), F32),
                pltpu.VMEM((32, NB + 2 * POLAR), F32),
                pltpu.SemaphoreType.DMA((lists,)),
            ],
            compiler_params=pltpu.CompilerParams(vmem_limit_bytes=VMEM_LIMIT // 2),
        )(
            meta,
            nest_place.reshape(lon_count, CAP),
            cosine,
            sine,
            turn,
            far,
            hats,
            own,
            *[incoming[index] for index in range(len(ranks))],
            *near_parts,
            updated,
        )
    return advanced, boundary


def padded_2(block, sides, width):
    for axis, dim in sides:
        count = lax.axis_size(axis)
        forward = [(i, i + 1) for i in range(count - 1)]
        forward.append((count - 1, 0))
        backward = [(target, source) for source, target in forward]
        low = lax.ppermute(
            lax.slice_in_dim(block, block.shape[dim] - width, None, axis=dim), axis, forward
        )
        high = lax.ppermute(lax.slice_in_dim(block, 0, width, axis=dim), axis, backward)
        block = jnp.concatenate([low, block, high], axis=dim)
    return block


def spectral_filter(rows, kept):
    top_wavenumber_kept = lax.Precision.HIGHEST
    length = rows.shape[3]
    width = math.gcd(KC, 128)
    column_grid = lax.broadcasted_iota(jnp.int32, (length, width), 0)
    step_output = jnp.zeros_like(rows)
    for block_index in range(KC // width):
        wavenumber = block_index * width + lax.broadcasted_iota(jnp.int32, (length, width), 1)
        phase = column_grid * wavenumber % length
        angle = phase.astype(jnp.float32) * (2.0 * math.pi / length)
        cosine = jnp.cos(angle)
        sine = jnp.sin(angle)
        along = block_index * width + jnp.arange(width, dtype=jnp.int32)
        scale = jnp.where(along == 0, 1.0 / length, 2.0 / length)
        weight = jnp.where(along[None, :] < kept[:, None], scale[None, :], 0.0)
        real_part = (
            jnp.einsum("flrn,nk->flrk", rows, cosine, precision=top_wavenumber_kept) * weight
        )
        imaginary_component = (
            jnp.einsum("flrn,nk->flrk", rows, sine, precision=top_wavenumber_kept) * weight
        )
        step_output = (
            step_output
            + jnp.einsum("flrk,nk->flrn", real_part, cosine, precision=top_wavenumber_kept)
            + jnp.einsum("flrk,nk->flrn", imaginary_component, sine, precision=top_wavenumber_kept)
        )
    return step_output


def polar_pass(work_rows, kept_start, kept_table):
    count = work_rows.shape[2] // lax.axis_size("lon")
    kept = lax.dynamic_slice_in_dim(kept_table, kept_start + lax.axis_index("lon") * count, count)
    return lax.all_to_all(
        spectral_filter(
            lax.all_to_all(work_rows, "lon", split_axis=2, concat_axis=3, tiled=True), kept
        ),
        "lon",
        split_axis=3,
        concat_axis=2,
        tiled=True,
    )


def transposed(model_state, diffusion, coupling, cutoff, strip_list, nest_place):
    top_wavenumber_kept = lax.Precision.HIGHEST
    lat_index = lax.axis_index("lat")
    lat_count = lax.axis_size("lat")
    lon_count = lax.axis_size("lon")
    fields, levels, lon_local, lat_local = model_state.shape
    padded = padded_2(model_state, (("lat", 3), ("lon", 2)), 1)
    east_west = padded[:, :, 2:, 1:-1] + padded[:, :, :-2, 1:-1]
    row_place = lax.broadcasted_iota(jnp.int32, (1, 1, 1, lat_local), 3)
    northern = jnp.where((lat_index == 0) & (row_place == 0), 0.0, padded[:, :, 1:-1, :-2])
    southern = jnp.where(
        (lat_index == lat_count - 1) & (row_place == lat_local - 1), 0.0, padded[:, :, 1:-1, 2:]
    )
    blended = jnp.einsum("lfg,glij->flij", coupling, model_state, precision=top_wavenumber_kept)
    updated = (
        model_state
        + diffusion[0] * (east_west - 2.0 * model_state)
        + diffusion[1] * (northern + southern - 2.0 * model_state)
        + blended
    )
    is_south = lat_index == lat_count - 1
    is_polar = (lat_index == 0) | is_south
    start = jnp.where(is_south, lat_local - POLAR, 0).astype(jnp.int32)
    band_base = jnp.where(lat_index < lat_count // 2, 0, POLAR).astype(jnp.int32)
    block_rows = lax.dynamic_slice_in_dim(updated, start, POLAR, 3)
    polar_rows = jnp.transpose(block_rows, (0, 1, 3, 2))
    filtered = polar_pass(polar_rows, band_base, cutoff)
    new_rows = jnp.where(is_polar, jnp.transpose(filtered, (0, 1, 3, 2)), block_rows)
    advanced_state = lax.dynamic_update_slice_in_dim(updated, new_rows, start, 3)
    slots = strip_list.shape[0]
    owners = strip_list[:, 0]
    columns = strip_list[:, 1]
    offsets = strip_list[:, 2]
    lengths = strip_list[:, 3]
    zero = jnp.zeros((), jnp.int32)

    def cut_strip(column, offset):
        return lax.dynamic_slice(
            updated, (zero, zero, column, offset), (fields, levels, 1, STRIP)
        ).reshape(fields * levels, STRIP)

    boundary_strips = jax.vmap(cut_strip)(columns, offsets)
    inside = lax.broadcasted_iota(jnp.int32, (1, 1, STRIP), 2) < lengths[:, None, None]
    boundary_strips = jnp.where(inside, boundary_strips, 0.0).reshape(
        slots, fields * levels * STRIP
    )
    slot_ids = jnp.arange(slots, dtype=jnp.int32)
    earlier = slot_ids[None, :] < slot_ids[:, None]
    same = owners[:, None] == owners[None, :]
    rank = jnp.sum((same & earlier).astype(jnp.int32), axis=1)
    target = owners * CAP + rank
    routing = (jnp.arange(lon_count * CAP, dtype=jnp.int32)[:, None] == target[None, :]).astype(
        jnp.float32
    )
    outgoing = jnp.dot(
        routing, boundary_strips, precision=top_wavenumber_kept, preferred_element_type=jnp.float32
    ).reshape(lon_count, CAP, fields * levels * STRIP)
    arrived = lax.all_to_all(outgoing, "lon", split_axis=0, concat_axis=0, tiled=True)
    total = lon_count * CAP
    group = math.gcd(total, 16)
    pieces = arrived.reshape(total // group, group, fields * levels, STRIP)
    starts = nest_place.reshape(total // group, group)
    point = lax.broadcasted_iota(jnp.int32, (1, 1, NB), 2)
    row_step = lax.broadcasted_iota(jnp.int32, (1, STRIP, 1), 1) * RATIO

    def accumulate(carry, item):
        piece, begin = item
        offset = point - begin[:, None, None]
        hat = jnp.maximum(RATIO - jnp.abs(offset - row_step), 0)
        hat = (
            jnp.where((offset >= 0) & (offset < STRIP * RATIO), hat, 0).astype(jnp.float32) / RATIO
        )
        return (carry + jnp.einsum("gat,gtp->ap", piece, hat, precision=top_wavenumber_kept), None)

    boundary = lax.scan(
        accumulate, jnp.zeros((fields * levels, NB), jnp.float32), (pieces, starts)
    )[0]
    return (advanced_state, boundary.reshape(1, fields, levels, NB))


def local(model_state, *others):
    columns = model_state.shape[2]
    fits = lax.axis_size("lon") * STRIP == POLAR and model_state.shape[3] == 2 * POLAR
    if fits and columns % STEP == 0 and columns >= 2 * HELD:
        return compressed(model_state, *others)
    return transposed(model_state, *others)


def solution(mesh):
    return jax.shard_map(
        local,
        mesh=mesh,
        in_specs=(
            P(None, None, "lon", "lat"),
            P(None, "lat"),
            P(),
            P(),
            P(("lat", "lon"), None),
            P(("lat", "lon"), None, None),
        ),
        out_specs=(P(None, None, "lon", "lat"), P(("lat", "lon"), None, None, None)),
        check_vma=False,
    )
```
